32 devices in a mesh: dp: 8 (over z, y), fsdp: 4 (over x, core).
Axes of the slice: x: 2, y: 2, z: 4, core: 2. Of those that a mesh axis runs over, the one named last changes fastest.
Arguments:
- tokens: bfloat16 [12288, 1024], P(('dp', 'fsdp')), may hold values from -6 to 6
- grad_out: bfloat16 [12288, 1024], P(('dp', 'fsdp')), may hold values from -6 to 6
- image_lengths: int32 [64], replicated, may hold values from 50 to 145, as said below
- image_device: int32 [64], replicated, may hold values from 0 to 31, as said below
- small_map: int32 [50], replicated, may hold values from 0 to 144, as said below
- ln1_gain: bfloat16 [1024], P(('dp', 'fsdp')), may hold values from 0.5 to 1.5
- ln1_bias: bfloat16 [1024], P(('dp', 'fsdp')), may hold values from -2 to 2
- qkv_weight: bfloat16 [1024, 3072], P(('dp', 'fsdp')), may hold values from -0.1875 to 0.1875
- q_bias: bfloat16 [1024], P(('dp', 'fsdp')), may hold values from -2 to 2
- v_bias: bfloat16 [1024], P(('dp', 'fsdp')), may hold values from -2 to 2
- out_weight: bfloat16 [1024, 1024], P(('dp', 'fsdp')), may hold values from -0.75 to 0.75
- out_bias: bfloat16 [1024], P(('dp', 'fsdp')), may hold values from -2 to 2
- ln2_gain: bfloat16 [1024], P(('dp', 'fsdp')), may hold values from 0.5 to 1.5
- ln2_bias: bfloat16 [1024], P(('dp', 'fsdp')), may hold values from -2 to 2
- up_weight: bfloat16 [1024, 4096], P(('dp', 'fsdp')), may hold values from -0.1875 to 0.1875
- up_bias: bfloat16 [4096], P(('dp', 'fsdp')), may hold values from -2 to 2
- down_weight: bfloat16 [4096, 1024], P(('dp', 'fsdp')), may hold values from -0.09375 to 0.09375
- down_bias: bfloat16 [1024], P(('dp', 'fsdp')), may hold values from -2 to 2
- pos_table: bfloat16 [145, 1024], P(None, ('dp', 'fsdp')), may hold values from -3 to 3
Outputs:
- layer_out: bfloat16 [12288, 1024], P(('dp', 'fsdp'))
- tokens_grad: bfloat16 [12288, 1024], P(('dp', 'fsdp'))
- ln1_gain_grad: float32 [1024], P(('dp', 'fsdp'))
- ln1_bias_grad: float32 [1024], P(('dp', 'fsdp'))
- qkv_weight_grad: float32 [1024, 3072], P(('dp', 'fsdp'))
- q_bias_grad: float32 [1024], P(('dp', 'fsdp'))
- v_bias_grad: float32 [1024], P(('dp', 'fsdp'))
- out_weight_grad: float32 [1024, 1024], P(('dp', 'fsdp'))
- out_bias_grad: float32 [1024], P(('dp', 'fsdp'))
- ln2_gain_grad: float32 [1024], P(('dp', 'fsdp'))
- ln2_bias_grad: float32 [1024], P(('dp', 'fsdp'))
- up_weight_grad: float32 [1024, 4096], P(('dp', 'fsdp'))
- up_bias_grad: float32 [4096], P(('dp', 'fsdp'))
- down_weight_grad: float32 [4096, 1024], P(('dp', 'fsdp'))
- down_bias_grad: float32 [1024], P(('dp', 'fsdp'))
- pos_table_grad: float32 [145, 1024], P(None, ('dp', 'fsdp'))
The draws below stay inside these ranges and needn't reach their ends.
Inputs may be any that keep to these rules, and one draw needn't show every extreme that they name: `image_lengths`: each image has 50 or 145 tokens; both occur. `image_device`: every device block holds exactly 2 images. `small_map`: entry 0 is 0, the class token's row.
All inputs are finite; a program needn't handle non-finite values.
Results may differ from the reference program's by a relative error of at most 0.013.
Values may be sent and summed in bfloat16 or wider, within the bound.
No kernel may reach another device: no remote copies, remote signals or barrier semaphores. Data moves between devices by JAX's collectives and lax.ppermute only.
A program may use at most 192 MiB of HBM per device.

```python
import jax
import jax.numpy as jnp
from jax import lax

D = 1024
HEADS = 16
HEAD = 64
FF = 4096
GRID_L = 12
GRID_S = 7
LONG = 145
SHORT = 50
IMG_DEV = 2
TOK_DEV = 384
IMAGES = 64
TOKENS = 12288
N_DP = 8
N_FSDP = 4


def draw_image_lengths(key, part):
    flips = jax.random.randint(key, (IMAGES,), 0, 2)
    lens = jnp.where(flips == 1, LONG, SHORT)
    spots = jnp.arange(IMAGES)
    lens = jnp.where(spots == 0, LONG, jnp.where(spots == 1, SHORT, lens))
    return lens.astype(jnp.int32)


def draw_image_device(key, part):
    order = jax.random.permutation(key, IMAGES)
    return (order // IMG_DEV).astype(jnp.int32)


def draw_small_map(key, part):
    cells = jnp.arange(SHORT - 1)
    across = cells // GRID_S
    along = cells % GRID_S
    jitter = jax.random.randint(key, (2, SHORT - 1), 0, 2)
    row_pick = jnp.where(across == GRID_S - 1, GRID_L - 1, jnp.minimum(across * GRID_L // GRID_S + jitter[0], GRID_L - 1))
    col_pick = jnp.where(along == GRID_S - 1, GRID_L - 1, jnp.minimum(along * GRID_L // GRID_S + jitter[1], GRID_L - 1))
    mapped = 1 + row_pick * GRID_L + col_pick
    return jnp.concatenate([jnp.zeros((1,), jnp.int32), mapped.astype(jnp.int32)])


def level_of(stream_key, extent, split, low, top_value):
    level, own = 1.0, jax.random.fold_in(stream_key, 6)
    for dim, shards_of in split:
        draws = jnp.exp(jax.random.uniform(jax.random.fold_in(own, dim), (shards_of,), jnp.float32, low / len(split), top_value / len(split)))
        level = level * jnp.repeat(draws, extent[dim] // shards_of).reshape([-1 if axis == dim else 1 for axis in range(len(extent))])
    return level


def centred(rng, dims, width, reach, split=(), held_as=jnp.bfloat16):
    values = width * jax.random.normal(rng, dims, jnp.float32)
    if split:
        values = values * level_of(rng, dims, split, -0.22, 0.18)
    return jnp.clip(values, -reach, reach).astype(held_as)


def setup_inputs(seed: int = 0) -> dict:
    key_list = jax.random.split(jax.random.key(seed), 20)
    tokens = centred(key_list[0], (TOKENS, D), 1.0, 6.0, ((0, 32),))
    grad_out = centred(key_list[1], (TOKENS, D), 1.0, 6.0, ((0, 32),))
    image_lengths = draw_image_lengths(jax.random.fold_in(key_list[19], 71), 0)
    image_device = draw_image_device(jax.random.fold_in(key_list[19], 71), 0)
    small_map = draw_small_map(jax.random.fold_in(key_list[19], 71), 0)
    ln1_gain = jnp.clip(1.0 + 0.1 * jax.random.normal(key_list[5], (D,), jnp.float32), 0.5, 1.5).astype(jnp.bfloat16)
    ln1_bias = centred(key_list[6], (D,), 0.3, 2.0, ((0, 32),))
    qkv_weight = centred(key_list[7], (D, 3 * D), D ** -0.5, 0.1875, ((0, 32),))
    q_bias = centred(key_list[8], (D,), 0.3, 2.0, ((0, 32),))
    v_bias = centred(key_list[9], (D,), 0.3, 2.0, ((0, 32),))
    out_weight = centred(key_list[10], (D, D), (D // 16) ** -0.5, 0.75, ((0, 32),))
    out_bias = centred(key_list[11], (D,), 0.3, 2.0, ((0, 32),))
    ln2_gain = jnp.clip(1.0 + 0.1 * jax.random.normal(key_list[12], (D,), jnp.float32), 0.5, 1.5).astype(jnp.bfloat16)
    ln2_bias = centred(key_list[13], (D,), 0.3, 2.0, ((0, 32),))
    up_weight = centred(key_list[14], (D, FF), D ** -0.5, 0.1875, ((0, 32),))
    up_bias = centred(key_list[15], (FF,), 0.3, 2.0, ((0, 32),))
    down_weight = centred(key_list[16], (FF, D), FF ** -0.5, 0.09375, ((0, 32),))
    down_bias = centred(key_list[17], (D,), 0.3, 2.0, ((0, 32),))
    pos_table = centred(key_list[18], (LONG, D), 0.5, 3.0, ((1, 32),))
    return {"tokens": tokens, "grad_out": grad_out, "image_lengths": image_lengths, "image_device": image_device, "small_map": small_map, "ln1_gain": ln1_gain, "ln1_bias": ln1_bias, "qkv_weight": qkv_weight, "q_bias": q_bias, "v_bias": v_bias, "out_weight": out_weight, "out_bias": out_bias, "ln2_gain": ln2_gain, "ln2_bias": ln2_bias, "up_weight": up_weight, "up_bias": up_bias, "down_weight": down_weight, "down_bias": down_bias, "pos_table": pos_table}


EPS = 1e-06
HIGH = lax.Precision.HIGHEST

@jax.custom_vjp
def low(v):
    return lax.optimization_barrier(v.astype(jnp.bfloat16)).astype(jnp.float32)

@jax.custom_vjp
def low_back(v):
    return v

def low_keep(v):
    return (low(v), None)

def low_pass(kept, upstream_gradient):
    return (upstream_gradient,)

def back_keep(v):
    return (v, None)

def back_low(kept, upstream_gradient):
    return (low(upstream_gradient),)
low.defvjp(low_keep, low_pass)
low_back.defvjp(back_keep, back_low)

def layout(image_lengths, image_device, small_map, device):
    mine = image_device == device
    lens = jnp.where(mine, image_lengths, 0).astype(jnp.int32)
    starts = (jnp.cumsum(lens) - lens).astype(jnp.int32)
    rows = jnp.arange(TOK_DEV, dtype=jnp.int32)
    inside = mine[None, :] & (starts[None, :] <= rows[:, None]) & (rows[:, None] < (starts + lens)[None, :])
    number = jnp.arange(IMAGES, dtype=jnp.int32)
    segment = (lax.optimization_barrier(jnp.sum(jnp.where(inside, number[None, :] + 1, 0), axis=1)) - 1).astype(jnp.int32)
    offset = (rows - lax.optimization_barrier(jnp.sum(jnp.where(inside, starts[None, :], 0), axis=1))).astype(jnp.int32)
    length = lax.optimization_barrier(jnp.sum(jnp.where(inside, lens[None, :], 0), axis=1)).astype(jnp.int32)
    spots = jnp.arange(SHORT, dtype=jnp.int32)
    mapped = lax.optimization_barrier(jnp.sum(jnp.where(offset[:, None] == spots[None, :], small_map[None, :], 0), axis=1)).astype(jnp.int32)
    place = jnp.where(length == LONG, offset, jnp.where(length == SHORT, mapped, 0)).astype(jnp.int32)
    return (segment, place)

def layer_norm(v, norm_gain, shift_bias):
    centred_rows = v - lax.optimization_barrier(jnp.mean(v, axis=1, keepdims=True))
    return centred_rows * lax.rsqrt(lax.optimization_barrier(jnp.mean(centred_rows * centred_rows, axis=1, keepdims=True)) + EPS) * norm_gain + shift_bias

def block(xb, place, segment, params):
    first_gain, first_centred, wqkv, bq, bv, wo, bo, second_gain, second_centred, w1, bf1, w2, bf2, pos = params
    rows = xb.shape[0]
    activation_rows = xb + jnp.take(pos, place, axis=0)
    first_normed = low(layer_norm(activation_rows, first_gain, first_centred))
    bias3 = jnp.concatenate([bq, jnp.zeros((D,), jnp.float32), bv])
    qkv = low_back(low(jnp.dot(first_normed, wqkv, precision=HIGH) + bias3))
    q = qkv[:, :D].reshape(rows, HEADS, HEAD)
    k = qkv[:, D:2 * D].reshape(rows, HEADS, HEAD)
    v = qkv[:, 2 * D:].reshape(rows, HEADS, HEAD)
    scores = low_back(jnp.einsum('thd,shd->hts', q, k, precision=HIGH) * HEAD ** (-0.5))
    same = segment[:, None] == segment[None, :]
    scores = jnp.where(same[None], scores, -1000000000.0)
    probs = low(jax.nn.softmax(scores, axis=2))
    o = jnp.einsum('hts,shd->thd', probs, v, precision=HIGH).reshape(rows, D)
    o = low_back(low(o))
    z = low_back(jnp.dot(o, wo, precision=HIGH) + bo)
    second_activation = activation_rows + z
    second_normed = low(layer_norm(second_activation, second_gain, second_centred))
    hpre = low_back(jnp.dot(second_normed, w1, precision=HIGH) + bf1)
    act = low(jax.nn.gelu(hpre, approximate=False))
    return second_activation + jnp.dot(act, w2, precision=HIGH) + bf2

def reference(tokens, grad_out, image_lengths, image_device, small_map, ln1_gain, ln1_bias, qkv_weight, q_bias, v_bias, out_weight, out_bias, ln2_gain, ln2_bias, up_weight, up_bias, down_weight, down_bias, pos_table):
    params = tuple((p.astype(jnp.float32) for p in (ln1_gain, ln1_bias, qkv_weight, q_bias, v_bias, out_weight, out_bias, ln2_gain, ln2_bias, up_weight, up_bias, down_weight, down_bias, pos_table)))
    devices = jnp.arange(N_DP * N_FSDP, dtype=jnp.int32)
    segment, place = lax.map(lambda d: layout(image_lengths, image_device, small_map, d), devices)
    xs = tokens.astype(jnp.float32).reshape(N_DP * N_FSDP, TOK_DEV, D)

    def forward(xs, params):
        step = jax.checkpoint(lambda item: block(item[0], item[1], item[2], params))
        return lax.map(step, (xs, place, segment))
    outputs, pull = jax.vjp(forward, xs, params)
    valid = (segment >= 0).astype(jnp.float32)[:, :, None]
    cotangent = grad_out.astype(jnp.float32).reshape(N_DP * N_FSDP, TOK_DEV, D) * valid
    dxs, grads = pull(cotangent)
    return (outputs.reshape(TOKENS, D).astype(jnp.bfloat16), dxs.reshape(TOKENS, D).astype(jnp.bfloat16), grads[0], grads[1], grads[2], grads[3], grads[4], grads[5], grads[6], grads[7], grads[8], grads[9], grads[10], grads[11], grads[12], grads[13])
```

```python
import jax
import jax.numpy as jnp
import numpy as np
from jax import lax
from jax.experimental import pallas as pl
from jax.experimental.pallas import tpu as pltpu
from jax.sharding import PartitionSpec as P

D = 1024
HEADS = 16
HEAD = 64
FF = 4096
LONG = 145
SHORT = 50


EPS = 1e-06


def fetch(parts):
    whole = (
        lax.all_gather(parts[0], ("dp", "fsdp"), axis=1, tiled=True),
        lax.all_gather(parts[1], ("dp", "fsdp"), axis=0, tiled=True),
        lax.all_gather(parts[2], ("dp", "fsdp"), axis=0, tiled=True),
        lax.all_gather(parts[3], ("dp", "fsdp"), axis=0, tiled=True),
        lax.all_gather(parts[4], ("dp", "fsdp"), axis=0, tiled=True),
        lax.all_gather(parts[5], ("dp", "fsdp"), axis=0, tiled=True),
        lax.all_gather(parts[6], ("dp", "fsdp"), axis=1, tiled=True),
    )
    return whole


def reduce_grads(parts):
    owned = (
        lax.psum_scatter(parts[0], ("dp", "fsdp"), scatter_dimension=1, tiled=True),
        lax.psum_scatter(parts[1], ("dp", "fsdp"), scatter_dimension=0, tiled=True),
        lax.psum_scatter(parts[2], ("dp", "fsdp"), scatter_dimension=0, tiled=True),
        lax.psum_scatter(parts[3], ("dp", "fsdp"), scatter_dimension=0, tiled=True),
        lax.psum_scatter(parts[4], ("dp", "fsdp"), scatter_dimension=0, tiled=True),
        lax.psum_scatter(parts[5], ("dp", "fsdp"), scatter_dimension=0, tiled=True),
        lax.psum_scatter(parts[6], ("dp", "fsdp"), scatter_dimension=1, tiled=True),
    )
    return owned


def layout(image_lengths, image_device, small_map, device, rows_dev):
    mine = image_device == device
    lens = jnp.where(mine, image_lengths, 0)
    starts = jnp.cumsum(lens) - lens
    rows = jnp.arange(rows_dev, dtype=jnp.int32)
    inside = (
        mine[None, :]
        & (starts[None, :] <= rows[:, None])
        & (rows[:, None] < (starts + lens)[None, :])
    )
    number = jnp.arange(image_lengths.shape[0], dtype=jnp.int32)
    segment = jnp.sum(jnp.where(inside, number[None, :] + 1, 0), axis=1) - 1
    offset = rows - jnp.sum(jnp.where(inside, starts[None, :], 0), axis=1)
    length = jnp.sum(jnp.where(inside, lens[None, :], 0), axis=1)
    spots = jnp.arange(SHORT, dtype=jnp.int32)
    mapped = jnp.sum(jnp.where(offset[:, None] == spots[None, :], small_map[None, :], 0), axis=1)
    place = jnp.where(length == LONG, offset, jnp.where(length == SHORT, mapped, 0))
    return (segment, place)


def layer_norm_forward_pass(v, norm_gain, shift_bias):
    centred_rows = v - jnp.mean(v, axis=1, keepdims=True)
    inverse_deviation = lax.rsqrt(
        jnp.mean(centred_rows * centred_rows, axis=1, keepdims=True) + EPS
    )
    normalized_rows = centred_rows * inverse_deviation
    return (normalized_rows * norm_gain + shift_bias, normalized_rows, inverse_deviation)


def layer_norm_backward_pass(upstream_gradient, normalized_rows, inverse_deviation, norm_gain):
    normalized_gradient = upstream_gradient * norm_gain
    first_input = jnp.mean(normalized_gradient, axis=1, keepdims=True)
    second_input = jnp.mean(normalized_gradient * normalized_rows, axis=1, keepdims=True)
    return (
        inverse_deviation * (normalized_gradient - first_input - normalized_rows * second_input),
        jnp.sum(upstream_gradient * normalized_rows, axis=0),
        jnp.sum(upstream_gradient, axis=0),
    )


def split_heads(values, groups):
    return values.reshape(values.shape[0], groups, HEADS // groups, HEAD).transpose(1, 0, 2, 3)


def join_heads(values):
    return values.transpose(1, 0, 2, 3).reshape(values.shape[1], D)


def masked_scores(query, keys, same):
    scores = jnp.einsum("thd,shd->hts", query, keys, preferred_element_type=jnp.float32) * HEAD ** (
        -0.5
    )
    return jnp.where(same[None], scores, -1000000000.0)


def attend_forward(qkvb, same):
    groups = HEADS // 4
    query = split_heads(qkvb[:, :D], groups)
    keys = split_heads(qkvb[:, D : 2 * D], groups)
    values = split_heads(qkvb[:, 2 * D :], groups)

    def one_group(item):
        scores = masked_scores(item[0], item[1], same)
        top = jnp.max(scores, axis=2, keepdims=True)
        lse = top + jnp.log(jnp.sum(jnp.exp(scores - top), axis=2, keepdims=True))
        probs = jnp.exp(scores - lse).astype(jnp.bfloat16)
        attended = jnp.einsum("hts,shd->thd", probs, item[2], preferred_element_type=jnp.float32)
        return (attended, lse[:, :, 0])

    attended, lse = lax.map(one_group, (query, keys, values))
    return (join_heads(attended), lse)


def attend_backward(qkvb, dob, lse, same):
    groups = HEADS // 4
    query = split_heads(qkvb[:, :D], groups)
    keys = split_heads(qkvb[:, D : 2 * D], groups)
    values = split_heads(qkvb[:, 2 * D :], groups)
    douts = split_heads(dob, groups)

    def one_group(item):
        scores = masked_scores(item[0], item[1], same)
        probs = jnp.exp(scores - item[4][:, :, None])
        dvalue = jnp.einsum(
            "hts,thd->shd", probs.astype(jnp.bfloat16), item[3], preferred_element_type=jnp.float32
        )
        dprobs = jnp.einsum("thd,shd->hts", item[3], item[2], preferred_element_type=jnp.float32)
        inner = jnp.sum(probs * dprobs, axis=2, keepdims=True)
        dscore = (probs * (dprobs - inner)).astype(jnp.bfloat16)
        dquery = jnp.einsum(
            "hts,shd->thd", dscore, item[1], preferred_element_type=jnp.float32
        ) * HEAD ** (-0.5)
        dkey = jnp.einsum(
            "hts,thd->shd", dscore, item[0], preferred_element_type=jnp.float32
        ) * HEAD ** (-0.5)
        return (dquery, dkey, dvalue)

    dquery, dkey, dvalue = lax.map(one_group, (query, keys, values, douts, lse))
    return jnp.concatenate([join_heads(dquery), join_heads(dkey), join_heads(dvalue)], axis=1)


def gelu_slope(x):
    return (
        0.5 * (1.0 + jax.scipy.special.erf(x * 0.7071067811865476))
        + x * jnp.exp(-0.5 * x * x) * 0.3989422804014327
    )


def on_device(
    tokens,
    grad_out,
    image_lengths,
    image_device,
    small_map,
    ln1_gain,
    ln1_bias,
    qkv_weight,
    q_bias,
    v_bias,
    out_weight,
    out_bias,
    ln2_gain,
    ln2_bias,
    up_weight,
    up_bias,
    down_weight,
    down_bias,
    pos_table,
):
    rows_dev = tokens.shape[0]
    device = lax.axis_index("dp") * lax.axis_size("fsdp") + lax.axis_index("fsdp")
    segment, place = layout(image_lengths, image_device, small_map, device, rows_dev)
    same = segment[:, None] == segment[None, :]
    valid = (segment >= 0).astype(jnp.float32)[:, None]
    table_rows = jnp.arange(LONG, dtype=jnp.int32)
    picker = place[:, None] == table_rows[None, :]
    vectors = jnp.stack(
        [ln1_gain, ln1_bias, q_bias, v_bias, out_bias, ln2_gain, ln2_bias, down_bias]
    )
    shards = (vectors, qkv_weight, out_weight, up_weight, up_bias, down_weight, pos_table)
    whole = fetch(shards)
    vec = whole[0].astype(jnp.float32)
    first_gain, first_centred, bq, bv, bo, second_gain, second_centred, bf2 = (
        vec[0],
        vec[1],
        vec[2],
        vec[3],
        vec[4],
        vec[5],
        vec[6],
        vec[7],
    )
    bf1 = whole[4].astype(jnp.float32)
    activation_rows = tokens.astype(jnp.float32) + jnp.dot(
        picker.astype(jnp.bfloat16), whole[6], preferred_element_type=jnp.float32
    )
    first_normed, first_normalized, first_inverse_deviation = layer_norm_forward_pass(
        activation_rows, first_gain, first_centred
    )
    n1b = first_normed.astype(jnp.bfloat16)
    bias3 = jnp.concatenate([bq, jnp.zeros_like(bq), bv])
    qkvb = (jnp.dot(n1b, whole[1], preferred_element_type=jnp.float32) + bias3).astype(jnp.bfloat16)
    attended, lse = attend_forward(qkvb, same)
    ob = attended.astype(jnp.bfloat16)
    second_activation = (
        activation_rows + jnp.dot(ob, whole[2], preferred_element_type=jnp.float32) + bo
    )
    second_normed, second_normalized, second_inverse_deviation = layer_norm_forward_pass(
        second_activation, second_gain, second_centred
    )
    n2b = second_normed.astype(jnp.bfloat16)
    hpre = jnp.dot(n2b, whole[3], preferred_element_type=jnp.float32) + bf1
    actb = jax.nn.gelu(hpre, approximate=False).astype(jnp.bfloat16)
    output = second_activation + jnp.dot(actb, whole[5], preferred_element_type=jnp.float32) + bf2
    layer_out = output.astype(jnp.bfloat16)
    dy = grad_out.astype(jnp.float32) * valid
    fenced, dy = lax.optimization_barrier((shards, dy))
    back = fetch(fenced)
    dyb = dy.astype(jnp.bfloat16)
    d_down = jnp.einsum("tf,td->fd", actb, dyb, preferred_element_type=jnp.float32)
    d_down_bias = jnp.sum(dy, axis=0)
    dgate = jnp.einsum("td,fd->tf", dyb, back[5], preferred_element_type=jnp.float32)
    dhb = (dgate * gelu_slope(hpre)).astype(jnp.bfloat16)
    d_up = jnp.einsum("td,tf->df", n2b, dhb, preferred_element_type=jnp.float32)
    d_up_bias = jnp.sum(dhb.astype(jnp.float32), axis=0)
    second_norm_gradient = jnp.einsum("tf,df->td", dhb, back[3], preferred_element_type=jnp.float32)
    second_activation_norm_gradient, second_gain_gradient, second_centred_gradient = (
        layer_norm_backward_pass(
            second_norm_gradient, second_normalized, second_inverse_deviation, second_gain
        )
    )
    da2 = dy + second_activation_norm_gradient
    dzb = da2.astype(jnp.bfloat16)
    d_out = jnp.einsum("te,td->ed", ob, dzb, preferred_element_type=jnp.float32)
    d_out_bias = jnp.sum(dzb.astype(jnp.float32), axis=0)
    dob = jnp.einsum("td,ed->te", dzb, back[2], preferred_element_type=jnp.float32).astype(
        jnp.bfloat16
    )
    dqkvb = attend_backward(qkvb, dob, lse, same).astype(jnp.bfloat16)
    d_qkv = jnp.einsum("td,te->de", n1b, dqkvb, preferred_element_type=jnp.float32)
    dqkv_sum = jnp.sum(dqkvb.astype(jnp.float32), axis=0)
    first_norm_gradient = jnp.einsum(
        "te,de->td", dqkvb, back[1], preferred_element_type=jnp.float32
    )
    first_activation_gradient, first_gain_gradient, first_centred_gradient = (
        layer_norm_backward_pass(
            first_norm_gradient, first_normalized, first_inverse_deviation, first_gain
        )
    )
    da = da2 + first_activation_gradient
    tokens_grad = da.astype(jnp.bfloat16)
    d_pos = jnp.dot(picker.astype(jnp.float32).T, da, precision=lax.Precision.HIGHEST)
    d_vectors = jnp.stack(
        [
            first_gain_gradient,
            first_centred_gradient,
            dqkv_sum[:D],
            dqkv_sum[2 * D :],
            d_out_bias,
            second_gain_gradient,
            second_centred_gradient,
            d_down_bias,
        ]
    )
    flat_parts = (
        d_vectors,
        d_qkv.reshape(-1, 128),
        d_out.reshape(-1, 128),
        d_up.reshape(-1, 128),
        d_up_bias,
        d_down,
        d_pos,
    )
    owned = reduce_grads(flat_parts)
    gv = owned[0]
    qkv_owned = owned[1].reshape(-1, 3 * D)
    out_owned = owned[2].reshape(-1, D)
    up_owned = owned[3].reshape(-1, FF)
    return (
        layer_out,
        tokens_grad,
        gv[0],
        gv[1],
        qkv_owned,
        gv[2],
        gv[3],
        out_owned,
        gv[4],
        gv[5],
        gv[6],
        up_owned,
        owned[4],
        owned[5],
        gv[7],
        owned[6],
    )


BF = jnp.bfloat16
F32 = jnp.float32
AXES = ("dp", "fsdp")
CORE, XBIT, YBIT, ZBIT = 1, 2, 4, 8


def swap(value, mask):
    return lax.ppermute(value, AXES, [(i, i ^ mask) for i in range(32)])


def coords():
    dp = lax.axis_index("dp")
    fs = lax.axis_index("fsdp")
    return dp // 2, dp % 2, fs // 2, fs % 2


def chip_of(rel):
    z, y, x, _ = coords()
    dz, dy, dx = rel
    bits = 0
    for part, off, width in ((z // 2, dz // 2, 8), (z % 2, dz % 2, 4), (y, dy, 2), (x, dx, 1)):
        bits = bits + (1 - part if off else part) * width
    return bits


ENTRIES_ZXY = (
    [(0, (k,), h, (k, 0, 0), h) for k in range(4) for h in range(2)]
    + [(1, (k,), h, (k, 0, 1), h) for k in range(4) for h in range(2)]
    + [(2, (k,), h, (k, 1, 0), h) for k in range(4) for h in range(2)]
    + [(3, (k,), h, (k, 1, 1), h) for k in range(2) for h in range(2)]
    + [(4, (k,), h, (k + 2, 1, 1), h) for k in range(2) for h in range(2)]
)
QUADS = (((0, 0), 0), ((0, 1), 0), ((0, 0), 1), ((1, 0), 1))
SIDE_A = ((1, 0), (1, 1))
SIDE_B = ((0, 1), (1, 1))
ENTRIES_XZY_GATHER = (
    [(k, (q,), 0, (k,) + QUADS[q][0], QUADS[q][1]) for k in range(4) for q in range(4)]
    + [(4, (k, q), 0, (k,) + SIDE_A[q], 0) for k in range(4) for q in range(2)]
    + [(5, (k, q), 0, (k,) + SIDE_B[q], 1) for k in range(4) for q in range(2)]
)
ENTRIES_XZY_SCATTER = (
    [(0, (k, q), 0, (k,) + QUADS[q][0], QUADS[q][1]) for k in range(4) for q in range(4)]
    + [(1, (k, q), 0, (k,) + SIDE_A[q], 0) for k in range(4) for q in range(2)]
    + [(2, (k, q), 0, (k,) + SIDE_B[q], 1) for k in range(4) for q in range(2)]
)


def gather_zxy(block):
    line = jnp.stack([block] + [swap(block, ZBIT * k) for k in range(1, 4)])
    from_x = swap(line, XBIT)
    from_y = swap(line, YBIT)
    corner_a = swap(from_x[:2], YBIT)
    corner_b = swap(from_y[2:], XBIT)
    return [line, from_x, from_y, corner_a, corner_b], ENTRIES_ZXY


def gather_xzy(block):
    half_a, half_b = block[:32], block[32:]
    quad = jnp.stack([half_a, swap(half_a, XBIT), half_b, swap(half_b, YBIT)])
    quads = [quad] + [swap(quad, ZBIT * k) for k in range(1, 4)]
    side_a = swap(jnp.stack([q[:2] for q in quads]), YBIT)
    side_b = swap(jnp.stack([q[2:] for q in quads]), XBIT)
    return quads + [side_a, side_b], ENTRIES_XZY_GATHER


def add(*values):
    total = values[0].astype(F32)
    for value in values[1:]:
        total = total + value.astype(F32)
    return total


def scatter_zxy(parts):
    line, to_x, to_y, corner_a, corner_b = parts
    got_a = swap(corner_a, XBIT)
    got_b = swap(corner_b, YBIT)
    to_x = jnp.concatenate([to_x[:2], add(to_x[2:], got_b).astype(BF)])
    to_y = jnp.concatenate([add(to_y[:2], got_a).astype(BF), to_y[2:]])
    got_x = swap(to_x, XBIT)
    got_y = swap(to_y, YBIT)
    sums = [add(line[k], got_x[k], got_y[k]) for k in range(4)]
    got_z = [swap(sums[k].astype(BF), ZBIT * k) for k in range(1, 4)]
    return add(sums[0], *got_z)


def scatter_xzy(parts):
    keep, side_a, side_b = parts
    got_a = swap(side_a, YBIT)
    got_b = swap(side_b, XBIT)
    quads = [add(keep[k], jnp.concatenate([got_a[k], got_b[k]])) for k in range(4)]
    got_z = [swap(quads[k].astype(BF), ZBIT * k) for k in range(1, 4)]
    quad = add(quads[0], *got_z)
    got_x = swap(quad[1].astype(BF), XBIT)
    got_y = swap(quad[3].astype(BF), YBIT)
    return jnp.concatenate([add(quad[0], got_x), add(quad[2], got_y)])


def shapes_for(kind, width):
    if kind == "zxy":
        return [(4, 64, width)] * 3 + [(2, 64, width)] * 2, ENTRIES_ZXY
    return [(4, 4, 32, width), (4, 2, 32, width), (4, 2, 32, width)], ENTRIES_XZY_SCATTER


def piece_of(ref, entry, lanes):
    _, index, row, _, _ = entry
    return ref.at[index + (pl.ds(32 * row, 32), pl.ds(*lanes))]


def run_copies(copies, sems):
    started = []
    for i, (src, dst) in enumerate(copies):
        copy = pltpu.make_async_copy(src, dst, sems.at[i])
        copy.start()
        started.append(copy)
    for copy in started:
        copy.wait()


def mover(sources, out_shapes, plan, count, inward):
    n_in, n_out = len(sources), len(out_shapes)

    def kernel(*refs):
        run_copies(plan(refs[:n_in], refs[n_in : n_in + n_out]), refs[-1])

    size = sum(int(np.prod(s)) for s in out_shapes) * 2
    return pl.pallas_call(
        kernel,
        out_shape=[jax.ShapeDtypeStruct(s, BF) for s in out_shapes],
        in_specs=[pl.BlockSpec(memory_space=pl.ANY if inward else pltpu.VMEM)] * n_in,
        out_specs=[pl.BlockSpec(memory_space=pltpu.VMEM if inward else pl.ANY)] * n_out,
        scratch_shapes=[pltpu.SemaphoreType.DMA((count,))],
        cost_estimate=pl.CostEstimate(flops=0, bytes_accessed=2 * size, transcendentals=0),
        compiler_params=pltpu.CompilerParams(vmem_limit_bytes=24 << 20),
    )(*sources)


def rows_of(rel, half):
    core = coords()[3]
    side = core if half == 0 else 1 - core
    return pl.multiple_of(chip_of(rel) * 64 + side * 32, 32)


SMALL = 384
QKV_OWN = 1536
HALF_D = 512
A_WIDTH = SMALL + QKV_OWN + HALF_D


def places_a(small, qkv, out, entry):
    rel, half = entry[3], entry[4]
    row = rows_of(rel, half)
    return [
        ((0, SMALL), small.at[pl.ds(row, 32), :]),
        ((SMALL, QKV_OWN), qkv.at[pl.ds(row, 32), :]),
        (
            (SMALL + QKV_OWN, HALF_D),
            out.at[chip_of(rel), :, pl.ds(HALF_D * half, HALF_D)],
        ),
    ]


def places_up(up, entry):
    return [((0, 2048), up.at[pl.ds(rows_of(entry[3], entry[4]), 32), :])]


def places_down(down, entry):
    rel, half = entry[3], entry[4]
    row = pl.multiple_of(chip_of(rel) * 128 + 32 * half, 32)
    return [
        ((0, D), down.at[pl.ds(row, 32), :]),
        ((D, D), down.at[pl.ds(row + 64, 32), :]),
    ]


A_SHAPES = [(D, SMALL), (D, QKV_OWN), (16, 32, D)]


def assemble(gathered, places, out_shapes):
    arrays, entries = gathered

    def plan(ins, outs):
        copies = []
        for entry in entries:
            for lanes, dst in places(*outs, entry):
                copies.append((piece_of(ins[entry[0]], entry, lanes), dst))
        return copies

    return mover(arrays, out_shapes, plan, len(entries) * 3, True)


def disassemble(wholes, places, kind, width):
    shapes, entries = shapes_for(kind, width)

    def plan(ins, outs):
        copies = []
        for entry in entries:
            for lanes, src in places(*ins, entry):
                copies.append((src, piece_of(outs[entry[0]], entry, lanes)))
        return copies

    return mover(wholes, shapes, plan, len(entries) * 3, False)


def softmax_parts(query, keys, same):
    scores = lax.dot_general(query, keys, (((1,), (1,)), ((), ())), preferred_element_type=F32)
    scores = jnp.where(same, scores * HEAD ** (-0.5), -1000000000.0)
    top = jnp.max(scores, axis=1, keepdims=True)
    powers = jnp.exp(scores - top)
    return powers / jnp.sum(powers, axis=1, keepdims=True)


def lane_masks(rows):
    lane = lax.broadcasted_iota(jnp.int32, (rows, 128), 1)
    return lane < 64


def attend_kernel(q_ref, k_ref, v_ref, col_ref, row_ref, o_ref):
    same = col_ref[...] == row_ref[0]
    first = lane_masks(q_ref.shape[0])
    q, k, v = q_ref[...], k_ref[...], v_ref[...]
    zero = jnp.zeros_like(q)
    outs = []
    for h in range(2):
        mask = first if h == 0 else ~first
        probs = softmax_parts(jnp.where(mask, q, zero), k, same).astype(BF)
        outs.append(jnp.dot(probs, v, preferred_element_type=F32))
    o_ref[...] = jnp.where(first, outs[0], outs[1]).astype(BF)


def attend_back_kernel(q_ref, k_ref, v_ref, g_ref, col_ref, row_ref, dq_ref, dk_ref, dv_ref):
    same = col_ref[...] == row_ref[0]
    first = lane_masks(q_ref.shape[0])
    q, k, v, g = q_ref[...], k_ref[...], v_ref[...], g_ref[...]
    zero = jnp.zeros_like(q)
    dq, dk, dv = [], [], []
    over_rows = (((0,), (0,)), ((), ()))
    for h in range(2):
        mask = first if h == 0 else ~first
        probs = softmax_parts(jnp.where(mask, q, zero), k, same)
        dv.append(lax.dot_general(probs.astype(BF), g, over_rows, preferred_element_type=F32))
        dprobs = lax.dot_general(
            jnp.where(mask, g, zero), v, (((1,), (1,)), ((), ())), preferred_element_type=F32
        )
        inner = jnp.sum(probs * dprobs, axis=1, keepdims=True)
        ds = (probs * (dprobs - inner)).astype(BF)
        dq.append(jnp.dot(ds, k, preferred_element_type=F32))
        dk.append(lax.dot_general(ds, q, over_rows, preferred_element_type=F32))
    scale = HEAD ** (-0.5)
    dq_ref[...] = (jnp.where(first, dq[0], dq[1]) * scale).astype(BF)
    dk_ref[...] = (jnp.where(first, dk[0], dk[1]) * scale).astype(BF)
    dv_ref[...] = jnp.where(first, dv[0], dv[1]).astype(BF)


def attend(qkv, seg):
    rows = qkv.shape[0] // 2
    col, row = seg[:, None], seg.reshape(2, 1, rows)
    part = lambda off: pl.BlockSpec((rows, 128), lambda i, j: (i, j + off))
    return pl.pallas_call(
        attend_kernel,
        grid=(2, 4),
        in_specs=[
            part(0),
            part(4),
            part(8),
            pl.BlockSpec((rows, 1), lambda i, j: (i, 0)),
            pl.BlockSpec((1, 1, rows), lambda i, j: (i, 0, 0)),
        ],
        out_specs=part(0),
        out_shape=jax.ShapeDtypeStruct((2 * rows, 512), BF),
        cost_estimate=pl.CostEstimate(flops=int(1.5e9), bytes_accessed=4000000, transcendentals=2400000),
        compiler_params=pltpu.CompilerParams(vmem_limit_bytes=40 << 20),
    )(qkv, qkv, qkv, col, row)


def attend_back(qkv, grad, seg):
    rows = qkv.shape[0] // 2
    col, row = seg[:, None], seg.reshape(2, 1, rows)
    part = lambda off: pl.BlockSpec((rows, 128), lambda i, j: (i, j + off))
    return pl.pallas_call(
        attend_back_kernel,
        grid=(2, 4),
        in_specs=[
            part(0),
            part(4),
            part(8),
            part(0),
            pl.BlockSpec((rows, 1), lambda i, j: (i, 0)),
            pl.BlockSpec((1, 1, rows), lambda i, j: (i, 0, 0)),
        ],
        out_specs=[part(0)] * 3,
        out_shape=[jax.ShapeDtypeStruct((2 * rows, 512), BF)] * 3,
        cost_estimate=pl.CostEstimate(flops=int(3e9), bytes_accessed=6000000, transcendentals=2400000),
        compiler_params=pltpu.CompilerParams(vmem_limit_bytes=40 << 20),
    )(qkv, qkv, qkv, grad, col, row)


def pick_blocks(value, which):
    n = value.shape[1] // 256
    even = jnp.concatenate([value[:, 256 * j : 256 * j + 128] for j in range(n)], axis=1)
    odd = jnp.concatenate([value[:, 256 * j + 128 : 256 * j + 256] for j in range(n)], axis=1)
    return jnp.where(which == 0, even, odd)


def weave_blocks(own, other, core):
    even = jnp.where(core == 0, own, other)
    odd = jnp.where(core == 0, other, own)
    n = own.shape[1] // 128
    parts = []
    for j in range(n):
        parts += [even[:, 128 * j : 128 * (j + 1)], odd[:, 128 * j : 128 * (j + 1)]]
    return jnp.concatenate(parts, axis=1)


def swap_halves(value):
    half = value.shape[0] // 2
    return jnp.concatenate([value[half:], value[:half]])


def fast_on_device(
    tokens,
    grad_out,
    image_lengths,
    image_device,
    small_map,
    ln1_gain,
    ln1_bias,
    qkv_weight,
    q_bias,
    v_bias,
    out_weight,
    out_bias,
    ln2_gain,
    ln2_bias,
    up_weight,
    up_bias,
    down_weight,
    down_bias,
    pos_table,
):
    rows = tokens.shape[0]
    core = coords()[3]
    device = lax.axis_index("dp") * 4 + lax.axis_index("fsdp")
    seg, place = layout(image_lengths, image_device, small_map, device, rows)
    seg2, place2 = layout(image_lengths, image_device, small_map, device ^ 1, rows)
    seg = jnp.concatenate([seg, seg2])
    place = jnp.concatenate([place, place2])
    valid = (seg >= 0).astype(F32)[:, None]
    picker = place[:, None] == jnp.arange(256, dtype=jnp.int32)[None, :]

    vectors = jnp.stack([ln1_gain, ln1_bias, q_bias, v_bias, out_bias, ln2_gain, ln2_bias, down_bias])
    small = jnp.concatenate([pos_table, vectors, jnp.zeros((103, 32), BF)]).T
    small = jnp.concatenate(
        [small, jnp.concatenate([up_bias[None, :], jnp.zeros((31, 128), BF)])], axis=1
    )
    keep = jnp.concatenate([small, pick_blocks(qkv_weight, core), pick_blocks(up_weight, core)], axis=1)
    send = jnp.concatenate(
        [small, pick_blocks(qkv_weight, 1 - core), pick_blocks(up_weight, 1 - core)], axis=1
    )
    got = swap(send, CORE)
    both = jnp.concatenate([keep, got])
    toks = jnp.concatenate([tokens, swap(tokens, CORE)])
    gout = jnp.concatenate([grad_out, swap(grad_out, CORE)])
    cut = SMALL + QKV_OWN
    out_part = jnp.concatenate([out_weight[:, :HALF_D], out_weight[:, HALF_D:]])
    chunk_a = jnp.concatenate([both[:, :cut], out_part], axis=1)
    chunk_u = both[:, cut:]
    chunk_d = jnp.concatenate([down_weight[:64], down_weight[64:]], axis=1)

    small_all, w_qkv, out_own = assemble(gather_zxy(chunk_a), places_a, A_SHAPES)
    (w_up,) = assemble(gather_zxy(chunk_u), places_up, [(D, 2048)])
    (w_down,) = assemble(gather_xzy(chunk_d), places_down, [(2048, D)])
    out_other = swap(out_own, CORE)

    def own_heads(value):
        return lax.dynamic_index_in_dim(value.reshape(4, 2, 2, 32, D), core, 1, False)

    mine, other = own_heads(out_own), own_heads(out_other)
    w_out = jnp.concatenate(
        [jnp.where(core == 0, mine, other), jnp.where(core == 0, other, mine)], axis=2
    ).reshape(512, D)

    vec = small_all[:, 145:153].T.astype(F32)
    gain1, shift1, bq, bv, bo, gain2, shift2, bf2 = (vec[i] for i in range(8))
    bf1 = small_all.reshape(16, 2, 32, SMALL)[:, :, 0, 256:]
    bf1 = lax.dynamic_index_in_dim(bf1, core, 1, False).reshape(2048).astype(F32)
    own_cols = lambda v: lax.dynamic_index_in_dim(v.reshape(4, 2, 128), core, 1, False).reshape(512)
    bias3 = jnp.concatenate([own_cols(bq), jnp.zeros((512,), F32), own_cols(bv)])

    a = toks.astype(F32) + lax.dot_general(
        picker.astype(BF), small_all[:, :256], (((1,), (1,)), ((), ())), preferred_element_type=F32
    )
    n1, hat1, inv1 = layer_norm_forward_pass(a, gain1, shift1)
    n1b = n1.astype(BF)
    qkvb = (jnp.dot(n1b, w_qkv, preferred_element_type=F32) + bias3).astype(BF)
    ob = attend(qkvb, seg)
    z_part = jnp.dot(ob, w_out, preferred_element_type=F32)
    z = z_part + swap_halves(swap(z_part.astype(BF), CORE)).astype(F32)
    a2 = a + z + bo
    n2, hat2, inv2 = layer_norm_forward_pass(a2, gain2, shift2)
    n2b = n2.astype(BF)
    hpre = jnp.dot(n2b, w_up, preferred_element_type=F32) + bf1
    actb = jax.nn.gelu(hpre, approximate=False).astype(BF)
    slope = gelu_slope(hpre)
    dy = gout.astype(F32) * valid
    dyb = dy.astype(BF)
    d_down = jnp.einsum("tf,td->fd", actb, dyb, preferred_element_type=F32).astype(BF)
    down_sum = scatter_xzy(disassemble([d_down], places_down, "xzy", 2048))

    y_part = jnp.dot(actb, w_down, preferred_element_type=F32)
    y = y_part[:rows] + swap(y_part[rows:].astype(BF), CORE).astype(F32)
    layer_out = (a2[:rows] + y + bf2).astype(BF)

    dgate = jnp.einsum("td,fd->tf", dyb, w_down, preferred_element_type=F32)
    dhb = (dgate * slope).astype(BF)
    d_up = jnp.einsum("td,tf->df", n2b, dhb, preferred_element_type=F32).astype(BF)
    up_sum = scatter_zxy(disassemble([d_up], places_up, "zxy", 2048))
    d_up_bias = jnp.sum(dhb.astype(F32), axis=0)
    dn2_part = jnp.einsum("tf,df->td", dhb, w_up, preferred_element_type=F32)
    dn2 = dn2_part + swap_halves(swap(dn2_part.astype(BF), CORE)).astype(F32)
    back2, _, _ = layer_norm_backward_pass(dn2, hat2, inv2, gain2)
    d_gain2 = jnp.sum(dn2[:rows] * hat2[:rows], axis=0)
    d_shift2 = jnp.sum(dn2[:rows], axis=0)
    da2 = dy + back2
    dzb = da2.astype(BF)
    d_out_bias = jnp.sum(dzb[:rows].astype(F32), axis=0)
    d_out = jnp.einsum("te,td->ed", ob, dzb, preferred_element_type=F32).astype(BF)
    dob = jnp.einsum("td,ed->te", dzb, w_out, preferred_element_type=F32).astype(BF)
    d_out = d_out.reshape(4, 2, 2, 32, D)
    mine = lax.dynamic_index_in_dim(d_out, core, 2, False)
    other = swap(lax.dynamic_index_in_dim(d_out, 1 - core, 2, False), CORE)
    d_out = jnp.stack(
        [jnp.where(core == 0, mine, other), jnp.where(core == 0, other, mine)], axis=1
    ).reshape(16, 32, D)

    dqkvb = jnp.concatenate(attend_back(qkvb, dob, seg), axis=1)
    d_qkv = jnp.einsum("td,te->de", n1b, dqkvb, preferred_element_type=F32).astype(BF)
    dqkv_sum = jnp.sum(dqkvb.astype(F32), axis=0)
    dn1_part = jnp.einsum("te,de->td", dqkvb, w_qkv, preferred_element_type=F32)
    dn1 = dn1_part[:rows] + swap(dn1_part[rows:].astype(BF), CORE).astype(F32)
    back1, d_gain1, d_shift1 = layer_norm_backward_pass(dn1, hat1[:rows], inv1[:rows], gain1)
    da = da2[:rows] + back1
    tokens_grad = da.astype(BF)
    d_pos = lax.dot_general(
        da, picker[:rows].astype(F32), (((0,), (0,)), ((), ())), precision=lax.Precision.HIGHEST
    )
    spread = lambda v: jnp.stack(
        [jnp.where(core == i, v.reshape(4, 128), 0.0) for i in range(2)], axis=1
    ).reshape(D)
    d_vec = jnp.stack(
        [
            d_gain1,
            d_shift1,
            spread(dqkv_sum[:512]),
            spread(dqkv_sum[1024:]),
            d_out_bias,
            d_gain2,
            d_shift2,
            jnp.sum(dy[:rows], axis=0),
        ],
        axis=1,
    )
    d_bias = jnp.where(
        (jnp.arange(2)[None, :, None, None] == core) & (jnp.arange(32)[None, None, :, None] == 0),
        d_up_bias.reshape(16, 1, 1, 128),
        0.0,
    ).reshape(D, 128)
    d_small = jnp.concatenate([d_pos[:, :145], d_vec, jnp.zeros((D, 103), F32), d_bias], axis=1).astype(BF)
    a_sum = scatter_zxy(disassemble([d_small, d_qkv, d_out], places_a, "zxy", A_WIDTH))

    own = jnp.concatenate([a_sum[:32, :cut], up_sum[:32]], axis=1)
    got = swap(jnp.concatenate([a_sum[32:, :cut], up_sum[32:]], axis=1), CORE)
    small_own = own[:, :SMALL] + got[:, :SMALL]
    qkv_grad = weave_blocks(own[:, SMALL:cut], got[:, SMALL:cut], core)
    up_grad = weave_blocks(own[:, cut:], got[:, cut:], core)
    out_grad = jnp.concatenate([a_sum[:32, cut:], a_sum[32:, cut:]], axis=1)
    down_grad = jnp.concatenate([down_sum[:, :D], down_sum[:, D:]])
    pos_grad = small_own[:, :145].T
    gv = small_own[:, 145:153].T
    return (
        layer_out,
        tokens_grad,
        gv[0],
        gv[1],
        qkv_grad,
        gv[2],
        gv[3],
        out_grad,
        gv[4],
        gv[5],
        gv[6],
        up_grad,
        small_own[0, 256:],
        down_grad,
        gv[7],
        pos_grad,
    )


def solution(mesh):
    in_specs = (
        P(("dp", "fsdp"), None),
        P(("dp", "fsdp"), None),
        P(),
        P(),
        P(),
        P(("dp", "fsdp")),
        P(("dp", "fsdp")),
        P(("dp", "fsdp"), None),
        P(("dp", "fsdp")),
        P(("dp", "fsdp")),
        P(("dp", "fsdp"), None),
        P(("dp", "fsdp")),
        P(("dp", "fsdp")),
        P(("dp", "fsdp")),
        P(("dp", "fsdp"), None),
        P(("dp", "fsdp")),
        P(("dp", "fsdp"), None),
        P(("dp", "fsdp")),
        P(None, ("dp", "fsdp")),
    )
    out_specs = (
        P(("dp", "fsdp"), None),
        P(("dp", "fsdp"), None),
        P(("dp", "fsdp")),
        P(("dp", "fsdp")),
        P(("dp", "fsdp"), None),
        P(("dp", "fsdp")),
        P(("dp", "fsdp")),
        P(("dp", "fsdp"), None),
        P(("dp", "fsdp")),
        P(("dp", "fsdp")),
        P(("dp", "fsdp")),
        P(("dp", "fsdp"), None),
        P(("dp", "fsdp")),
        P(("dp", "fsdp"), None),
        P(("dp", "fsdp")),
        P(None, ("dp", "fsdp")),
    )
    eight_by_four = mesh.shape["dp"] == 8 and mesh.shape["fsdp"] == 4
    return jax.shard_map(
        fast_on_device if eight_by_four else on_device, mesh=mesh, in_specs=in_specs, out_specs=out_specs, check_vma=False
    )
```

```python
import jax
import jax.numpy as jnp
import numpy as np
from jax import lax
from jax.experimental import pallas as pl
from jax.experimental.pallas import tpu as pltpu
from jax.sharding import PartitionSpec as P

D = 1024
HEADS = 16
HEAD = 64
FF = 4096
LONG = 145
SHORT = 50


EPS = 1e-06


def fetch(parts):
    whole = (
        lax.all_gather(parts[0], ("dp", "fsdp"), axis=1, tiled=True),
        lax.all_gather(parts[1], ("dp", "fsdp"), axis=0, tiled=True),
        lax.all_gather(parts[2], ("dp", "fsdp"), axis=0, tiled=True),
        lax.all_gather(parts[3], ("dp", "fsdp"), axis=0, tiled=True),
        lax.all_gather(parts[4], ("dp", "fsdp"), axis=0, tiled=True),
        lax.all_gather(parts[5], ("dp", "fsdp"), axis=0, tiled=True),
        lax.all_gather(parts[6], ("dp", "fsdp"), axis=1, tiled=True),
    )
    return whole


def reduce_grads(parts):
    owned = (
        lax.psum_scatter(parts[0], ("dp", "fsdp"), scatter_dimension=1, tiled=True),
        lax.psum_scatter(parts[1], ("dp", "fsdp"), scatter_dimension=0, tiled=True),
        lax.psum_scatter(parts[2], ("dp", "fsdp"), scatter_dimension=0, tiled=True),
        lax.psum_scatter(parts[3], ("dp", "fsdp"), scatter_dimension=0, tiled=True),
        lax.psum_scatter(parts[4], ("dp", "fsdp"), scatter_dimension=0, tiled=True),
        lax.psum_scatter(parts[5], ("dp", "fsdp"), scatter_dimension=0, tiled=True),
        lax.psum_scatter(parts[6], ("dp", "fsdp"), scatter_dimension=1, tiled=True),
    )
    return owned


def layout(image_lengths, image_device, small_map, device, rows_dev):
    mine = image_device == device
    lens = jnp.where(mine, image_lengths, 0)
    starts = jnp.cumsum(lens) - lens
    rows = jnp.arange(rows_dev, dtype=jnp.int32)
    inside = (
        mine[None, :]
        & (starts[None, :] <= rows[:, None])
        & (rows[:, None] < (starts + lens)[None, :])
    )
    number = jnp.arange(image_lengths.shape[0], dtype=jnp.int32)
    segment = jnp.sum(jnp.where(inside, number[None, :] + 1, 0), axis=1) - 1
    offset = rows - jnp.sum(jnp.where(inside, starts[None, :], 0), axis=1)
    length = jnp.sum(jnp.where(inside, lens[None, :], 0), axis=1)
    spots = jnp.arange(SHORT, dtype=jnp.int32)
    mapped = jnp.sum(jnp.where(offset[:, None] == spots[None, :], small_map[None, :], 0), axis=1)
    place = jnp.where(length == LONG, offset, jnp.where(length == SHORT, mapped, 0))
    return (segment, place)


def layer_norm_forward_pass(v, norm_gain, shift_bias):
    centred_rows = v - jnp.mean(v, axis=1, keepdims=True)
    inverse_deviation = lax.rsqrt(
        jnp.mean(centred_rows * centred_rows, axis=1, keepdims=True) + EPS
    )
    normalized_rows = centred_rows * inverse_deviation
    return (normalized_rows * norm_gain + shift_bias, normalized_rows, inverse_deviation)


def layer_norm_backward_pass(upstream_gradient, normalized_rows, inverse_deviation, norm_gain):
    normalized_gradient = upstream_gradient * norm_gain
    first_input = jnp.mean(normalized_gradient, axis=1, keepdims=True)
    second_input = jnp.mean(normalized_gradient * normalized_rows, axis=1, keepdims=True)
    return (
        inverse_deviation * (normalized_gradient - first_input - normalized_rows * second_input),
        jnp.sum(upstream_gradient * normalized_rows, axis=0),
        jnp.sum(upstream_gradient, axis=0),
    )


def split_heads(values, groups):
    return values.reshape(values.shape[0], groups, HEADS // groups, HEAD).transpose(1, 0, 2, 3)


def join_heads(values):
    return values.transpose(1, 0, 2, 3).reshape(values.shape[1], D)


def masked_scores(query, keys, same):
    scores = jnp.einsum("thd,shd->hts", query, keys, preferred_element_type=jnp.float32) * HEAD ** (
        -0.5
    )
    return jnp.where(same[None], scores, -1000000000.0)


def attend_forward(qkvb, same):
    groups = HEADS // 4
    query = split_heads(qkvb[:, :D], groups)
    keys = split_heads(qkvb[:, D : 2 * D], groups)
    values = split_heads(qkvb[:, 2 * D :], groups)

    def one_group(item):
        scores = masked_scores(item[0], item[1], same)
        top = jnp.max(scores, axis=2, keepdims=True)
        lse = top + jnp.log(jnp.sum(jnp.exp(scores - top), axis=2, keepdims=True))
        probs = jnp.exp(scores - lse).astype(jnp.bfloat16)
        attended = jnp.einsum("hts,shd->thd", probs, item[2], preferred_element_type=jnp.float32)
        return (attended, lse[:, :, 0])

    attended, lse = lax.map(one_group, (query, keys, values))
    return (join_heads(attended), lse)


def attend_backward(qkvb, dob, lse, same):
    groups = HEADS // 4
    query = split_heads(qkvb[:, :D], groups)
    keys = split_heads(qkvb[:, D : 2 * D], groups)
    values = split_heads(qkvb[:, 2 * D :], groups)
    douts = split_heads(dob, groups)

    def one_group(item):
        scores = masked_scores(item[0], item[1], same)
        probs = jnp.exp(scores - item[4][:, :, None])
        dvalue = jnp.einsum(
            "hts,thd->shd", probs.astype(jnp.bfloat16), item[3], preferred_element_type=jnp.float32
        )
        dprobs = jnp.einsum("thd,shd->hts", item[3], item[2], preferred_element_type=jnp.float32)
        inner = jnp.sum(probs * dprobs, axis=2, keepdims=True)
        dscore = (probs * (dprobs - inner)).astype(jnp.bfloat16)
        dquery = jnp.einsum(
            "hts,shd->thd", dscore, item[1], preferred_element_type=jnp.float32
        ) * HEAD ** (-0.5)
        dkey = jnp.einsum(
            "hts,thd->shd", dscore, item[0], preferred_element_type=jnp.float32
        ) * HEAD ** (-0.5)
        return (dquery, dkey, dvalue)

    dquery, dkey, dvalue = lax.map(one_group, (query, keys, values, douts, lse))
    return jnp.concatenate([join_heads(dquery), join_heads(dkey), join_heads(dvalue)], axis=1)


def gelu_slope(x):
    return (
        0.5 * (1.0 + jax.scipy.special.erf(x * 0.7071067811865476))
        + x * jnp.exp(-0.5 * x * x) * 0.3989422804014327
    )


def on_device(
    tokens,
    grad_out,
    image_lengths,
    image_device,
    small_map,
    ln1_gain,
    ln1_bias,
    qkv_weight,
    q_bias,
    v_bias,
    out_weight,
    out_bias,
    ln2_gain,
    ln2_bias,
    up_weight,
    up_bias,
    down_weight,
    down_bias,
    pos_table,
):
    rows_dev = tokens.shape[0]
    device = lax.axis_index("dp") * lax.axis_size("fsdp") + lax.axis_index("fsdp")
    segment, place = layout(image_lengths, image_device, small_map, device, rows_dev)
    same = segment[:, None] == segment[None, :]
    valid = (segment >= 0).astype(jnp.float32)[:, None]
    table_rows = jnp.arange(LONG, dtype=jnp.int32)
    picker = place[:, None] == table_rows[None, :]
    vectors = jnp.stack(
        [ln1_gain, ln1_bias, q_bias, v_bias, out_bias, ln2_gain, ln2_bias, down_bias]
    )
    shards = (vectors, qkv_weight, out_weight, up_weight, up_bias, down_weight, pos_table)
    whole = fetch(shards)
    vec = whole[0].astype(jnp.float32)
    first_gain, first_centred, bq, bv, bo, second_gain, second_centred, bf2 = (
        vec[0],
        vec[1],
        vec[2],
        vec[3],
        vec[4],
        vec[5],
        vec[6],
        vec[7],
    )
    bf1 = whole[4].astype(jnp.float32)
    activation_rows = tokens.astype(jnp.float32) + jnp.dot(
        picker.astype(jnp.bfloat16), whole[6], preferred_element_type=jnp.float32
    )
    first_normed, first_normalized, first_inverse_deviation = layer_norm_forward_pass(
        activation_rows, first_gain, first_centred
    )
    n1b = first_normed.astype(jnp.bfloat16)
    bias3 = jnp.concatenate([bq, jnp.zeros_like(bq), bv])
    qkvb = (jnp.dot(n1b, whole[1], preferred_element_type=jnp.float32) + bias3).astype(jnp.bfloat16)
    attended, lse = attend_forward(qkvb, same)
    ob = attended.astype(jnp.bfloat16)
    second_activation = (
        activation_rows + jnp.dot(ob, whole[2], preferred_element_type=jnp.float32) + bo
    )
    second_normed, second_normalized, second_inverse_deviation = layer_norm_forward_pass(
        second_activation, second_gain, second_centred
    )
    n2b = second_normed.astype(jnp.bfloat16)
    hpre = jnp.dot(n2b, whole[3], preferred_element_type=jnp.float32) + bf1
    actb = jax.nn.gelu(hpre, approximate=False).astype(jnp.bfloat16)
    output = second_activation + jnp.dot(actb, whole[5], preferred_element_type=jnp.float32) + bf2
    layer_out = output.astype(jnp.bfloat16)
    dy = grad_out.astype(jnp.float32) * valid
    fenced, dy = lax.optimization_barrier((shards, dy))
    back = fetch(fenced)
    dyb = dy.astype(jnp.bfloat16)
    d_down = jnp.einsum("tf,td->fd", actb, dyb, preferred_element_type=jnp.float32)
    d_down_bias = jnp.sum(dy, axis=0)
    dgate = jnp.einsum("td,fd->tf", dyb, back[5], preferred_element_type=jnp.float32)
    dhb = (dgate * gelu_slope(hpre)).astype(jnp.bfloat16)
    d_up = jnp.einsum("td,tf->df", n2b, dhb, preferred_element_type=jnp.float32)
    d_up_bias = jnp.sum(dhb.astype(jnp.float32), axis=0)
    second_norm_gradient = jnp.einsum("tf,df->td", dhb, back[3], preferred_element_type=jnp.float32)
    second_activation_norm_gradient, second_gain_gradient, second_centred_gradient = (
        layer_norm_backward_pass(
            second_norm_gradient, second_normalized, second_inverse_deviation, second_gain
        )
    )
    da2 = dy + second_activation_norm_gradient
    dzb = da2.astype(jnp.bfloat16)
    d_out = jnp.einsum("te,td->ed", ob, dzb, preferred_element_type=jnp.float32)
    d_out_bias = jnp.sum(dzb.astype(jnp.float32), axis=0)
    dob = jnp.einsum("td,ed->te", dzb, back[2], preferred_element_type=jnp.float32).astype(
        jnp.bfloat16
    )
    dqkvb = attend_backward(qkvb, dob, lse, same).astype(jnp.bfloat16)
    d_qkv = jnp.einsum("td,te->de", n1b, dqkvb, preferred_element_type=jnp.float32)
    dqkv_sum = jnp.sum(dqkvb.astype(jnp.float32), axis=0)
    first_norm_gradient = jnp.einsum(
        "te,de->td", dqkvb, back[1], preferred_element_type=jnp.float32
    )
    first_activation_gradient, first_gain_gradient, first_centred_gradient = (
        layer_norm_backward_pass(
            first_norm_gradient, first_normalized, first_inverse_deviation, first_gain
        )
    )
    da = da2 + first_activation_gradient
    tokens_grad = da.astype(jnp.bfloat16)
    d_pos = jnp.dot(picker.astype(jnp.float32).T, da, precision=lax.Precision.HIGHEST)
    d_vectors = jnp.stack(
        [
            first_gain_gradient,
            first_centred_gradient,
            dqkv_sum[:D],
            dqkv_sum[2 * D :],
            d_out_bias,
            second_gain_gradient,
            second_centred_gradient,
            d_down_bias,
        ]
    )
    flat_parts = (
        d_vectors,
        d_qkv.reshape(-1, 128),
        d_out.reshape(-1, 128),
        d_up.reshape(-1, 128),
        d_up_bias,
        d_down,
        d_pos,
    )
    owned = reduce_grads(flat_parts)
    gv = owned[0]
    qkv_owned = owned[1].reshape(-1, 3 * D)
    out_owned = owned[2].reshape(-1, D)
    up_owned = owned[3].reshape(-1, FF)
    return (
        layer_out,
        tokens_grad,
        gv[0],
        gv[1],
        qkv_owned,
        gv[2],
        gv[3],
        out_owned,
        gv[4],
        gv[5],
        gv[6],
        up_owned,
        owned[4],
        owned[5],
        gv[7],
        owned[6],
    )


BF = jnp.bfloat16
F32 = jnp.float32
AXES = ("dp", "fsdp")
CORE, XBIT, YBIT, ZBIT = 1, 2, 4, 8
PACK = 384
LIVE = -(-2 * LONG // 64) * 64
REST = PACK - LIVE
ROWS = 2 * PACK
BACK = 2 * LIVE
HALF_FF = FF // 2
QKV = 3 * D // 2
HALF_D = D // 2
SMALL = 384
A_WIDTH = SMALL + QKV + HALF_D
CUT = SMALL + QKV // 2
VEC0 = LONG
QKV_ORDER = (0, HALF_D, 2 * HALF_D, 256, HALF_D + 256, 2 * HALF_D + 256)
SEGMENTS = ((0, 0, LIVE, 0), (1, 0, LIVE, LIVE), (0, LIVE, REST, BACK), (1, LIVE, REST, BACK + REST))
NT = (((1,), (1,)), ((), ()))
TN = (((0,), (0,)), ((), ()))


def swap(value, mask):
    return lax.ppermute(value, AXES, [(i, i ^ mask) for i in range(32)])


def coords():
    dp = lax.axis_index("dp")
    fs = lax.axis_index("fsdp")
    return dp // 2, dp % 2, fs // 2, fs % 2


def chip_of(rel):
    z, y, x, _ = coords()
    dz, dy, dx = rel
    bits = 0
    for part, off, width in ((z // 2, dz // 2, 8), (z % 2, dz % 2, 4), (y, dy, 2), (x, dx, 1)):
        bits = bits + (1 - part if off else part) * width
    return bits


ENTRIES_ZXY = (
    [(0, (k,), h, (k, 0, 0), h) for k in range(4) for h in range(2)]
    + [(1, (k,), h, (k, 0, 1), h) for k in range(4) for h in range(2)]
    + [(2, (k,), h, (k, 1, 0), h) for k in range(4) for h in range(2)]
    + [(3, (k,), h, (k, 1, 1), h) for k in range(2) for h in range(2)]
    + [(4, (k,), h, (k + 2, 1, 1), h) for k in range(2) for h in range(2)]
)
QUADS = (((0, 0), 0), ((0, 1), 0), ((0, 0), 1), ((1, 0), 1))
SIDE_A = ((1, 0), (1, 1))
SIDE_B = ((0, 1), (1, 1))
ENTRIES_XZY_GATHER = (
    [(k, (q,), 0, (k,) + QUADS[q][0], QUADS[q][1]) for k in range(4) for q in range(4)]
    + [(4, (k, q), 0, (k,) + SIDE_A[q], 0) for k in range(4) for q in range(2)]
    + [(5, (k, q), 0, (k,) + SIDE_B[q], 1) for k in range(4) for q in range(2)]
)
ENTRIES_XZY_SCATTER = (
    [(0, (k, q), 0, (k,) + QUADS[q][0], QUADS[q][1]) for k in range(4) for q in range(4)]
    + [(1, (k, q), 0, (k,) + SIDE_A[q], 0) for k in range(4) for q in range(2)]
    + [(2, (k, q), 0, (k,) + SIDE_B[q], 1) for k in range(4) for q in range(2)]
)


class Lane:
    def __init__(self):
        self.last = None

    def go(self, *pairs):
        values = tuple(value for value, _ in pairs)
        if self.last is not None:
            values, _ = lax.optimization_barrier((values, self.last))
        self.last = tuple(swap(value, mask) for value, (_, mask) in zip(values, pairs))
        return self.last


def along_z(lane, block):
    return [block, *lane.go(*((block, ZBIT * k) for k in range(1, 4)))]


def cross(lane, line):
    from_x, from_y = lane.go((line, XBIT), (line, YBIT))
    corners = lane.go((from_x[:2], YBIT), (from_y[2:], XBIT))
    return [line, from_x, from_y, *corners]


def sides(lane, quads):
    side_a = jnp.stack([q[:2] for q in quads])
    side_b = jnp.stack([q[2:] for q in quads])
    return [*quads, *lane.go((side_a, YBIT), (side_b, XBIT))]


def add(*values):
    total = values[0].astype(F32)
    for value in values[1:]:
        total = total + value.astype(F32)
    return total


def scatter_zxy(flat, deep, parts):
    line, to_x, to_y, corner_a, corner_b = parts
    got_a, got_b = flat.go((corner_a, XBIT), (corner_b, YBIT))
    to_x = jnp.concatenate([to_x[:2], add(to_x[2:], got_b).astype(BF)])
    to_y = jnp.concatenate([add(to_y[:2], got_a).astype(BF), to_y[2:]])
    got_x, got_y = flat.go((to_x, XBIT), (to_y, YBIT))
    sums = [add(line[k], got_x[k], got_y[k]) for k in range(4)]
    got_z = deep.go(*((sums[k].astype(BF), ZBIT * k) for k in range(1, 4)))
    return add(sums[0], *got_z)


def scatter_xzy_start(flat, deep, parts):
    keep, side_a, side_b = parts
    got_a, got_b = flat.go((side_a, YBIT), (side_b, XBIT))
    quads = [add(keep[k], jnp.concatenate([got_a[k], got_b[k]])) for k in range(4)]
    got_z = deep.go(*((quads[k].astype(BF), ZBIT * k) for k in range(1, 4)))
    return add(quads[0], *got_z)


def scatter_xzy_end(flat, quad):
    got_x, got_y = flat.go((quad[1].astype(BF), XBIT), (quad[3].astype(BF), YBIT))
    return jnp.concatenate([add(quad[0], got_x), add(quad[2], got_y)])


def scatter_shapes(kind, rows, width):
    if kind == "zxy":
        return [(4, 2 * rows, width)] * 3 + [(2, 2 * rows, width)] * 2
    return [(4, 4, rows, width), (4, 2, rows, width), (4, 2, rows, width)]


SCATTER_ENTRIES = {"zxy": ENTRIES_ZXY, "xzy": ENTRIES_XZY_SCATTER}


def piece_of(refs, entry, rows, lanes=None):
    array, index, row, _, _ = entry
    width = pl.ds(*lanes) if lanes else slice(None)
    return refs[array].at[index + (pl.ds(rows * row, rows), width)]


def start_all(copies, sems, first=0):
    started = []
    for i, (src, dst) in enumerate(copies):
        copy = pltpu.make_async_copy(src, dst, sems.at[first + i])
        copy.start()
        started.append(copy)
    return started


def wait_all(started):
    for copy in started:
        copy.wait()


def core_rows(entry):
    core = coords()[3]
    side = core if entry[4] == 0 else 1 - core
    return pl.multiple_of(chip_of(entry[3]) * 64 + side * 32, 32)


def half_rows(entry):
    return pl.multiple_of(chip_of(entry[3]) * 128 + 64 * entry[4], 64)


def tile(i, width):
    return pl.ds(pl.multiple_of(i * width, width), width)


ANY = pl.BlockSpec(memory_space=pl.ANY)
VMEM = pl.BlockSpec(memory_space=pltpu.VMEM)


def launch(kernel, ins, outs, scratch=(), flops=0, limit=56):
    size = sum(int(np.prod(o[0])) * jnp.dtype(o[1]).itemsize for o in outs)
    for value, _ in ins:
        size += value.size * value.dtype.itemsize
    return pl.pallas_call(
        kernel,
        out_shape=[jax.ShapeDtypeStruct(o[0], o[1]) for o in outs],
        in_specs=[spec for _, spec in ins],
        out_specs=[o[2] if len(o) > 2 else VMEM for o in outs],
        scratch_shapes=list(scratch),
        cost_estimate=pl.CostEstimate(flops=int(flops), bytes_accessed=int(size), transcendentals=0),
        compiler_params=pltpu.CompilerParams(vmem_limit_bytes=limit << 20),
    )(*[value for value, _ in ins])


def dma(count):
    return pltpu.SemaphoreType.DMA((count,))


def norm_rows(v):
    mean = jnp.mean(v, axis=1, keepdims=True)
    centred = v - mean
    inverse = lax.rsqrt(jnp.mean(centred * centred, axis=1, keepdims=True) + EPS)
    return centred * inverse, mean, inverse


def stats(mean, inverse):
    lane = lax.broadcasted_iota(jnp.int32, (mean.shape[0], 128), 1)
    return jnp.where(lane == 0, mean, inverse)


def normed(v, stat):
    return (v - stat[:, 0:1]) * stat[:, 1:2], stat[:, 1:2]


def gelu_parts(h):
    bell = jnp.exp(h * h * -0.5)
    base = 1.0 + jnp.abs(h) * (0.3275911 * 0.7071067811865476)
    t = pl.reciprocal(base, approx=True)
    t = t * (2.0 - base * t)
    poly = 0.5 * 1.061405429
    for factor in (-1.453152027, 1.421413741, -0.284496736, 0.254829592):
        poly = poly * t + 0.5 * factor
    tail = poly * t * bell
    return jnp.where(h >= 0, 1.0 - tail, tail), bell


def norm_back(dn, hat, inverse, gain):
    scaled = dn * gain
    first = jnp.mean(scaled, axis=1, keepdims=True)
    second = jnp.mean(scaled * hat, axis=1, keepdims=True)
    return inverse * (scaled - first - hat * second)


def slot_of(block):
    which, j = divmod(block, 4)
    return 768 * (j // 2) + 256 * which + 128 * (j % 2)


def prepare_kernel(
    pos_ref, bias_ref, qkv_ref, up_ref, out_ref, small_ref, keep_q, send_q, keep_u, send_u, out2_ref
):
    core = coords()[3]
    eye = (
        lax.broadcasted_iota(jnp.int32, (32, 32), 0) == lax.broadcasted_iota(jnp.int32, (32, 32), 1)
    ).astype(BF)
    small = lax.dot_general(eye, pos_ref[...], NT, preferred_element_type=F32)
    first_row = lax.broadcasted_iota(jnp.int32, (32, 128), 0) == 0
    bias = jnp.where(first_row, bias_ref[...].astype(F32), 0.0)
    small = jnp.concatenate([small, bias], axis=1).astype(BF)
    small_ref[...] = small
    for src, keep, send, count in (
        (qkv_ref, keep_q, send_q, 12),
        (up_ref, keep_u, send_u, 16),
    ):
        for j in range(count):
            own = pl.ds(pl.multiple_of(256 * j + 128 * core, 128), 128)
            other = pl.ds(pl.multiple_of(256 * j + 128 * (1 - core), 128), 128)
            to = slot_of(j) if count == 12 else 128 * j
            keep[:, to : to + 128] = src[:, own]
            send[:, to : to + 128] = src[:, other]
    out2_ref[:32] = out_ref[:, :HALF_D]
    out2_ref[32:] = out_ref[:, HALF_D:]


def prepare(pos, bias, qkv, up, out):
    shapes = [(32, SMALL), (32, QKV), (32, QKV), (32, HALF_FF), (32, HALF_FF), (64, HALF_D)]
    return launch(
        prepare_kernel,
        [(v, VMEM) for v in (pos, bias, qkv, up, out)],
        [(s, BF) for s in shapes],
        limit=8,
    )


def first_kernel(own_hbm, sib_hbm, place_ref, *refs):
    parts, more, refs = refs[:5], refs[5:10], refs[10:]
    a_hbm, n1_hbm, qkv_hbm, wq_hbm, wo_hbm, vec_ref, bf1_ref, stat_ref = refs[:8]
    tok_ref, a_ref, n1_ref, qkv_ref, wq_ref, wo_ref, small_ref, bias_ref, sems, out_sems = refs[8:]
    core = coords()[3]
    count = len(ENTRIES_ZXY)
    one = start_all(
        [
            (piece_of(parts, e, 32, (0, SMALL)), small_ref.at[pl.ds(core_rows(e), 32), :])
            for e in ENTRIES_ZXY
        ]
        + [
            (
                (own_hbm if which == 0 else sib_hbm).at[pl.ds(start, size), :],
                tok_ref.at[pl.ds(to, size), :],
            )
            for which, start, size, to in SEGMENTS
        ],
        sems,
    )
    two = start_all(
        [
            (
                piece_of(group, e, 32, lanes),
                wq_ref.at[pl.ds(core_rows(e), 32), pl.ds(to, QKV // 2)],
            )
            for group, lanes, to in (
                (parts, (SMALL, QKV // 2), 0),
                (more, (0, QKV // 2), QKV // 2),
            )
            for e in ENTRIES_ZXY
        ],
        sems,
        count + 4,
    )
    three = start_all(
        [
            (
                piece_of(more, e, 32, (QKV // 2, HALF_D)),
                wo_ref.at[chip_of(e[3]), :, pl.ds(HALF_D * e[4], HALF_D)],
            )
            for e in ENTRIES_ZXY
        ],
        sems,
        3 * count + 4,
    )
    wait_all(one)
    lane = lax.broadcasted_iota(jnp.int32, (16, 256), 1)
    pick = (lane == lax.broadcasted_iota(jnp.int32, (16, 256), 0) + VEC0).astype(BF)
    vec_ref[...] = lax.dot_general(pick, small_ref[:, :256], NT, preferred_element_type=F32)
    for chip in range(16):
        row = pl.multiple_of(64 * chip + 32 * core, 32)
        bf1_ref[:, 128 * chip : 128 * (chip + 1)] = small_ref[pl.ds(row, 16), 256:384][:1].astype(F32)
    for j in range(4):
        own = pl.ds(pl.multiple_of(256 * j + 128 * core, 128), 128)
        at = slice(128 * j, 128 * (j + 1))
        bias_ref[0:1, at] = vec_ref[2:3, own]
        bias_ref[1:2, at] = jnp.zeros((1, 128), F32)
        bias_ref[2:3, at] = vec_ref[3:4, own]
    hot = (place_ref[...] == lax.broadcasted_iota(jnp.int32, (ROWS, 256), 1)).astype(BF)
    for j in range(4):
        at = slice(256 * j, 256 * (j + 1))
        a_ref[:, at] = tok_ref[:, at].astype(F32) + lax.dot_general(
            hot, small_ref[at, :256], NT, preferred_element_type=F32
        )
    gain, shift = vec_ref[0:1, :], vec_ref[1:2, :]

    def rows(i, carry):
        hat, mean, inverse = norm_rows(a_ref[tile(i, 64), :])
        n1_ref[tile(i, 64), :] = (hat * gain + shift).astype(BF)
        stat_ref[tile(i, 64), :] = stats(mean, inverse)
        return carry

    lax.fori_loop(0, ROWS // 64, rows, 0)
    wait_all(three)
    outs = start_all(
        [(wo_ref, wo_hbm), (a_ref, a_hbm), (n1_ref.at[pl.ds(0, BACK), :], n1_hbm)], out_sems
    )
    wait_all(two)
    outs += start_all([(wq_ref, wq_hbm)], out_sems, 3)
    for j in range(6):
        to = QKV_ORDER[j]
        product = jnp.dot(
            n1_ref[...], wq_ref[:, 256 * j : 256 * (j + 1)], preferred_element_type=F32
        )
        which, off = to // HALF_D, to % HALF_D
        at = pl.ds(to, 256)
        qkv_ref[:, at] = (product + bias_ref[which : which + 1, off : off + 256]).astype(BF)
        outs += start_all([(qkv_ref.at[:, at], qkv_hbm.at[:, at])], out_sems, 4 + j)
    wait_all(outs)


def first_stage(own, sib, place, gathered):
    return launch(
        first_kernel,
        [(own, ANY), (sib, ANY), (place, VMEM)] + [(g, ANY) for g in gathered],
        [
            ((ROWS, D), F32, ANY),
            ((BACK, D), BF, ANY),
            ((ROWS, QKV), BF, ANY),
            ((D, QKV), BF, ANY),
            ((16, 32, D), BF, ANY),
            ((16, D), F32),
            ((1, HALF_FF), F32),
            ((ROWS, 128), F32),
        ],
        [
            pltpu.VMEM((ROWS, D), BF),
            pltpu.VMEM((ROWS, D), F32),
            pltpu.VMEM((ROWS, D), BF),
            pltpu.VMEM((ROWS, QKV), BF),
            pltpu.VMEM((D, QKV), BF),
            pltpu.VMEM((16, 32, D), BF),
            pltpu.VMEM((D, SMALL), BF),
            pltpu.VMEM((8, HALF_D), F32),
            dma(4 * len(ENTRIES_ZXY) + 4),
            dma(10),
        ],
        flops=2.5e9,
    )


def pack_rows(ref, pack):
    main = ref[LIVE * pack : LIVE * (pack + 1), :]
    return jnp.concatenate([main, ref[BACK + REST * pack : BACK + REST * (pack + 1), :]])


def attend_kernel(q_ref, k_ref, v_ref, col_ref, row_ref, o_ref, lse_ref):
    first = lax.broadcasted_iota(jnp.int32, (PACK, 128), 1) < HEAD
    for pack in range(2):
        q, k, v = (pack_rows(r, pack) for r in (q_ref, k_ref, v_ref))
        same = pack_rows(col_ref, pack) == row_ref[pack : pack + 1, :]
        outs, logs = [], []
        for h in range(2):
            mine = first if h == 0 else ~first
            scores = lax.dot_general(
                jnp.where(mine, q * HEAD ** (-0.5), 0), k, NT, preferred_element_type=F32
            )
            scores = jnp.where(same, scores, -1000000000.0)
            top = jnp.max(scores, axis=1, keepdims=True)
            powers = jnp.exp(scores - top)
            total = jnp.sum(powers, axis=1, keepdims=True)
            mixed = jnp.dot(powers.astype(BF), v, preferred_element_type=F32)
            outs.append(mixed * (1.0 / total))
            logs.append(top + jnp.log(total))
        o = jnp.where(first, outs[0], outs[1]).astype(BF)
        lse = jnp.where(first, logs[0], logs[1])
        o_ref[LIVE * pack : LIVE * (pack + 1), :] = o[:LIVE]
        o_ref[BACK + REST * pack : BACK + REST * (pack + 1), :] = o[LIVE:]
        lse_ref[LIVE * pack : LIVE * (pack + 1), :] = lse[:LIVE]


def attend(qkv, col, row):
    part = lambda off: pl.BlockSpec((ROWS, 128), lambda j: (0, j + off))
    return pl.pallas_call(
        attend_kernel,
        grid=(4,),
        in_specs=[
            part(0),
            part(4),
            part(8),
            pl.BlockSpec((ROWS, 1), lambda j: (0, 0)),
            pl.BlockSpec((2, PACK), lambda j: (0, 0)),
        ],
        out_specs=[part(0), pl.BlockSpec((BACK, 128), lambda j: (0, j))],
        out_shape=[
            jax.ShapeDtypeStruct((ROWS, HALF_D), BF),
            jax.ShapeDtypeStruct((BACK, HALF_D), F32),
        ],
        cost_estimate=pl.CostEstimate(
            flops=int(1.5e9), bytes_accessed=4000000, transcendentals=2400000
        ),
        compiler_params=pltpu.CompilerParams(vmem_limit_bytes=32 << 20),
    )(qkv, qkv, qkv, col, row)


def attend_back_kernel(q_ref, k_ref, v_ref, g_ref, o_ref, lse_ref, col_ref, row_ref, *outs):
    first = lax.broadcasted_iota(jnp.int32, (LIVE, 128), 1) < HEAD
    scale = HEAD ** (-0.5)
    for pack in range(2):
        at = slice(LIVE * pack, LIVE * (pack + 1))
        q, k, v, g = q_ref[at, :], k_ref[at, :], v_ref[at, :], g_ref[at, :]
        weighted = g.astype(F32) * o_ref[at, :].astype(F32)
        same = col_ref[at, :] == row_ref[pack : pack + 1, :LIVE]
        dq, dk, dv = [], [], []
        for h in range(2):
            mine = first if h == 0 else ~first
            lse = lse_ref[at, HEAD * h : HEAD * h + 1]
            inner = jnp.sum(jnp.where(mine, weighted, 0.0), axis=1, keepdims=True)
            qs = jnp.where(mine, q * scale, 0)
            scores = lax.dot_general(qs, k, NT, preferred_element_type=F32)
            probs = jnp.where(same, jnp.exp(scores - lse), 0.0)
            dprobs = lax.dot_general(jnp.where(mine, g, 0), v, NT, preferred_element_type=F32)
            ds = (probs * (dprobs - inner)).astype(BF)
            dv.append(lax.dot_general(probs.astype(BF), g, TN, preferred_element_type=F32))
            dq.append(jnp.dot(ds, k, preferred_element_type=F32))
            dk.append(lax.dot_general(ds, q, TN, preferred_element_type=F32))
        outs[0][at, :] = (jnp.where(first, dq[0], dq[1]) * scale).astype(BF)
        outs[1][at, :] = (jnp.where(first, dk[0], dk[1]) * scale).astype(BF)
        outs[2][at, :] = jnp.where(first, dv[0], dv[1]).astype(BF)


def attend_back(qkv, grad, out, lse, col, row):
    part = lambda off: pl.BlockSpec((BACK, 128), lambda j: (0, j + off))
    return pl.pallas_call(
        attend_back_kernel,
        grid=(4,),
        in_specs=[
            part(0),
            part(4),
            part(8),
            part(0),
            part(0),
            part(0),
            pl.BlockSpec((BACK, 1), lambda j: (0, 0)),
            pl.BlockSpec((2, PACK), lambda j: (0, 0)),
        ],
        out_specs=[part(0)] * 3,
        out_shape=[jax.ShapeDtypeStruct((BACK, HALF_D), BF)] * 3,
        cost_estimate=pl.CostEstimate(
            flops=int(3e9), bytes_accessed=6000000, transcendentals=2400000
        ),
        compiler_params=pltpu.CompilerParams(vmem_limit_bytes=32 << 20),
    )(qkv, qkv, qkv, grad, out, lse, col, row)


def head_rows(k, core):
    return (k // 2) * 4 + 2 * core + k % 2


def project_kernel(o_ref, a_hbm, vec_ref, own_hbm, other_hbm, *refs):
    wo_ref, sum_ref, send_ref, a_ref, sems = refs
    core = coords()[3]
    copies = []
    for k in range(8):
        head = head_rows(k, core)
        copies.append(
            (own_hbm.at[head], wo_ref.at[pl.ds(pl.multiple_of(64 * k + 32 * core, 32), 32), :])
        )
        copies.append(
            (other_hbm.at[head], wo_ref.at[pl.ds(pl.multiple_of(64 * k + 32 - 32 * core, 32), 32), :])
        )
    started = start_all(copies + [(a_hbm, a_ref)], sems)
    wait_all(started)
    for j in range(4):
        at = slice(256 * j, 256 * (j + 1))
        part = jnp.dot(o_ref[...], wo_ref[:, at], preferred_element_type=F32)
        send_ref[:, at] = part.astype(BF)
        sum_ref[:, at] = a_ref[:, at] + part + vec_ref[4:5, at]


def project(o, a, vec, own, other):
    return launch(
        project_kernel,
        [(o, VMEM), (a, ANY), (vec, VMEM), (own, ANY), (other, ANY)],
        [((HALF_D, D), BF), ((ROWS, D), F32), ((ROWS, D), BF)],
        [pltpu.VMEM((ROWS, D), F32), dma(17)],
        flops=0.8e9,
    )


SWAPPED = ((0, LIVE, LIVE), (LIVE, 0, LIVE), (BACK, BACK + REST, REST), (BACK + REST, BACK, REST))


def widen_kernel(sum_hbm, got_hbm, vec_ref, bf1_ref, own_hbm, sib_hbm, col_ref, *refs):
    parts, refs = refs[:5], refs[5:]
    a2_hbm, n2_hbm, act_hbm, slope_hbm, wu_hbm, dy_hbm, stat_ref = refs[:7]
    outs, refs = refs[7:10], refs[10:]
    a2_ref, got_ref, n2_ref, wu_ref, act_ref, slope_ref, dy_ref, whole_ref, h0, h1 = refs[:10]
    sems, out_sems, grad_sems = refs[10:]
    first = start_all(
        [(sum_hbm, a2_ref)]
        + [
            (got_hbm.at[pl.ds(start, size), :], got_ref.at[pl.ds(to, size), :])
            for to, start, size in SWAPPED
        ],
        sems,
    )
    grads = start_all(
        [
            (src.at[pl.ds(0, LIVE), :], dy_ref.at[pl.ds(LIVE * i, LIVE), :])
            for i, src in enumerate((own_hbm, sib_hbm))
        ],
        sems,
        5,
    )
    weights = start_all(
        [(piece_of(parts, e, 32), wu_ref.at[pl.ds(core_rows(e), 32), :]) for e in ENTRIES_ZXY],
        sems,
        7,
    )
    gain, shift = vec_ref[5:6, :], vec_ref[6:7, :]
    wait_all(first)

    def rows(i, carry):
        at = tile(i, 64)
        a2 = a2_ref[at, :] + got_ref[at, :].astype(F32)
        a2_ref[at, :] = a2
        hat, mean, inverse = norm_rows(a2)
        n2_ref[at, :] = (hat * gain + shift).astype(BF)
        stat_ref[at, :] = stats(mean, inverse)
        return carry

    lax.fori_loop(0, ROWS // 64, rows, 0)
    wait_all(weights)
    sent = start_all(
        [(a2_ref, a2_hbm), (n2_ref.at[pl.ds(0, BACK), :], n2_hbm), (wu_ref, wu_hbm)], out_sems
    )
    steps = HALF_FF // 256
    hidden = (h0, h1)

    def product(j):
        hidden[j % 2][...] = jnp.dot(
            n2_ref[...], wu_ref[:, 256 * j : 256 * (j + 1)], preferred_element_type=F32
        )

    product(0)
    for j in range(steps):
        if j + 1 < steps:
            product(j + 1)
        at = slice(256 * j, 256 * (j + 1))
        h = hidden[j % 2][...] + bf1_ref[:, at]
        area, bell = gelu_parts(h)
        act_ref[:, at] = (h * area).astype(BF)
        slope_ref[:, at] = (
            area[:BACK] + h[:BACK] * bell[:BACK] * 0.3989422804014327
        ).astype(BF)
        sent += start_all(
            [
                (act_ref.at[:, pl.ds(256 * j, 256)], act_hbm.at[:, pl.ds(256 * j, 256)]),
                (slope_ref.at[:, pl.ds(256 * j, 256)], slope_hbm.at[:, pl.ds(256 * j, 256)]),
            ],
            out_sems,
            3 + 2 * j,
        )
    wait_all(grads)
    dy_ref[...] = jnp.where(col_ref[:BACK, :] >= 0, dy_ref[...], 0)
    sent += start_all([(dy_ref, dy_hbm)], out_sems, 3 + 2 * steps)

    def block(j, carry):
        at = tile(j, 256)
        part = lax.dot_general(act_ref[:BACK, at], dy_ref[...], TN, preferred_element_type=F32)
        whole_ref[at, :] = part.astype(BF)
        return carry

    lax.fori_loop(0, steps, block, 0)
    sent += start_all(
        [
            (whole_ref.at[pl.ds(half_rows(e), 64), :], piece_of(outs, e, 64))
            for e in ENTRIES_XZY_SCATTER
        ],
        grad_sems,
    )
    wait_all(sent)


def widen(total, got, vec, bf1, own, sib, col, gathered):
    return launch(
        widen_kernel,
        [(total, ANY), (got, ANY), (vec, VMEM), (bf1, VMEM), (own, ANY), (sib, ANY), (col, VMEM)]
        + [(g, ANY) for g in gathered],
        [
            ((ROWS, D), F32, ANY),
            ((BACK, D), BF, ANY),
            ((ROWS, HALF_FF), BF, ANY),
            ((BACK, HALF_FF), BF, ANY),
            ((D, HALF_FF), BF, ANY),
            ((BACK, D), BF, ANY),
            ((ROWS, 128), F32),
        ]
        + [(s, BF, ANY) for s in scatter_shapes("xzy", 64, D)],
        [
            pltpu.VMEM((ROWS, D), F32),
            pltpu.VMEM((ROWS, D), BF),
            pltpu.VMEM((ROWS, D), BF),
            pltpu.VMEM((D, HALF_FF), BF),
            pltpu.VMEM((ROWS, HALF_FF), BF),
            pltpu.VMEM((BACK, HALF_FF), BF),
            pltpu.VMEM((BACK, D), BF),
            pltpu.VMEM((HALF_FF, D), BF),
            pltpu.VMEM((ROWS, 256), F32),
            pltpu.VMEM((ROWS, 256), F32),
            dma(7 + len(ENTRIES_ZXY)),
            dma(4 + 2 * (HALF_FF // 256)),
            dma(len(ENTRIES_XZY_SCATTER)),
        ],
        flops=5.8e9,
    )


def hidden_grad_kernel(dy_hbm, slope_hbm, n2_hbm, wu_hbm, *refs):
    parts, (sum_ref, part_ref, send_ref), outs = refs[:6], refs[6:9], refs[9:14]
    dy_ref, slope_ref, n2_ref, n2t_ref, wu_ref, wd_ref, dh_ref, whole_ref, sems, out_sems = refs[14:]
    count = len(ENTRIES_XZY_GATHER)
    one = start_all(
        [(n2_hbm, n2_ref), (dy_hbm, dy_ref)]
        + [
            (piece_of(parts, e, 64), wd_ref.at[pl.ds(half_rows(e), 64), :])
            for e in ENTRIES_XZY_GATHER
        ]
        + [(slope_hbm, slope_ref)],
        sems,
    )
    two = start_all([(wu_hbm, wu_ref)], sems, count + 3)
    wait_all(one[:1])
    n2t_ref[...] = n2_ref[...].T
    wait_all(one[1:])

    def block(j, carry):
        at = tile(j, 256)
        gate = lax.dot_general(dy_ref[...], wd_ref[at, :], NT, preferred_element_type=F32)
        dh = (gate * slope_ref[:, at].astype(F32)).astype(BF)
        dh_ref[:, at] = dh
        sum_ref[:, at] = jnp.sum(dh.astype(F32), axis=0, keepdims=True)
        whole_ref[:, at] = jnp.dot(n2t_ref[...], dh, preferred_element_type=F32).astype(BF)
        return carry

    lax.fori_loop(0, HALF_FF // 256, block, 0)
    sent = start_all(
        [(whole_ref.at[pl.ds(core_rows(e), 32), :], piece_of(outs, e, 32)) for e in ENTRIES_ZXY],
        out_sems,
    )
    wait_all(two)
    for j in range(4):
        at = slice(256 * j, 256 * (j + 1))
        part = lax.dot_general(dh_ref[...], wu_ref[at, :], NT, preferred_element_type=F32)
        part_ref[:, at] = part
        send_ref[:, at] = part.astype(BF)
    wait_all(sent)


def hidden_grads(dy, slope, n2, wu, gathered):
    return launch(
        hidden_grad_kernel,
        [(v, ANY) for v in (dy, slope, n2, wu)] + [(g, ANY) for g in gathered],
        [((1, HALF_FF), F32), ((BACK, D), F32), ((BACK, D), BF)]
        + [(s, BF, ANY) for s in scatter_shapes("zxy", 32, HALF_FF)],
        [
            pltpu.VMEM((BACK, D), BF),
            pltpu.VMEM((BACK, HALF_FF), BF),
            pltpu.VMEM((BACK, D), BF),
            pltpu.VMEM((D, BACK), BF),
            pltpu.VMEM((D, HALF_FF), BF),
            pltpu.VMEM((HALF_FF, D), BF),
            pltpu.VMEM((BACK, HALF_FF), BF),
            pltpu.VMEM((D, HALF_FF), BF),
            dma(len(ENTRIES_XZY_GATHER) + 4),
            dma(len(ENTRIES_ZXY)),
        ],
        flops=7.5e9,
    )


def middle_kernel(part_hbm, got_hbm, a2_hbm, stat_ref, dy_hbm, vec_ref, o_hbm, wo_hbm, *refs):
    da2_ref, do_ref, sums_ref, mine_ref, send_ref = refs[:5]
    part_ref, got_ref, a2_ref, dy_ref, o_ref, wo_ref, dz_ref, whole_ref, sems = refs[5:]
    core = coords()[3]
    one = start_all(
        [
            (part_hbm, part_ref),
            (got_hbm.at[pl.ds(0, LIVE), :], got_ref.at[pl.ds(LIVE, LIVE), :]),
            (got_hbm.at[pl.ds(LIVE, LIVE), :], got_ref.at[pl.ds(0, LIVE), :]),
            (a2_hbm.at[pl.ds(0, BACK), :], a2_ref),
            (dy_hbm, dy_ref),
            (o_hbm.at[pl.ds(0, BACK), :], o_ref),
            (wo_hbm, wo_ref),
        ],
        sems,
    )
    gain = vec_ref[5:6, :]
    wait_all(one)

    def rows(i, sums):
        at = tile(i, 64)
        dn = part_ref[at, :] + got_ref[at, :].astype(F32)
        hat, inverse = normed(a2_ref[at, :], stat_ref[at, :])
        dy = dy_ref[at, :].astype(F32)
        da2 = dy + norm_back(dn, hat, inverse, gain)
        dz = da2.astype(BF)
        dz_ref[at, :] = dz
        if sums is None:
            return 0
        da2_ref[at, :] = da2
        return tuple(
            s + jnp.sum(v.reshape(8, 8, D), axis=0)
            for s, v in zip(sums, (dn * hat, dn, dz.astype(F32), dy))
        )

    steps = LIVE // 64
    sums = lax.fori_loop(0, steps, rows, (jnp.zeros((8, D), F32),) * 4)
    lax.fori_loop(steps, 2 * steps, lambda i, c: rows(i, None), 0)
    for i, s in enumerate(sums):
        sums_ref[i : i + 1, :] = jnp.sum(s, axis=0, keepdims=True)
    sums_ref[4:8, :] = jnp.zeros((4, D), F32)
    do_ref[...] = lax.dot_general(dz_ref[...], wo_ref[...], NT, preferred_element_type=F32).astype(BF)
    for j in range(2):
        at = slice(256 * j, 256 * (j + 1))
        whole_ref[at, :] = lax.dot_general(
            o_ref[:, at], dz_ref[...], TN, preferred_element_type=F32
        ).astype(BF)
    for k in range(8):
        mine_ref[k] = whole_ref[pl.ds(pl.multiple_of(64 * k + 32 * core, 32), 32), :]
        send_ref[k] = whole_ref[pl.ds(pl.multiple_of(64 * k + 32 - 32 * core, 32), 32), :]


def middle(part, got, a2, stat, dy, vec, o, wo):
    spec = (ANY, ANY, ANY, VMEM, ANY, VMEM, ANY, ANY)
    return launch(
        middle_kernel,
        list(zip((part, got, a2, stat, dy, vec, o, wo), spec)),
        [
            ((LIVE, D), F32),
            ((BACK, HALF_D), BF),
            ((8, D), F32),
            ((8, 32, D), BF),
            ((8, 32, D), BF),
        ],
        [
            pltpu.VMEM((BACK, D), F32),
            pltpu.VMEM((BACK, D), BF),
            pltpu.VMEM((BACK, D), F32),
            pltpu.VMEM((BACK, D), BF),
            pltpu.VMEM((BACK, HALF_D), BF),
            pltpu.VMEM((HALF_D, D), BF),
            pltpu.VMEM((BACK, D), BF),
            pltpu.VMEM((HALF_D, D), BF),
            dma(7),
        ],
        flops=1.4e9,
    )


def norm1_grad_kernel(dq_ref, dk_ref, dv_ref, wq_ref, own_ref, send_ref):
    for j in range(4):
        at = slice(256 * j, 256 * (j + 1))
        total = None
        for i in range(6):
            src = (dq_ref, dk_ref, dv_ref)[i % 3]
            off = 256 * (i // 3)
            part = lax.dot_general(
                src[:, off : off + 256],
                wq_ref[at, 256 * i : 256 * (i + 1)],
                NT,
                preferred_element_type=F32,
            )
            total = part if total is None else total + part
        own_ref[:, at] = total[:LIVE]
        send_ref[:, at] = total[LIVE:].astype(BF)


def norm1_grads(dq, dk, dv, wq):
    return launch(
        norm1_grad_kernel,
        [(v, VMEM) for v in (dq, dk, dv, wq)],
        [((LIVE, D), F32), ((LIVE, D), BF)],
        flops=1.9e9,
    )


def last_kernel(
    n1_ref, dq_ref, dk_ref, dv_ref, dn_ref, got_ref, a_ref, stat_ref, da2_ref, vec_ref, *refs
):
    place_ref, sums_ref, upsum_ref, mine_ref, theirs_ref, tok_ref = refs[:6]
    outs = refs[6:11]
    n1t_ref, whole_ref, small_ref, da_ref, rows_ref, sems = refs[11:]
    core = coords()[3]
    n1t_ref[...] = n1_ref[...].T
    for i, src in enumerate((dq_ref, dk_ref, dv_ref)):
        for j in range(2):
            at = slice(256 * j, 256 * (j + 1))
            part = jnp.dot(n1t_ref[...], src[:, at], preferred_element_type=F32)
            to = 768 * j + 256 * i
            whole_ref[:, to : to + 256] = part.astype(BF)
    count = len(ENTRIES_ZXY)
    one = start_all(
        [
            (
                whole_ref.at[pl.ds(core_rows(e), 32), :],
                piece_of(outs, e, 32, (SMALL, QKV)),
            )
            for e in ENTRIES_ZXY
        ],
        sems,
    )
    two = []
    for i, e in enumerate(ENTRIES_ZXY):
        rel, half = e[3], e[4]
        y = coords()[1]
        chip = chip_of(rel)
        slot = (chip // 4) * 2 + chip % 2
        at = pl.ds(HALF_D * half, HALF_D)
        dst = piece_of(outs, e, 32, (SMALL + QKV, HALF_D))
        here = (y if rel[1] == 0 else 1 - y) == core
        sem = sems.at[2 * count + i]
        two.append(pltpu.make_async_copy(mine_ref.at[slot, :, at], dst, sem))

        @pl.when(here)
        def _():
            pltpu.make_async_copy(mine_ref.at[slot, :, at], dst, sem).start()

        @pl.when(jnp.logical_not(here))
        def _():
            pltpu.make_async_copy(theirs_ref.at[slot, :, at], dst, sem).start()

    gain = vec_ref[0:1, :]
    zero = jnp.zeros((8, D), F32)

    def rows(i, sums):
        at = tile(i, 64)
        dn = dn_ref[at, :] + got_ref[at, :].astype(F32)
        hat, inverse = normed(a_ref[at, :], stat_ref[at, :])
        da = da2_ref[at, :] + norm_back(dn, hat, inverse, gain)
        da_ref[at, :] = da.astype(BF)
        tok_ref[at, :] = da.astype(BF)
        return tuple(
            s + jnp.sum(v.reshape(8, 8, D), axis=0) for s, v in zip(sums, (dn * hat, dn))
        )

    sums = lax.fori_loop(0, LIVE // 64, rows, (zero,) * 2)
    tok_ref[LIVE:, :] = jnp.zeros((REST, D), BF)
    lane = lax.broadcasted_iota(jnp.int32, (LIVE, 256), 1)
    hot = (place_ref[:LIVE, :] == lane).astype(BF)
    small = lax.dot_general(da_ref[...], hot, TN, preferred_element_type=F32)
    rows_ref[...] = jnp.zeros((16, D), F32)
    rows_ref[0:1, :] = jnp.sum(sums[0], axis=0, keepdims=True)
    rows_ref[1:2, :] = jnp.sum(sums[1], axis=0, keepdims=True)
    for row, src in ((2, dq_ref), (3, dv_ref)):
        total = jnp.sum(src[...].astype(F32), axis=0, keepdims=True)
        for j in range(4):
            own = pl.ds(pl.multiple_of(256 * j + 128 * core, 128), 128)
            rows_ref[row : row + 1, own] = total[:, 128 * j : 128 * (j + 1)]
    rows_ref[4:5, :] = sums_ref[2:3, :]
    rows_ref[5:6, :] = sums_ref[0:1, :]
    rows_ref[6:7, :] = sums_ref[1:2, :]
    rows_ref[7:8, :] = sums_ref[3:4, :]
    spot = lax.broadcasted_iota(jnp.int32, (16, 256), 0)
    place = (lax.broadcasted_iota(jnp.int32, (16, 256), 1) == spot + VEC0).astype(BF)
    value = rows_ref[...]
    for _ in range(2):
        piece = value.astype(BF)
        small = small + lax.dot_general(piece, place, TN, preferred_element_type=F32)
        value = value - piece.astype(F32)
    small_ref[:, :256] = small.astype(BF)
    small_ref[:, 256:] = jnp.zeros((D, SMALL - 256), BF)
    top = lax.broadcasted_iota(jnp.int32, (16, 128), 0) == 0
    for chip in range(16):
        row = pl.multiple_of(64 * chip + 32 * core, 32)
        bias = jnp.where(top, upsum_ref[:, 128 * chip : 128 * (chip + 1)], 0.0)
        small_ref[pl.ds(row, 16), 256:384] = bias.astype(BF)
    three = start_all(
        [
            (small_ref.at[pl.ds(core_rows(e), 32), :], piece_of(outs, e, 32, (0, SMALL)))
            for e in ENTRIES_ZXY
        ],
        sems,
        count,
    )
    wait_all(one + two + three)


def last_stage(n1, dq, dk, dv, dn, got, a, stat, da2, vec, place, sums, upsum, mine, theirs):
    return launch(
        last_kernel,
        [
            (v, VMEM)
            for v in (n1, dq, dk, dv, dn, got, a, stat, da2, vec, place, sums, upsum, mine, theirs)
        ],
        [((PACK, D), BF)] + [(s, BF, ANY) for s in scatter_shapes("zxy", 32, A_WIDTH)],
        [
            pltpu.VMEM((D, BACK), BF),
            pltpu.VMEM((D, QKV), BF),
            pltpu.VMEM((D, SMALL), BF),
            pltpu.VMEM((LIVE, D), BF),
            pltpu.VMEM((16, D), F32),
            dma(3 * len(ENTRIES_ZXY)),
        ],
        flops=2.2e9,
    )


def output_kernel(act_hbm, a2_hbm, vec_ref, *refs):
    parts, (own_ref, send_ref) = refs[:6], refs[6:8]
    act_ref, a2_ref, wd_ref, sems = refs[8:]
    wait_all(
        start_all(
            [
                (piece_of(parts, e, 64), wd_ref.at[pl.ds(half_rows(e), 64), :])
                for e in ENTRIES_XZY_GATHER
            ]
            + [(act_hbm, act_ref), (a2_hbm, a2_ref)],
            sems,
        )
    )
    for j in range(4):
        at = slice(256 * j, 256 * (j + 1))
        part = jnp.dot(act_ref[...], wd_ref[:, at], preferred_element_type=F32)
        whole = part + a2_ref[:, at] + vec_ref[7:8, at]
        for which, start, size, to in SEGMENTS:
            if which == 0:
                own_ref[start : start + size, at] = whole[to : to + size]
            else:
                send_ref[start : start + size, at] = part[to : to + size].astype(BF)


def output_stage(act, a2, vec, gathered):
    return launch(
        output_kernel,
        [(act, ANY), (a2, ANY), (vec, VMEM)] + [(g, ANY) for g in gathered],
        [((PACK, D), F32), ((PACK, D), BF)],
        [
            pltpu.VMEM((ROWS, HALF_FF), BF),
            pltpu.VMEM((ROWS, D), F32),
            pltpu.VMEM((HALF_FF, D), BF),
            dma(len(ENTRIES_XZY_GATHER) + 2),
        ],
        flops=3.2e9,
    )


def finish_kernel(a_ref, up_ref, small_got, qkv_got, up_got, small_ref, qkv_ref, grad_ref, out_ref):
    core = coords()[3]
    small_ref[...] = a_ref[:32, :SMALL] + small_got[...]
    for count, own, first, got, dst in (
        (12, a_ref, SMALL, qkv_got, qkv_ref),
        (16, up_ref, 0, up_got, grad_ref),
    ):
        for j in range(count):
            at = slot_of(j) if count == 12 else 128 * j
            mine = pl.ds(pl.multiple_of(256 * j + 128 * core, 128), 128)
            other = pl.ds(pl.multiple_of(256 * j + 128 - 128 * core, 128), 128)
            dst[:, mine] = own[:32, first + at : first + at + 128]
            dst[:, other] = got[:, at : at + 128]
    out_ref[:, :HALF_D] = a_ref[:32, SMALL + QKV :]
    out_ref[:, HALF_D:] = a_ref[32:, SMALL + QKV :]


def finish(a_sum, up_sum, small_got, qkv_got, up_got):
    return launch(
        finish_kernel,
        [(v, VMEM) for v in (a_sum, up_sum, small_got, qkv_got, up_got)],
        [((32, SMALL), F32), ((32, 3 * D), F32), ((32, FF), F32), ((32, D), F32)],
        limit=8,
    )


def in_order(own, sib):
    return jnp.concatenate([own[:LIVE], sib[:LIVE], own[LIVE:], sib[LIVE:]])


def fast_on_device(
    tokens,
    grad_out,
    image_lengths,
    image_device,
    small_map,
    ln1_gain,
    ln1_bias,
    qkv_weight,
    q_bias,
    v_bias,
    out_weight,
    out_bias,
    ln2_gain,
    ln2_bias,
    up_weight,
    up_bias,
    down_weight,
    down_bias,
    pos_table,
):
    device = lax.axis_index("dp") * 4 + lax.axis_index("fsdp")
    seg, place = layout(image_lengths, image_device, small_map, device, PACK)
    seg2, place2 = layout(image_lengths, image_device, small_map, device ^ 1, PACK)
    col = in_order(seg, seg2)[:, None]
    row = jnp.stack([seg, seg2])
    place = in_order(place, place2)[:, None]

    vectors = [ln1_gain, ln1_bias, q_bias, v_bias, out_bias, ln2_gain, ln2_bias, down_bias]
    table = jnp.concatenate([pos_table, jnp.stack(vectors), jnp.zeros((103, 32), BF)])
    small, keep_q, send_q, keep_u, send_u, out2 = prepare(
        table, up_bias[None, :], qkv_weight, up_weight, out_weight
    )
    got_small, got_q, got_u = swap(small, CORE), swap(send_q, CORE), swap(send_u, CORE)
    chunk_a = jnp.concatenate(
        [jnp.concatenate([small, got_small]), jnp.concatenate([keep_q, got_q]), out2], axis=1
    )
    chunk_u = jnp.concatenate([keep_u, got_u])
    sib_tokens = swap(tokens, CORE)
    sib_grad = swap(grad_out, CORE)

    flat, deep = Lane(), Lane()
    down_a, down_b = down_weight[:64], down_weight[64:]
    down_x, down_y = flat.go((down_a, XBIT), (down_b, YBIT))
    line_1 = jnp.stack(along_z(deep, chunk_a[:, :CUT]))
    line_2 = jnp.stack(along_z(deep, chunk_a[:, CUT:]))
    gathered_a = cross(flat, line_1)
    line_u = jnp.stack(along_z(deep, chunk_u))
    gathered_a += cross(flat, line_2)
    quads = along_z(deep, jnp.stack([down_a, down_x, down_b, down_y]))
    gathered_u = cross(flat, line_u)
    gathered_d = sides(flat, quads)

    a, n1, qkv, wq, out_own, vec, bf1, stat1 = first_stage(tokens, sib_tokens, place, gathered_a)
    out_other = swap(out_own, CORE)
    o, lse = attend(qkv, col, row)
    wo, total, send = project(o, a, vec, out_own, out_other)
    a2, n2, act, slope, wu, dy, stat2, *down_parts = widen(
        total, swap(send, CORE), vec, bf1, grad_out, sib_grad, col, gathered_u
    )
    quad = scatter_xzy_start(flat, deep, down_parts)
    up_bias_sum, part, send, *up_parts = hidden_grads(dy, slope, n2, wu, gathered_d)
    up_sum = scatter_zxy(flat, deep, up_parts)
    down_sum = scatter_xzy_end(flat, quad)
    da2, do, sums, mine, theirs = middle(part, swap(send, CORE), a2, stat2, dy, vec, o, wo)
    theirs = swap(theirs, CORE)
    dq, dk, dv = attend_back(qkv, do, o, lse, col, row)
    dn, send = norm1_grads(dq, dk, dv, wq)
    tokens_grad, *a_parts = last_stage(
        n1,
        dq,
        dk,
        dv,
        dn,
        swap(send, CORE),
        a,
        stat1,
        da2,
        vec,
        place,
        sums,
        up_bias_sum,
        mine,
        theirs,
    )
    a_sum = scatter_zxy(flat, deep, a_parts)
    own, send = output_stage(act, a2, vec, gathered_d)
    layer_out = (own + swap(send, CORE).astype(F32)).astype(BF)

    small_got = swap(a_sum[32:, :SMALL], CORE)
    qkv_got = swap(a_sum[32:, SMALL : SMALL + QKV], CORE)
    up_got = swap(up_sum[32:], CORE)
    small, qkv_grad, up_grad, out_grad = finish(a_sum, up_sum, small_got, qkv_got, up_got)
    gv = small[:, VEC0 : VEC0 + 8].T
    return (
        layer_out,
        tokens_grad,
        gv[0],
        gv[1],
        qkv_grad,
        gv[2],
        gv[3],
        out_grad,
        gv[4],
        gv[5],
        gv[6],
        up_grad,
        small[0, 256:],
        down_sum,
        gv[7],
        small[:, :LONG].T,
    )


def solution(mesh):
    in_specs = (
        P(("dp", "fsdp"), None),
        P(("dp", "fsdp"), None),
        P(),
        P(),
        P(),
        P(("dp", "fsdp")),
        P(("dp", "fsdp")),
        P(("dp", "fsdp"), None),
        P(("dp", "fsdp")),
        P(("dp", "fsdp")),
        P(("dp", "fsdp"), None),
        P(("dp", "fsdp")),
        P(("dp", "fsdp")),
        P(("dp", "fsdp")),
        P(("dp", "fsdp"), None),
        P(("dp", "fsdp")),
        P(("dp", "fsdp"), None),
        P(("dp", "fsdp")),
        P(None, ("dp", "fsdp")),
    )
    out_specs = (
        P(("dp", "fsdp"), None),
        P(("dp", "fsdp"), None),
        P(("dp", "fsdp")),
        P(("dp", "fsdp")),
        P(("dp", "fsdp"), None),
        P(("dp", "fsdp")),
        P(("dp", "fsdp")),
        P(("dp", "fsdp"), None),
        P(("dp", "fsdp")),
        P(("dp", "fsdp")),
        P(("dp", "fsdp")),
        P(("dp", "fsdp"), None),
        P(("dp", "fsdp")),
        P(("dp", "fsdp"), None),
        P(("dp", "fsdp")),
        P(None, ("dp", "fsdp")),
    )
    eight_by_four = mesh.shape["dp"] == 8 and mesh.shape["fsdp"] == 4
    return jax.shard_map(
        fast_on_device if eight_by_four else on_device, mesh=mesh, in_specs=in_specs, out_specs=out_specs, check_vma=False
    )
```

```python
import jax
import jax.numpy as jnp
import numpy as np
from jax import lax
from jax.experimental import pallas as pl
from jax.experimental.pallas import tpu as pltpu
from jax.sharding import PartitionSpec as P

D = 1024
HEADS = 16
HEAD = 64
FF = 4096
LONG = 145
SHORT = 50


EPS = 1e-06


def fetch(parts):
    whole = (
        lax.all_gather(parts[0], ("dp", "fsdp"), axis=1, tiled=True),
        lax.all_gather(parts[1], ("dp", "fsdp"), axis=0, tiled=True),
        lax.all_gather(parts[2], ("dp", "fsdp"), axis=0, tiled=True),
        lax.all_gather(parts[3], ("dp", "fsdp"), axis=0, tiled=True),
        lax.all_gather(parts[4], ("dp", "fsdp"), axis=0, tiled=True),
        lax.all_gather(parts[5], ("dp", "fsdp"), axis=0, tiled=True),
        lax.all_gather(parts[6], ("dp", "fsdp"), axis=1, tiled=True),
    )
    return whole


def reduce_grads(parts):
    owned = (
        lax.psum_scatter(parts[0], ("dp", "fsdp"), scatter_dimension=1, tiled=True),
        lax.psum_scatter(parts[1], ("dp", "fsdp"), scatter_dimension=0, tiled=True),
        lax.psum_scatter(parts[2], ("dp", "fsdp"), scatter_dimension=0, tiled=True),
        lax.psum_scatter(parts[3], ("dp", "fsdp"), scatter_dimension=0, tiled=True),
        lax.psum_scatter(parts[4], ("dp", "fsdp"), scatter_dimension=0, tiled=True),
        lax.psum_scatter(parts[5], ("dp", "fsdp"), scatter_dimension=0, tiled=True),
        lax.psum_scatter(parts[6], ("dp", "fsdp"), scatter_dimension=1, tiled=True),
    )
    return owned


def layout(image_lengths, image_device, small_map, device, rows_dev):
    mine = image_device == device
    lens = jnp.where(mine, image_lengths, 0)
    starts = jnp.cumsum(lens) - lens
    rows = jnp.arange(rows_dev, dtype=jnp.int32)
    inside = (
        mine[None, :]
        & (starts[None, :] <= rows[:, None])
        & (rows[:, None] < (starts + lens)[None, :])
    )
    number = jnp.arange(image_lengths.shape[0], dtype=jnp.int32)
    segment = jnp.sum(jnp.where(inside, number[None, :] + 1, 0), axis=1) - 1
    offset = rows - jnp.sum(jnp.where(inside, starts[None, :], 0), axis=1)
    length = jnp.sum(jnp.where(inside, lens[None, :], 0), axis=1)
    spots = jnp.arange(SHORT, dtype=jnp.int32)
    mapped = jnp.sum(jnp.where(offset[:, None] == spots[None, :], small_map[None, :], 0), axis=1)
    place = jnp.where(length == LONG, offset, jnp.where(length == SHORT, mapped, 0))
    return (segment, place)


def layer_norm_forward_pass(v, norm_gain, shift_bias):
    centred_rows = v - jnp.mean(v, axis=1, keepdims=True)
    inverse_deviation = lax.rsqrt(
        jnp.mean(centred_rows * centred_rows, axis=1, keepdims=True) + EPS
    )
    normalized_rows = centred_rows * inverse_deviation
    return (normalized_rows * norm_gain + shift_bias, normalized_rows, inverse_deviation)


def layer_norm_backward_pass(upstream_gradient, normalized_rows, inverse_deviation, norm_gain):
    normalized_gradient = upstream_gradient * norm_gain
    first_input = jnp.mean(normalized_gradient, axis=1, keepdims=True)
    second_input = jnp.mean(normalized_gradient * normalized_rows, axis=1, keepdims=True)
    return (
        inverse_deviation * (normalized_gradient - first_input - normalized_rows * second_input),
        jnp.sum(upstream_gradient * normalized_rows, axis=0),
        jnp.sum(upstream_gradient, axis=0),
    )


def split_heads(values, groups):
    return values.reshape(values.shape[0], groups, HEADS // groups, HEAD).transpose(1, 0, 2, 3)


def join_heads(values):
    return values.transpose(1, 0, 2, 3).reshape(values.shape[1], D)


def masked_scores(query, keys, same):
    scores = jnp.einsum("thd,shd->hts", query, keys, preferred_element_type=jnp.float32) * HEAD ** (
        -0.5
    )
    return jnp.where(same[None], scores, -1000000000.0)


def attend_forward(qkvb, same):
    groups = HEADS // 4
    query = split_heads(qkvb[:, :D], groups)
    keys = split_heads(qkvb[:, D : 2 * D], groups)
    values = split_heads(qkvb[:, 2 * D :], groups)

    def one_group(item):
        scores = masked_scores(item[0], item[1], same)
        top = jnp.max(scores, axis=2, keepdims=True)
        lse = top + jnp.log(jnp.sum(jnp.exp(scores - top), axis=2, keepdims=True))
        probs = jnp.exp(scores - lse).astype(jnp.bfloat16)
        attended = jnp.einsum("hts,shd->thd", probs, item[2], preferred_element_type=jnp.float32)
        return (attended, lse[:, :, 0])

    attended, lse = lax.map(one_group, (query, keys, values))
    return (join_heads(attended), lse)


def attend_backward(qkvb, dob, lse, same):
    groups = HEADS // 4
    query = split_heads(qkvb[:, :D], groups)
    keys = split_heads(qkvb[:, D : 2 * D], groups)
    values = split_heads(qkvb[:, 2 * D :], groups)
    douts = split_heads(dob, groups)

    def one_group(item):
        scores = masked_scores(item[0], item[1], same)
        probs = jnp.exp(scores - item[4][:, :, None])
        dvalue = jnp.einsum(
            "hts,thd->shd", probs.astype(jnp.bfloat16), item[3], preferred_element_type=jnp.float32
        )
        dprobs = jnp.einsum("thd,shd->hts", item[3], item[2], preferred_element_type=jnp.float32)
        inner = jnp.sum(probs * dprobs, axis=2, keepdims=True)
        dscore = (probs * (dprobs - inner)).astype(jnp.bfloat16)
        dquery = jnp.einsum(
            "hts,shd->thd", dscore, item[1], preferred_element_type=jnp.float32
        ) * HEAD ** (-0.5)
        dkey = jnp.einsum(
            "hts,thd->shd", dscore, item[0], preferred_element_type=jnp.float32
        ) * HEAD ** (-0.5)
        return (dquery, dkey, dvalue)

    dquery, dkey, dvalue = lax.map(one_group, (query, keys, values, douts, lse))
    return jnp.concatenate([join_heads(dquery), join_heads(dkey), join_heads(dvalue)], axis=1)


def gelu_slope(x):
    return (
        0.5 * (1.0 + jax.scipy.special.erf(x * 0.7071067811865476))
        + x * jnp.exp(-0.5 * x * x) * 0.3989422804014327
    )


def on_device(
    tokens,
    grad_out,
    image_lengths,
    image_device,
    small_map,
    ln1_gain,
    ln1_bias,
    qkv_weight,
    q_bias,
    v_bias,
    out_weight,
    out_bias,
    ln2_gain,
    ln2_bias,
    up_weight,
    up_bias,
    down_weight,
    down_bias,
    pos_table,
):
    rows_dev = tokens.shape[0]
    device = lax.axis_index("dp") * lax.axis_size("fsdp") + lax.axis_index("fsdp")
    segment, place = layout(image_lengths, image_device, small_map, device, rows_dev)
    same = segment[:, None] == segment[None, :]
    valid = (segment >= 0).astype(jnp.float32)[:, None]
    table_rows = jnp.arange(LONG, dtype=jnp.int32)
    picker = place[:, None] == table_rows[None, :]
    vectors = jnp.stack(
        [ln1_gain, ln1_bias, q_bias, v_bias, out_bias, ln2_gain, ln2_bias, down_bias]
    )
    shards = (vectors, qkv_weight, out_weight, up_weight, up_bias, down_weight, pos_table)
    whole = fetch(shards)
    vec = whole[0].astype(jnp.float32)
    first_gain, first_centred, bq, bv, bo, second_gain, second_centred, bf2 = (
        vec[0],
        vec[1],
        vec[2],
        vec[3],
        vec[4],
        vec[5],
        vec[6],
        vec[7],
    )
    bf1 = whole[4].astype(jnp.float32)
    activation_rows = tokens.astype(jnp.float32) + jnp.dot(
        picker.astype(jnp.bfloat16), whole[6], preferred_element_type=jnp.float32
    )
    first_normed, first_normalized, first_inverse_deviation = layer_norm_forward_pass(
        activation_rows, first_gain, first_centred
    )
    n1b = first_normed.astype(jnp.bfloat16)
    bias3 = jnp.concatenate([bq, jnp.zeros_like(bq), bv])
    qkvb = (jnp.dot(n1b, whole[1], preferred_element_type=jnp.float32) + bias3).astype(jnp.bfloat16)
    attended, lse = attend_forward(qkvb, same)
    ob = attended.astype(jnp.bfloat16)
    second_activation = (
        activation_rows + jnp.dot(ob, whole[2], preferred_element_type=jnp.float32) + bo
    )
    second_normed, second_normalized, second_inverse_deviation = layer_norm_forward_pass(
        second_activation, second_gain, second_centred
    )
    n2b = second_normed.astype(jnp.bfloat16)
    hpre = jnp.dot(n2b, whole[3], preferred_element_type=jnp.float32) + bf1
    actb = jax.nn.gelu(hpre, approximate=False).astype(jnp.bfloat16)
    output = second_activation + jnp.dot(actb, whole[5], preferred_element_type=jnp.float32) + bf2
    layer_out = output.astype(jnp.bfloat16)
    dy = grad_out.astype(jnp.float32) * valid
    fenced, dy = lax.optimization_barrier((shards, dy))
    back = fetch(fenced)
    dyb = dy.astype(jnp.bfloat16)
    d_down = jnp.einsum("tf,td->fd", actb, dyb, preferred_element_type=jnp.float32)
    d_down_bias = jnp.sum(dy, axis=0)
    dgate = jnp.einsum("td,fd->tf", dyb, back[5], preferred_element_type=jnp.float32)
    dhb = (dgate * gelu_slope(hpre)).astype(jnp.bfloat16)
    d_up = jnp.einsum("td,tf->df", n2b, dhb, preferred_element_type=jnp.float32)
    d_up_bias = jnp.sum(dhb.astype(jnp.float32), axis=0)
    second_norm_gradient = jnp.einsum("tf,df->td", dhb, back[3], preferred_element_type=jnp.float32)
    second_activation_norm_gradient, second_gain_gradient, second_centred_gradient = (
        layer_norm_backward_pass(
            second_norm_gradient, second_normalized, second_inverse_deviation, second_gain
        )
    )
    da2 = dy + second_activation_norm_gradient
    dzb = da2.astype(jnp.bfloat16)
    d_out = jnp.einsum("te,td->ed", ob, dzb, preferred_element_type=jnp.float32)
    d_out_bias = jnp.sum(dzb.astype(jnp.float32), axis=0)
    dob = jnp.einsum("td,ed->te", dzb, back[2], preferred_element_type=jnp.float32).astype(
        jnp.bfloat16
    )
    dqkvb = attend_backward(qkvb, dob, lse, same).astype(jnp.bfloat16)
    d_qkv = jnp.einsum("td,te->de", n1b, dqkvb, preferred_element_type=jnp.float32)
    dqkv_sum = jnp.sum(dqkvb.astype(jnp.float32), axis=0)
    first_norm_gradient = jnp.einsum(
        "te,de->td", dqkvb, back[1], preferred_element_type=jnp.float32
    )
    first_activation_gradient, first_gain_gradient, first_centred_gradient = (
        layer_norm_backward_pass(
            first_norm_gradient, first_normalized, first_inverse_deviation, first_gain
        )
    )
    da = da2 + first_activation_gradient
    tokens_grad = da.astype(jnp.bfloat16)
    d_pos = jnp.dot(picker.astype(jnp.float32).T, da, precision=lax.Precision.HIGHEST)
    d_vectors = jnp.stack(
        [
            first_gain_gradient,
            first_centred_gradient,
            dqkv_sum[:D],
            dqkv_sum[2 * D :],
            d_out_bias,
            second_gain_gradient,
            second_centred_gradient,
            d_down_bias,
        ]
    )
    flat_parts = (
        d_vectors,
        d_qkv.reshape(-1, 128),
        d_out.reshape(-1, 128),
        d_up.reshape(-1, 128),
        d_up_bias,
        d_down,
        d_pos,
    )
    owned = reduce_grads(flat_parts)
    gv = owned[0]
    qkv_owned = owned[1].reshape(-1, 3 * D)
    out_owned = owned[2].reshape(-1, D)
    up_owned = owned[3].reshape(-1, FF)
    return (
        layer_out,
        tokens_grad,
        gv[0],
        gv[1],
        qkv_owned,
        gv[2],
        gv[3],
        out_owned,
        gv[4],
        gv[5],
        gv[6],
        up_owned,
        owned[4],
        owned[5],
        gv[7],
        owned[6],
    )


BF = jnp.bfloat16
F32 = jnp.float32
AXES = ("dp", "fsdp")
CORE, XBIT, YBIT, ZBIT = 1, 2, 4, 8
PACK = 384
LIVE = -(-2 * LONG // 64) * 64
REST = PACK - LIVE
ROWS = 2 * PACK
BACK = 2 * LIVE
HALF_FF = FF // 2
QKV = 3 * D // 2
HALF_D = D // 2
SMALL = 384
HALF_QKV = QKV // 2
CUT = SMALL + HALF_QKV
VEC0 = LONG
SEGMENTS = ((0, 0, LIVE, 0), (1, 0, LIVE, LIVE), (0, LIVE, REST, BACK), (1, LIVE, REST, BACK + REST))
NT = (((1,), (1,)), ((), ()))
TN = (((0,), (0,)), ((), ()))


def swap(value, mask):
    return lax.ppermute(value, AXES, [(i, i ^ mask) for i in range(32)])


def coords():
    dp = lax.axis_index("dp")
    fs = lax.axis_index("fsdp")
    return dp // 2, dp % 2, fs // 2, fs % 2


def chip_of(rel):
    z, y, x, _ = coords()
    dz, dy, dx = rel
    bits = 0
    for part, off, width in ((z // 2, dz // 2, 8), (z % 2, dz % 2, 4), (y, dy, 2), (x, dx, 1)):
        bits = bits + (1 - part if off else part) * width
    return bits


ZORDER = (0, 2, 1, 3)
ENTRIES_ZXY = (
    [(0, (k,), h, (z, 0, 0), h) for k, z in enumerate(ZORDER) for h in range(2)]
    + [(1, (k,), h, (z, 0, 1), h) for k, z in enumerate(ZORDER) for h in range(2)]
    + [(2, (k,), h, (z, 1, 0), h) for k, z in enumerate(ZORDER) for h in range(2)]
    + [(3, (k,), h, (z, 1, 1), h) for k, z in enumerate(ZORDER[:2]) for h in range(2)]
    + [(4, (k,), h, (z, 1, 1), h) for k, z in enumerate(ZORDER[2:]) for h in range(2)]
)
QUADS = (((0, 0), 0), ((0, 1), 0), ((0, 0), 1), ((1, 0), 1))
SIDE_A = ((1, 0), (1, 1))
SIDE_B = ((0, 1), (1, 1))
ENTRIES_XZY_GATHER = (
    [
        (k // 2, (k % 2, q), 0, (z,) + QUADS[q][0], QUADS[q][1])
        for k, z in enumerate(ZORDER)
        for q in range(4)
    ]
    + [(2, (k, q), 0, (z,) + SIDE_A[q], 0) for k, z in enumerate(ZORDER) for q in range(2)]
    + [(3, (k, q), 0, (z,) + SIDE_B[q], 1) for k, z in enumerate(ZORDER) for q in range(2)]
)
ENTRIES_XZY_SCATTER = (
    [
        (0, (k, q), 0, (z,) + QUADS[q][0], QUADS[q][1])
        for k, z in enumerate(ZORDER)
        for q in range(4)
    ]
    + [(1, (k, q), 0, (z,) + SIDE_A[q], 0) for k, z in enumerate(ZORDER) for q in range(2)]
    + [(2, (k, q), 0, (z,) + SIDE_B[q], 1) for k, z in enumerate(ZORDER) for q in range(2)]
)


class Lane:
    def __init__(self, depth):
        self.depth = depth
        self.groups = []

    def go(self, *pairs):
        values = tuple(value for value, _ in pairs)
        if len(self.groups) >= self.depth:
            values, _ = lax.optimization_barrier((values, self.groups[-self.depth]))
        got = tuple(swap(value, mask) for value, (_, mask) in zip(values, pairs))
        self.groups.append(got)
        return got


def after(value, *done):
    return lax.optimization_barrier((value, done))[0]


def along_z(lane, block):
    (far,) = lane.go((block, 2 * ZBIT))
    pair = jnp.stack([block, far])
    (near,) = lane.go((pair, ZBIT))
    return pair, near


def cross(lane, line):
    from_x, from_y = lane.go((line, XBIT), (line, YBIT))
    corners = lane.go((from_x[:2], YBIT), (from_y[2:], XBIT))
    return [line, from_x, from_y, *corners]


def sides(lane, quads):
    side_a = jnp.concatenate([q[:, :2] for q in quads])
    side_b = jnp.concatenate([q[:, 2:] for q in quads])
    return [*quads, *lane.go((side_a, YBIT), (side_b, XBIT))]


def add(*values):
    total = values[0].astype(F32)
    for value in values[1:]:
        total = total + value.astype(F32)
    return total


def down_z(lane, blocks):
    (near,) = lane.go((blocks[2:].astype(BF), ZBIT))
    pair = add(blocks[:2], near)
    (far,) = lane.go((pair[1].astype(BF), 2 * ZBIT))
    return add(pair[0], far)


def scatter_zxy(flat, deep, parts):
    line, to_x, to_y, corner_a, corner_b = parts
    got_a, got_b = flat.go((corner_a, XBIT), (corner_b, YBIT))
    to_x = jnp.concatenate([to_x[:2], add(to_x[2:], got_b).astype(BF)])
    to_y = jnp.concatenate([add(to_y[:2], got_a).astype(BF), to_y[2:]])
    got_x, got_y = flat.go((to_x, XBIT), (to_y, YBIT))
    return down_z(deep, add(line, got_x, got_y))


def scatter_xzy_start(flat, deep, parts):
    keep, side_a, side_b = parts
    got_a, got_b = flat.go((side_a, YBIT), (side_b, XBIT))
    return down_z(deep, add(keep, jnp.concatenate([got_a, got_b], axis=1)))


def scatter_xzy_end(flat, quad):
    got_x, got_y = flat.go((quad[1].astype(BF), XBIT), (quad[3].astype(BF), YBIT))
    return jnp.concatenate([add(quad[0], got_x), add(quad[2], got_y)])


def scatter_shapes(kind, rows, width):
    if kind == "zxy":
        return [(4, 2 * rows, width)] * 3 + [(2, 2 * rows, width)] * 2
    return [(4, 4, rows, width), (4, 2, rows, width), (4, 2, rows, width)]


SCATTER_ENTRIES = {"zxy": ENTRIES_ZXY, "xzy": ENTRIES_XZY_SCATTER}


def piece_of(refs, entry, rows, lanes=None):
    array, index, row, _, _ = entry
    width = pl.ds(*lanes) if lanes else slice(None)
    return refs[array].at[index + (pl.ds(rows * row, rows), width)]


def start_all(copies, sems, first=0):
    started = []
    for i, (src, dst) in enumerate(copies):
        copy = pltpu.make_async_copy(src, dst, sems.at[first + i])
        copy.start()
        started.append(copy)
    return started


def wait_all(started):
    for copy in started:
        copy.wait()


def core_rows(entry):
    core = coords()[3]
    side = core if entry[4] == 0 else 1 - core
    return pl.multiple_of(chip_of(entry[3]) * 64 + side * 32, 32)


def z_of(dz):
    z = coords()[0]
    high, low = z // 2, z % 2
    return 2 * (1 - high if dz // 2 else high) + (1 - low if dz % 2 else low)


def half_rows(entry):
    return pl.multiple_of(chip_of(entry[3]) * 128 + 64 * entry[4], 64)


def tile(i, width):
    return pl.ds(pl.multiple_of(i * width, width), width)


ANY = pl.BlockSpec(memory_space=pl.ANY)
VMEM = pl.BlockSpec(memory_space=pltpu.VMEM)


def launch(kernel, ins, outs, scratch=(), flops=0, limit=56):
    size = sum(int(np.prod(o[0])) * jnp.dtype(o[1]).itemsize for o in outs)
    for value, _ in ins:
        size += value.size * value.dtype.itemsize
    return pl.pallas_call(
        kernel,
        out_shape=[jax.ShapeDtypeStruct(o[0], o[1]) for o in outs],
        in_specs=[spec for _, spec in ins],
        out_specs=[o[2] if len(o) > 2 else VMEM for o in outs],
        scratch_shapes=list(scratch),
        cost_estimate=pl.CostEstimate(flops=int(flops), bytes_accessed=int(size), transcendentals=0),
        compiler_params=pltpu.CompilerParams(vmem_limit_bytes=limit << 20),
    )(*[value for value, _ in ins])


def dma(count):
    return pltpu.SemaphoreType.DMA((count,))


def norm_rows(v):
    mean = jnp.mean(v, axis=1, keepdims=True)
    centred = v - mean
    inverse = lax.rsqrt(jnp.mean(centred * centred, axis=1, keepdims=True) + EPS)
    return centred * inverse, mean, inverse


def stats(mean, inverse):
    lane = lax.broadcasted_iota(jnp.int32, (mean.shape[0], 128), 1)
    return jnp.where(lane == 0, mean, inverse)


def normed(v, stat):
    return (v - stat[:, 0:1]) * stat[:, 1:2], stat[:, 1:2]


def gelu_parts(h):
    bell = jnp.exp(h * h * -0.5)
    base = 1.0 + jnp.abs(h) * (0.3275911 * 0.7071067811865476)
    t = pl.reciprocal(base, approx=True)
    t = t * (2.0 - base * t)
    poly = 0.5 * 1.061405429
    for factor in (-1.453152027, 1.421413741, -0.284496736, 0.254829592):
        poly = poly * t + 0.5 * factor
    tail = poly * t * bell
    return jnp.where(h >= 0, 1.0 - tail, tail), bell


def norm_back(dn, hat, inverse, gain):
    scaled = dn * gain
    first = jnp.mean(scaled, axis=1, keepdims=True)
    second = jnp.mean(scaled * hat, axis=1, keepdims=True)
    return inverse * (scaled - first - hat * second)


def slot_of(block):
    which, j = divmod(block, 4)
    return 768 * (j // 2) + 256 * which + 128 * (j % 2)


def prepare_kernel(pos_ref, bias_ref, qkv_ref, up_ref, out_ref, keep_ref, send_ref, out2_ref):
    core = coords()[3]
    eye = (
        lax.broadcasted_iota(jnp.int32, (32, 32), 0) == lax.broadcasted_iota(jnp.int32, (32, 32), 1)
    ).astype(BF)
    small = lax.dot_general(eye, pos_ref[...], NT, preferred_element_type=F32)
    first_row = lax.broadcasted_iota(jnp.int32, (32, 128), 0) == 0
    bias = jnp.where(first_row, bias_ref[...].astype(F32), 0.0)
    small = jnp.concatenate([small, bias], axis=1).astype(BF)
    keep_ref[:, :SMALL] = small
    send_ref[:, :SMALL] = small
    for src, first, count in ((qkv_ref, SMALL, 12), (up_ref, SMALL + QKV, 16)):
        for j in range(count):
            own = pl.ds(pl.multiple_of(256 * j + 128 * core, 128), 128)
            other = pl.ds(pl.multiple_of(256 * j + 128 * (1 - core), 128), 128)
            to = first + (slot_of(j) if count == 12 else 128 * j)
            keep_ref[:, to : to + 128] = src[:, own]
            send_ref[:, to : to + 128] = src[:, other]
    out2_ref[:32] = out_ref[:, :HALF_D]
    out2_ref[32:] = out_ref[:, HALF_D:]


def prepare(pos, bias, qkv, up, out):
    shapes = [(32, SMALL + QKV + HALF_FF)] * 2 + [(64, HALF_D)]
    return launch(
        prepare_kernel,
        [(v, VMEM) for v in (pos, bias, qkv, up, out)],
        [(s, BF) for s in shapes],
        limit=8,
    )


def fill_bias(bias_ref, vec_ref, half):
    core = coords()[3]
    for j in range(2):
        own = pl.ds(pl.multiple_of(256 * (2 * half + j) + 128 * core, 128), 128)
        bias_ref[0:1, 128 * j : 128 * (j + 1)] = vec_ref[2:3, own]
        bias_ref[0:1, 256 + 128 * j : 256 + 128 * (j + 1)] = jnp.zeros((1, 128), F32)
        bias_ref[0:1, 512 + 128 * j : 512 + 128 * (j + 1)] = vec_ref[3:4, own]


def first_kernel(own_hbm, sib_hbm, place_ref, *refs):
    parts, refs = refs[:5], refs[5:]
    a_hbm, n1_hbm, wq_hbm, qkv_ref, vec_ref, bf1_ref, stat_ref = refs[:7]
    tok_ref, a_ref, n1_ref, wq_ref, small_ref, bias_ref, sems, out_sems = refs[7:]
    core = coords()[3]
    count = len(ENTRIES_ZXY)
    one = start_all(
        [
            (piece_of(parts, e, 32, (0, SMALL)), small_ref.at[pl.ds(core_rows(e), 32), :])
            for e in ENTRIES_ZXY
        ]
        + [
            (
                (own_hbm if which == 0 else sib_hbm).at[pl.ds(start, size), :],
                tok_ref.at[pl.ds(to, size), :],
            )
            for which, start, size, to in SEGMENTS
        ],
        sems,
    )
    two = start_all(
        [
            (piece_of(parts, e, 32, (SMALL, HALF_QKV)), wq_ref.at[pl.ds(core_rows(e), 32), :])
            for e in ENTRIES_ZXY
        ],
        sems,
        count + 4,
    )
    wait_all(one)
    lane = lax.broadcasted_iota(jnp.int32, (16, 256), 1)
    pick = (lane == lax.broadcasted_iota(jnp.int32, (16, 256), 0) + VEC0).astype(BF)
    vec_ref[...] = lax.dot_general(pick, small_ref[:, :256], NT, preferred_element_type=F32)
    for chip in range(16):
        row = pl.multiple_of(64 * chip + 32 * core, 32)
        bf1_ref[:, 128 * chip : 128 * (chip + 1)] = small_ref[pl.ds(row, 16), 256:384][:1].astype(F32)
    fill_bias(bias_ref, vec_ref, 0)
    hot = (place_ref[...] == lax.broadcasted_iota(jnp.int32, (ROWS, 256), 1)).astype(BF)
    for j in range(2):
        at = slice(512 * j, 512 * (j + 1))
        a_ref[:, at] = tok_ref[:, at].astype(F32) + lax.dot_general(
            hot, small_ref[at, :256], NT, preferred_element_type=F32
        )
    gain, shift = vec_ref[0:1, :], vec_ref[1:2, :]

    def rows(i, carry):
        hat, mean, inverse = norm_rows(a_ref[tile(i, 64), :])
        n1_ref[tile(i, 64), :] = (hat * gain + shift).astype(BF)
        stat_ref[tile(i, 64), :] = stats(mean, inverse)
        return carry

    lax.fori_loop(0, ROWS // 64, rows, 0)
    outs = start_all([(a_ref, a_hbm), (n1_ref, n1_hbm)], out_sems)
    wait_all(two)
    outs += start_all([(wq_ref, wq_hbm)], out_sems, 2)
    product = jnp.dot(n1_ref[...], wq_ref[...], preferred_element_type=F32)
    qkv_ref[...] = (product + bias_ref[0:1, :]).astype(BF)
    wait_all(outs)


def first_stage(own, sib, place, gathered):
    return launch(
        first_kernel,
        [(own, ANY), (sib, ANY), (place, VMEM)] + [(g, ANY) for g in gathered],
        [
            ((ROWS, D), F32, ANY),
            ((ROWS, D), BF, ANY),
            ((D, HALF_QKV), BF, ANY),
            ((ROWS, HALF_QKV), BF),
            ((16, D), F32),
            ((1, HALF_FF), F32),
            ((ROWS, 128), F32),
        ],
        [
            pltpu.VMEM((ROWS, D), BF),
            pltpu.VMEM((ROWS, D), F32),
            pltpu.VMEM((ROWS, D), BF),
            pltpu.VMEM((D, HALF_QKV), BF),
            pltpu.VMEM((D, SMALL), BF),
            pltpu.VMEM((8, HALF_QKV), F32),
            dma(2 * len(ENTRIES_ZXY) + 4),
            dma(3),
        ],
        flops=1.2e9,
    )


def second_kernel(n1_hbm, vec_ref, *refs):
    parts, refs = refs[:5], refs[5:]
    wq_hbm, qkv_ref, wo_ref, n1_ref, wq_ref, bias_ref, sems, out_sem = refs
    count = len(ENTRIES_ZXY)
    one = start_all(
        [(n1_hbm, n1_ref)]
        + [
            (piece_of(parts, e, 32, (0, HALF_QKV)), wq_ref.at[pl.ds(core_rows(e), 32), :])
            for e in ENTRIES_ZXY
        ],
        sems,
    )
    two = start_all(
        [
            (
                piece_of(parts, e, 32, (HALF_QKV, HALF_D)),
                wo_ref.at[chip_of(e[3]), :, pl.ds(HALF_D * e[4], HALF_D)],
            )
            for e in ENTRIES_ZXY
        ],
        sems,
        count + 1,
    )
    fill_bias(bias_ref, vec_ref, 1)
    wait_all(one)
    outs = start_all([(wq_ref, wq_hbm)], out_sem)
    product = jnp.dot(n1_ref[...], wq_ref[...], preferred_element_type=F32)
    qkv_ref[...] = (product + bias_ref[0:1, :]).astype(BF)
    wait_all(two + outs)


def second_stage(n1, vec, gathered):
    return launch(
        second_kernel,
        [(n1, ANY), (vec, VMEM)] + [(g, ANY) for g in gathered],
        [((D, HALF_QKV), BF, ANY), ((ROWS, HALF_QKV), BF), ((16, 32, D), BF)],
        [
            pltpu.VMEM((ROWS, D), BF),
            pltpu.VMEM((D, HALF_QKV), BF),
            pltpu.VMEM((8, HALF_QKV), F32),
            dma(2 * len(ENTRIES_ZXY) + 1),
            dma(1),
        ],
        flops=1.2e9,
    )


def pack_rows(ref, pack):
    main = ref[LIVE * pack : LIVE * (pack + 1), :]
    return jnp.concatenate([main, ref[BACK + REST * pack : BACK + REST * (pack + 1), :]])


def attend_kernel(q_ref, k_ref, v_ref, col_ref, row_ref, o_ref, lse_ref):
    first = lax.broadcasted_iota(jnp.int32, (PACK, 128), 1) < HEAD
    for pack in range(2):
        q, k, v = (pack_rows(r, pack) for r in (q_ref, k_ref, v_ref))
        same = pack_rows(col_ref, pack) == row_ref[pack : pack + 1, :]
        outs, logs = [], []
        for h in range(2):
            mine = first if h == 0 else ~first
            scores = lax.dot_general(
                jnp.where(mine, q * HEAD ** (-0.5), 0), k, NT, preferred_element_type=F32
            )
            scores = jnp.where(same, scores, -1000000000.0)
            top = jnp.max(scores, axis=1, keepdims=True)
            powers = jnp.exp(scores - top)
            total = jnp.sum(powers, axis=1, keepdims=True)
            mixed = jnp.dot(powers.astype(BF), v, preferred_element_type=F32)
            outs.append(mixed * (1.0 / total))
            logs.append(top + jnp.log(total))
        o = jnp.where(first, outs[0], outs[1]).astype(BF)
        lse = jnp.where(first, logs[0], logs[1])
        o_ref[LIVE * pack : LIVE * (pack + 1), :] = o[:LIVE]
        o_ref[BACK + REST * pack : BACK + REST * (pack + 1), :] = o[LIVE:]
        lse_ref[LIVE * pack : LIVE * (pack + 1), :] = lse[:LIVE]


def attend(qkv, col, row):
    part = lambda off: pl.BlockSpec((ROWS, 128), lambda j: (0, j + off))
    return pl.pallas_call(
        attend_kernel,
        grid=(2,),
        in_specs=[
            part(0),
            part(2),
            part(4),
            pl.BlockSpec((ROWS, 1), lambda j: (0, 0)),
            pl.BlockSpec((2, PACK), lambda j: (0, 0)),
        ],
        out_specs=[part(0), pl.BlockSpec((BACK, 128), lambda j: (0, j))],
        out_shape=[
            jax.ShapeDtypeStruct((ROWS, 256), BF),
            jax.ShapeDtypeStruct((BACK, 256), F32),
        ],
        cost_estimate=pl.CostEstimate(flops=int(8e8), bytes_accessed=4000000, transcendentals=0),
        compiler_params=pltpu.CompilerParams(vmem_limit_bytes=32 << 20),
    )(qkv, qkv, qkv, col, row)


def attend_back(q_ref, g_ref, o_ref, lse_ref, col_ref, row_ref, out_ref):
    first = lax.broadcasted_iota(jnp.int32, (LIVE, 128), 1) < HEAD
    scale = HEAD ** (-0.5)

    def pair(i, carry):
        pack, j = i // 2, i % 2
        at = pl.ds(pl.multiple_of(LIVE * pack, LIVE), LIVE)
        lanes = lambda which: pl.ds(pl.multiple_of(256 * which + 128 * j, 128), 128)
        q, k, v = (q_ref[at, lanes(which)] for which in range(3))
        g = g_ref[at, lanes(0)]
        weighted = g.astype(F32) * o_ref[at, lanes(0)].astype(F32)
        logs = lse_ref[at, lanes(0)]
        same = col_ref[at, :] == row_ref[pl.ds(pack, 1), :LIVE]
        dq, dk, dv = [], [], []
        for h in range(2):
            mine = first if h == 0 else ~first
            lse = logs[:, HEAD * h : HEAD * h + 1]
            inner = jnp.sum(jnp.where(mine, weighted, 0.0), axis=1, keepdims=True)
            qs = jnp.where(mine, q * scale, 0)
            scores = lax.dot_general(qs, k, NT, preferred_element_type=F32)
            probs = jnp.where(same, jnp.exp(scores - lse), 0.0)
            dprobs = lax.dot_general(jnp.where(mine, g, 0), v, NT, preferred_element_type=F32)
            ds = (probs * (dprobs - inner)).astype(BF)
            dv.append(lax.dot_general(probs.astype(BF), g, TN, preferred_element_type=F32))
            dq.append(jnp.dot(ds, k, preferred_element_type=F32))
            dk.append(lax.dot_general(ds, q, TN, preferred_element_type=F32))
        out_ref[at, lanes(0)] = (jnp.where(first, dq[0], dq[1]) * scale).astype(BF)
        out_ref[at, lanes(1)] = (jnp.where(first, dk[0], dk[1]) * scale).astype(BF)
        out_ref[at, lanes(2)] = jnp.where(first, dv[0], dv[1]).astype(BF)
        return carry

    lax.fori_loop(0, 4, pair, 0)


def head_rows(k, core):
    return (k // 2) * 4 + 2 * core + k % 2


def project_kernel(o0_ref, o1_ref, a_hbm, vec_ref, own_hbm, other_hbm, *refs):
    wo_ref, sum_ref, send0_ref, send1_ref, a_ref, sems = refs
    core = coords()[3]
    copies = []
    for k in range(8):
        head = head_rows(k, core)
        copies.append(
            (own_hbm.at[head], wo_ref.at[pl.ds(pl.multiple_of(64 * k + 32 * core, 32), 32), :])
        )
        copies.append(
            (other_hbm.at[head], wo_ref.at[pl.ds(pl.multiple_of(64 * k + 32 - 32 * core, 32), 32), :])
        )
    started = start_all(copies + [(a_hbm, a_ref)], sems)
    wait_all(started)
    for j in range(4):
        at = slice(256 * j, 256 * (j + 1))
        part = jnp.dot(o0_ref[...], wo_ref[:256, at], preferred_element_type=F32) + jnp.dot(
            o1_ref[...], wo_ref[256:, at], preferred_element_type=F32
        )
        send_ref = (send0_ref, send1_ref)[j // 2]
        send_ref[:, 256 * (j % 2) : 256 * (j % 2 + 1)] = part.astype(BF)
        sum_ref[:, at] = a_ref[:, at] + part + vec_ref[4:5, at]


def project(o, a, vec, own, other):
    return launch(
        project_kernel,
        [(o[0], VMEM), (o[1], VMEM), (a, ANY), (vec, VMEM), (own, ANY), (other, ANY)],
        [((HALF_D, D), BF), ((ROWS, D), F32), ((ROWS, HALF_D), BF), ((ROWS, HALF_D), BF)],
        [pltpu.VMEM((ROWS, D), F32), dma(17)],
        flops=0.8e9,
    )


SWAPPED = ((0, LIVE, LIVE), (LIVE, 0, LIVE), (BACK, BACK + REST, REST), (BACK + REST, BACK, REST))


def widen_kernel(sum_hbm, got0_hbm, got1_hbm, vec_ref, bf1_ref, own_hbm, sib_hbm, col_ref, *refs):
    parts, refs = refs[:5], refs[5:]
    n2_hbm, act_hbm, slope_hbm, stat_ref = refs[:4]
    outs, refs = refs[4:7], refs[7:]
    a2_ref, got_ref, n2_ref, wu_ref, act_ref, slope_ref, dy_ref, whole_ref, h0, h1 = refs[:10]
    sems, out_sems, grad_sems = refs[10:]
    first = start_all(
        [(sum_hbm, a2_ref)]
        + [
            (src.at[pl.ds(start, size), :], got_ref.at[pl.ds(to, size), pl.ds(HALF_D * i, HALF_D)])
            for i, src in enumerate((got0_hbm, got1_hbm))
            for to, start, size in SWAPPED
        ],
        sems,
    )
    grads = start_all(
        [
            (src.at[pl.ds(0, LIVE), :], dy_ref.at[pl.ds(LIVE * i, LIVE), :])
            for i, src in enumerate((own_hbm, sib_hbm))
        ],
        sems,
        9,
    )
    weights = start_all(
        [(piece_of(parts, e, 32), wu_ref.at[pl.ds(core_rows(e), 32), :]) for e in ENTRIES_ZXY],
        sems,
        11,
    )
    gain, shift = vec_ref[5:6, :], vec_ref[6:7, :]
    wait_all(first)

    def rows(i, carry):
        at = tile(i, 64)
        a2 = a2_ref[at, :] + got_ref[at, :].astype(F32)
        hat, mean, inverse = norm_rows(a2)
        n2_ref[at, :] = (hat * gain + shift).astype(BF)
        stat_ref[at, :] = stats(mean, inverse)
        return carry

    lax.fori_loop(0, ROWS // 64, rows, 0)
    wait_all(weights)
    sent = start_all([(n2_ref.at[pl.ds(0, BACK), :], n2_hbm)], out_sems)
    steps = HALF_FF // 256
    hidden = (h0, h1)

    def product(j):
        hidden[j % 2][...] = jnp.dot(
            n2_ref[...], wu_ref[:, 256 * j : 256 * (j + 1)], preferred_element_type=F32
        )

    product(0)
    for j in range(steps):
        if j + 1 < steps:
            product(j + 1)
        at = slice(256 * j, 256 * (j + 1))
        h = hidden[j % 2][...] + bf1_ref[:, at]
        area, bell = gelu_parts(h)
        act_ref[:, at] = (h * area).astype(BF)
        slope_ref[:, at] = (
            area[:BACK] + h[:BACK] * bell[:BACK] * 0.3989422804014327
        ).astype(BF)
        sent += start_all(
            [
                (act_ref.at[:, pl.ds(256 * j, 256)], act_hbm.at[:, pl.ds(256 * j, 256)]),
                (slope_ref.at[:, pl.ds(256 * j, 256)], slope_hbm.at[:, pl.ds(256 * j, 256)]),
            ],
            out_sems,
            1 + 2 * j,
        )
    wait_all(grads)
    dy_ref[...] = jnp.where(col_ref[:BACK, :] >= 0, dy_ref[...], 0)

    for k, dz in enumerate(ZORDER):
        first_row = pl.multiple_of(512 * z_of(dz), 512)
        at = pl.ds(first_row, 512)
        part = lax.dot_general(act_ref[:BACK, at], dy_ref[...], TN, preferred_element_type=F32)
        whole_ref[at, :] = part.astype(BF)
        mine = [e for e in ENTRIES_XZY_SCATTER if e[3][0] == dz]
        sent += start_all(
            [(whole_ref.at[pl.ds(half_rows(e), 64), :], piece_of(outs, e, 64)) for e in mine],
            grad_sems,
            len(mine) * k,
        )
    wait_all(sent)


def widen(total, got, vec, bf1, own, sib, col, gathered):
    return launch(
        widen_kernel,
        [(total, ANY), (got[0], ANY), (got[1], ANY), (vec, VMEM), (bf1, VMEM), (own, ANY), (sib, ANY), (col, VMEM)]
        + [(g, ANY) for g in gathered],
        [
            ((BACK, D), BF, ANY),
            ((ROWS, HALF_FF), BF, ANY),
            ((BACK, HALF_FF), BF, ANY),
            ((ROWS, 128), F32),
        ]
        + [(s, BF, ANY) for s in scatter_shapes("xzy", 64, D)],
        [
            pltpu.VMEM((ROWS, D), F32),
            pltpu.VMEM((ROWS, D), BF),
            pltpu.VMEM((ROWS, D), BF),
            pltpu.VMEM((D, HALF_FF), BF),
            pltpu.VMEM((ROWS, HALF_FF), BF),
            pltpu.VMEM((BACK, HALF_FF), BF),
            pltpu.VMEM((BACK, D), BF),
            pltpu.VMEM((HALF_FF, D), BF),
            pltpu.VMEM((ROWS, 256), F32),
            pltpu.VMEM((ROWS, 256), F32),
            dma(11 + len(ENTRIES_ZXY)),
            dma(1 + 2 * (HALF_FF // 256)),
            dma(len(ENTRIES_XZY_SCATTER)),
        ],
        flops=5.8e9,
    )


def hidden_grad_kernel(own_hbm, sib_hbm, col_ref, slope_hbm, n2_hbm, *refs):
    ups, parts, refs = refs[:5], refs[5:9], refs[9:]
    sum_ref, part_hbm, send0_hbm, send1_hbm = refs[:4]
    outs, refs = refs[4:9], refs[9:]
    dy_ref, slope_ref, n2_ref, n2t_ref, wu_ref, wd_ref, dh_ref, whole_ref = refs[:8]
    part_ref, send_ref, sems, slope_sems, wd_sems, out_sems, last_sems = refs[8:]
    one = start_all(
        [(n2_hbm, n2_ref)]
        + [
            (src.at[pl.ds(0, LIVE), :], dy_ref.at[pl.ds(LIVE * i, LIVE), :])
            for i, src in enumerate((own_hbm, sib_hbm))
        ],
        sems,
    )
    weights, slopes = [], []
    for k, dz in enumerate(ZORDER):
        at = tile(z_of(dz), 512)
        mine = [e for e in ENTRIES_XZY_GATHER if e[3][0] == dz]
        weights.append(
            start_all(
                [(piece_of(parts, e, 64), wd_ref.at[pl.ds(half_rows(e), 64), :]) for e in mine],
                wd_sems,
                len(mine) * k,
            )
        )
        slopes.append(start_all([(slope_hbm.at[:, at], slope_ref.at[:, at])], slope_sems, k))
    two = start_all(
        [(piece_of(ups, e, 32), wu_ref.at[pl.ds(core_rows(e), 32), :]) for e in ENTRIES_ZXY],
        sems,
        3,
    )
    wait_all(one)
    n2t_ref[...] = n2_ref[...].T
    dy_ref[...] = jnp.where(col_ref[:BACK, :] >= 0, dy_ref[...], 0)
    sent = []
    count = len(ENTRIES_ZXY)
    for k, dz in enumerate(ZORDER):
        at = tile(z_of(dz), 512)
        wait_all(weights[k] + slopes[k])
        gate = lax.dot_general(dy_ref[...], wd_ref[at, :], NT, preferred_element_type=F32)
        dh = (gate * slope_ref[:, at].astype(F32)).astype(BF)
        dh_ref[:, at] = dh
        sum_ref[:, at] = jnp.sum(dh.astype(F32), axis=0, keepdims=True)
        whole_ref[:, at] = jnp.dot(
            n2t_ref[...], dh_ref[:, at], preferred_element_type=F32
        ).astype(BF)
        for i, e in enumerate(ENTRIES_ZXY):
            src = whole_ref.at[pl.ds(core_rows(e), 32), at]
            array, index, row = e[:3]
            dst = outs[array].at[index + (pl.ds(32 * row, 32), at)]
            sent += start_all([(src, dst)], out_sems, count * k + i)
    wait_all(two)
    for j in range(2):
        at = slice(512 * j, 512 * (j + 1))
        part = lax.dot_general(dh_ref[...], wu_ref[at, :], NT, preferred_element_type=F32)
        part_ref[:, at] = part
        send_ref[j] = part.astype(BF)
        sent += start_all(
            [
                (part_ref.at[:, pl.ds(512 * j, 512)], part_hbm.at[:, pl.ds(512 * j, 512)]),
                (send_ref.at[j], (send0_hbm, send1_hbm)[j]),
            ],
            last_sems,
            2 * j,
        )
    wait_all(sent)


def hidden_grads(own, sib, col, slope, n2, up_blocks, down_blocks):
    return launch(
        hidden_grad_kernel,
        [(own, ANY), (sib, ANY), (col, VMEM), (slope, ANY), (n2, ANY)]
        + [(g, ANY) for g in up_blocks + down_blocks],
        [
            ((1, HALF_FF), F32),
            ((BACK, D), F32, ANY),
            ((BACK, HALF_D), BF, ANY),
            ((BACK, HALF_D), BF, ANY),
        ]
        + [(s, BF, ANY) for s in scatter_shapes("zxy", 32, HALF_FF)],
        [
            pltpu.VMEM((BACK, D), BF),
            pltpu.VMEM((BACK, HALF_FF), BF),
            pltpu.VMEM((BACK, D), BF),
            pltpu.VMEM((D, BACK), BF),
            pltpu.VMEM((D, HALF_FF), BF),
            pltpu.VMEM((HALF_FF, D), BF),
            pltpu.VMEM((BACK, HALF_FF), BF),
            pltpu.VMEM((D, HALF_FF), BF),
            pltpu.VMEM((BACK, D), F32),
            pltpu.VMEM((2, BACK, HALF_D), BF),
            dma(3 + len(ENTRIES_ZXY)),
            dma(4),
            dma(len(ENTRIES_XZY_GATHER)),
            dma(4 * len(ENTRIES_ZXY)),
            dma(4),
        ],
        flops=7.5e9,
    )


def middle_kernel(part_hbm, got0_hbm, got1_hbm, sum_hbm, z0_hbm, z1_hbm, *refs):
    stat_ref, own_hbm, sib_hbm, col_ref, vec_ref, o0_ref, o1_ref, wo_hbm = refs[:8]
    da2_ref, do0_ref, do1_ref, sums_ref, mine_ref, send_ref = refs[8:14]
    part_ref, got_ref, a2_ref, z_ref, dy_ref, wo_ref, dz_ref, whole_ref, sems = refs[14:]
    core = coords()[3]
    one = start_all(
        [
            (part_hbm, part_ref),
            (sum_hbm.at[pl.ds(0, BACK), :], a2_ref),
            (own_hbm.at[pl.ds(0, LIVE), :], dy_ref.at[pl.ds(0, LIVE), :]),
            (sib_hbm.at[pl.ds(0, LIVE), :], dy_ref.at[pl.ds(LIVE, LIVE), :]),
        ]
        + [
            (src.at[pl.ds(start, LIVE), :], dst.at[pl.ds(LIVE - start, LIVE), pl.ds(off, HALF_D)])
            for dst, src, off in (
                (got_ref, got0_hbm, 0),
                (got_ref, got1_hbm, HALF_D),
                (z_ref, z0_hbm, 0),
                (z_ref, z1_hbm, HALF_D),
            )
            for start in (0, LIVE)
        ]
        + [(wo_hbm, wo_ref)],
        sems,
    )
    gain = vec_ref[5:6, :]
    wait_all(one)

    def rows(i, sums):
        at = tile(i, 64)
        dn = part_ref[at, :] + got_ref[at, :].astype(F32)
        a2 = a2_ref[at, :] + z_ref[at, :].astype(F32)
        hat, inverse = normed(a2, stat_ref[at, :])
        dy = jnp.where(col_ref[at, :] >= 0, dy_ref[at, :].astype(F32), 0.0)
        da2 = dy + norm_back(dn, hat, inverse, gain)
        dz = da2.astype(BF)
        dz_ref[at, :] = dz
        if sums is None:
            return 0
        da2_ref[at, :] = da2
        return tuple(
            s + jnp.sum(v.reshape(8, 8, D), axis=0)
            for s, v in zip(sums, (dn * hat, dn, dz.astype(F32), dy))
        )

    steps = LIVE // 64
    sums = lax.fori_loop(0, steps, rows, (jnp.zeros((8, D), F32),) * 4)
    lax.fori_loop(steps, 2 * steps, lambda i, c: rows(i, None), 0)
    for i, s in enumerate(sums):
        sums_ref[i : i + 1, :] = jnp.sum(s, axis=0, keepdims=True)
    sums_ref[4:8, :] = jnp.zeros((4, D), F32)
    for half, (do_ref, o_ref) in enumerate(((do0_ref, o0_ref), (do1_ref, o1_ref))):
        at = slice(256 * half, 256 * (half + 1))
        do_ref[...] = lax.dot_general(
            dz_ref[...], wo_ref[at, :], NT, preferred_element_type=F32
        ).astype(BF)
        whole_ref[at, :] = lax.dot_general(
            o_ref[:BACK, :], dz_ref[...], TN, preferred_element_type=F32
        ).astype(BF)
    for k in range(8):
        mine_ref[k] = whole_ref[pl.ds(pl.multiple_of(64 * k + 32 * core, 32), 32), :]
        send_ref[k] = whole_ref[pl.ds(pl.multiple_of(64 * k + 32 - 32 * core, 32), 32), :]


def middle(part, got, total, z, stat, own, sib, col, vec, o, wo):
    ins = [(v, ANY) for v in (part, *got, total, *z)]
    ins += [(stat, VMEM), (own, ANY), (sib, ANY), (col, VMEM), (vec, VMEM)]
    ins += [(o[0], VMEM), (o[1], VMEM), (wo, ANY)]
    return launch(
        middle_kernel,
        ins,
        [
            ((LIVE, D), F32),
            ((BACK, 256), BF),
            ((BACK, 256), BF),
            ((8, D), F32),
            ((8, 32, D), BF),
            ((8, 32, D), BF),
        ],
        [
            pltpu.VMEM((BACK, D), F32),
            pltpu.VMEM((BACK, D), BF),
            pltpu.VMEM((BACK, D), F32),
            pltpu.VMEM((BACK, D), BF),
            pltpu.VMEM((BACK, D), BF),
            pltpu.VMEM((HALF_D, D), BF),
            pltpu.VMEM((BACK, D), BF),
            pltpu.VMEM((HALF_D, D), BF),
            dma(13),
        ],
        flops=1.4e9,
    )


def back_one_kernel(q_ref, g_ref, o_ref, lse_ref, col_ref, row_ref, n1_hbm, *refs):
    mine_ref, theirs_ref, out_ref, n1t_hbm = refs[:4]
    outs, refs = refs[4:9], refs[9:]
    n1_ref, n1t_ref, whole_ref, sems, sent_sem = refs
    count = len(ENTRIES_ZXY)
    load = start_all([(n1_hbm.at[pl.ds(0, BACK), :], n1_ref)], sent_sem)
    two = []
    for i, e in enumerate(ENTRIES_ZXY):
        rel, half = e[3], e[4]
        _, y, _, core = coords()
        chip = chip_of(rel)
        slot = (chip // 4) * 2 + chip % 2
        at = pl.ds(HALF_D * half, HALF_D)
        dst = piece_of(outs, e, 32, (HALF_QKV, HALF_D))
        here = (y if rel[1] == 0 else 1 - y) == core
        sem = sems.at[count + i]
        two.append(pltpu.make_async_copy(mine_ref.at[slot, :, at], dst, sem))

        @pl.when(here)
        def _():
            pltpu.make_async_copy(mine_ref.at[slot, :, at], dst, sem).start()

        @pl.when(jnp.logical_not(here))
        def _():
            pltpu.make_async_copy(theirs_ref.at[slot, :, at], dst, sem).start()

    attend_back(q_ref, g_ref, o_ref, lse_ref, col_ref, row_ref, out_ref)
    wait_all(load)
    n1t_ref[...] = n1_ref[...].T
    load = start_all([(n1t_ref, n1t_hbm)], sent_sem)
    whole_ref[...] = jnp.dot(n1t_ref[...], out_ref[...], preferred_element_type=F32).astype(BF)
    one = start_all(
        [
            (whole_ref.at[pl.ds(core_rows(e), 32), :], piece_of(outs, e, 32, (0, HALF_QKV)))
            for e in ENTRIES_ZXY
        ],
        sems,
    )
    wait_all(one + two + load)


def back_one(qkv, do, o, lse, col, row, n1, mine, theirs):
    return launch(
        back_one_kernel,
        [(v, VMEM) for v in (qkv, do, o, lse, col, row)]
        + [(n1, ANY), (mine, VMEM), (theirs, VMEM)],
        [((BACK, HALF_QKV), BF), ((D, BACK), BF, ANY)]
        + [(s, BF, ANY) for s in scatter_shapes("zxy", 32, HALF_QKV + HALF_D)],
        [
            pltpu.VMEM((BACK, D), BF),
            pltpu.VMEM((D, BACK), BF),
            pltpu.VMEM((D, HALF_QKV), BF),
            dma(2 * len(ENTRIES_ZXY)),
            dma(1),
        ],
        flops=2.5e9,
    )


def back_two_kernel(q_ref, g_ref, o_ref, lse_ref, col_ref, row_ref, one_ref, *refs):
    w0_hbm, w1_hbm, out_ref, own_ref, send_ref, w0_ref, w1_ref, sems = refs
    load = start_all([(w0_hbm, w0_ref), (w1_hbm, w1_ref)], sems)
    attend_back(q_ref, g_ref, o_ref, lse_ref, col_ref, row_ref, out_ref)
    wait_all(load)
    for j in range(2):
        at = slice(512 * j, 512 * (j + 1))
        total = lax.dot_general(
            one_ref[...], w0_ref[at, :], NT, preferred_element_type=F32
        ) + lax.dot_general(out_ref[...], w1_ref[at, :], NT, preferred_element_type=F32)
        own_ref[:, at] = total[:LIVE]
        send_ref[:, at] = total[LIVE:].astype(BF)


def back_two(qkv, do, o, lse, col, row, one, w0, w1):
    return launch(
        back_two_kernel,
        [(v, VMEM) for v in (qkv, do, o, lse, col, row, one)] + [(w0, ANY), (w1, ANY)],
        [((BACK, HALF_QKV), BF), ((LIVE, D), F32), ((LIVE, D), BF)],
        [pltpu.VMEM((D, HALF_QKV), BF), pltpu.VMEM((D, HALF_QKV), BF), dma(2)],
        flops=3.2e9,
    )


def last_kernel(n1t_hbm, one_ref, two_ref, dn_ref, got_ref, a_hbm, stat_ref, *refs):
    da2_ref, vec_ref, place_ref, sums_ref, upsum_ref, tok_ref = refs[:6]
    outs, refs = refs[6:11], refs[11:]
    n1t_ref, a_ref, whole_ref, small_ref, da_ref, rows_ref, sems, in_sems = refs
    core = coords()[3]
    count = len(ENTRIES_ZXY)
    load = start_all([(n1t_hbm, n1t_ref), (a_hbm.at[pl.ds(0, LIVE), :], a_ref)], in_sems)
    wait_all(load)
    whole_ref[...] = jnp.dot(n1t_ref[...], two_ref[...], preferred_element_type=F32).astype(BF)
    one = start_all(
        [
            (whole_ref.at[pl.ds(core_rows(e), 32), :], piece_of(outs, e, 32, (SMALL, HALF_QKV)))
            for e in ENTRIES_ZXY
        ],
        sems,
    )
    gain = vec_ref[0:1, :]

    def rows(i, sums):
        at = tile(i, 64)
        dn = dn_ref[at, :] + got_ref[at, :].astype(F32)
        hat, inverse = normed(a_ref[at, :], stat_ref[at, :])
        da = da2_ref[at, :] + norm_back(dn, hat, inverse, gain)
        da_ref[at, :] = da.astype(BF)
        tok_ref[at, :] = da.astype(BF)
        return tuple(
            s + jnp.sum(v.reshape(8, 8, D), axis=0) for s, v in zip(sums, (dn * hat, dn))
        )

    sums = lax.fori_loop(0, LIVE // 64, rows, (jnp.zeros((8, D), F32),) * 2)
    tok_ref[LIVE:, :] = jnp.zeros((REST, D), BF)
    lane = lax.broadcasted_iota(jnp.int32, (LIVE, 256), 1)
    hot = (place_ref[:LIVE, :] == lane).astype(BF)
    small = lax.dot_general(da_ref[...], hot, TN, preferred_element_type=F32)
    rows_ref[...] = jnp.zeros((16, D), F32)
    rows_ref[0:1, :] = jnp.sum(sums[0], axis=0, keepdims=True)
    rows_ref[1:2, :] = jnp.sum(sums[1], axis=0, keepdims=True)
    for half, src in enumerate((one_ref, two_ref)):
        total = jnp.sum(src[...].astype(F32), axis=0, keepdims=True)
        for j in range(2):
            own = pl.ds(pl.multiple_of(256 * (2 * half + j) + 128 * core, 128), 128)
            rows_ref[2:3, own] = total[:, 128 * j : 128 * (j + 1)]
            rows_ref[3:4, own] = total[:, 512 + 128 * j : 512 + 128 * (j + 1)]
    rows_ref[4:5, :] = sums_ref[2:3, :]
    rows_ref[5:6, :] = sums_ref[0:1, :]
    rows_ref[6:7, :] = sums_ref[1:2, :]
    rows_ref[7:8, :] = sums_ref[3:4, :]
    spot = lax.broadcasted_iota(jnp.int32, (16, 256), 0)
    place = (lax.broadcasted_iota(jnp.int32, (16, 256), 1) == spot + VEC0).astype(BF)
    value = rows_ref[...]
    for _ in range(2):
        piece = value.astype(BF)
        small = small + lax.dot_general(piece, place, TN, preferred_element_type=F32)
        value = value - piece.astype(F32)
    small_ref[:, :256] = small.astype(BF)
    small_ref[:, 256:] = jnp.zeros((D, SMALL - 256), BF)
    top = lax.broadcasted_iota(jnp.int32, (16, 128), 0) == 0
    for chip in range(16):
        row = pl.multiple_of(64 * chip + 32 * core, 32)
        bias = jnp.where(top, upsum_ref[:, 128 * chip : 128 * (chip + 1)], 0.0)
        small_ref[pl.ds(row, 16), 256:384] = bias.astype(BF)
    three = start_all(
        [
            (small_ref.at[pl.ds(core_rows(e), 32), :], piece_of(outs, e, 32, (0, SMALL)))
            for e in ENTRIES_ZXY
        ],
        sems,
        count,
    )
    wait_all(one + three)


def last_stage(n1t, one, two, dn, got, a, stat, da2, vec, place, sums, upsum):
    return launch(
        last_kernel,
        [(n1t, ANY)]
        + [(v, VMEM) for v in (one, two, dn, got)]
        + [(a, ANY)]
        + [(v, VMEM) for v in (stat, da2, vec, place, sums, upsum)],
        [((PACK, D), BF)] + [(s, BF, ANY) for s in scatter_shapes("zxy", 32, CUT)],
        [
            pltpu.VMEM((D, BACK), BF),
            pltpu.VMEM((LIVE, D), F32),
            pltpu.VMEM((D, HALF_QKV), BF),
            pltpu.VMEM((D, SMALL), BF),
            pltpu.VMEM((LIVE, D), BF),
            pltpu.VMEM((16, D), F32),
            dma(2 * len(ENTRIES_ZXY)),
            dma(2),
        ],
        flops=1.2e9,
    )


def output_kernel(act_hbm, sum_hbm, z0_hbm, z1_hbm, vec_ref, *refs):
    parts, (own_ref, send_ref) = refs[:4], refs[4:6]
    act_ref, a2_ref, z_ref, wd_ref, sems = refs[6:]
    copies = [
        (piece_of(parts, e, 64), wd_ref.at[pl.ds(half_rows(e), 64), :]) for e in ENTRIES_XZY_GATHER
    ]
    copies += [(act_hbm, act_ref)]
    for which, start, size, to in SEGMENTS:
        if which == 0:
            at = pl.ds(start, size)
            copies.append((sum_hbm.at[pl.ds(to, size), :], a2_ref.at[at, :]))
            src = pl.ds(to + size, size)
            copies.append((z0_hbm.at[src, :], z_ref.at[at, pl.ds(0, HALF_D)]))
            copies.append((z1_hbm.at[src, :], z_ref.at[at, pl.ds(HALF_D, HALF_D)]))
    wait_all(start_all(copies, sems))
    for j in range(2):
        at = slice(512 * j, 512 * (j + 1))
        part = jnp.dot(act_ref[...], wd_ref[:, at], preferred_element_type=F32)
        a2 = a2_ref[:, at] + z_ref[:, at].astype(F32) + vec_ref[7:8, at]
        for which, start, size, to in SEGMENTS:
            if which == 0:
                own_ref[start : start + size, at] = part[to : to + size] + a2[start : start + size]
            else:
                send_ref[start : start + size, at] = part[to : to + size].astype(BF)


def output_stage(act, total, z, vec, gathered):
    return launch(
        output_kernel,
        [(act, ANY), (total, ANY), (z[0], ANY), (z[1], ANY), (vec, VMEM)]
        + [(g, ANY) for g in gathered],
        [((PACK, D), F32), ((PACK, D), BF)],
        [
            pltpu.VMEM((ROWS, HALF_FF), BF),
            pltpu.VMEM((PACK, D), F32),
            pltpu.VMEM((PACK, D), BF),
            pltpu.VMEM((HALF_FF, D), BF),
            dma(len(ENTRIES_XZY_GATHER) + 7),
        ],
        flops=3.2e9,
    )


def finish_kernel(a_ref, b_ref, up_ref, a_got, b_got, up_got, small_ref, qkv_ref, grad_ref, out_ref):
    core = coords()[3]
    small_ref[...] = b_ref[:32, :SMALL] + b_got[:, :SMALL]
    for j in range(12):
        at = slot_of(j)
        mine = pl.ds(pl.multiple_of(256 * j + 128 * core, 128), 128)
        other = pl.ds(pl.multiple_of(256 * j + 128 - 128 * core, 128), 128)
        own, got = (a_ref, a_got) if at < HALF_QKV else (b_ref, b_got)
        at = slice(at, at + 128) if at < HALF_QKV else slice(at + SMALL - HALF_QKV, at + SMALL - HALF_QKV + 128)
        qkv_ref[:, mine] = own[:32, at]
        qkv_ref[:, other] = got[:, at]
    for j in range(16):
        at = slice(128 * j, 128 * (j + 1))
        mine = pl.ds(pl.multiple_of(256 * j + 128 * core, 128), 128)
        other = pl.ds(pl.multiple_of(256 * j + 128 - 128 * core, 128), 128)
        grad_ref[:, mine] = up_ref[:32, at]
        grad_ref[:, other] = up_got[:, at]
    out_ref[:, :HALF_D] = a_ref[:32, HALF_QKV:]
    out_ref[:, HALF_D:] = a_ref[32:, HALF_QKV:]


def finish(a_sum, b_sum, up_sum, a_got, b_got, up_got):
    return launch(
        finish_kernel,
        [(v, VMEM) for v in (a_sum, b_sum, up_sum, a_got, b_got, up_got)],
        [((32, SMALL), F32), ((32, 3 * D), F32), ((32, FF), F32), ((32, D), F32)],
        limit=8,
    )


def in_order(own, sib):
    return jnp.concatenate([own[:LIVE], sib[:LIVE], own[LIVE:], sib[LIVE:]])


def fast_on_device(
    tokens,
    grad_out,
    image_lengths,
    image_device,
    small_map,
    ln1_gain,
    ln1_bias,
    qkv_weight,
    q_bias,
    v_bias,
    out_weight,
    out_bias,
    ln2_gain,
    ln2_bias,
    up_weight,
    up_bias,
    down_weight,
    down_bias,
    pos_table,
):
    device = lax.axis_index("dp") * 4 + lax.axis_index("fsdp")
    seg, place = layout(image_lengths, image_device, small_map, device, PACK)
    seg2, place2 = layout(image_lengths, image_device, small_map, device ^ 1, PACK)
    col = in_order(seg, seg2)[:, None]
    row = jnp.stack([seg, seg2])
    place = in_order(place, place2)[:, None]

    vectors = [ln1_gain, ln1_bias, q_bias, v_bias, out_bias, ln2_gain, ln2_bias, down_bias]
    table = jnp.concatenate([pos_table, jnp.stack(vectors), jnp.zeros((103, 32), BF)])
    keep, send, out2 = prepare(table, up_bias[None, :], qkv_weight, up_weight, out_weight)
    got = swap(send, CORE)
    chunk_1 = jnp.concatenate([keep[:, :CUT], got[:, :CUT]])
    rest = slice(CUT, SMALL + QKV)
    chunk_2 = jnp.concatenate([jnp.concatenate([keep[:, rest], got[:, rest]]), out2], axis=1)
    flat, deep = Lane(1), Lane(2)
    chunk_u = jnp.concatenate([keep[:, SMALL + QKV :], got[:, SMALL + QKV :]])
    down_a, down_b = down_weight[:64], down_weight[64:]
    line_1 = jnp.concatenate(along_z(deep, chunk_1))
    down_x, down_y = flat.go((down_a, XBIT), (down_b, YBIT))
    line_2 = jnp.concatenate(along_z(deep, chunk_2))
    gathered_1 = cross(flat, line_1)
    line_u = jnp.concatenate(along_z(deep, chunk_u))
    gathered_2 = cross(flat, line_2)
    quads_d = along_z(deep, jnp.stack([down_a, down_x, down_b, down_y]))
    gathered_u = cross(flat, line_u)
    gathered_d = sides(flat, quads_d)
    sib_tokens = swap(tokens, CORE)
    sib_grad = swap(grad_out, CORE)

    a, n1, wq0, qkv0, vec, bf1, stat1 = first_stage(tokens, sib_tokens, place, gathered_1)
    o0, lse0 = attend(qkv0, col, row)
    wq1, qkv1, out_own = second_stage(n1, vec, gathered_2)
    out_other = swap(out_own, CORE)
    o1, lse1 = attend(qkv1, col, row)
    o = (o0, o1)
    wo, total, *send = project(o, a, vec, out_own, out_other)
    z = [swap(part, CORE) for part in send]
    n2, act, slope, stat2, *down_parts = widen(
        total, z, vec, bf1, grad_out, sib_grad, col, gathered_u
    )
    down_quad = scatter_xzy_start(flat, deep, down_parts)
    up_bias_sum, part, *send = hidden_grads(
        grad_out, sib_grad, col, slope, n2, gathered_u, gathered_d
    )
    send, up_parts = send[:2], send[2:]
    got = [swap(half, CORE) for half in send]
    up_sum = scatter_zxy(flat, deep, up_parts)
    da2, do0, do1, sums, mine, theirs = middle(
        part, got, total, z, stat2, grad_out, sib_grad, col, vec, o, wo
    )
    theirs = swap(theirs, CORE)
    d_one, n1t, *a_parts = back_one(qkv0, do0, o0, lse0, col, row, n1, mine, theirs)
    down_sum = scatter_xzy_end(flat, down_quad)
    a_sum = scatter_zxy(flat, deep, a_parts)
    d_two, dn, send = back_two(qkv1, do1, o1, lse1, col, row, d_one, wq0, wq1)
    tokens_grad, *b_parts = last_stage(
        n1t, d_one, d_two, dn, swap(send, CORE), a, stat1, da2, vec, place, sums, up_bias_sum
    )
    b_sum = scatter_zxy(flat, deep, b_parts)
    own, send = output_stage(after(act, tokens_grad), total, z, vec, gathered_d)
    layer_out = (own + swap(send, CORE).astype(F32)).astype(BF)

    up_got = swap(up_sum[32:], CORE)
    a_got = swap(a_sum[32:, :HALF_QKV], CORE)
    b_got = swap(b_sum[32:], CORE)
    small, qkv_grad, up_grad, out_grad = finish(a_sum, b_sum, up_sum, a_got, b_got, up_got)
    gv = small[:, VEC0 : VEC0 + 8].T
    return (
        layer_out,
        tokens_grad,
        gv[0],
        gv[1],
        qkv_grad,
        gv[2],
        gv[3],
        out_grad,
        gv[4],
        gv[5],
        gv[6],
        up_grad,
        small[0, 256:],
        down_sum,
        gv[7],
        small[:, :LONG].T,
    )


def solution(mesh):
    in_specs = (
        P(("dp", "fsdp"), None),
        P(("dp", "fsdp"), None),
        P(),
        P(),
        P(),
        P(("dp", "fsdp")),
        P(("dp", "fsdp")),
        P(("dp", "fsdp"), None),
        P(("dp", "fsdp")),
        P(("dp", "fsdp")),
        P(("dp", "fsdp"), None),
        P(("dp", "fsdp")),
        P(("dp", "fsdp")),
        P(("dp", "fsdp")),
        P(("dp", "fsdp"), None),
        P(("dp", "fsdp")),
        P(("dp", "fsdp"), None),
        P(("dp", "fsdp")),
        P(None, ("dp", "fsdp")),
    )
    out_specs = (
        P(("dp", "fsdp"), None),
        P(("dp", "fsdp"), None),
        P(("dp", "fsdp")),
        P(("dp", "fsdp")),
        P(("dp", "fsdp"), None),
        P(("dp", "fsdp")),
        P(("dp", "fsdp")),
        P(("dp", "fsdp"), None),
        P(("dp", "fsdp")),
        P(("dp", "fsdp")),
        P(("dp", "fsdp")),
        P(("dp", "fsdp"), None),
        P(("dp", "fsdp")),
        P(("dp", "fsdp"), None),
        P(("dp", "fsdp")),
        P(None, ("dp", "fsdp")),
    )
    eight_by_four = mesh.shape["dp"] == 8 and mesh.shape["fsdp"] == 4
    return jax.shard_map(
        fast_on_device if eight_by_four else on_device, mesh=mesh, in_specs=in_specs, out_specs=out_specs, check_vma=False
    )
```

```python
import jax
import jax.numpy as jnp
import numpy as np
from jax import lax
from jax.experimental import pallas as pl
from jax.experimental.pallas import tpu as pltpu
from jax.sharding import PartitionSpec as P

D = 1024
HEADS = 16
HEAD = 64
FF = 4096
LONG = 145
SHORT = 50


EPS = 1e-06


def fetch(parts):
    whole = (
        lax.all_gather(parts[0], ("dp", "fsdp"), axis=1, tiled=True),
        lax.all_gather(parts[1], ("dp", "fsdp"), axis=0, tiled=True),
        lax.all_gather(parts[2], ("dp", "fsdp"), axis=0, tiled=True),
        lax.all_gather(parts[3], ("dp", "fsdp"), axis=0, tiled=True),
        lax.all_gather(parts[4], ("dp", "fsdp"), axis=0, tiled=True),
        lax.all_gather(parts[5], ("dp", "fsdp"), axis=0, tiled=True),
        lax.all_gather(parts[6], ("dp", "fsdp"), axis=1, tiled=True),
    )
    return whole


def reduce_grads(parts):
    owned = (
        lax.psum_scatter(parts[0], ("dp", "fsdp"), scatter_dimension=1, tiled=True),
        lax.psum_scatter(parts[1], ("dp", "fsdp"), scatter_dimension=0, tiled=True),
        lax.psum_scatter(parts[2], ("dp", "fsdp"), scatter_dimension=0, tiled=True),
        lax.psum_scatter(parts[3], ("dp", "fsdp"), scatter_dimension=0, tiled=True),
        lax.psum_scatter(parts[4], ("dp", "fsdp"), scatter_dimension=0, tiled=True),
        lax.psum_scatter(parts[5], ("dp", "fsdp"), scatter_dimension=0, tiled=True),
        lax.psum_scatter(parts[6], ("dp", "fsdp"), scatter_dimension=1, tiled=True),
    )
    return owned


def layout(image_lengths, image_device, small_map, device, rows_dev):
    mine = image_device == device
    lens = jnp.where(mine, image_lengths, 0)
    starts = jnp.cumsum(lens) - lens
    rows = jnp.arange(rows_dev, dtype=jnp.int32)
    inside = (
        mine[None, :]
        & (starts[None, :] <= rows[:, None])
        & (rows[:, None] < (starts + lens)[None, :])
    )
    number = jnp.arange(image_lengths.shape[0], dtype=jnp.int32)
    segment = jnp.sum(jnp.where(inside, number[None, :] + 1, 0), axis=1) - 1
    offset = rows - jnp.sum(jnp.where(inside, starts[None, :], 0), axis=1)
    length = jnp.sum(jnp.where(inside, lens[None, :], 0), axis=1)
    spots = jnp.arange(SHORT, dtype=jnp.int32)
    mapped = jnp.sum(jnp.where(offset[:, None] == spots[None, :], small_map[None, :], 0), axis=1)
    place = jnp.where(length == LONG, offset, jnp.where(length == SHORT, mapped, 0))
    return (segment, place)


def layer_norm_forward_pass(v, norm_gain, shift_bias):
    centred_rows = v - jnp.mean(v, axis=1, keepdims=True)
    inverse_deviation = lax.rsqrt(
        jnp.mean(centred_rows * centred_rows, axis=1, keepdims=True) + EPS
    )
    normalized_rows = centred_rows * inverse_deviation
    return (normalized_rows * norm_gain + shift_bias, normalized_rows, inverse_deviation)


def layer_norm_backward_pass(upstream_gradient, normalized_rows, inverse_deviation, norm_gain):
    normalized_gradient = upstream_gradient * norm_gain
    first_input = jnp.mean(normalized_gradient, axis=1, keepdims=True)
    second_input = jnp.mean(normalized_gradient * normalized_rows, axis=1, keepdims=True)
    return (
        inverse_deviation * (normalized_gradient - first_input - normalized_rows * second_input),
        jnp.sum(upstream_gradient * normalized_rows, axis=0),
        jnp.sum(upstream_gradient, axis=0),
    )


def split_heads(values, groups):
    return values.reshape(values.shape[0], groups, HEADS // groups, HEAD).transpose(1, 0, 2, 3)


def join_heads(values):
    return values.transpose(1, 0, 2, 3).reshape(values.shape[1], D)


def masked_scores(query, keys, same):
    scores = jnp.einsum("thd,shd->hts", query, keys, preferred_element_type=jnp.float32) * HEAD ** (
        -0.5
    )
    return jnp.where(same[None], scores, -1000000000.0)


def attend_forward(qkvb, same):
    groups = HEADS // 4
    query = split_heads(qkvb[:, :D], groups)
    keys = split_heads(qkvb[:, D : 2 * D], groups)
    values = split_heads(qkvb[:, 2 * D :], groups)

    def one_group(item):
        scores = masked_scores(item[0], item[1], same)
        top = jnp.max(scores, axis=2, keepdims=True)
        lse = top + jnp.log(jnp.sum(jnp.exp(scores - top), axis=2, keepdims=True))
        probs = jnp.exp(scores - lse).astype(jnp.bfloat16)
        attended = jnp.einsum("hts,shd->thd", probs, item[2], preferred_element_type=jnp.float32)
        return (attended, lse[:, :, 0])

    attended, lse = lax.map(one_group, (query, keys, values))
    return (join_heads(attended), lse)


def attend_backward(qkvb, dob, lse, same):
    groups = HEADS // 4
    query = split_heads(qkvb[:, :D], groups)
    keys = split_heads(qkvb[:, D : 2 * D], groups)
    values = split_heads(qkvb[:, 2 * D :], groups)
    douts = split_heads(dob, groups)

    def one_group(item):
        scores = masked_scores(item[0], item[1], same)
        probs = jnp.exp(scores - item[4][:, :, None])
        dvalue = jnp.einsum(
            "hts,thd->shd", probs.astype(jnp.bfloat16), item[3], preferred_element_type=jnp.float32
        )
        dprobs = jnp.einsum("thd,shd->hts", item[3], item[2], preferred_element_type=jnp.float32)
        inner = jnp.sum(probs * dprobs, axis=2, keepdims=True)
        dscore = (probs * (dprobs - inner)).astype(jnp.bfloat16)
        dquery = jnp.einsum(
            "hts,shd->thd", dscore, item[1], preferred_element_type=jnp.float32
        ) * HEAD ** (-0.5)
        dkey = jnp.einsum(
            "hts,thd->shd", dscore, item[0], preferred_element_type=jnp.float32
        ) * HEAD ** (-0.5)
        return (dquery, dkey, dvalue)

    dquery, dkey, dvalue = lax.map(one_group, (query, keys, values, douts, lse))
    return jnp.concatenate([join_heads(dquery), join_heads(dkey), join_heads(dvalue)], axis=1)


def gelu_slope(x):
    return (
        0.5 * (1.0 + jax.scipy.special.erf(x * 0.7071067811865476))
        + x * jnp.exp(-0.5 * x * x) * 0.3989422804014327
    )


def on_device(
    tokens,
    grad_out,
    image_lengths,
    image_device,
    small_map,
    ln1_gain,
    ln1_bias,
    qkv_weight,
    q_bias,
    v_bias,
    out_weight,
    out_bias,
    ln2_gain,
    ln2_bias,
    up_weight,
    up_bias,
    down_weight,
    down_bias,
    pos_table,
):
    rows_dev = tokens.shape[0]
    device = lax.axis_index("dp") * lax.axis_size("fsdp") + lax.axis_index("fsdp")
    segment, place = layout(image_lengths, image_device, small_map, device, rows_dev)
    same = segment[:, None] == segment[None, :]
    valid = (segment >= 0).astype(jnp.float32)[:, None]
    table_rows = jnp.arange(LONG, dtype=jnp.int32)
    picker = place[:, None] == table_rows[None, :]
    vectors = jnp.stack(
        [ln1_gain, ln1_bias, q_bias, v_bias, out_bias, ln2_gain, ln2_bias, down_bias]
    )
    shards = (vectors, qkv_weight, out_weight, up_weight, up_bias, down_weight, pos_table)
    whole = fetch(shards)
    vec = whole[0].astype(jnp.float32)
    first_gain, first_centred, bq, bv, bo, second_gain, second_centred, bf2 = (
        vec[0],
        vec[1],
        vec[2],
        vec[3],
        vec[4],
        vec[5],
        vec[6],
        vec[7],
    )
    bf1 = whole[4].astype(jnp.float32)
    activation_rows = tokens.astype(jnp.float32) + jnp.dot(
        picker.astype(jnp.bfloat16), whole[6], preferred_element_type=jnp.float32
    )
    first_normed, first_normalized, first_inverse_deviation = layer_norm_forward_pass(
        activation_rows, first_gain, first_centred
    )
    n1b = first_normed.astype(jnp.bfloat16)
    bias3 = jnp.concatenate([bq, jnp.zeros_like(bq), bv])
    qkvb = (jnp.dot(n1b, whole[1], preferred_element_type=jnp.float32) + bias3).astype(jnp.bfloat16)
    attended, lse = attend_forward(qkvb, same)
    ob = attended.astype(jnp.bfloat16)
    second_activation = (
        activation_rows + jnp.dot(ob, whole[2], preferred_element_type=jnp.float32) + bo
    )
    second_normed, second_normalized, second_inverse_deviation = layer_norm_forward_pass(
        second_activation, second_gain, second_centred
    )
    n2b = second_normed.astype(jnp.bfloat16)
    hpre = jnp.dot(n2b, whole[3], preferred_element_type=jnp.float32) + bf1
    actb = jax.nn.gelu(hpre, approximate=False).astype(jnp.bfloat16)
    output = second_activation + jnp.dot(actb, whole[5], preferred_element_type=jnp.float32) + bf2
    layer_out = output.astype(jnp.bfloat16)
    dy = grad_out.astype(jnp.float32) * valid
    fenced, dy = lax.optimization_barrier((shards, dy))
    back = fetch(fenced)
    dyb = dy.astype(jnp.bfloat16)
    d_down = jnp.einsum("tf,td->fd", actb, dyb, preferred_element_type=jnp.float32)
    d_down_bias = jnp.sum(dy, axis=0)
    dgate = jnp.einsum("td,fd->tf", dyb, back[5], preferred_element_type=jnp.float32)
    dhb = (dgate * gelu_slope(hpre)).astype(jnp.bfloat16)
    d_up = jnp.einsum("td,tf->df", n2b, dhb, preferred_element_type=jnp.float32)
    d_up_bias = jnp.sum(dhb.astype(jnp.float32), axis=0)
    second_norm_gradient = jnp.einsum("tf,df->td", dhb, back[3], preferred_element_type=jnp.float32)
    second_activation_norm_gradient, second_gain_gradient, second_centred_gradient = (
        layer_norm_backward_pass(
            second_norm_gradient, second_normalized, second_inverse_deviation, second_gain
        )
    )
    da2 = dy + second_activation_norm_gradient
    dzb = da2.astype(jnp.bfloat16)
    d_out = jnp.einsum("te,td->ed", ob, dzb, preferred_element_type=jnp.float32)
    d_out_bias = jnp.sum(dzb.astype(jnp.float32), axis=0)
    dob = jnp.einsum("td,ed->te", dzb, back[2], preferred_element_type=jnp.float32).astype(
        jnp.bfloat16
    )
    dqkvb = attend_backward(qkvb, dob, lse, same).astype(jnp.bfloat16)
    d_qkv = jnp.einsum("td,te->de", n1b, dqkvb, preferred_element_type=jnp.float32)
    dqkv_sum = jnp.sum(dqkvb.astype(jnp.float32), axis=0)
    first_norm_gradient = jnp.einsum(
        "te,de->td", dqkvb, back[1], preferred_element_type=jnp.float32
    )
    first_activation_gradient, first_gain_gradient, first_centred_gradient = (
        layer_norm_backward_pass(
            first_norm_gradient, first_normalized, first_inverse_deviation, first_gain
        )
    )
    da = da2 + first_activation_gradient
    tokens_grad = da.astype(jnp.bfloat16)
    d_pos = jnp.dot(picker.astype(jnp.float32).T, da, precision=lax.Precision.HIGHEST)
    d_vectors = jnp.stack(
        [
            first_gain_gradient,
            first_centred_gradient,
            dqkv_sum[:D],
            dqkv_sum[2 * D :],
            d_out_bias,
            second_gain_gradient,
            second_centred_gradient,
            d_down_bias,
        ]
    )
    flat_parts = (
        d_vectors,
        d_qkv.reshape(-1, 128),
        d_out.reshape(-1, 128),
        d_up.reshape(-1, 128),
        d_up_bias,
        d_down,
        d_pos,
    )
    owned = reduce_grads(flat_parts)
    gv = owned[0]
    qkv_owned = owned[1].reshape(-1, 3 * D)
    out_owned = owned[2].reshape(-1, D)
    up_owned = owned[3].reshape(-1, FF)
    return (
        layer_out,
        tokens_grad,
        gv[0],
        gv[1],
        qkv_owned,
        gv[2],
        gv[3],
        out_owned,
        gv[4],
        gv[5],
        gv[6],
        up_owned,
        owned[4],
        owned[5],
        gv[7],
        owned[6],
    )


BF = jnp.bfloat16
F32 = jnp.float32
AXES = ("dp", "fsdp")
CORE, XBIT, YBIT, ZBIT, FAR = 1, 2, 4, 8, 16
PACK = 384
LIVE = -(-2 * LONG // 64) * 64
REST = PACK - LIVE
ROWS = 2 * PACK
BACK = 2 * LIVE
HALF_FF = FF // 2
QKV = 3 * D // 2
HALF_D = D // 2
SMALL = 384
HALF_QKV = QKV // 2
CUT = SMALL + HALF_QKV
VEC0 = LONG
SEGMENTS = ((0, 0, LIVE, 0), (1, 0, LIVE, LIVE), (0, LIVE, REST, BACK), (1, LIVE, REST, BACK + REST))
NT = (((1,), (1,)), ((), ()))
TN = (((0,), (0,)), ((), ()))


def swap(value, mask):
    return lax.ppermute(value, AXES, [(i, i ^ mask) for i in range(32)])


def coords():
    dp = lax.axis_index("dp")
    fs = lax.axis_index("fsdp")
    return dp // 2, dp % 2, fs // 2, fs % 2


def chip_of(rel):
    z, y, x, _ = coords()
    dz, dy, dx = rel
    bits = 0
    for part, off, width in ((z // 2, dz // 2, 8), (z % 2, dz % 2, 4), (y, dy, 2), (x, dx, 1)):
        bits = bits + (1 - part if off else part) * width
    return bits


ZORDER = (0, 2, 1, 3)
ENTRIES_ZXY = (
    [(0, (k,), h, (z, 0, 0), h) for k, z in enumerate(ZORDER) for h in range(2)]
    + [(1, (k,), h, (z, 0, 1), h) for k, z in enumerate(ZORDER) for h in range(2)]
    + [(2, (k,), h, (z, 1, 0), h) for k, z in enumerate(ZORDER) for h in range(2)]
    + [(3, (k,), h, (z, 1, 1), h) for k, z in enumerate(ZORDER[:2]) for h in range(2)]
    + [(4, (k,), h, (z, 1, 1), h) for k, z in enumerate(ZORDER[2:]) for h in range(2)]
)
QUADS = (((0, 0), 0), ((0, 1), 0), ((0, 0), 1), ((1, 0), 1))
SIDE_A = ((1, 0), (1, 1))
SIDE_B = ((0, 1), (1, 1))
ENTRIES_XZY_GATHER = (
    [
        (k // 2, (k % 2, q), 0, (z,) + QUADS[q][0], QUADS[q][1])
        for k, z in enumerate(ZORDER)
        for q in range(4)
    ]
    + [(2, (k, q), 0, (z,) + SIDE_A[q], 0) for k, z in enumerate(ZORDER) for q in range(2)]
    + [(3, (k, q), 0, (z,) + SIDE_B[q], 1) for k, z in enumerate(ZORDER) for q in range(2)]
)
ENTRIES_XZY_SCATTER = (
    [
        (0, (k, q), 0, (z,) + QUADS[q][0], QUADS[q][1])
        for k, z in enumerate(ZORDER)
        for q in range(4)
    ]
    + [(1, (k, q), 0, (z,) + SIDE_A[q], 0) for k, z in enumerate(ZORDER) for q in range(2)]
    + [(2, (k, q), 0, (z,) + SIDE_B[q], 1) for k, z in enumerate(ZORDER) for q in range(2)]
)


def after(value, *done):
    return lax.optimization_barrier((value, done))[0]


def send_all(*pairs, wait=()):
    values = tuple(value for value, _ in pairs)
    if wait:
        values, _ = lax.optimization_barrier((values, tuple(wait)))
    return tuple(swap(value, mask) for value, (_, mask) in zip(values, pairs))


def corners(from_x, from_y, wait=()):
    return send_all((from_x[:2], YBIT), (from_y[2:], XBIT), wait=wait)


def add(*values):
    total = values[0].astype(F32)
    for value in values[1:]:
        total = total + value.astype(F32)
    return total


def to_neighbours(parts, got_a, got_b):
    _, to_x, to_y, _, _ = parts
    to_x = jnp.concatenate([to_x[:2], add(to_x[2:], got_b).astype(BF)])
    to_y = jnp.concatenate([add(to_y[:2], got_a).astype(BF), to_y[2:]])
    return to_x, to_y


def corner_pairs(parts):
    return (parts[3], XBIT), (parts[4], YBIT)


def scatter_shapes(kind, rows, width):
    if kind == "zxy":
        return [(4, 2 * rows, width)] * 3 + [(2, 2 * rows, width)] * 2
    return [(4, 4, rows, width), (4, 2, rows, width), (4, 2, rows, width)]


SCATTER_ENTRIES = {"zxy": ENTRIES_ZXY, "xzy": ENTRIES_XZY_SCATTER}


def piece_of(refs, entry, rows, lanes=None):
    array, index, row, _, _ = entry
    width = pl.ds(*lanes) if lanes else slice(None)
    return refs[array].at[index + (pl.ds(rows * row, rows), width)]


def start_all(copies, sems, first=0):
    started = []
    for i, (src, dst) in enumerate(copies):
        copy = pltpu.make_async_copy(src, dst, sems.at[first + i])
        copy.start()
        started.append(copy)
    return started


def wait_all(started):
    for copy in started:
        copy.wait()


def core_rows(entry):
    core = coords()[3]
    side = core if entry[4] == 0 else 1 - core
    return pl.multiple_of(chip_of(entry[3]) * 64 + side * 32, 32)


def z_of(dz):
    z = coords()[0]
    high, low = z // 2, z % 2
    return 2 * (1 - high if dz // 2 else high) + (1 - low if dz % 2 else low)


def half_rows(entry):
    return pl.multiple_of(chip_of(entry[3]) * 128 + 64 * entry[4], 64)


def tile(i, width):
    return pl.ds(pl.multiple_of(i * width, width), width)


ANY = pl.BlockSpec(memory_space=pl.ANY)
VMEM = pl.BlockSpec(memory_space=pltpu.VMEM)


def launch(kernel, ins, outs, scratch=(), flops=0, limit=56):
    size = sum(int(np.prod(o[0])) * jnp.dtype(o[1]).itemsize for o in outs)
    for value, _ in ins:
        size += value.size * value.dtype.itemsize
    return pl.pallas_call(
        kernel,
        out_shape=[jax.ShapeDtypeStruct(o[0], o[1]) for o in outs],
        in_specs=[spec for _, spec in ins],
        out_specs=[o[2] if len(o) > 2 else VMEM for o in outs],
        scratch_shapes=list(scratch),
        cost_estimate=pl.CostEstimate(flops=int(flops), bytes_accessed=int(size), transcendentals=0),
        compiler_params=pltpu.CompilerParams(vmem_limit_bytes=limit << 20),
    )(*[value for value, _ in ins])


def dma(count):
    return pltpu.SemaphoreType.DMA((count,))


def norm_rows(v):
    mean = jnp.mean(v, axis=1, keepdims=True)
    centred = v - mean
    inverse = lax.rsqrt(jnp.mean(centred * centred, axis=1, keepdims=True) + EPS)
    return centred * inverse, mean, inverse


def stats(mean, inverse):
    lane = lax.broadcasted_iota(jnp.int32, (mean.shape[0], 128), 1)
    return jnp.where(lane == 0, mean, inverse)


def normed(v, stat):
    return (v - stat[:, 0:1]) * stat[:, 1:2], stat[:, 1:2]


def gelu_parts(h):
    bell = jnp.exp(h * h * -0.5)
    base = 1.0 + jnp.abs(h) * (0.3275911 * 0.7071067811865476)
    t = pl.reciprocal(base, approx=True)
    t = t * (2.0 - base * t)
    poly = 0.5 * 1.061405429
    for factor in (-1.453152027, 1.421413741, -0.284496736, 0.254829592):
        poly = poly * t + 0.5 * factor
    tail = poly * t * bell
    return jnp.where(h >= 0, 1.0 - tail, tail), bell


PIECES = ((0, 384), (384, 384), (768, 256))


def norm_back(dn, hat, inverse, gain):
    scaled = dn * gain
    first = jnp.mean(scaled, axis=1, keepdims=True)
    second = jnp.mean(scaled * hat, axis=1, keepdims=True)
    return inverse * (scaled - first - hat * second)


def slot_of(block):
    which, j = divmod(block, 4)
    return 768 * (j // 2) + 256 * which + 128 * (j % 2)


def prepare_kernel(pos_ref, bias_ref, qkv_ref, up_ref, out_ref, keep_ref, send_ref, out2_ref):
    core = coords()[3]
    eye = (
        lax.broadcasted_iota(jnp.int32, (32, 32), 0) == lax.broadcasted_iota(jnp.int32, (32, 32), 1)
    ).astype(BF)
    small = lax.dot_general(eye, pos_ref[...], NT, preferred_element_type=F32)
    first_row = lax.broadcasted_iota(jnp.int32, (32, 128), 0) == 0
    bias = jnp.where(first_row, bias_ref[...].astype(F32), 0.0)
    small = jnp.concatenate([small, bias], axis=1).astype(BF)
    keep_ref[:, :SMALL] = small
    send_ref[:, :SMALL] = small
    for src, first, count in ((qkv_ref, SMALL, 12), (up_ref, SMALL + QKV, 16)):
        for j in range(count):
            own = pl.ds(pl.multiple_of(256 * j + 128 * core, 128), 128)
            other = pl.ds(pl.multiple_of(256 * j + 128 * (1 - core), 128), 128)
            to = first + (slot_of(j) if count == 12 else 128 * j)
            keep_ref[:, to : to + 128] = src[:, own]
            send_ref[:, to : to + 128] = src[:, other]
    out2_ref[:32] = out_ref[:, :HALF_D]
    out2_ref[32:] = out_ref[:, HALF_D:]


def prepare(pos, bias, qkv, up, out):
    shapes = [(32, SMALL + QKV + HALF_FF)] * 2 + [(64, HALF_D)]
    return launch(
        prepare_kernel,
        [(v, VMEM) for v in (pos, bias, qkv, up, out)],
        [(s, BF) for s in shapes],
        limit=8,
    )


def fill_bias(bias_ref, vec_ref, half):
    core = coords()[3]
    for j in range(2):
        own = pl.ds(pl.multiple_of(256 * (2 * half + j) + 128 * core, 128), 128)
        bias_ref[0:1, 128 * j : 128 * (j + 1)] = vec_ref[2:3, own]
        bias_ref[0:1, 256 + 128 * j : 256 + 128 * (j + 1)] = jnp.zeros((1, 128), F32)
        bias_ref[0:1, 512 + 128 * j : 512 + 128 * (j + 1)] = vec_ref[3:4, own]


def first_kernel(own_hbm, sib_hbm, place_ref, *refs):
    parts, refs = refs[:5], refs[5:]
    a_hbm, n1_hbm, wq_hbm, qkv_ref, vec_ref, bf1_ref, stat_ref = refs[:7]
    tok_ref, a_ref, n1_ref, wq_ref, small_ref, bias_ref, sems, out_sems = refs[7:]
    core = coords()[3]
    count = len(ENTRIES_ZXY)
    one = start_all(
        [
            (piece_of(parts, e, 32, (0, SMALL)), small_ref.at[pl.ds(core_rows(e), 32), :])
            for e in ENTRIES_ZXY
        ]
        + [
            (
                (own_hbm if which == 0 else sib_hbm).at[pl.ds(start, size), :],
                tok_ref.at[pl.ds(to, size), :],
            )
            for which, start, size, to in SEGMENTS
        ],
        sems,
    )
    two = start_all(
        [
            (piece_of(parts, e, 32, (SMALL, HALF_QKV)), wq_ref.at[pl.ds(core_rows(e), 32), :])
            for e in ENTRIES_ZXY
        ],
        sems,
        count + 4,
    )
    wait_all(one)
    lane = lax.broadcasted_iota(jnp.int32, (16, 256), 1)
    pick = (lane == lax.broadcasted_iota(jnp.int32, (16, 256), 0) + VEC0).astype(BF)
    vec_ref[...] = lax.dot_general(pick, small_ref[:, :256], NT, preferred_element_type=F32)
    for chip in range(16):
        row = pl.multiple_of(64 * chip + 32 * core, 32)
        bf1_ref[:, 128 * chip : 128 * (chip + 1)] = small_ref[pl.ds(row, 16), 256:384][:1].astype(F32)
    fill_bias(bias_ref, vec_ref, 0)
    hot = (place_ref[...] == lax.broadcasted_iota(jnp.int32, (ROWS, 256), 1)).astype(BF)
    for j in range(2):
        at = slice(512 * j, 512 * (j + 1))
        a_ref[:, at] = tok_ref[:, at].astype(F32) + lax.dot_general(
            hot, small_ref[at, :256], NT, preferred_element_type=F32
        )
    gain, shift = vec_ref[0:1, :], vec_ref[1:2, :]

    def rows(i, carry):
        hat, mean, inverse = norm_rows(a_ref[tile(i, 64), :])
        n1_ref[tile(i, 64), :] = (hat * gain + shift).astype(BF)
        stat_ref[tile(i, 64), :] = stats(mean, inverse)
        return carry

    lax.fori_loop(0, ROWS // 64, rows, 0)
    outs = start_all([(a_ref, a_hbm), (n1_ref, n1_hbm)], out_sems)
    wait_all(two)
    outs += start_all([(wq_ref, wq_hbm)], out_sems, 2)
    product = jnp.dot(n1_ref[...], wq_ref[...], preferred_element_type=F32)
    qkv_ref[...] = (product + bias_ref[0:1, :]).astype(BF)
    wait_all(outs)


def first_stage(own, sib, place, gathered):
    return launch(
        first_kernel,
        [(own, ANY), (sib, ANY), (place, VMEM)] + [(g, ANY) for g in gathered],
        [
            ((ROWS, D), F32, ANY),
            ((ROWS, D), BF, ANY),
            ((D, HALF_QKV), BF, ANY),
            ((ROWS, HALF_QKV), BF),
            ((16, D), F32),
            ((1, HALF_FF), F32),
            ((ROWS, 128), F32),
        ],
        [
            pltpu.VMEM((ROWS, D), BF),
            pltpu.VMEM((ROWS, D), F32),
            pltpu.VMEM((ROWS, D), BF),
            pltpu.VMEM((D, HALF_QKV), BF),
            pltpu.VMEM((D, SMALL), BF),
            pltpu.VMEM((8, HALF_QKV), F32),
            dma(2 * len(ENTRIES_ZXY) + 4),
            dma(3),
        ],
        flops=1.2e9,
    )


def second_kernel(n1_hbm, vec_ref, *refs):
    parts, refs = refs[:5], refs[5:]
    wq_hbm, qkv_ref, left_ref, right_ref, n1_ref, wq_ref, bias_ref, sems, out_sem = refs
    count = len(ENTRIES_ZXY)
    one = start_all(
        [(n1_hbm, n1_ref)]
        + [
            (piece_of(parts, e, 32, (0, HALF_QKV)), wq_ref.at[pl.ds(core_rows(e), 32), :])
            for e in ENTRIES_ZXY
        ],
        sems,
    )
    two = start_all(
        [
            (
                piece_of(parts, e, 32, (HALF_QKV, HALF_D)),
                (left_ref, right_ref)[e[4]].at[chip_of(e[3])],
            )
            for e in ENTRIES_ZXY
        ],
        sems,
        count + 1,
    )
    fill_bias(bias_ref, vec_ref, 1)
    wait_all(one)
    outs = start_all([(wq_ref, wq_hbm)], out_sem)
    product = jnp.dot(n1_ref[...], wq_ref[...], preferred_element_type=F32)
    qkv_ref[...] = (product + bias_ref[0:1, :]).astype(BF)
    wait_all(two + outs)


def second_stage(n1, vec, gathered):
    return launch(
        second_kernel,
        [(n1, ANY), (vec, VMEM)] + [(g, ANY) for g in gathered],
        [((D, HALF_QKV), BF, ANY), ((ROWS, HALF_QKV), BF)] + [((16, 32, HALF_D), BF)] * 2,
        [
            pltpu.VMEM((ROWS, D), BF),
            pltpu.VMEM((D, HALF_QKV), BF),
            pltpu.VMEM((8, HALF_QKV), F32),
            dma(2 * len(ENTRIES_ZXY) + 1),
            dma(1),
        ],
        flops=1.2e9,
    )


def pack_rows(ref, pack):
    main = ref[LIVE * pack : LIVE * (pack + 1), :]
    return jnp.concatenate([main, ref[BACK + REST * pack : BACK + REST * (pack + 1), :]])


def attend_kernel(q_ref, k_ref, v_ref, col_ref, row_ref, o_ref, lse_ref):
    first = lax.broadcasted_iota(jnp.int32, (PACK, 128), 1) < HEAD
    for pack in range(2):
        q, k, v = (pack_rows(r, pack) for r in (q_ref, k_ref, v_ref))
        same = pack_rows(col_ref, pack) == row_ref[pack : pack + 1, :]
        outs, logs = [], []
        for h in range(2):
            mine = first if h == 0 else ~first
            scores = lax.dot_general(
                jnp.where(mine, q * HEAD ** (-0.5), 0), k, NT, preferred_element_type=F32
            )
            scores = jnp.where(same, scores, -1000000000.0)
            top = jnp.max(scores, axis=1, keepdims=True)
            powers = jnp.exp(scores - top)
            total = jnp.sum(powers, axis=1, keepdims=True)
            mixed = jnp.dot(powers.astype(BF), v, preferred_element_type=F32)
            outs.append(mixed * (1.0 / total))
            logs.append(top + jnp.log(total))
        o = jnp.where(first, outs[0], outs[1]).astype(BF)
        lse = jnp.where(first, logs[0], logs[1])
        o_ref[LIVE * pack : LIVE * (pack + 1), :] = o[:LIVE]
        o_ref[BACK + REST * pack : BACK + REST * (pack + 1), :] = o[LIVE:]
        lse_ref[LIVE * pack : LIVE * (pack + 1), :] = lse[:LIVE]


def attend(qkv, col, row):
    part = lambda off: pl.BlockSpec((ROWS, 128), lambda j: (0, j + off))
    return pl.pallas_call(
        attend_kernel,
        grid=(2,),
        in_specs=[
            part(0),
            part(2),
            part(4),
            pl.BlockSpec((ROWS, 1), lambda j: (0, 0)),
            pl.BlockSpec((2, PACK), lambda j: (0, 0)),
        ],
        out_specs=[part(0), pl.BlockSpec((BACK, 128), lambda j: (0, j))],
        out_shape=[
            jax.ShapeDtypeStruct((ROWS, 256), BF),
            jax.ShapeDtypeStruct((BACK, 256), F32),
        ],
        cost_estimate=pl.CostEstimate(flops=int(8e8), bytes_accessed=4000000, transcendentals=0),
        compiler_params=pltpu.CompilerParams(vmem_limit_bytes=32 << 20),
    )(qkv, qkv, qkv, col, row)


def attend_back(q_ref, g_ref, o_ref, lse_ref, col_ref, row_ref, out_ref):
    first = lax.broadcasted_iota(jnp.int32, (LIVE, 128), 1) < HEAD
    scale = HEAD ** (-0.5)

    def pair(i, carry):
        pack, j = i // 2, i % 2
        at = pl.ds(pl.multiple_of(LIVE * pack, LIVE), LIVE)
        lanes = lambda which: pl.ds(pl.multiple_of(256 * which + 128 * j, 128), 128)
        q, k, v = (q_ref[at, lanes(which)] for which in range(3))
        g = g_ref[at, lanes(0)]
        weighted = g.astype(F32) * o_ref[at, lanes(0)].astype(F32)
        logs = lse_ref[at, lanes(0)]
        same = col_ref[at, :] == row_ref[pl.ds(pack, 1), :LIVE]
        dq, dk, dv = [], [], []
        for h in range(2):
            mine = first if h == 0 else ~first
            lse = logs[:, HEAD * h : HEAD * h + 1]
            inner = jnp.sum(jnp.where(mine, weighted, 0.0), axis=1, keepdims=True)
            qs = jnp.where(mine, q * scale, 0)
            scores = lax.dot_general(qs, k, NT, preferred_element_type=F32)
            probs = jnp.where(same, jnp.exp(scores - lse), 0.0)
            dprobs = lax.dot_general(jnp.where(mine, g, 0), v, NT, preferred_element_type=F32)
            ds = (probs * (dprobs - inner)).astype(BF)
            dv.append(lax.dot_general(probs.astype(BF), g, TN, preferred_element_type=F32))
            dq.append(jnp.dot(ds, k, preferred_element_type=F32))
            dk.append(lax.dot_general(ds, q, TN, preferred_element_type=F32))
        out_ref[at, lanes(0)] = (jnp.where(first, dq[0], dq[1]) * scale).astype(BF)
        out_ref[at, lanes(1)] = (jnp.where(first, dk[0], dk[1]) * scale).astype(BF)
        out_ref[at, lanes(2)] = jnp.where(first, dv[0], dv[1]).astype(BF)
        return carry

    lax.fori_loop(0, 4, pair, 0)


def head_rows(k, core):
    return (k // 2) * 4 + 2 * core + k % 2


def project_kernel(o0_ref, o1_ref, a_hbm, vec_ref, own0, own1, other0, other1, *refs):
    wo_ref, sum_ref, send0_ref, send1_ref, a_ref, sems = refs
    core = coords()[3]
    copies = []
    for k in range(8):
        head = head_rows(k, core)
        for parts, row in (((own0, own1), 32 * core), ((other0, other1), 32 - 32 * core)):
            at = pl.ds(pl.multiple_of(64 * k + row, 32), 32)
            for half, part in enumerate(parts):
                copies.append((part.at[head], wo_ref.at[at, pl.ds(HALF_D * half, HALF_D)]))
    started = start_all(copies + [(a_hbm, a_ref)], sems)
    wait_all(started)
    for j in range(2):
        at = slice(512 * j, 512 * (j + 1))
        part = jnp.dot(o0_ref[...], wo_ref[:256, at], preferred_element_type=F32) + jnp.dot(
            o1_ref[...], wo_ref[256:, at], preferred_element_type=F32
        )
        (send0_ref, send1_ref)[j][...] = part.astype(BF)
        sum_ref[:, at] = a_ref[:, at] + part + vec_ref[4:5, at]


def project(o, a, vec, own, other):
    return launch(
        project_kernel,
        [(o[0], VMEM), (o[1], VMEM), (a, ANY), (vec, VMEM)] + [(v, ANY) for v in (*own, *other)],
        [((HALF_D, D), BF), ((ROWS, D), F32), ((ROWS, HALF_D), BF), ((ROWS, HALF_D), BF)],
        [pltpu.VMEM((ROWS, D), F32), dma(33)],
        flops=0.8e9,
    )


SWAPPED = ((0, LIVE, LIVE), (LIVE, 0, LIVE), (BACK, BACK + REST, REST), (BACK + REST, BACK, REST))


def widen_kernel(sum_hbm, got0_hbm, got1_hbm, vec_ref, bf1_ref, own_hbm, sib_hbm, col_ref, *refs):
    parts, refs = refs[:5], refs[5:]
    n2_hbm, act_hbm, slope_hbm, stat_ref = refs[:4]
    outs, refs = refs[4:7], refs[7:]
    a2_ref, got_ref, n2_ref, wu_ref, act_ref, slope_ref, dy_ref, whole_ref, h0, h1 = refs[:10]
    sems, out_sems, grad_sems = refs[10:]
    first = start_all(
        [(sum_hbm, a2_ref)]
        + [
            (src.at[pl.ds(start, size), :], got_ref.at[pl.ds(to, size), pl.ds(HALF_D * i, HALF_D)])
            for i, src in enumerate((got0_hbm, got1_hbm))
            for to, start, size in SWAPPED
        ],
        sems,
    )
    grads = start_all(
        [
            (src.at[pl.ds(0, LIVE), :], dy_ref.at[pl.ds(LIVE * i, LIVE), :])
            for i, src in enumerate((own_hbm, sib_hbm))
        ],
        sems,
        9,
    )
    weights = start_all(
        [(piece_of(parts, e, 32), wu_ref.at[pl.ds(core_rows(e), 32), :]) for e in ENTRIES_ZXY],
        sems,
        11,
    )
    gain, shift = vec_ref[5:6, :], vec_ref[6:7, :]
    wait_all(first)

    def rows(i, carry):
        at = tile(i, 64)
        a2 = a2_ref[at, :] + got_ref[at, :].astype(F32)
        hat, mean, inverse = norm_rows(a2)
        n2_ref[at, :] = (hat * gain + shift).astype(BF)
        stat_ref[at, :] = stats(mean, inverse)
        return carry

    lax.fori_loop(0, ROWS // 64, rows, 0)
    wait_all(weights)
    sent = start_all([(n2_ref.at[pl.ds(0, BACK), :], n2_hbm)], out_sems)
    steps = HALF_FF // 512
    hidden = (h0, h1)

    def product(j):
        hidden[j % 2][...] = jnp.dot(
            n2_ref[...], wu_ref[:, 512 * j : 512 * (j + 1)], preferred_element_type=F32
        )

    product(0)
    for j in range(steps):
        if j + 1 < steps:
            product(j + 1)
        at = slice(512 * j, 512 * (j + 1))
        h = hidden[j % 2][...] + bf1_ref[:, at]
        area, bell = gelu_parts(h)
        act_ref[j] = (h * area).astype(BF)
        slope_ref[j] = (
            area[:BACK] + h[:BACK] * bell[:BACK] * 0.3989422804014327
        ).astype(BF)
        sent += start_all(
            [(act_ref.at[j], act_hbm.at[j]), (slope_ref.at[j], slope_hbm.at[j])],
            out_sems,
            1 + 2 * j,
        )
    wait_all(grads)
    dy_ref[...] = jnp.where(col_ref[:BACK, :] >= 0, dy_ref[...], 0)

    for k, dz in enumerate(ZORDER):
        at = tile(z_of(dz), 512)
        part = lax.dot_general(
            act_ref[z_of(dz), :BACK, :], dy_ref[...], TN, preferred_element_type=F32
        )
        whole_ref[at, :] = part.astype(BF)
        mine = [e for e in ENTRIES_XZY_SCATTER if e[3][0] == dz]
        sent += start_all(
            [(whole_ref.at[pl.ds(half_rows(e), 64), :], piece_of(outs, e, 64)) for e in mine],
            grad_sems,
            len(mine) * k,
        )
    wait_all(sent)


def widen(total, got, vec, bf1, own, sib, col, gathered):
    return launch(
        widen_kernel,
        [(total, ANY), (got[0], ANY), (got[1], ANY), (vec, VMEM), (bf1, VMEM), (own, ANY), (sib, ANY), (col, VMEM)]
        + [(g, ANY) for g in gathered],
        [
            ((BACK, D), BF, ANY),
            ((4, ROWS, 512), BF, ANY),
            ((4, BACK, 512), BF, ANY),
            ((ROWS, 128), F32),
        ]
        + [(s, BF, ANY) for s in scatter_shapes("xzy", 64, D)],
        [
            pltpu.VMEM((ROWS, D), F32),
            pltpu.VMEM((ROWS, D), BF),
            pltpu.VMEM((ROWS, D), BF),
            pltpu.VMEM((D, HALF_FF), BF),
            pltpu.VMEM((4, ROWS, 512), BF),
            pltpu.VMEM((4, BACK, 512), BF),
            pltpu.VMEM((BACK, D), BF),
            pltpu.VMEM((HALF_FF, D), BF),
            pltpu.VMEM((ROWS, 512), F32),
            pltpu.VMEM((ROWS, 512), F32),
            dma(11 + len(ENTRIES_ZXY)),
            dma(1 + 2 * (HALF_FF // 512)),
            dma(len(ENTRIES_XZY_SCATTER)),
        ],
        flops=5.8e9,
    )


def hidden_grad_kernel(own_hbm, sib_hbm, col_ref, slope_hbm, n2_hbm, *refs):
    ups, parts, refs = refs[:5], refs[5:9], refs[9:]
    sum_ref, part_hbm, sends, outs, refs = refs[0], refs[1], refs[2:5], refs[5:10], refs[10:]
    dy_ref, slope_ref, n2_ref, n2t_ref, wu_ref, wd_ref, dh_ref, whole_ref = refs[:8]
    part_ref, send_ref, sems, slope_sems, wd_sems, out_sems, last_sems = refs[8:]
    one = start_all(
        [(n2_hbm, n2_ref)]
        + [
            (src.at[pl.ds(0, LIVE), :], dy_ref.at[pl.ds(LIVE * i, LIVE), :])
            for i, src in enumerate((own_hbm, sib_hbm))
        ],
        sems,
    )
    weights, slopes = [], []
    for k, dz in enumerate(ZORDER):
        mine = [e for e in ENTRIES_XZY_GATHER if e[3][0] == dz]
        weights.append(
            start_all(
                [(piece_of(parts, e, 64), wd_ref.at[pl.ds(half_rows(e), 64), :]) for e in mine],
                wd_sems,
                len(mine) * k,
            )
        )
        slopes.append(start_all([(slope_hbm.at[z_of(dz)], slope_ref.at[z_of(dz)])], slope_sems, k))
    two = start_all(
        [(piece_of(ups, e, 32), wu_ref.at[pl.ds(core_rows(e), 32), :]) for e in ENTRIES_ZXY],
        sems,
        3,
    )
    wait_all(one)
    n2t_ref[...] = n2_ref[...].T
    dy_ref[...] = jnp.where(col_ref[:BACK, :] >= 0, dy_ref[...], 0)
    for k, dz in enumerate(ZORDER):
        at = tile(z_of(dz), 512)
        wait_all(weights[k] + slopes[k])
        gate = lax.dot_general(dy_ref[...], wd_ref[at, :], NT, preferred_element_type=F32)
        dh = (gate * slope_ref[z_of(dz)].astype(F32)).astype(BF)
        dh_ref[:, at] = dh
        sum_ref[:, at] = jnp.sum(dh.astype(F32), axis=0, keepdims=True)
        whole_ref[:, at] = jnp.dot(
            n2t_ref[...], dh_ref[:, at], preferred_element_type=F32
        ).astype(BF)
    sent = start_all(
        [(whole_ref.at[pl.ds(core_rows(e), 32), :], piece_of(outs, e, 32)) for e in ENTRIES_ZXY],
        out_sems,
    )
    wait_all(two)
    for j, (to, width) in enumerate(PIECES):
        part = lax.dot_general(
            dh_ref[...], wu_ref[to : to + width, :], NT, preferred_element_type=F32
        )
        part_ref[:, to : to + width] = part
        send_ref[:, to : to + width] = part.astype(BF)
        sent += start_all([(send_ref.at[:, pl.ds(to, width)], sends[j])], last_sems, j)
    sent += start_all([(part_ref, part_hbm)], last_sems, 3)
    wait_all(sent)


def hidden_grads(own, sib, col, slope, n2, up_blocks, down_blocks):
    return launch(
        hidden_grad_kernel,
        [(own, ANY), (sib, ANY), (col, VMEM), (slope, ANY), (n2, ANY)]
        + [(g, ANY) for g in up_blocks + down_blocks],
        [
            ((1, HALF_FF), F32),
            ((BACK, D), F32, ANY),
        ]
        + [((BACK, width), BF, ANY) for _, width in PIECES]
        + [(s, BF, ANY) for s in scatter_shapes("zxy", 32, HALF_FF)],
        [
            pltpu.VMEM((BACK, D), BF),
            pltpu.VMEM((4, BACK, 512), BF),
            pltpu.VMEM((BACK, D), BF),
            pltpu.VMEM((D, BACK), BF),
            pltpu.VMEM((D, HALF_FF), BF),
            pltpu.VMEM((HALF_FF, D), BF),
            pltpu.VMEM((BACK, HALF_FF), BF),
            pltpu.VMEM((D, HALF_FF), BF),
            pltpu.VMEM((BACK, D), F32),
            pltpu.VMEM((BACK, D), BF),
            dma(3 + len(ENTRIES_ZXY)),
            dma(4),
            dma(len(ENTRIES_XZY_GATHER)),
            dma(len(ENTRIES_ZXY)),
            dma(4),
        ],
        flops=7.5e9,
    )


def middle_kernel(part_hbm, got0_hbm, got1_hbm, got2_hbm, sum_hbm, z0_hbm, z1_hbm, *refs):
    stat_ref, own_hbm, sib_hbm, col_ref, vec_ref, o0_ref, o1_ref, wo_hbm = refs[:8]
    da2_ref, do0_ref, do1_ref, sums_ref, mine_ref, send_ref = refs[8:14]
    part_ref, got_ref, a2_ref, z_ref, dy_ref, wo_ref, dz_ref, whole_ref, sems = refs[14:]
    core = coords()[3]
    one = start_all(
        [
            (part_hbm, part_ref),
            (sum_hbm.at[pl.ds(0, BACK), :], a2_ref),
            (own_hbm.at[pl.ds(0, LIVE), :], dy_ref.at[pl.ds(0, LIVE), :]),
            (sib_hbm.at[pl.ds(0, LIVE), :], dy_ref.at[pl.ds(LIVE, LIVE), :]),
        ]
        + [
            (src.at[pl.ds(start, LIVE), :], dst.at[pl.ds(LIVE - start, LIVE), pl.ds(off, width)])
            for dst, src, off, width in (
                (got_ref, got0_hbm, *PIECES[0]),
                (got_ref, got1_hbm, *PIECES[1]),
                (got_ref, got2_hbm, *PIECES[2]),
                (z_ref, z0_hbm, 0, HALF_D),
                (z_ref, z1_hbm, HALF_D, HALF_D),
            )
            for start in (0, LIVE)
        ]
        + [(wo_hbm, wo_ref)],
        sems,
    )
    gain = vec_ref[5:6, :]
    wait_all(one)

    def rows(i, sums):
        at = tile(i, 64)
        dn = part_ref[at, :] + got_ref[at, :].astype(F32)
        a2 = a2_ref[at, :] + z_ref[at, :].astype(F32)
        hat, inverse = normed(a2, stat_ref[at, :])
        dy = jnp.where(col_ref[at, :] >= 0, dy_ref[at, :].astype(F32), 0.0)
        da2 = dy + norm_back(dn, hat, inverse, gain)
        dz = da2.astype(BF)
        dz_ref[at, :] = dz
        if sums is None:
            return 0
        da2_ref[at, :] = da2
        return tuple(
            s + jnp.sum(v.reshape(8, 8, D), axis=0)
            for s, v in zip(sums, (dn * hat, dn, dz.astype(F32), dy))
        )

    steps = LIVE // 64
    sums = lax.fori_loop(0, steps, rows, (jnp.zeros((8, D), F32),) * 4)
    lax.fori_loop(steps, 2 * steps, lambda i, c: rows(i, None), 0)
    for i, s in enumerate(sums):
        sums_ref[i : i + 1, :] = jnp.sum(s, axis=0, keepdims=True)
    sums_ref[4:8, :] = jnp.zeros((4, D), F32)
    for half, (do_ref, o_ref) in enumerate(((do0_ref, o0_ref), (do1_ref, o1_ref))):
        at = slice(256 * half, 256 * (half + 1))
        do_ref[...] = lax.dot_general(
            dz_ref[...], wo_ref[at, :], NT, preferred_element_type=F32
        ).astype(BF)
        whole_ref[at, :] = lax.dot_general(
            o_ref[:BACK, :], dz_ref[...], TN, preferred_element_type=F32
        ).astype(BF)
    for k in range(8):
        mine_ref[k] = whole_ref[pl.ds(pl.multiple_of(64 * k + 32 * core, 32), 32), :]
        send_ref[k] = whole_ref[pl.ds(pl.multiple_of(64 * k + 32 - 32 * core, 32), 32), :]


def middle(part, got, total, z, stat, own, sib, col, vec, o, wo):
    ins = [(v, ANY) for v in (part, *got, total, *z)]
    ins += [(stat, VMEM), (own, ANY), (sib, ANY), (col, VMEM), (vec, VMEM)]
    ins += [(o[0], VMEM), (o[1], VMEM), (wo, ANY)]
    return launch(
        middle_kernel,
        ins,
        [
            ((LIVE, D), F32),
            ((BACK, 256), BF),
            ((BACK, 256), BF),
            ((8, D), F32),
            ((8, 32, D), BF),
            ((8, 32, D), BF),
        ],
        [
            pltpu.VMEM((BACK, D), F32),
            pltpu.VMEM((BACK, D), BF),
            pltpu.VMEM((BACK, D), F32),
            pltpu.VMEM((BACK, D), BF),
            pltpu.VMEM((BACK, D), BF),
            pltpu.VMEM((HALF_D, D), BF),
            pltpu.VMEM((BACK, D), BF),
            pltpu.VMEM((HALF_D, D), BF),
            dma(15),
        ],
        flops=1.4e9,
    )


def back_one_kernel(q_ref, g_ref, o_ref, lse_ref, col_ref, row_ref, n1_hbm, *refs):
    mine_ref, theirs_ref, out_ref, n1t_hbm = refs[:4]
    outs, refs = refs[4:9], refs[9:]
    n1_ref, n1t_ref, whole_ref, sems, sent_sem = refs
    count = len(ENTRIES_ZXY)
    load = start_all([(n1_hbm.at[pl.ds(0, BACK), :], n1_ref)], sent_sem)
    two = []
    for i, e in enumerate(ENTRIES_ZXY):
        rel, half = e[3], e[4]
        _, y, _, core = coords()
        chip = chip_of(rel)
        slot = (chip // 4) * 2 + chip % 2
        at = pl.ds(HALF_D * half, HALF_D)
        dst = piece_of(outs, e, 32, (HALF_QKV, HALF_D))
        here = (y if rel[1] == 0 else 1 - y) == core
        sem = sems.at[count + i]
        two.append(pltpu.make_async_copy(mine_ref.at[slot, :, at], dst, sem))

        @pl.when(here)
        def _():
            pltpu.make_async_copy(mine_ref.at[slot, :, at], dst, sem).start()

        @pl.when(jnp.logical_not(here))
        def _():
            pltpu.make_async_copy(theirs_ref.at[slot, :, at], dst, sem).start()

    attend_back(q_ref, g_ref, o_ref, lse_ref, col_ref, row_ref, out_ref)
    wait_all(load)
    n1t_ref[...] = n1_ref[...].T
    load = start_all([(n1t_ref, n1t_hbm)], sent_sem)
    whole_ref[...] = jnp.dot(n1t_ref[...], out_ref[...], preferred_element_type=F32).astype(BF)
    one = start_all(
        [
            (whole_ref.at[pl.ds(core_rows(e), 32), :], piece_of(outs, e, 32, (0, HALF_QKV)))
            for e in ENTRIES_ZXY
        ],
        sems,
    )
    wait_all(one + two + load)


def back_one(qkv, do, o, lse, col, row, n1, mine, theirs):
    return launch(
        back_one_kernel,
        [(v, VMEM) for v in (qkv, do, o, lse, col, row)]
        + [(n1, ANY), (mine, VMEM), (theirs, VMEM)],
        [((BACK, HALF_QKV), BF), ((D, BACK), BF, ANY)]
        + [(s, BF, ANY) for s in scatter_shapes("zxy", 32, HALF_QKV + HALF_D)],
        [
            pltpu.VMEM((BACK, D), BF),
            pltpu.VMEM((D, BACK), BF),
            pltpu.VMEM((D, HALF_QKV), BF),
            dma(2 * len(ENTRIES_ZXY)),
            dma(1),
        ],
        flops=2.5e9,
    )


def back_two_kernel(q_ref, g_ref, o_ref, lse_ref, col_ref, row_ref, one_ref, *refs):
    w0_hbm, w1_hbm, out_ref, own_ref, send_ref, w0_ref, w1_ref, sems = refs
    load = start_all([(w0_hbm, w0_ref), (w1_hbm, w1_ref)], sems)
    attend_back(q_ref, g_ref, o_ref, lse_ref, col_ref, row_ref, out_ref)
    wait_all(load)
    for j in range(2):
        at = slice(512 * j, 512 * (j + 1))
        total = lax.dot_general(
            one_ref[...], w0_ref[at, :], NT, preferred_element_type=F32
        ) + lax.dot_general(out_ref[...], w1_ref[at, :], NT, preferred_element_type=F32)
        own_ref[:, at] = total[:LIVE]
        send_ref[:, at] = total[LIVE:].astype(BF)


def back_two(qkv, do, o, lse, col, row, one, w0, w1):
    return launch(
        back_two_kernel,
        [(v, VMEM) for v in (qkv, do, o, lse, col, row, one)] + [(w0, ANY), (w1, ANY)],
        [((BACK, HALF_QKV), BF), ((LIVE, D), F32), ((LIVE, D), BF)],
        [pltpu.VMEM((D, HALF_QKV), BF), pltpu.VMEM((D, HALF_QKV), BF), dma(2)],
        flops=3.2e9,
    )


def last_kernel(n1t_hbm, one_ref, two_ref, dn_ref, got_ref, a_hbm, stat_ref, *refs):
    da2_ref, vec_ref, place_ref, sums_ref, upsum_ref, tok_ref = refs[:6]
    outs, refs = refs[6:11], refs[11:]
    n1t_ref, a_ref, whole_ref, small_ref, da_ref, rows_ref, sems, in_sems = refs
    core = coords()[3]
    count = len(ENTRIES_ZXY)
    load = start_all([(n1t_hbm, n1t_ref), (a_hbm.at[pl.ds(0, LIVE), :], a_ref)], in_sems)
    wait_all(load)
    whole_ref[...] = jnp.dot(n1t_ref[...], two_ref[...], preferred_element_type=F32).astype(BF)
    one = start_all(
        [
            (whole_ref.at[pl.ds(core_rows(e), 32), :], piece_of(outs, e, 32, (SMALL, HALF_QKV)))
            for e in ENTRIES_ZXY
        ],
        sems,
    )
    gain = vec_ref[0:1, :]

    def rows(i, sums):
        at = tile(i, 64)
        dn = dn_ref[at, :] + got_ref[at, :].astype(F32)
        hat, inverse = normed(a_ref[at, :], stat_ref[at, :])
        da = da2_ref[at, :] + norm_back(dn, hat, inverse, gain)
        da_ref[at, :] = da.astype(BF)
        tok_ref[at, :] = da.astype(BF)
        return tuple(
            s + jnp.sum(v.reshape(8, 8, D), axis=0) for s, v in zip(sums, (dn * hat, dn))
        )

    sums = lax.fori_loop(0, LIVE // 64, rows, (jnp.zeros((8, D), F32),) * 2)
    tok_ref[LIVE:, :] = jnp.zeros((REST, D), BF)
    lane = lax.broadcasted_iota(jnp.int32, (LIVE, 256), 1)
    hot = (place_ref[:LIVE, :] == lane).astype(BF)
    small = lax.dot_general(da_ref[...], hot, TN, preferred_element_type=F32)
    rows_ref[...] = jnp.zeros((16, D), F32)
    rows_ref[0:1, :] = jnp.sum(sums[0], axis=0, keepdims=True)
    rows_ref[1:2, :] = jnp.sum(sums[1], axis=0, keepdims=True)
    for half, src in enumerate((one_ref, two_ref)):
        total = jnp.sum(src[...].astype(F32), axis=0, keepdims=True)
        for j in range(2):
            own = pl.ds(pl.multiple_of(256 * (2 * half + j) + 128 * core, 128), 128)
            rows_ref[2:3, own] = total[:, 128 * j : 128 * (j + 1)]
            rows_ref[3:4, own] = total[:, 512 + 128 * j : 512 + 128 * (j + 1)]
    rows_ref[4:5, :] = sums_ref[2:3, :]
    rows_ref[5:6, :] = sums_ref[0:1, :]
    rows_ref[6:7, :] = sums_ref[1:2, :]
    rows_ref[7:8, :] = sums_ref[3:4, :]
    spot = lax.broadcasted_iota(jnp.int32, (16, 256), 0)
    place = (lax.broadcasted_iota(jnp.int32, (16, 256), 1) == spot + VEC0).astype(BF)
    value = rows_ref[...]
    for _ in range(2):
        piece = value.astype(BF)
        small = small + lax.dot_general(piece, place, TN, preferred_element_type=F32)
        value = value - piece.astype(F32)
    small_ref[:, :256] = small.astype(BF)
    small_ref[:, 256:] = jnp.zeros((D, SMALL - 256), BF)
    top = lax.broadcasted_iota(jnp.int32, (16, 128), 0) == 0
    for chip in range(16):
        row = pl.multiple_of(64 * chip + 32 * core, 32)
        bias = jnp.where(top, upsum_ref[:, 128 * chip : 128 * (chip + 1)], 0.0)
        small_ref[pl.ds(row, 16), 256:384] = bias.astype(BF)
    three = start_all(
        [
            (small_ref.at[pl.ds(core_rows(e), 32), :], piece_of(outs, e, 32, (0, SMALL)))
            for e in ENTRIES_ZXY
        ],
        sems,
        count,
    )
    wait_all(one + three)


def last_stage(n1t, one, two, dn, got, a, stat, da2, vec, place, sums, upsum):
    return launch(
        last_kernel,
        [(n1t, ANY)]
        + [(v, VMEM) for v in (one, two, dn, got)]
        + [(a, ANY)]
        + [(v, VMEM) for v in (stat, da2, vec, place, sums, upsum)],
        [((PACK, D), BF)] + [(s, BF, ANY) for s in scatter_shapes("zxy", 32, CUT)],
        [
            pltpu.VMEM((D, BACK), BF),
            pltpu.VMEM((LIVE, D), F32),
            pltpu.VMEM((D, HALF_QKV), BF),
            pltpu.VMEM((D, SMALL), BF),
            pltpu.VMEM((LIVE, D), BF),
            pltpu.VMEM((16, D), F32),
            dma(2 * len(ENTRIES_ZXY)),
            dma(2),
        ],
        flops=1.2e9,
    )


def output_kernel(act_hbm, sum_hbm, z0_hbm, z1_hbm, vec_ref, *refs):
    parts, (own_ref, send_ref) = refs[:4], refs[4:6]
    act_ref, a2_ref, z_ref, wd_ref, sems = refs[6:]
    copies = [
        (piece_of(parts, e, 64), wd_ref.at[pl.ds(half_rows(e), 64), :]) for e in ENTRIES_XZY_GATHER
    ]
    copies += [(act_hbm, act_ref)]
    for which, start, size, to in SEGMENTS:
        if which == 0:
            at = pl.ds(start, size)
            copies.append((sum_hbm.at[pl.ds(to, size), :], a2_ref.at[at, :]))
            src = pl.ds(to + size, size)
            copies.append((z0_hbm.at[src, :], z_ref.at[at, pl.ds(0, HALF_D)]))
            copies.append((z1_hbm.at[src, :], z_ref.at[at, pl.ds(HALF_D, HALF_D)]))
    wait_all(start_all(copies, sems))
    for j in range(2):
        at = slice(512 * j, 512 * (j + 1))
        part = jnp.dot(act_ref[0], wd_ref[:512, at], preferred_element_type=F32)
        for k in range(1, 4):
            part += jnp.dot(
                act_ref[k], wd_ref[512 * k : 512 * (k + 1), at], preferred_element_type=F32
            )
        a2 = a2_ref[:, at] + z_ref[:, at].astype(F32) + vec_ref[7:8, at]
        for which, start, size, to in SEGMENTS:
            if which == 0:
                own_ref[start : start + size, at] = part[to : to + size] + a2[start : start + size]
            else:
                send_ref[start : start + size, at] = part[to : to + size].astype(BF)


def output_stage(act, total, z, vec, gathered):
    return launch(
        output_kernel,
        [(act, ANY), (total, ANY), (z[0], ANY), (z[1], ANY), (vec, VMEM)]
        + [(g, ANY) for g in gathered],
        [((PACK, D), F32), ((PACK, D), BF)],
        [
            pltpu.VMEM((4, ROWS, 512), BF),
            pltpu.VMEM((PACK, D), F32),
            pltpu.VMEM((PACK, D), BF),
            pltpu.VMEM((HALF_FF, D), BF),
            dma(len(ENTRIES_XZY_GATHER) + 7),
        ],
        flops=3.2e9,
    )


def finish_kernel(a_ref, b_ref, up_ref, a_got, b_got, up_got, small_ref, qkv_ref, grad_ref, out_ref):
    core = coords()[3]
    small_ref[...] = b_ref[:32, :SMALL] + b_got[:, :SMALL]
    for j in range(12):
        at = slot_of(j)
        mine = pl.ds(pl.multiple_of(256 * j + 128 * core, 128), 128)
        other = pl.ds(pl.multiple_of(256 * j + 128 - 128 * core, 128), 128)
        own, got = (a_ref, a_got) if at < HALF_QKV else (b_ref, b_got)
        at = slice(at, at + 128) if at < HALF_QKV else slice(at + SMALL - HALF_QKV, at + SMALL - HALF_QKV + 128)
        qkv_ref[:, mine] = own[:32, at]
        qkv_ref[:, other] = got[:, at]
    for j in range(16):
        at = slice(128 * j, 128 * (j + 1))
        mine = pl.ds(pl.multiple_of(256 * j + 128 * core, 128), 128)
        other = pl.ds(pl.multiple_of(256 * j + 128 - 128 * core, 128), 128)
        grad_ref[:, mine] = up_ref[:32, at]
        grad_ref[:, other] = up_got[:, at]
    out_ref[:, :HALF_D] = a_ref[:32, HALF_QKV:]
    out_ref[:, HALF_D:] = a_ref[32:, HALF_QKV:]


def finish(a_sum, b_sum, up_sum, a_got, b_got, up_got):
    return launch(
        finish_kernel,
        [(v, VMEM) for v in (a_sum, b_sum, up_sum, a_got, b_got, up_got)],
        [((32, SMALL), F32), ((32, 3 * D), F32), ((32, FF), F32), ((32, D), F32)],
        limit=8,
    )


def in_order(own, sib):
    return jnp.concatenate([own[:LIVE], sib[:LIVE], own[LIVE:], sib[LIVE:]])


def fast_on_device(
    tokens,
    grad_out,
    image_lengths,
    image_device,
    small_map,
    ln1_gain,
    ln1_bias,
    qkv_weight,
    q_bias,
    v_bias,
    out_weight,
    out_bias,
    ln2_gain,
    ln2_bias,
    up_weight,
    up_bias,
    down_weight,
    down_bias,
    pos_table,
):
    device = lax.axis_index("dp") * 4 + lax.axis_index("fsdp")
    seg, place = layout(image_lengths, image_device, small_map, device, PACK)
    seg2, place2 = layout(image_lengths, image_device, small_map, device ^ 1, PACK)
    col = in_order(seg, seg2)[:, None]
    row = jnp.stack([seg, seg2])
    place = in_order(place, place2)[:, None]

    vectors = [ln1_gain, ln1_bias, q_bias, v_bias, out_bias, ln2_gain, ln2_bias, down_bias]
    table = jnp.concatenate([pos_table, jnp.stack(vectors), jnp.zeros((103, 32), BF)])
    keep, send, out2 = prepare(table, up_bias[None, :], qkv_weight, up_weight, out_weight)
    got = swap(send, CORE)
    chunk_1 = jnp.concatenate([keep[:, :CUT], got[:, :CUT]])
    rest = slice(CUT, SMALL + QKV)
    chunk_2 = jnp.concatenate([jnp.concatenate([keep[:, rest], got[:, rest]]), out2], axis=1)
    chunk_u = jnp.concatenate([keep[:, SMALL + QKV :], got[:, SMALL + QKV :]])
    down_a, down_b = down_weight[:64], down_weight[64:]
    sib_tokens = swap(tokens, CORE)
    sib_grad = swap(grad_out, CORE)

    (far_1,) = send_all((chunk_1, FAR))
    pair_1 = jnp.stack([chunk_1, far_1])
    (near_1,) = send_all((pair_1, ZBIT))
    down_x, down_y = send_all((down_a, XBIT), (down_b, YBIT), wait=(far_1,))
    line_1 = jnp.concatenate([pair_1, near_1])
    x_1, y_1 = send_all((line_1, XBIT), (line_1, YBIT), wait=(down_x, down_y))
    (far_2,) = send_all((chunk_2, FAR), wait=(near_1, down_x, down_y))
    pair_2 = jnp.stack([chunk_2, far_2])
    (near_2,) = send_all((pair_2, ZBIT))
    line_2 = jnp.concatenate([pair_2, near_2])
    corner_1 = corners(x_1, y_1)
    gathered_1 = [line_1, x_1, y_1, *corner_1]
    x_2, y_2 = send_all((line_2, XBIT), (line_2, YBIT), wait=corner_1)
    (far_u,) = send_all((chunk_u, FAR), wait=(near_2, *corner_1))
    pair_u = jnp.stack([chunk_u, far_u])
    a, n1, wq0, qkv0, vec, bf1, stat1 = first_stage(tokens, sib_tokens, place, gathered_1)
    (near_u,) = send_all((pair_u, ZBIT), wait=(stat1,))
    line_u = jnp.concatenate([pair_u, near_u])
    corner_2 = corners(x_2, y_2, wait=(stat1,))
    gathered_2 = [line_2, x_2, y_2, *corner_2]
    o0, lse0 = attend(after(qkv0, x_2, y_2, sib_grad), col, row)
    x_u, y_u = send_all((line_u, XBIT), (line_u, YBIT), wait=(*corner_2, lse0))
    quad_d = jnp.stack([down_a, down_x, down_b, down_y])
    (far_d,) = send_all((quad_d, FAR), wait=(near_u,))
    wq1, qkv1, *out_own = second_stage(n1, vec, gathered_2)
    out_other = [swap(half, CORE) for half in out_own]
    o1, lse1 = attend(qkv1, col, row)
    o = (o0, o1)
    pair_d = jnp.stack([quad_d, after(far_d, lse1)])
    wo, total, *send = project(o, a, vec, out_own, out_other)
    z = [swap(part, CORE) for part in send]
    corner_u = corners(x_u, y_u, wait=(send[0],))
    gathered_u = [line_u, x_u, y_u, *corner_u]
    (near_d,) = send_all((pair_d, ZBIT), wait=(lse1,))
    pairs_d = (pair_d, near_d)
    side_a = jnp.concatenate([p[:, :2] for p in pairs_d])
    side_b = jnp.concatenate([p[:, 2:] for p in pairs_d])
    gathered_d = [*pairs_d, *send_all((side_a, YBIT), (side_b, XBIT), wait=corner_u)]
    n2, act, slope, stat2, *d_parts = widen(
        total, z, vec, bf1, grad_out, sib_grad, col, gathered_u
    )

    keep, side_a, side_b = d_parts
    side_a, side_b = send_all((side_a, YBIT), (side_b, XBIT), wait=gathered_d[2:])
    up_bias_sum, part, *u_parts = hidden_grads(
        grad_out, sib_grad, col, slope, n2, gathered_u, gathered_d
    )
    got = [swap(piece, CORE) for piece in u_parts[:3]]
    u_parts = u_parts[3:]
    d_sum = add(keep, jnp.concatenate([side_a, side_b], axis=1))
    d_send = d_sum[2:].astype(BF)
    u_got = send_all(*corner_pairs(u_parts), wait=(side_a, side_b))
    (d_near,) = send_all((d_send, ZBIT))
    da2, do0, do1, sums, mine, theirs = middle(
        after(part, d_send), got, total, z, stat2, grad_out, sib_grad, col, vec, o, wo
    )
    theirs = swap(theirs, CORE)

    u_x, u_y = to_neighbours(u_parts, *(after(u, sums) for u in u_got))
    u_line = send_all((u_x, XBIT), (u_y, YBIT))
    d_one, n1t, *a_parts = back_one(
        qkv0, after(do0, u_x, u_y), o0, lse0, col, row, n1, mine, theirs
    )
    d_pair = add(d_sum[:2], after(d_near, d_one))
    d_send = d_pair[1].astype(BF)
    (d_far,) = send_all((d_send, FAR))
    d_two, dn, send = back_two(
        qkv1, after(do1, d_send), o1, lse1, col, row, d_one, wq0, wq1
    )
    u_sum = add(u_parts[0], *(after(u, send) for u in u_line))
    u_send = u_sum[2:].astype(BF)
    a_got = send_all(*corner_pairs(a_parts), wait=(*u_line, send))
    (u_near,) = send_all((u_send, ZBIT))
    tokens_grad, *b_parts = last_stage(
        n1t, d_one, d_two, dn, swap(send, CORE), a, stat1, da2, vec, place, sums, up_bias_sum
    )
    a_x, a_y = to_neighbours(a_parts, *(after(v, tokens_grad) for v in a_got))
    a_line = send_all((a_x, XBIT), (a_y, YBIT))
    u_pair = add(u_sum[:2], after(u_near, tokens_grad))
    u_send = u_pair[1].astype(BF)
    (u_far,) = send_all((u_send, FAR))
    own, send = output_stage(
        after(act, a_x, a_y, u_send, tokens_grad), total, z, vec, gathered_d
    )
    layer_out = (own + swap(send, CORE).astype(F32)).astype(BF)

    b_got = send_all(*corner_pairs(b_parts))
    d_quad = add(d_pair[0], after(d_far, own))
    b_x, b_y = to_neighbours(b_parts, *(after(v, own) for v in b_got))
    a_sum = add(a_parts[0], *a_line)
    b_line = send_all((b_x, XBIT), (b_y, YBIT), wait=a_line)
    d_x, d_y = send_all(
        (d_quad[1].astype(BF), XBIT), (d_quad[3].astype(BF), YBIT), wait=b_line
    )
    down_sum = jnp.concatenate([add(d_quad[0], d_x), add(d_quad[2], d_y)])
    (a_near,) = send_all((a_sum[2:].astype(BF), ZBIT), wait=(u_far,))
    up_sum = add(u_pair[0], u_far)
    a_pair = add(a_sum[:2], a_near)
    (a_far,) = send_all((a_pair[1].astype(BF), FAR))
    b_sum = add(b_parts[0], *b_line)
    (b_near,) = send_all((b_sum[2:].astype(BF), ZBIT))
    a_sum = add(a_pair[0], a_far)
    b_pair = add(b_sum[:2], b_near)
    (b_far,) = send_all((b_pair[1].astype(BF), FAR))
    b_sum = add(b_pair[0], b_far)

    up_got = swap(up_sum[32:], CORE)
    a_got = swap(a_sum[32:, :HALF_QKV], CORE)
    b_got = swap(b_sum[32:], CORE)
    small, qkv_grad, up_grad, out_grad = finish(a_sum, b_sum, up_sum, a_got, b_got, up_got)
    gv = small[:, VEC0 : VEC0 + 8].T
    return (
        layer_out,
        tokens_grad,
        gv[0],
        gv[1],
        qkv_grad,
        gv[2],
        gv[3],
        out_grad,
        gv[4],
        gv[5],
        gv[6],
        up_grad,
        small[0, 256:],
        down_sum,
        gv[7],
        small[:, :LONG].T,
    )


def solution(mesh):
    in_specs = (
        P(("dp", "fsdp"), None),
        P(("dp", "fsdp"), None),
        P(),
        P(),
        P(),
        P(("dp", "fsdp")),
        P(("dp", "fsdp")),
        P(("dp", "fsdp"), None),
        P(("dp", "fsdp")),
        P(("dp", "fsdp")),
        P(("dp", "fsdp"), None),
        P(("dp", "fsdp")),
        P(("dp", "fsdp")),
        P(("dp", "fsdp")),
        P(("dp", "fsdp"), None),
        P(("dp", "fsdp")),
        P(("dp", "fsdp"), None),
        P(("dp", "fsdp")),
        P(None, ("dp", "fsdp")),
    )
    out_specs = (
        P(("dp", "fsdp"), None),
        P(("dp", "fsdp"), None),
        P(("dp", "fsdp")),
        P(("dp", "fsdp")),
        P(("dp", "fsdp"), None),
        P(("dp", "fsdp")),
        P(("dp", "fsdp")),
        P(("dp", "fsdp"), None),
        P(("dp", "fsdp")),
        P(("dp", "fsdp")),
        P(("dp", "fsdp")),
        P(("dp", "fsdp"), None),
        P(("dp", "fsdp")),
        P(("dp", "fsdp"), None),
        P(("dp", "fsdp")),
        P(None, ("dp", "fsdp")),
    )
    eight_by_four = mesh.shape["dp"] == 8 and mesh.shape["fsdp"] == 4
    return jax.shard_map(
        fast_on_device if eight_by_four else on_device, mesh=mesh, in_specs=in_specs, out_specs=out_specs, check_vma=False
    )
```

```python
import functools

import jax
import jax.numpy as jnp
import numpy as np
from jax import lax
from jax.experimental import pallas as pl
from jax.experimental.pallas import tpu as pltpu
from jax.sharding import PartitionSpec as P

D = 1024
HEADS = 16
HEAD = 64
FF = 4096
LONG = 145
SHORT = 50


EPS = 1e-06


def fetch(parts):
    whole = (
        lax.all_gather(parts[0], ("dp", "fsdp"), axis=1, tiled=True),
        lax.all_gather(parts[1], ("dp", "fsdp"), axis=0, tiled=True),
        lax.all_gather(parts[2], ("dp", "fsdp"), axis=0, tiled=True),
        lax.all_gather(parts[3], ("dp", "fsdp"), axis=0, tiled=True),
        lax.all_gather(parts[4], ("dp", "fsdp"), axis=0, tiled=True),
        lax.all_gather(parts[5], ("dp", "fsdp"), axis=0, tiled=True),
        lax.all_gather(parts[6], ("dp", "fsdp"), axis=1, tiled=True),
    )
    return whole


def reduce_grads(parts):
    owned = (
        lax.psum_scatter(parts[0], ("dp", "fsdp"), scatter_dimension=1, tiled=True),
        lax.psum_scatter(parts[1], ("dp", "fsdp"), scatter_dimension=0, tiled=True),
        lax.psum_scatter(parts[2], ("dp", "fsdp"), scatter_dimension=0, tiled=True),
        lax.psum_scatter(parts[3], ("dp", "fsdp"), scatter_dimension=0, tiled=True),
        lax.psum_scatter(parts[4], ("dp", "fsdp"), scatter_dimension=0, tiled=True),
        lax.psum_scatter(parts[5], ("dp", "fsdp"), scatter_dimension=0, tiled=True),
        lax.psum_scatter(parts[6], ("dp", "fsdp"), scatter_dimension=1, tiled=True),
    )
    return owned


def layout(image_lengths, image_device, small_map, device, rows_dev):
    mine = image_device == device
    lens = jnp.where(mine, image_lengths, 0)
    starts = jnp.cumsum(lens) - lens
    rows = jnp.arange(rows_dev, dtype=jnp.int32)
    inside = (
        mine[None, :]
        & (starts[None, :] <= rows[:, None])
        & (rows[:, None] < (starts + lens)[None, :])
    )
    number = jnp.arange(image_lengths.shape[0], dtype=jnp.int32)
    segment = jnp.sum(jnp.where(inside, number[None, :] + 1, 0), axis=1) - 1
    offset = rows - jnp.sum(jnp.where(inside, starts[None, :], 0), axis=1)
    length = jnp.sum(jnp.where(inside, lens[None, :], 0), axis=1)
    spots = jnp.arange(SHORT, dtype=jnp.int32)
    mapped = jnp.sum(jnp.where(offset[:, None] == spots[None, :], small_map[None, :], 0), axis=1)
    place = jnp.where(length == LONG, offset, jnp.where(length == SHORT, mapped, 0))
    return (segment, place)


def layer_norm_forward_pass(v, norm_gain, shift_bias):
    centred_rows = v - jnp.mean(v, axis=1, keepdims=True)
    inverse_deviation = lax.rsqrt(
        jnp.mean(centred_rows * centred_rows, axis=1, keepdims=True) + EPS
    )
    normalized_rows = centred_rows * inverse_deviation
    return (normalized_rows * norm_gain + shift_bias, normalized_rows, inverse_deviation)


def layer_norm_backward_pass(upstream_gradient, normalized_rows, inverse_deviation, norm_gain):
    normalized_gradient = upstream_gradient * norm_gain
    first_input = jnp.mean(normalized_gradient, axis=1, keepdims=True)
    second_input = jnp.mean(normalized_gradient * normalized_rows, axis=1, keepdims=True)
    return (
        inverse_deviation * (normalized_gradient - first_input - normalized_rows * second_input),
        jnp.sum(upstream_gradient * normalized_rows, axis=0),
        jnp.sum(upstream_gradient, axis=0),
    )


def split_heads(values, groups):
    return values.reshape(values.shape[0], groups, HEADS // groups, HEAD).transpose(1, 0, 2, 3)


def join_heads(values):
    return values.transpose(1, 0, 2, 3).reshape(values.shape[1], D)


def masked_scores(query, keys, same):
    scores = jnp.einsum("thd,shd->hts", query, keys, preferred_element_type=jnp.float32) * HEAD ** (
        -0.5
    )
    return jnp.where(same[None], scores, -1000000000.0)


def attend_forward(qkvb, same):
    groups = HEADS // 4
    query = split_heads(qkvb[:, :D], groups)
    keys = split_heads(qkvb[:, D : 2 * D], groups)
    values = split_heads(qkvb[:, 2 * D :], groups)

    def one_group(item):
        scores = masked_scores(item[0], item[1], same)
        top = jnp.max(scores, axis=2, keepdims=True)
        lse = top + jnp.log(jnp.sum(jnp.exp(scores - top), axis=2, keepdims=True))
        probs = jnp.exp(scores - lse).astype(jnp.bfloat16)
        attended = jnp.einsum("hts,shd->thd", probs, item[2], preferred_element_type=jnp.float32)
        return (attended, lse[:, :, 0])

    attended, lse = lax.map(one_group, (query, keys, values))
    return (join_heads(attended), lse)


def attend_backward(qkvb, dob, lse, same):
    groups = HEADS // 4
    query = split_heads(qkvb[:, :D], groups)
    keys = split_heads(qkvb[:, D : 2 * D], groups)
    values = split_heads(qkvb[:, 2 * D :], groups)
    douts = split_heads(dob, groups)

    def one_group(item):
        scores = masked_scores(item[0], item[1], same)
        probs = jnp.exp(scores - item[4][:, :, None])
        dvalue = jnp.einsum(
            "hts,thd->shd", probs.astype(jnp.bfloat16), item[3], preferred_element_type=jnp.float32
        )
        dprobs = jnp.einsum("thd,shd->hts", item[3], item[2], preferred_element_type=jnp.float32)
        inner = jnp.sum(probs * dprobs, axis=2, keepdims=True)
        dscore = (probs * (dprobs - inner)).astype(jnp.bfloat16)
        dquery = jnp.einsum(
            "hts,shd->thd", dscore, item[1], preferred_element_type=jnp.float32
        ) * HEAD ** (-0.5)
        dkey = jnp.einsum(
            "hts,thd->shd", dscore, item[0], preferred_element_type=jnp.float32
        ) * HEAD ** (-0.5)
        return (dquery, dkey, dvalue)

    dquery, dkey, dvalue = lax.map(one_group, (query, keys, values, douts, lse))
    return jnp.concatenate([join_heads(dquery), join_heads(dkey), join_heads(dvalue)], axis=1)


def gelu_slope(x):
    return (
        0.5 * (1.0 + jax.scipy.special.erf(x * 0.7071067811865476))
        + x * jnp.exp(-0.5 * x * x) * 0.3989422804014327
    )


def on_device(
    tokens,
    grad_out,
    image_lengths,
    image_device,
    small_map,
    ln1_gain,
    ln1_bias,
    qkv_weight,
    q_bias,
    v_bias,
    out_weight,
    out_bias,
    ln2_gain,
    ln2_bias,
    up_weight,
    up_bias,
    down_weight,
    down_bias,
    pos_table,
):
    rows_dev = tokens.shape[0]
    device = lax.axis_index("dp") * lax.axis_size("fsdp") + lax.axis_index("fsdp")
    segment, place = layout(image_lengths, image_device, small_map, device, rows_dev)
    same = segment[:, None] == segment[None, :]
    valid = (segment >= 0).astype(jnp.float32)[:, None]
    table_rows = jnp.arange(LONG, dtype=jnp.int32)
    picker = place[:, None] == table_rows[None, :]
    vectors = jnp.stack(
        [ln1_gain, ln1_bias, q_bias, v_bias, out_bias, ln2_gain, ln2_bias, down_bias]
    )
    shards = (vectors, qkv_weight, out_weight, up_weight, up_bias, down_weight, pos_table)
    whole = fetch(shards)
    vec = whole[0].astype(jnp.float32)
    first_gain, first_centred, bq, bv, bo, second_gain, second_centred, bf2 = (
        vec[0],
        vec[1],
        vec[2],
        vec[3],
        vec[4],
        vec[5],
        vec[6],
        vec[7],
    )
    bf1 = whole[4].astype(jnp.float32)
    activation_rows = tokens.astype(jnp.float32) + jnp.dot(
        picker.astype(jnp.bfloat16), whole[6], preferred_element_type=jnp.float32
    )
    first_normed, first_normalized, first_inverse_deviation = layer_norm_forward_pass(
        activation_rows, first_gain, first_centred
    )
    n1b = first_normed.astype(jnp.bfloat16)
    bias3 = jnp.concatenate([bq, jnp.zeros_like(bq), bv])
    qkvb = (jnp.dot(n1b, whole[1], preferred_element_type=jnp.float32) + bias3).astype(jnp.bfloat16)
    attended, lse = attend_forward(qkvb, same)
    ob = attended.astype(jnp.bfloat16)
    second_activation = (
        activation_rows + jnp.dot(ob, whole[2], preferred_element_type=jnp.float32) + bo
    )
    second_normed, second_normalized, second_inverse_deviation = layer_norm_forward_pass(
        second_activation, second_gain, second_centred
    )
    n2b = second_normed.astype(jnp.bfloat16)
    hpre = jnp.dot(n2b, whole[3], preferred_element_type=jnp.float32) + bf1
    actb = jax.nn.gelu(hpre, approximate=False).astype(jnp.bfloat16)
    output = second_activation + jnp.dot(actb, whole[5], preferred_element_type=jnp.float32) + bf2
    layer_out = output.astype(jnp.bfloat16)
    dy = grad_out.astype(jnp.float32) * valid
    fenced, dy = lax.optimization_barrier((shards, dy))
    back = fetch(fenced)
    dyb = dy.astype(jnp.bfloat16)
    d_down = jnp.einsum("tf,td->fd", actb, dyb, preferred_element_type=jnp.float32)
    d_down_bias = jnp.sum(dy, axis=0)
    dgate = jnp.einsum("td,fd->tf", dyb, back[5], preferred_element_type=jnp.float32)
    dhb = (dgate * gelu_slope(hpre)).astype(jnp.bfloat16)
    d_up = jnp.einsum("td,tf->df", n2b, dhb, preferred_element_type=jnp.float32)
    d_up_bias = jnp.sum(dhb.astype(jnp.float32), axis=0)
    second_norm_gradient = jnp.einsum("tf,df->td", dhb, back[3], preferred_element_type=jnp.float32)
    second_activation_norm_gradient, second_gain_gradient, second_centred_gradient = (
        layer_norm_backward_pass(
            second_norm_gradient, second_normalized, second_inverse_deviation, second_gain
        )
    )
    da2 = dy + second_activation_norm_gradient
    dzb = da2.astype(jnp.bfloat16)
    d_out = jnp.einsum("te,td->ed", ob, dzb, preferred_element_type=jnp.float32)
    d_out_bias = jnp.sum(dzb.astype(jnp.float32), axis=0)
    dob = jnp.einsum("td,ed->te", dzb, back[2], preferred_element_type=jnp.float32).astype(
        jnp.bfloat16
    )
    dqkvb = attend_backward(qkvb, dob, lse, same).astype(jnp.bfloat16)
    d_qkv = jnp.einsum("td,te->de", n1b, dqkvb, preferred_element_type=jnp.float32)
    dqkv_sum = jnp.sum(dqkvb.astype(jnp.float32), axis=0)
    first_norm_gradient = jnp.einsum(
        "te,de->td", dqkvb, back[1], preferred_element_type=jnp.float32
    )
    first_activation_gradient, first_gain_gradient, first_centred_gradient = (
        layer_norm_backward_pass(
            first_norm_gradient, first_normalized, first_inverse_deviation, first_gain
        )
    )
    da = da2 + first_activation_gradient
    tokens_grad = da.astype(jnp.bfloat16)
    d_pos = jnp.dot(picker.astype(jnp.float32).T, da, precision=lax.Precision.HIGHEST)
    d_vectors = jnp.stack(
        [
            first_gain_gradient,
            first_centred_gradient,
            dqkv_sum[:D],
            dqkv_sum[2 * D :],
            d_out_bias,
            second_gain_gradient,
            second_centred_gradient,
            d_down_bias,
        ]
    )
    flat_parts = (
        d_vectors,
        d_qkv.reshape(-1, 128),
        d_out.reshape(-1, 128),
        d_up.reshape(-1, 128),
        d_up_bias,
        d_down,
        d_pos,
    )
    owned = reduce_grads(flat_parts)
    gv = owned[0]
    qkv_owned = owned[1].reshape(-1, 3 * D)
    out_owned = owned[2].reshape(-1, D)
    up_owned = owned[3].reshape(-1, FF)
    return (
        layer_out,
        tokens_grad,
        gv[0],
        gv[1],
        qkv_owned,
        gv[2],
        gv[3],
        out_owned,
        gv[4],
        gv[5],
        gv[6],
        up_owned,
        owned[4],
        owned[5],
        gv[7],
        owned[6],
    )


BF = jnp.bfloat16
F32 = jnp.float32
AXES = ("dp", "fsdp")
CORE, XBIT, YBIT, ZBIT, FAR = 1, 2, 4, 8, 16
PACK = 384
LIVE = -(-2 * LONG // 64) * 64
REST = PACK - LIVE
ROWS = 2 * PACK
BACK = 2 * LIVE
HALF_FF = FF // 2
QKV = 3 * D // 2
HALF_D = D // 2
SMALL = 384
HALF_QKV = QKV // 2
CUT = SMALL + HALF_QKV
VEC0 = LONG
SEGMENTS = ((0, 0, LIVE, 0), (1, 0, LIVE, LIVE), (0, LIVE, REST, BACK), (1, LIVE, REST, BACK + REST))
NT = (((1,), (1,)), ((), ()))
TN = (((0,), (0,)), ((), ()))


def swap(value, mask):
    return lax.ppermute(value, AXES, [(i, i ^ mask) for i in range(32)])


def coords():
    dp = lax.axis_index("dp")
    fs = lax.axis_index("fsdp")
    return dp // 2, dp % 2, fs // 2, fs % 2


def chip_of(rel):
    z, y, x, _ = coords()
    dz, dy, dx = rel
    bits = 0
    for part, off, width in ((z // 2, dz // 2, 8), (z % 2, dz % 2, 4), (y, dy, 2), (x, dx, 1)):
        bits = bits + (1 - part if off else part) * width
    return bits


ZORDER = (0, 2, 1, 3)
ENTRIES_ZXY = (
    [(0, (k,), h, (z, 0, 0), h) for k, z in enumerate(ZORDER) for h in range(2)]
    + [(1, (k,), h, (z, 0, 1), h) for k, z in enumerate(ZORDER) for h in range(2)]
    + [(2, (k,), h, (z, 1, 0), h) for k, z in enumerate(ZORDER) for h in range(2)]
    + [(3, (k,), h, (z, 1, 1), h) for k, z in enumerate(ZORDER[:2]) for h in range(2)]
    + [(4, (k,), h, (z, 1, 1), h) for k, z in enumerate(ZORDER[2:]) for h in range(2)]
)
QUADS = (((0, 0), 0), ((0, 1), 0), ((0, 0), 1), ((1, 0), 1))
SIDE_A = ((1, 0), (1, 1))
SIDE_B = ((0, 1), (1, 1))
ENTRIES_XZY_GATHER = (
    [
        (k // 2, (k % 2, q), 0, (z,) + QUADS[q][0], QUADS[q][1])
        for k, z in enumerate(ZORDER)
        for q in range(4)
    ]
    + [(2, (k, q), 0, (z,) + SIDE_A[q], 0) for k, z in enumerate(ZORDER) for q in range(2)]
    + [(3, (k, q), 0, (z,) + SIDE_B[q], 1) for k, z in enumerate(ZORDER) for q in range(2)]
)
ENTRIES_XZY_SCATTER = (
    [
        (0, (k, q), 0, (z,) + QUADS[q][0], QUADS[q][1])
        for k, z in enumerate(ZORDER)
        for q in range(4)
    ]
    + [(1, (k, q), 0, (z,) + SIDE_A[q], 0) for k, z in enumerate(ZORDER) for q in range(2)]
    + [(2, (k, q), 0, (z,) + SIDE_B[q], 1) for k, z in enumerate(ZORDER) for q in range(2)]
)


def after(value, *done):
    return lax.optimization_barrier((value, done))[0]


def send_all(*pairs, wait=()):
    values = tuple(value for value, _ in pairs)
    if wait:
        values, _ = lax.optimization_barrier((values, tuple(wait)))
    return tuple(swap(value, mask) for value, (_, mask) in zip(values, pairs))


def corners(from_x, from_y, wait=()):
    return send_all((from_x[:2], YBIT), (from_y[2:], XBIT), wait=wait)


def add(*values):
    total = values[0].astype(F32)
    for value in values[1:]:
        total = total + value.astype(F32)
    return total


def corner_pairs(parts):
    return (parts[3], XBIT), (parts[4], YBIT)


def scatter_shapes(kind, rows, width):
    if kind == "zxy":
        return [(4, 2 * rows, width)] * 3 + [(2, 2 * rows, width)] * 2
    return [(4, 4, rows, width), (4, 2, rows, width), (4, 2, rows, width)]


SCATTER_ENTRIES = {"zxy": ENTRIES_ZXY, "xzy": ENTRIES_XZY_SCATTER}


def piece_of(refs, entry, rows, lanes=None):
    array, index, row, _, _ = entry
    width = pl.ds(*lanes) if lanes else slice(None)
    return refs[array].at[index + (pl.ds(rows * row, rows), width)]


def start_all(copies, sems, first=0):
    started = []
    for i, (src, dst) in enumerate(copies):
        copy = pltpu.make_async_copy(src, dst, sems.at[first + i])
        copy.start()
        started.append(copy)
    return started


def wait_all(started):
    for copy in started:
        copy.wait()


def core_rows(entry):
    core = coords()[3]
    side = core if entry[4] == 0 else 1 - core
    return pl.multiple_of(chip_of(entry[3]) * 64 + side * 32, 32)


def z_of(dz):
    z = coords()[0]
    high, low = z // 2, z % 2
    return 2 * (1 - high if dz // 2 else high) + (1 - low if dz % 2 else low)


def half_rows(entry):
    return pl.multiple_of(chip_of(entry[3]) * 128 + 64 * entry[4], 64)


def tile(i, width):
    return pl.ds(pl.multiple_of(i * width, width), width)


ANY = pl.BlockSpec(memory_space=pl.ANY)
VMEM = pl.BlockSpec(memory_space=pltpu.VMEM)


def launch(kernel, ins, outs, scratch=(), flops=0, limit=56):
    size = sum(int(np.prod(o[0])) * jnp.dtype(o[1]).itemsize for o in outs)
    for value, _ in ins:
        size += value.size * value.dtype.itemsize
    return pl.pallas_call(
        kernel,
        out_shape=[jax.ShapeDtypeStruct(o[0], o[1]) for o in outs],
        in_specs=[spec for _, spec in ins],
        out_specs=[o[2] if len(o) > 2 else VMEM for o in outs],
        scratch_shapes=list(scratch),
        cost_estimate=pl.CostEstimate(flops=int(flops), bytes_accessed=int(size), transcendentals=0),
        compiler_params=pltpu.CompilerParams(vmem_limit_bytes=limit << 20),
    )(*[value for value, _ in ins])


def dma(count):
    return pltpu.SemaphoreType.DMA((count,))


def norm_rows(v):
    mean = jnp.mean(v, axis=1, keepdims=True)
    centred = v - mean
    inverse = lax.rsqrt(jnp.mean(centred * centred, axis=1, keepdims=True) + EPS)
    return centred * inverse, mean, inverse


def stats(mean, inverse):
    lane = lax.broadcasted_iota(jnp.int32, (mean.shape[0], 128), 1)
    return jnp.where(lane == 0, mean, inverse)


def normed(v, stat):
    return (v - stat[:, 0:1]) * stat[:, 1:2], stat[:, 1:2]


def gelu_parts(h):
    bell = jnp.exp(h * h * -0.5)
    base = 1.0 + jnp.abs(h) * (0.3275911 * 0.7071067811865476)
    t = pl.reciprocal(base, approx=True)
    t = t * (2.0 - base * t)
    poly = 0.5 * 1.061405429
    for factor in (-1.453152027, 1.421413741, -0.284496736, 0.254829592):
        poly = poly * t + 0.5 * factor
    tail = poly * t * bell
    return jnp.where(h >= 0, 1.0 - tail, tail), bell


PIECES = ((0, 384), (384, 384), (768, 256))


def norm_back(dn, hat, inverse, gain):
    scaled = dn * gain
    first = jnp.mean(scaled, axis=1, keepdims=True)
    second = jnp.mean(scaled * hat, axis=1, keepdims=True)
    return inverse * (scaled - first - hat * second)


def slot_of(block):
    which, j = divmod(block, 4)
    return 768 * (j // 2) + 256 * which + 128 * (j % 2)


def prepare_kernel(pos_ref, bias_ref, qkv_ref, up_ref, out_ref, keep_ref, send_ref, out2_ref):
    core = coords()[3]
    eye = (
        lax.broadcasted_iota(jnp.int32, (32, 32), 0) == lax.broadcasted_iota(jnp.int32, (32, 32), 1)
    ).astype(BF)
    small = lax.dot_general(eye, pos_ref[...], NT, preferred_element_type=F32)
    first_row = lax.broadcasted_iota(jnp.int32, (32, 128), 0) == 0
    bias = jnp.where(first_row, bias_ref[...].astype(F32), 0.0)
    small = jnp.concatenate([small, bias], axis=1).astype(BF)
    keep_ref[:, :SMALL] = small
    send_ref[:, :SMALL] = small
    for src, first, count in ((qkv_ref, SMALL, 12), (up_ref, SMALL + QKV, 16)):
        for j in range(count):
            own = pl.ds(pl.multiple_of(256 * j + 128 * core, 128), 128)
            other = pl.ds(pl.multiple_of(256 * j + 128 * (1 - core), 128), 128)
            to = first + (slot_of(j) if count == 12 else 128 * j)
            keep_ref[:, to : to + 128] = src[:, own]
            send_ref[:, to : to + 128] = src[:, other]
    out2_ref[:32] = out_ref[:, :HALF_D]
    out2_ref[32:] = out_ref[:, HALF_D:]


def prepare(pos, bias, qkv, up, out):
    shapes = [(32, SMALL + QKV + HALF_FF)] * 2 + [(64, HALF_D)]
    return launch(
        prepare_kernel,
        [(v, VMEM) for v in (pos, bias, qkv, up, out)],
        [(s, BF) for s in shapes],
        limit=8,
    )


def fill_bias(bias_ref, vec_ref, half):
    core = coords()[3]
    for j in range(2):
        own = pl.ds(pl.multiple_of(256 * (2 * half + j) + 128 * core, 128), 128)
        bias_ref[0:1, 128 * j : 128 * (j + 1)] = vec_ref[2:3, own]
        bias_ref[0:1, 256 + 128 * j : 256 + 128 * (j + 1)] = jnp.zeros((1, 128), F32)
        bias_ref[0:1, 512 + 128 * j : 512 + 128 * (j + 1)] = vec_ref[3:4, own]


def first_kernel(own_hbm, sib_hbm, place_ref, *refs):
    parts, refs = refs[:5], refs[5:]
    a_hbm, n1_hbm, wq_hbm, qkv_ref, vec_ref, bf1_ref, stat_ref = refs[:7]
    tok_ref, a_ref, n1_ref, wq_ref, small_ref, bias_ref, sems, out_sems = refs[7:]
    core = coords()[3]
    count = len(ENTRIES_ZXY)
    one = start_all(
        [
            (piece_of(parts, e, 32, (0, SMALL)), small_ref.at[pl.ds(core_rows(e), 32), :])
            for e in ENTRIES_ZXY
        ]
        + [
            (
                (own_hbm if which == 0 else sib_hbm).at[pl.ds(start, size), :],
                tok_ref.at[pl.ds(to, size), :],
            )
            for which, start, size, to in SEGMENTS
        ],
        sems,
    )
    two = start_all(
        [
            (piece_of(parts, e, 32, (SMALL, HALF_QKV)), wq_ref.at[pl.ds(core_rows(e), 32), :])
            for e in ENTRIES_ZXY
        ],
        sems,
        count + 4,
    )
    wait_all(one)
    lane = lax.broadcasted_iota(jnp.int32, (16, 256), 1)
    pick = (lane == lax.broadcasted_iota(jnp.int32, (16, 256), 0) + VEC0).astype(BF)
    vec_ref[...] = lax.dot_general(pick, small_ref[:, :256], NT, preferred_element_type=F32)
    for chip in range(16):
        row = pl.multiple_of(64 * chip + 32 * core, 32)
        bf1_ref[:, 128 * chip : 128 * (chip + 1)] = small_ref[pl.ds(row, 16), 256:384][:1].astype(F32)
    fill_bias(bias_ref, vec_ref, 0)
    hot = (place_ref[...] == lax.broadcasted_iota(jnp.int32, (ROWS, 256), 1)).astype(BF)
    for j in range(2):
        at = slice(512 * j, 512 * (j + 1))
        a_ref[:, at] = tok_ref[:, at].astype(F32) + lax.dot_general(
            hot, small_ref[at, :256], NT, preferred_element_type=F32
        )
    gain, shift = vec_ref[0:1, :], vec_ref[1:2, :]

    def rows(i, carry):
        hat, mean, inverse = norm_rows(a_ref[tile(i, 64), :])
        n1_ref[tile(i, 64), :] = (hat * gain + shift).astype(BF)
        stat_ref[tile(i, 64), :] = stats(mean, inverse)
        return carry

    lax.fori_loop(0, ROWS // 64, rows, 0)
    outs = start_all([(a_ref, a_hbm), (n1_ref, n1_hbm)], out_sems)
    wait_all(two)
    outs += start_all([(wq_ref, wq_hbm)], out_sems, 2)

    def columns(j, carry):
        at = tile(j, 256)
        product = jnp.dot(n1_ref[...], wq_ref[:, at], preferred_element_type=F32)
        qkv_ref[:, at] = (product + bias_ref[0:1, at]).astype(BF)
        return carry

    lax.fori_loop(0, 3, columns, 0)
    wait_all(outs)


def first_stage(own, sib, place, gathered):
    return launch(
        first_kernel,
        [(own, ANY), (sib, ANY), (place, VMEM)] + [(g, ANY) for g in gathered],
        [
            ((ROWS, D), F32, ANY),
            ((ROWS, D), BF, ANY),
            ((D, HALF_QKV), BF, ANY),
            ((ROWS, HALF_QKV), BF),
            ((16, D), F32),
            ((1, HALF_FF), F32),
            ((ROWS, 128), F32),
        ],
        [
            pltpu.VMEM((ROWS, D), BF),
            pltpu.VMEM((ROWS, D), F32),
            pltpu.VMEM((ROWS, D), BF),
            pltpu.VMEM((D, HALF_QKV), BF),
            pltpu.VMEM((D, SMALL), BF),
            pltpu.VMEM((8, HALF_QKV), F32),
            dma(2 * len(ENTRIES_ZXY) + 4),
            dma(3),
        ],
        flops=1.2e9,
    )


def second_kernel(n1_hbm, vec_ref, *refs):
    parts, refs = refs[:5], refs[5:]
    wq_hbm, qkv_ref, left_ref, right_ref, n1_ref, wq_ref, bias_ref, sems, out_sem = refs
    count = len(ENTRIES_ZXY)
    one = start_all(
        [(n1_hbm, n1_ref)]
        + [
            (piece_of(parts, e, 32, (0, HALF_QKV)), wq_ref.at[pl.ds(core_rows(e), 32), :])
            for e in ENTRIES_ZXY
        ],
        sems,
    )
    two = start_all(
        [
            (
                piece_of(parts, e, 32, (HALF_QKV, HALF_D)),
                (left_ref, right_ref)[e[4]].at[chip_of(e[3])],
            )
            for e in ENTRIES_ZXY
        ],
        sems,
        count + 1,
    )
    fill_bias(bias_ref, vec_ref, 1)
    wait_all(one)
    outs = start_all([(wq_ref, wq_hbm)], out_sem)

    def columns(j, carry):
        at = tile(j, 256)
        product = jnp.dot(n1_ref[...], wq_ref[:, at], preferred_element_type=F32)
        qkv_ref[:, at] = (product + bias_ref[0:1, at]).astype(BF)
        return carry

    lax.fori_loop(0, 3, columns, 0)
    wait_all(two + outs)


def second_stage(n1, vec, gathered):
    return launch(
        second_kernel,
        [(n1, ANY), (vec, VMEM)] + [(g, ANY) for g in gathered],
        [((D, HALF_QKV), BF, ANY), ((ROWS, HALF_QKV), BF)] + [((16, 32, HALF_D), BF)] * 2,
        [
            pltpu.VMEM((ROWS, D), BF),
            pltpu.VMEM((D, HALF_QKV), BF),
            pltpu.VMEM((8, HALF_QKV), F32),
            dma(2 * len(ENTRIES_ZXY) + 1),
            dma(1),
        ],
        flops=1.2e9,
    )


def pack_rows(ref, pack):
    main = ref[LIVE * pack : LIVE * (pack + 1), :]
    return jnp.concatenate([main, ref[BACK + REST * pack : BACK + REST * (pack + 1), :]])


def attend_kernel(q_ref, k_ref, v_ref, col_ref, row_ref, o_ref, lse_ref):
    first = lax.broadcasted_iota(jnp.int32, (PACK, 128), 1) < HEAD
    for pack in range(2):
        q, k, v = (pack_rows(r, pack) for r in (q_ref, k_ref, v_ref))
        same = pack_rows(col_ref, pack) == row_ref[pack : pack + 1, :]
        outs, logs = [], []
        for h in range(2):
            mine = first if h == 0 else ~first
            scores = lax.dot_general(
                jnp.where(mine, q * HEAD ** (-0.5), 0), k, NT, preferred_element_type=F32
            )
            scores = jnp.where(same, scores, -1000000000.0)
            top = jnp.max(scores, axis=1, keepdims=True)
            powers = jnp.exp(scores - top)
            total = jnp.sum(powers, axis=1, keepdims=True)
            mixed = jnp.dot(powers.astype(BF), v, preferred_element_type=F32)
            outs.append(mixed * (1.0 / total))
            logs.append(top + jnp.log(total))
        o = jnp.where(first, outs[0], outs[1]).astype(BF)
        lse = jnp.where(first, logs[0], logs[1])
        o_ref[LIVE * pack : LIVE * (pack + 1), :] = o[:LIVE]
        o_ref[BACK + REST * pack : BACK + REST * (pack + 1), :] = o[LIVE:]
        lse_ref[LIVE * pack : LIVE * (pack + 1), :] = lse[:LIVE]


def attend(qkv, col, row):
    part = lambda off: pl.BlockSpec((ROWS, 128), lambda j: (0, j + off))
    return pl.pallas_call(
        attend_kernel,
        grid=(2,),
        in_specs=[
            part(0),
            part(2),
            part(4),
            pl.BlockSpec((ROWS, 1), lambda j: (0, 0)),
            pl.BlockSpec((2, PACK), lambda j: (0, 0)),
        ],
        out_specs=[part(0), pl.BlockSpec((BACK, 128), lambda j: (0, j))],
        out_shape=[
            jax.ShapeDtypeStruct((ROWS, 256), BF),
            jax.ShapeDtypeStruct((BACK, 256), F32),
        ],
        cost_estimate=pl.CostEstimate(flops=int(8e8), bytes_accessed=4000000, transcendentals=0),
        compiler_params=pltpu.CompilerParams(vmem_limit_bytes=32 << 20),
    )(qkv, qkv, qkv, col, row)


def attend_back(q_ref, g_ref, o_ref, lse_ref, col_ref, row_ref, out_ref):
    first = lax.broadcasted_iota(jnp.int32, (LIVE, 128), 1) < HEAD
    scale = HEAD ** (-0.5)

    def pair(i, carry):
        pack, j = i // 2, i % 2
        at = pl.ds(pl.multiple_of(LIVE * pack, LIVE), LIVE)
        lanes = lambda which: pl.ds(pl.multiple_of(256 * which + 128 * j, 128), 128)
        q, k, v = (q_ref[at, lanes(which)] for which in range(3))
        g = g_ref[at, lanes(0)]
        weighted = g.astype(F32) * o_ref[at, lanes(0)].astype(F32)
        logs = lse_ref[at, lanes(0)]
        same = col_ref[at, :] == row_ref[pl.ds(pack, 1), :LIVE]
        dq, dk, dv = [], [], []
        for h in range(2):
            mine = first if h == 0 else ~first
            lse = logs[:, HEAD * h : HEAD * h + 1]
            inner = jnp.sum(jnp.where(mine, weighted, 0.0), axis=1, keepdims=True)
            qs = jnp.where(mine, q * scale, 0)
            scores = lax.dot_general(qs, k, NT, preferred_element_type=F32)
            probs = jnp.where(same, jnp.exp(scores - lse), 0.0)
            dprobs = lax.dot_general(jnp.where(mine, g, 0), v, NT, preferred_element_type=F32)
            ds = (probs * (dprobs - inner)).astype(BF)
            dv.append(lax.dot_general(probs.astype(BF), g, TN, preferred_element_type=F32))
            dq.append(jnp.dot(ds, k, preferred_element_type=F32))
            dk.append(lax.dot_general(ds, q, TN, preferred_element_type=F32))
        out_ref[at, lanes(0)] = (jnp.where(first, dq[0], dq[1]) * scale).astype(BF)
        out_ref[at, lanes(1)] = (jnp.where(first, dk[0], dk[1]) * scale).astype(BF)
        out_ref[at, lanes(2)] = jnp.where(first, dv[0], dv[1]).astype(BF)
        return carry

    lax.fori_loop(0, 4, pair, 0)


def head_rows(k, core):
    return (k // 2) * 4 + 2 * core + k % 2


def project_kernel(o0_ref, o1_ref, a_hbm, vec_ref, own0, own1, other0, other1, *refs):
    wo_ref, sum_ref, send0_ref, send1_ref, a_ref, sems = refs
    core = coords()[3]
    copies = []
    for k in range(8):
        head = head_rows(k, core)
        for parts, row in (((own0, own1), 32 * core), ((other0, other1), 32 - 32 * core)):
            at = pl.ds(pl.multiple_of(64 * k + row, 32), 32)
            for half, part in enumerate(parts):
                copies.append((part.at[head], wo_ref.at[at, pl.ds(HALF_D * half, HALF_D)]))
    started = start_all(copies + [(a_hbm, a_ref)], sems)
    wait_all(started)
    for j in range(2):
        at = slice(512 * j, 512 * (j + 1))
        part = jnp.dot(o0_ref[...], wo_ref[:256, at], preferred_element_type=F32) + jnp.dot(
            o1_ref[...], wo_ref[256:, at], preferred_element_type=F32
        )
        (send0_ref, send1_ref)[j][...] = part.astype(BF)
        sum_ref[:, at] = a_ref[:, at] + part + vec_ref[4:5, at]


def project(o, a, vec, own, other):
    return launch(
        project_kernel,
        [(o[0], VMEM), (o[1], VMEM), (a, ANY), (vec, VMEM)] + [(v, ANY) for v in (*own, *other)],
        [((HALF_D, D), BF), ((ROWS, D), F32), ((ROWS, HALF_D), BF), ((ROWS, HALF_D), BF)],
        [pltpu.VMEM((ROWS, D), F32), dma(33)],
        flops=0.8e9,
    )


SWAPPED = ((0, LIVE, LIVE), (LIVE, 0, LIVE), (BACK, BACK + REST, REST), (BACK + REST, BACK, REST))


def widen_kernel(sum_hbm, got0_hbm, got1_hbm, vec_ref, bf1_ref, own_hbm, sib_hbm, col_ref, *refs):
    parts, refs = refs[:5], refs[5:]
    n2_hbm, act_hbm, slope_hbm, stat_ref = refs[:4]
    outs, refs = refs[4:7], refs[7:]
    a2_ref, got_ref, n2_ref, wu_ref, act_ref, slope_ref, dy_ref, whole_ref, h0, h1 = refs[:10]
    sems, out_sems, grad_sems = refs[10:]
    first = start_all(
        [(sum_hbm, a2_ref)]
        + [
            (src.at[pl.ds(start, size), :], got_ref.at[pl.ds(to, size), pl.ds(HALF_D * i, HALF_D)])
            for i, src in enumerate((got0_hbm, got1_hbm))
            for to, start, size in SWAPPED
        ],
        sems,
    )
    grads = start_all(
        [
            (src.at[pl.ds(0, LIVE), :], dy_ref.at[pl.ds(LIVE * i, LIVE), :])
            for i, src in enumerate((own_hbm, sib_hbm))
        ],
        sems,
        9,
    )
    weights = start_all(
        [(piece_of(parts, e, 32), wu_ref.at[pl.ds(core_rows(e), 32), :]) for e in ENTRIES_ZXY],
        sems,
        11,
    )
    gain, shift = vec_ref[5:6, :], vec_ref[6:7, :]
    wait_all(first)

    def rows(i, carry):
        at = tile(i, 64)
        a2 = a2_ref[at, :] + got_ref[at, :].astype(F32)
        hat, mean, inverse = norm_rows(a2)
        n2_ref[at, :] = (hat * gain + shift).astype(BF)
        stat_ref[at, :] = stats(mean, inverse)
        return carry

    lax.fori_loop(0, ROWS // 64, rows, 0)
    wait_all(weights)
    sent = start_all([(n2_ref.at[pl.ds(0, BACK), :], n2_hbm)], out_sems)
    steps = HALF_FF // 512
    hidden = (h0, h1)

    def product(j):
        hidden[j % 2][...] = jnp.dot(
            n2_ref[...], wu_ref[:, 512 * j : 512 * (j + 1)], preferred_element_type=F32
        )

    product(0)
    for j in range(steps):
        if j + 1 < steps:
            product(j + 1)
        at = slice(512 * j, 512 * (j + 1))
        h = hidden[j % 2][...] + bf1_ref[:, at]
        area, bell = gelu_parts(h)
        act_ref[j] = (h * area).astype(BF)
        slope_ref[j] = (
            area[:BACK] + h[:BACK] * bell[:BACK] * 0.3989422804014327
        ).astype(BF)
        sent += start_all(
            [(act_ref.at[j], act_hbm.at[j]), (slope_ref.at[j], slope_hbm.at[j])],
            out_sems,
            1 + 2 * j,
        )
    wait_all(grads)
    dy_ref[...] = jnp.where(col_ref[:BACK, :] >= 0, dy_ref[...], 0)

    for k, dz in enumerate(ZORDER):
        at = tile(z_of(dz), 512)
        part = lax.dot_general(
            act_ref[z_of(dz), :BACK, :], dy_ref[...], TN, preferred_element_type=F32
        )
        whole_ref[at, :] = part.astype(BF)
        mine = [e for e in ENTRIES_XZY_SCATTER if e[3][0] == dz]
        sent += start_all(
            [(whole_ref.at[pl.ds(half_rows(e), 64), :], piece_of(outs, e, 64)) for e in mine],
            grad_sems,
            len(mine) * k,
        )
    wait_all(sent)


def widen(total, got, vec, bf1, own, sib, col, gathered):
    return launch(
        widen_kernel,
        [(total, ANY), (got[0], ANY), (got[1], ANY), (vec, VMEM), (bf1, VMEM), (own, ANY), (sib, ANY), (col, VMEM)]
        + [(g, ANY) for g in gathered],
        [
            ((BACK, D), BF, ANY),
            ((4, ROWS, 512), BF, ANY),
            ((4, BACK, 512), BF, ANY),
            ((ROWS, 128), F32),
        ]
        + [(s, BF, ANY) for s in scatter_shapes("xzy", 64, D)],
        [
            pltpu.VMEM((ROWS, D), F32),
            pltpu.VMEM((ROWS, D), BF),
            pltpu.VMEM((ROWS, D), BF),
            pltpu.VMEM((D, HALF_FF), BF),
            pltpu.VMEM((4, ROWS, 512), BF),
            pltpu.VMEM((4, BACK, 512), BF),
            pltpu.VMEM((BACK, D), BF),
            pltpu.VMEM((HALF_FF, D), BF),
            pltpu.VMEM((ROWS, 512), F32),
            pltpu.VMEM((ROWS, 512), F32),
            dma(11 + len(ENTRIES_ZXY)),
            dma(1 + 2 * (HALF_FF // 512)),
            dma(len(ENTRIES_XZY_SCATTER)),
        ],
        flops=5.8e9,
    )


def hidden_grad_kernel(own_hbm, sib_hbm, col_ref, slope_hbm, n2_hbm, *refs):
    ups, parts, refs = refs[:5], refs[5:9], refs[9:]
    sum_ref, part_hbm, sends, outs, refs = refs[0], refs[1], refs[2:5], refs[5:10], refs[10:]
    dy_ref, slope_ref, n2_ref, n2t_ref, wu_ref, wd_ref, dh_ref, whole_ref = refs[:8]
    part_ref, send_ref, sems, slope_sems, wd_sems, out_sems, last_sems = refs[8:]
    one = start_all(
        [(n2_hbm, n2_ref)]
        + [
            (src.at[pl.ds(0, LIVE), :], dy_ref.at[pl.ds(LIVE * i, LIVE), :])
            for i, src in enumerate((own_hbm, sib_hbm))
        ],
        sems,
    )

    def load(k):
        dz = ZORDER[k]
        mine = [e for e in ENTRIES_XZY_GATHER if e[3][0] == dz]
        return start_all(
            [(piece_of(parts, e, 64), wd_ref.at[pl.ds(half_rows(e), 64), :]) for e in mine],
            wd_sems,
            len(mine) * k,
        ) + start_all([(slope_hbm.at[z_of(dz)], slope_ref.at[z_of(dz)])], slope_sems, k)

    loads = [copy for k in range(4) for copy in load(k)]
    two = start_all(
        [(piece_of(ups, e, 32), wu_ref.at[pl.ds(core_rows(e), 32), :]) for e in ENTRIES_ZXY],
        sems,
        3,
    )
    wait_all(one)
    n2t_ref[...] = n2_ref[...].T
    dy_ref[...] = jnp.where(col_ref[:BACK, :] >= 0, dy_ref[...], 0)
    wait_all(loads)

    def block(j, carry):
        at = tile(j, 512)
        gate = lax.dot_general(dy_ref[...], wd_ref[at, :], NT, preferred_element_type=F32)
        dh = (gate * slope_ref[j].astype(F32)).astype(BF)
        dh_ref[:, at] = dh
        sum_ref[:, at] = jnp.sum(dh.astype(F32), axis=0, keepdims=True)
        whole_ref[:, at] = jnp.dot(
            n2t_ref[...], dh_ref[:, at], preferred_element_type=F32
        ).astype(BF)
        return carry

    lax.fori_loop(0, 4, block, 0)
    sent = start_all(
        [(whole_ref.at[pl.ds(core_rows(e), 32), :], piece_of(outs, e, 32)) for e in ENTRIES_ZXY],
        out_sems,
    )
    wait_all(two)

    def columns(j, carry):
        at = tile(j, 512)
        part = lax.dot_general(dh_ref[...], wu_ref[at, :], NT, preferred_element_type=F32)
        part_ref[:, at] = part
        send_ref[:, at] = part.astype(BF)
        return carry

    lax.fori_loop(0, 2, columns, 0)
    for j, (to, width) in enumerate(PIECES):
        sent += start_all([(send_ref.at[:, pl.ds(to, width)], sends[j])], last_sems, j)
    sent += start_all([(part_ref, part_hbm)], last_sems, 3)
    wait_all(sent)


def hidden_grads(own, sib, col, slope, n2, up_blocks, down_blocks):
    return launch(
        hidden_grad_kernel,
        [(own, ANY), (sib, ANY), (col, VMEM), (slope, ANY), (n2, ANY)]
        + [(g, ANY) for g in up_blocks + down_blocks],
        [
            ((1, HALF_FF), F32),
            ((BACK, D), F32, ANY),
        ]
        + [((BACK, width), BF, ANY) for _, width in PIECES]
        + [(s, BF, ANY) for s in scatter_shapes("zxy", 32, HALF_FF)],
        [
            pltpu.VMEM((BACK, D), BF),
            pltpu.VMEM((4, BACK, 512), BF),
            pltpu.VMEM((BACK, D), BF),
            pltpu.VMEM((D, BACK), BF),
            pltpu.VMEM((D, HALF_FF), BF),
            pltpu.VMEM((HALF_FF, D), BF),
            pltpu.VMEM((BACK, HALF_FF), BF),
            pltpu.VMEM((D, HALF_FF), BF),
            pltpu.VMEM((BACK, D), F32),
            pltpu.VMEM((BACK, D), BF),
            dma(3 + len(ENTRIES_ZXY)),
            dma(4),
            dma(len(ENTRIES_XZY_GATHER)),
            dma(len(ENTRIES_ZXY)),
            dma(4),
        ],
        flops=7.5e9,
    )


def middle_kernel(part_hbm, got0_hbm, got1_hbm, got2_hbm, sum_hbm, z0_hbm, z1_hbm, *refs):
    stat_ref, own_hbm, sib_hbm, col_ref, vec_ref, o0_ref, o1_ref, wo_hbm = refs[:8]
    da2_ref, do0_ref, do1_ref, sums_ref, mine_ref, send_ref = refs[8:14]
    part_ref, got_ref, a2_ref, z_ref, dy_ref, wo_ref, dz_ref, whole_ref, sems = refs[14:]
    core = coords()[3]
    one = start_all(
        [
            (part_hbm, part_ref),
            (sum_hbm.at[pl.ds(0, BACK), :], a2_ref),
            (own_hbm.at[pl.ds(0, LIVE), :], dy_ref.at[pl.ds(0, LIVE), :]),
            (sib_hbm.at[pl.ds(0, LIVE), :], dy_ref.at[pl.ds(LIVE, LIVE), :]),
        ]
        + [
            (src.at[pl.ds(start, LIVE), :], dst.at[pl.ds(LIVE - start, LIVE), pl.ds(off, width)])
            for dst, src, off, width in (
                (got_ref, got0_hbm, *PIECES[0]),
                (got_ref, got1_hbm, *PIECES[1]),
                (got_ref, got2_hbm, *PIECES[2]),
                (z_ref, z0_hbm, 0, HALF_D),
                (z_ref, z1_hbm, HALF_D, HALF_D),
            )
            for start in (0, LIVE)
        ]
        + [(wo_hbm, wo_ref)],
        sems,
    )
    gain = vec_ref[5:6, :]
    wait_all(one)

    def rows(i, sums):
        at = tile(i, 64)
        dn = part_ref[at, :] + got_ref[at, :].astype(F32)
        a2 = a2_ref[at, :] + z_ref[at, :].astype(F32)
        hat, inverse = normed(a2, stat_ref[at, :])
        dy = jnp.where(col_ref[at, :] >= 0, dy_ref[at, :].astype(F32), 0.0)
        da2 = dy + norm_back(dn, hat, inverse, gain)
        dz = da2.astype(BF)
        dz_ref[at, :] = dz
        if sums is None:
            return 0
        da2_ref[at, :] = da2
        return tuple(
            s + jnp.sum(v.reshape(8, 8, D), axis=0)
            for s, v in zip(sums, (dn * hat, dn, dz.astype(F32), dy))
        )

    steps = LIVE // 64
    sums = lax.fori_loop(0, steps, rows, (jnp.zeros((8, D), F32),) * 4)
    lax.fori_loop(steps, 2 * steps, lambda i, c: rows(i, None), 0)
    for i, s in enumerate(sums):
        sums_ref[i : i + 1, :] = jnp.sum(s, axis=0, keepdims=True)
    sums_ref[4:8, :] = jnp.zeros((4, D), F32)
    for half, (do_ref, o_ref) in enumerate(((do0_ref, o0_ref), (do1_ref, o1_ref))):
        at = slice(256 * half, 256 * (half + 1))
        do_ref[...] = lax.dot_general(
            dz_ref[...], wo_ref[at, :], NT, preferred_element_type=F32
        ).astype(BF)
        whole_ref[at, :] = lax.dot_general(
            o_ref[:BACK, :], dz_ref[...], TN, preferred_element_type=F32
        ).astype(BF)
    for k in range(8):
        mine_ref[k] = whole_ref[pl.ds(pl.multiple_of(64 * k + 32 * core, 32), 32), :]
        send_ref[k] = whole_ref[pl.ds(pl.multiple_of(64 * k + 32 - 32 * core, 32), 32), :]


def middle(part, got, total, z, stat, own, sib, col, vec, o, wo):
    ins = [(v, ANY) for v in (part, *got, total, *z)]
    ins += [(stat, VMEM), (own, ANY), (sib, ANY), (col, VMEM), (vec, VMEM)]
    ins += [(o[0], VMEM), (o[1], VMEM), (wo, ANY)]
    return launch(
        middle_kernel,
        ins,
        [
            ((LIVE, D), F32),
            ((BACK, 256), BF),
            ((BACK, 256), BF),
            ((8, D), F32),
            ((8, 32, D), BF),
            ((8, 32, D), BF),
        ],
        [
            pltpu.VMEM((BACK, D), F32),
            pltpu.VMEM((BACK, D), BF),
            pltpu.VMEM((BACK, D), F32),
            pltpu.VMEM((BACK, D), BF),
            pltpu.VMEM((BACK, D), BF),
            pltpu.VMEM((HALF_D, D), BF),
            pltpu.VMEM((BACK, D), BF),
            pltpu.VMEM((HALF_D, D), BF),
            dma(15),
        ],
        flops=1.4e9,
    )


def back_one_kernel(q_ref, g_ref, o_ref, lse_ref, col_ref, row_ref, n1_hbm, *refs):
    mine_ref, theirs_ref, out_ref, n1t_hbm = refs[:4]
    outs, refs = refs[4:9], refs[9:]
    n1_ref, n1t_ref, whole_ref, sems, sent_sem = refs
    count = len(ENTRIES_ZXY)
    load = start_all([(n1_hbm.at[pl.ds(0, BACK), :], n1_ref)], sent_sem)
    two = []
    for i, e in enumerate(ENTRIES_ZXY):
        rel, half = e[3], e[4]
        _, y, _, core = coords()
        chip = chip_of(rel)
        slot = (chip // 4) * 2 + chip % 2
        at = pl.ds(HALF_D * half, HALF_D)
        dst = piece_of(outs, e, 32, (HALF_QKV, HALF_D))
        here = (y if rel[1] == 0 else 1 - y) == core
        sem = sems.at[count + i]
        two.append(pltpu.make_async_copy(mine_ref.at[slot, :, at], dst, sem))

        @pl.when(here)
        def _():
            pltpu.make_async_copy(mine_ref.at[slot, :, at], dst, sem).start()

        @pl.when(jnp.logical_not(here))
        def _():
            pltpu.make_async_copy(theirs_ref.at[slot, :, at], dst, sem).start()

    attend_back(q_ref, g_ref, o_ref, lse_ref, col_ref, row_ref, out_ref)
    wait_all(load)
    n1t_ref[...] = n1_ref[...].T
    load = start_all([(n1t_ref, n1t_hbm)], sent_sem)
    whole_ref[...] = jnp.dot(n1t_ref[...], out_ref[...], preferred_element_type=F32).astype(BF)
    one = start_all(
        [
            (whole_ref.at[pl.ds(core_rows(e), 32), :], piece_of(outs, e, 32, (0, HALF_QKV)))
            for e in ENTRIES_ZXY
        ],
        sems,
    )
    wait_all(one + two + load)


def back_one(qkv, do, o, lse, col, row, n1, mine, theirs):
    return launch(
        back_one_kernel,
        [(v, VMEM) for v in (qkv, do, o, lse, col, row)]
        + [(n1, ANY), (mine, VMEM), (theirs, VMEM)],
        [((BACK, HALF_QKV), BF), ((D, BACK), BF, ANY)]
        + [(s, BF, ANY) for s in scatter_shapes("zxy", 32, HALF_QKV + HALF_D)],
        [
            pltpu.VMEM((BACK, D), BF),
            pltpu.VMEM((D, BACK), BF),
            pltpu.VMEM((D, HALF_QKV), BF),
            dma(2 * len(ENTRIES_ZXY)),
            dma(1),
        ],
        flops=2.5e9,
    )


def back_two_kernel(q_ref, g_ref, o_ref, lse_ref, col_ref, row_ref, one_ref, *refs):
    w0_hbm, w1_hbm, out_ref, own_ref, send_ref, w0_ref, w1_ref, sems = refs
    load = start_all([(w0_hbm, w0_ref), (w1_hbm, w1_ref)], sems)
    attend_back(q_ref, g_ref, o_ref, lse_ref, col_ref, row_ref, out_ref)
    wait_all(load)
    for j in range(2):
        at = slice(512 * j, 512 * (j + 1))
        total = lax.dot_general(
            one_ref[...], w0_ref[at, :], NT, preferred_element_type=F32
        ) + lax.dot_general(out_ref[...], w1_ref[at, :], NT, preferred_element_type=F32)
        own_ref[:, at] = total[:LIVE]
        send_ref[:, at] = total[LIVE:].astype(BF)


def back_two(qkv, do, o, lse, col, row, one, w0, w1):
    return launch(
        back_two_kernel,
        [(v, VMEM) for v in (qkv, do, o, lse, col, row, one)] + [(w0, ANY), (w1, ANY)],
        [((BACK, HALF_QKV), BF), ((LIVE, D), F32), ((LIVE, D), BF)],
        [pltpu.VMEM((D, HALF_QKV), BF), pltpu.VMEM((D, HALF_QKV), BF), dma(2)],
        flops=3.2e9,
    )


def last_kernel(n1t_hbm, one_ref, two_ref, dn_ref, got_ref, a_hbm, stat_ref, *refs):
    da2_ref, vec_ref, place_ref, sums_ref, upsum_ref, tok_ref = refs[:6]
    outs, refs = refs[6:11], refs[11:]
    n1t_ref, a_ref, whole_ref, small_ref, da_ref, rows_ref, sems, in_sems = refs
    core = coords()[3]
    count = len(ENTRIES_ZXY)
    load = start_all([(n1t_hbm, n1t_ref), (a_hbm.at[pl.ds(0, LIVE), :], a_ref)], in_sems)
    wait_all(load)

    def columns(j, carry):
        at = tile(j, 256)
        part = jnp.dot(n1t_ref[...], two_ref[:, at], preferred_element_type=F32)
        whole_ref[:, at] = part.astype(BF)
        return carry

    lax.fori_loop(0, 3, columns, 0)
    one = start_all(
        [
            (whole_ref.at[pl.ds(core_rows(e), 32), :], piece_of(outs, e, 32, (SMALL, HALF_QKV)))
            for e in ENTRIES_ZXY
        ],
        sems,
    )
    gain = vec_ref[0:1, :]

    def rows(i, sums):
        at = tile(i, 64)
        dn = dn_ref[at, :] + got_ref[at, :].astype(F32)
        hat, inverse = normed(a_ref[at, :], stat_ref[at, :])
        da = da2_ref[at, :] + norm_back(dn, hat, inverse, gain)
        da_ref[at, :] = da.astype(BF)
        tok_ref[at, :] = da.astype(BF)
        return tuple(
            s + jnp.sum(v.reshape(8, 8, D), axis=0) for s, v in zip(sums, (dn * hat, dn))
        )

    sums = lax.fori_loop(0, LIVE // 64, rows, (jnp.zeros((8, D), F32),) * 2)
    tok_ref[LIVE:, :] = jnp.zeros((REST, D), BF)
    lane = lax.broadcasted_iota(jnp.int32, (LIVE, 256), 1)
    hot = (place_ref[:LIVE, :] == lane).astype(BF)
    small = lax.dot_general(da_ref[...], hot, TN, preferred_element_type=F32)
    rows_ref[...] = jnp.zeros((16, D), F32)
    rows_ref[0:1, :] = jnp.sum(sums[0], axis=0, keepdims=True)
    rows_ref[1:2, :] = jnp.sum(sums[1], axis=0, keepdims=True)
    for half, src in enumerate((one_ref, two_ref)):
        total = jnp.sum(src[...].astype(F32), axis=0, keepdims=True)
        for j in range(2):
            own = pl.ds(pl.multiple_of(256 * (2 * half + j) + 128 * core, 128), 128)
            rows_ref[2:3, own] = total[:, 128 * j : 128 * (j + 1)]
            rows_ref[3:4, own] = total[:, 512 + 128 * j : 512 + 128 * (j + 1)]
    rows_ref[4:5, :] = sums_ref[2:3, :]
    rows_ref[5:6, :] = sums_ref[0:1, :]
    rows_ref[6:7, :] = sums_ref[1:2, :]
    rows_ref[7:8, :] = sums_ref[3:4, :]
    spot = lax.broadcasted_iota(jnp.int32, (16, 256), 0)
    place = (lax.broadcasted_iota(jnp.int32, (16, 256), 1) == spot + VEC0).astype(BF)
    value = rows_ref[...]
    for _ in range(2):
        piece = value.astype(BF)
        small = small + lax.dot_general(piece, place, TN, preferred_element_type=F32)
        value = value - piece.astype(F32)
    small_ref[:, :256] = small.astype(BF)
    small_ref[:, 256:] = jnp.zeros((D, SMALL - 256), BF)
    top = lax.broadcasted_iota(jnp.int32, (16, 128), 0) == 0
    for chip in range(16):
        row = pl.multiple_of(64 * chip + 32 * core, 32)
        bias = jnp.where(top, upsum_ref[:, 128 * chip : 128 * (chip + 1)], 0.0)
        small_ref[pl.ds(row, 16), 256:384] = bias.astype(BF)
    three = start_all(
        [
            (small_ref.at[pl.ds(core_rows(e), 32), :], piece_of(outs, e, 32, (0, SMALL)))
            for e in ENTRIES_ZXY
        ],
        sems,
        count,
    )
    wait_all(one + three)


def last_stage(n1t, one, two, dn, got, a, stat, da2, vec, place, sums, upsum):
    return launch(
        last_kernel,
        [(n1t, ANY)]
        + [(v, VMEM) for v in (one, two, dn, got)]
        + [(a, ANY)]
        + [(v, VMEM) for v in (stat, da2, vec, place, sums, upsum)],
        [((PACK, D), BF)] + [(s, BF, ANY) for s in scatter_shapes("zxy", 32, CUT)],
        [
            pltpu.VMEM((D, BACK), BF),
            pltpu.VMEM((LIVE, D), F32),
            pltpu.VMEM((D, HALF_QKV), BF),
            pltpu.VMEM((D, SMALL), BF),
            pltpu.VMEM((LIVE, D), BF),
            pltpu.VMEM((16, D), F32),
            dma(2 * len(ENTRIES_ZXY)),
            dma(2),
        ],
        flops=1.2e9,
    )


def output_kernel(act_hbm, sum_hbm, z0_hbm, z1_hbm, vec_ref, *refs):
    parts, (own_ref, send_ref) = refs[:4], refs[4:6]
    act_ref, a2_ref, z_ref, wd_ref, sems = refs[6:]
    copies = [
        (piece_of(parts, e, 64), wd_ref.at[pl.ds(half_rows(e), 64), :]) for e in ENTRIES_XZY_GATHER
    ]
    copies += [(act_hbm, act_ref)]
    for which, start, size, to in SEGMENTS:
        if which == 0:
            at = pl.ds(start, size)
            copies.append((sum_hbm.at[pl.ds(to, size), :], a2_ref.at[at, :]))
            src = pl.ds(to + size, size)
            copies.append((z0_hbm.at[src, :], z_ref.at[at, pl.ds(0, HALF_D)]))
            copies.append((z1_hbm.at[src, :], z_ref.at[at, pl.ds(HALF_D, HALF_D)]))
    wait_all(start_all(copies, sems))
    for j in range(2):
        at = slice(512 * j, 512 * (j + 1))
        part = jnp.dot(act_ref[0], wd_ref[:512, at], preferred_element_type=F32)
        for k in range(1, 4):
            part += jnp.dot(
                act_ref[k], wd_ref[512 * k : 512 * (k + 1), at], preferred_element_type=F32
            )
        a2 = a2_ref[:, at] + z_ref[:, at].astype(F32) + vec_ref[7:8, at]
        for which, start, size, to in SEGMENTS:
            if which == 0:
                own_ref[start : start + size, at] = part[to : to + size] + a2[start : start + size]
            else:
                send_ref[start : start + size, at] = part[to : to + size].astype(BF)


def output_stage(act, total, z, vec, gathered):
    return launch(
        output_kernel,
        [(act, ANY), (total, ANY), (z[0], ANY), (z[1], ANY), (vec, VMEM)]
        + [(g, ANY) for g in gathered],
        [((PACK, D), F32), ((PACK, D), BF)],
        [
            pltpu.VMEM((4, ROWS, 512), BF),
            pltpu.VMEM((PACK, D), F32),
            pltpu.VMEM((PACK, D), BF),
            pltpu.VMEM((HALF_FF, D), BF),
            dma(len(ENTRIES_XZY_GATHER) + 7),
        ],
        flops=3.2e9,
    )


def merge_kernel(x_hbm, y_hbm, a_hbm, b_hbm, x_out, y_out, *scratch):
    x_ref, y_ref, a_ref, b_ref, sems, out_sems = scratch
    upper, lower = pl.ds(2, 2), pl.ds(0, 2)
    wait_all(
        start_all(
            [
                (x_hbm.at[upper], x_ref),
                (b_hbm, b_ref),
                (y_hbm.at[lower], y_ref),
                (a_hbm, a_ref),
            ],
            sems,
        )
    )
    x_ref[...] = (x_ref[...].astype(F32) + b_ref[...].astype(F32)).astype(BF)
    y_ref[...] = (y_ref[...].astype(F32) + a_ref[...].astype(F32)).astype(BF)
    wait_all(start_all([(x_ref, x_out.at[upper]), (y_ref, y_out.at[lower])], out_sems))


def to_neighbours(parts, got_a, got_b):
    whole = parts[1].shape
    half = pltpu.VMEM((2,) + whole[1:], BF)
    return pl.pallas_call(
        merge_kernel,
        out_shape=[jax.ShapeDtypeStruct(whole, BF)] * 2,
        in_specs=[ANY] * 4,
        out_specs=[ANY] * 2,
        scratch_shapes=[half] * 4 + [dma(4), dma(2)],
        input_output_aliases={0: 0, 1: 1},
        cost_estimate=pl.CostEstimate(flops=0, bytes_accessed=3000000, transcendentals=0),
        compiler_params=pltpu.CompilerParams(vmem_limit_bytes=8 << 20),
    )(parts[1], parts[2], got_a, got_b)


def split_kernel(count, *refs):
    values, (keep_ref, send_ref) = refs[:count], refs[count:]
    total = values[0][0].astype(F32)
    if count == 3 and total.ndim == 2:
        total = total + values[1][0].astype(F32) + values[2][0].astype(F32)
    else:
        total = total + jnp.concatenate([v[0].astype(F32) for v in values[1:]])

    @pl.when(pl.program_id(0) < 2)
    def _():
        keep_ref[0] = total

    @pl.when(pl.program_id(0) >= 2)
    def _():
        send_ref[0] = total.astype(BF)


def split_sum(*values):
    block = values[0].shape[1:]
    spec = lambda shape, at: pl.BlockSpec(
        (1,) + shape, lambda k: (at(k),) + (0,) * len(shape)
    )
    return pl.pallas_call(
        functools.partial(split_kernel, len(values)),
        grid=(4,),
        in_specs=[spec(v.shape[1:], lambda k: k) for v in values],
        out_specs=[
            spec(block, lambda k: jnp.minimum(k, 1)),
            spec(block, lambda k: jnp.maximum(k - 2, 0)),
        ],
        out_shape=[
            jax.ShapeDtypeStruct((2,) + block, F32),
            jax.ShapeDtypeStruct((2,) + block, BF),
        ],
        cost_estimate=pl.CostEstimate(flops=0, bytes_accessed=6000000, transcendentals=0),
        compiler_params=pltpu.CompilerParams(vmem_limit_bytes=16 << 20),
    )(*values)


def finish_kernel(a_ref, b_ref, up_ref, a_got, b_got, up_got, small_ref, qkv_ref, grad_ref, out_ref):
    core = coords()[3]
    small_ref[...] = b_ref[:32, :SMALL] + b_got[:, :SMALL]
    for j in range(12):
        at = slot_of(j)
        mine = pl.ds(pl.multiple_of(256 * j + 128 * core, 128), 128)
        other = pl.ds(pl.multiple_of(256 * j + 128 - 128 * core, 128), 128)
        own, got = (a_ref, a_got) if at < HALF_QKV else (b_ref, b_got)
        at = slice(at, at + 128) if at < HALF_QKV else slice(at + SMALL - HALF_QKV, at + SMALL - HALF_QKV + 128)
        qkv_ref[:, mine] = own[:32, at]
        qkv_ref[:, other] = got[:, at]
    for j in range(16):
        at = slice(128 * j, 128 * (j + 1))
        mine = pl.ds(pl.multiple_of(256 * j + 128 * core, 128), 128)
        other = pl.ds(pl.multiple_of(256 * j + 128 - 128 * core, 128), 128)
        grad_ref[:, mine] = up_ref[:32, at]
        grad_ref[:, other] = up_got[:, at]
    out_ref[:, :HALF_D] = a_ref[:32, HALF_QKV:]
    out_ref[:, HALF_D:] = a_ref[32:, HALF_QKV:]


def finish(a_sum, b_sum, up_sum, a_got, b_got, up_got):
    return launch(
        finish_kernel,
        [(v, VMEM) for v in (a_sum, b_sum, up_sum, a_got, b_got, up_got)],
        [((32, SMALL), F32), ((32, 3 * D), F32), ((32, FF), F32), ((32, D), F32)],
        limit=8,
    )


def in_order(own, sib):
    return jnp.concatenate([own[:LIVE], sib[:LIVE], own[LIVE:], sib[LIVE:]])


def fast_on_device(
    tokens,
    grad_out,
    image_lengths,
    image_device,
    small_map,
    ln1_gain,
    ln1_bias,
    qkv_weight,
    q_bias,
    v_bias,
    out_weight,
    out_bias,
    ln2_gain,
    ln2_bias,
    up_weight,
    up_bias,
    down_weight,
    down_bias,
    pos_table,
):
    device = lax.axis_index("dp") * 4 + lax.axis_index("fsdp")
    seg, place = layout(image_lengths, image_device, small_map, device, PACK)
    seg2, place2 = layout(image_lengths, image_device, small_map, device ^ 1, PACK)
    col = in_order(seg, seg2)[:, None]
    row = jnp.stack([seg, seg2])
    place = in_order(place, place2)[:, None]

    vectors = [ln1_gain, ln1_bias, q_bias, v_bias, out_bias, ln2_gain, ln2_bias, down_bias]
    table = jnp.concatenate([pos_table, jnp.stack(vectors), jnp.zeros((103, 32), BF)])
    keep, send, out2 = prepare(table, up_bias[None, :], qkv_weight, up_weight, out_weight)
    got = swap(send, CORE)
    chunk_1 = jnp.concatenate([keep[:, :CUT], got[:, :CUT]])
    rest = slice(CUT, SMALL + QKV)
    chunk_2 = jnp.concatenate([jnp.concatenate([keep[:, rest], got[:, rest]]), out2], axis=1)
    chunk_u = jnp.concatenate([keep[:, SMALL + QKV :], got[:, SMALL + QKV :]])
    down_a, down_b = down_weight[:64], down_weight[64:]
    sib_tokens = swap(tokens, CORE)
    sib_grad = swap(grad_out, CORE)

    (far_1,) = send_all((chunk_1, FAR))
    pair_1 = jnp.stack([chunk_1, far_1])
    (near_1,) = send_all((pair_1, ZBIT))
    down_x, down_y = send_all((down_a, XBIT), (down_b, YBIT), wait=(far_1,))
    line_1 = jnp.concatenate([pair_1, near_1])
    x_1, y_1 = send_all((line_1, XBIT), (line_1, YBIT), wait=(down_x, down_y))
    (far_2,) = send_all((chunk_2, FAR), wait=(near_1, down_x, down_y))
    pair_2 = jnp.stack([chunk_2, far_2])
    (near_2,) = send_all((pair_2, ZBIT))
    line_2 = jnp.concatenate([pair_2, near_2])
    corner_1 = corners(x_1, y_1)
    gathered_1 = [line_1, x_1, y_1, *corner_1]
    x_2, y_2 = send_all((line_2, XBIT), (line_2, YBIT), wait=corner_1)
    (far_u,) = send_all((chunk_u, FAR), wait=(near_2, *corner_1))
    pair_u = jnp.stack([chunk_u, far_u])
    a, n1, wq0, qkv0, vec, bf1, stat1 = first_stage(tokens, sib_tokens, place, gathered_1)
    (near_u,) = send_all((pair_u, ZBIT), wait=(stat1,))
    line_u = jnp.concatenate([pair_u, near_u])
    corner_2 = corners(x_2, y_2, wait=(stat1,))
    gathered_2 = [line_2, x_2, y_2, *corner_2]
    o0, lse0 = attend(after(qkv0, x_2, y_2, sib_grad), col, row)
    x_u, y_u = send_all((line_u, XBIT), (line_u, YBIT), wait=(*corner_2, lse0))
    quad_d = jnp.stack([down_a, down_x, down_b, down_y])
    (far_d,) = send_all((quad_d, FAR), wait=(near_u,))
    wq1, qkv1, *out_own = second_stage(n1, vec, gathered_2)
    out_other = [swap(half, CORE) for half in out_own]
    o1, lse1 = attend(qkv1, col, row)
    o = (o0, o1)
    pair_d = jnp.stack([quad_d, after(far_d, lse1)])
    wo, total, *send = project(o, a, vec, out_own, out_other)
    z = [swap(part, CORE) for part in send]
    corner_u = corners(x_u, y_u, wait=(send[0],))
    gathered_u = [line_u, x_u, y_u, *corner_u]
    (near_d,) = send_all((pair_d, ZBIT), wait=(lse1,))
    pairs_d = (pair_d, near_d)
    side_a = jnp.concatenate([p[:, :2] for p in pairs_d])
    side_b = jnp.concatenate([p[:, 2:] for p in pairs_d])
    gathered_d = [*pairs_d, *send_all((side_a, YBIT), (side_b, XBIT), wait=corner_u)]
    n2, act, slope, stat2, *d_parts = widen(
        total, z, vec, bf1, grad_out, sib_grad, col, gathered_u
    )

    keep, side_a, side_b = d_parts
    side_a, side_b = send_all((side_a, YBIT), (side_b, XBIT), wait=gathered_d[2:])
    up_bias_sum, part, *u_parts = hidden_grads(
        grad_out, sib_grad, col, slope, n2, gathered_u, gathered_d
    )
    got = [swap(piece, CORE) for piece in u_parts[:3]]
    u_parts = u_parts[3:]
    d_keep, d_send = split_sum(keep, side_a, side_b)
    u_got = send_all(*corner_pairs(u_parts), wait=(side_a, side_b))
    (d_near,) = send_all((d_send, ZBIT))
    da2, do0, do1, sums, mine, theirs = middle(
        after(part, d_send), got, total, z, stat2, grad_out, sib_grad, col, vec, o, wo
    )
    theirs = swap(theirs, CORE)

    u_x, u_y = to_neighbours(u_parts, *(after(u, sums) for u in u_got))
    u_line = send_all((u_x, XBIT), (u_y, YBIT))
    d_one, n1t, *a_parts = back_one(
        qkv0, after(do0, u_x, u_y), o0, lse0, col, row, n1, mine, theirs
    )
    d_pair = add(d_keep, after(d_near, d_one))
    d_send = d_pair[1].astype(BF)
    (d_far,) = send_all((d_send, FAR))
    d_two, dn, send = back_two(
        qkv1, after(do1, d_send), o1, lse1, col, row, d_one, wq0, wq1
    )
    u_keep, u_send = split_sum(u_parts[0], *(after(u, send) for u in u_line))
    a_got = send_all(*corner_pairs(a_parts), wait=(*u_line, send))
    (u_near,) = send_all((u_send, ZBIT))
    tokens_grad, *b_parts = last_stage(
        n1t, d_one, d_two, dn, swap(send, CORE), a, stat1, da2, vec, place, sums, up_bias_sum
    )
    a_x, a_y = to_neighbours(a_parts, *(after(v, tokens_grad) for v in a_got))
    a_line = send_all((a_x, XBIT), (a_y, YBIT))
    u_pair = add(u_keep, after(u_near, tokens_grad))
    u_send = u_pair[1].astype(BF)
    (u_far,) = send_all((u_send, FAR))
    own, send = output_stage(
        after(act, a_x, a_y, u_send, tokens_grad), total, z, vec, gathered_d
    )
    layer_out = (own + swap(send, CORE).astype(F32)).astype(BF)

    b_got = send_all(*corner_pairs(b_parts))
    d_quad = add(d_pair[0], after(d_far, own))
    b_x, b_y = to_neighbours(b_parts, *(after(v, own) for v in b_got))
    a_keep, a_send = split_sum(a_parts[0], *a_line)
    b_line = send_all((b_x, XBIT), (b_y, YBIT), wait=a_line)
    d_x, d_y = send_all(
        (d_quad[1].astype(BF), XBIT), (d_quad[3].astype(BF), YBIT), wait=b_line
    )
    down_sum = jnp.concatenate([add(d_quad[0], d_x), add(d_quad[2], d_y)])
    (a_near,) = send_all((a_send, ZBIT))
    up_sum = add(u_pair[0], after(u_far, *b_line))
    a_pair = add(a_keep, a_near)
    (a_far,) = send_all((a_pair[1].astype(BF), FAR))
    b_keep, b_send = split_sum(b_parts[0], *b_line)
    (b_near,) = send_all((b_send, ZBIT))
    a_sum = add(a_pair[0], a_far)
    b_pair = add(b_keep, b_near)
    (b_far,) = send_all((b_pair[1].astype(BF), FAR))
    b_sum = add(b_pair[0], b_far)

    up_got = swap(up_sum[32:], CORE)
    a_got = swap(a_sum[32:, :HALF_QKV], CORE)
    b_got = swap(b_sum[32:], CORE)
    small, qkv_grad, up_grad, out_grad = finish(a_sum, b_sum, up_sum, a_got, b_got, up_got)
    gv = small[:, VEC0 : VEC0 + 8].T
    return (
        layer_out,
        tokens_grad,
        gv[0],
        gv[1],
        qkv_grad,
        gv[2],
        gv[3],
        out_grad,
        gv[4],
        gv[5],
        gv[6],
        up_grad,
        small[0, 256:],
        down_sum,
        gv[7],
        small[:, :LONG].T,
    )


def solution(mesh):
    in_specs = (
        P(("dp", "fsdp"), None),
        P(("dp", "fsdp"), None),
        P(),
        P(),
        P(),
        P(("dp", "fsdp")),
        P(("dp", "fsdp")),
        P(("dp", "fsdp"), None),
        P(("dp", "fsdp")),
        P(("dp", "fsdp")),
        P(("dp", "fsdp"), None),
        P(("dp", "fsdp")),
        P(("dp", "fsdp")),
        P(("dp", "fsdp")),
        P(("dp", "fsdp"), None),
        P(("dp", "fsdp")),
        P(("dp", "fsdp"), None),
        P(("dp", "fsdp")),
        P(None, ("dp", "fsdp")),
    )
    out_specs = (
        P(("dp", "fsdp"), None),
        P(("dp", "fsdp"), None),
        P(("dp", "fsdp")),
        P(("dp", "fsdp")),
        P(("dp", "fsdp"), None),
        P(("dp", "fsdp")),
        P(("dp", "fsdp")),
        P(("dp", "fsdp"), None),
        P(("dp", "fsdp")),
        P(("dp", "fsdp")),
        P(("dp", "fsdp")),
        P(("dp", "fsdp"), None),
        P(("dp", "fsdp")),
        P(("dp", "fsdp"), None),
        P(("dp", "fsdp")),
        P(None, ("dp", "fsdp")),
    )
    eight_by_four = mesh.shape["dp"] == 8 and mesh.shape["fsdp"] == 4
    return jax.shard_map(
        fast_on_device if eight_by_four else on_device, mesh=mesh, in_specs=in_specs, out_specs=out_specs, check_vma=False
    )
```

```python
import functools

import jax
import jax.numpy as jnp
import numpy as np
from jax import lax
from jax.experimental import pallas as pl
from jax.experimental.pallas import tpu as pltpu
from jax.sharding import PartitionSpec as P

D = 1024
HEADS = 16
HEAD = 64
FF = 4096
LONG = 145
SHORT = 50


EPS = 1e-06


def fetch(parts):
    whole = (
        lax.all_gather(parts[0], ("dp", "fsdp"), axis=1, tiled=True),
        lax.all_gather(parts[1], ("dp", "fsdp"), axis=0, tiled=True),
        lax.all_gather(parts[2], ("dp", "fsdp"), axis=0, tiled=True),
        lax.all_gather(parts[3], ("dp", "fsdp"), axis=0, tiled=True),
        lax.all_gather(parts[4], ("dp", "fsdp"), axis=0, tiled=True),
        lax.all_gather(parts[5], ("dp", "fsdp"), axis=0, tiled=True),
        lax.all_gather(parts[6], ("dp", "fsdp"), axis=1, tiled=True),
    )
    return whole


def reduce_grads(parts):
    owned = (
        lax.psum_scatter(parts[0], ("dp", "fsdp"), scatter_dimension=1, tiled=True),
        lax.psum_scatter(parts[1], ("dp", "fsdp"), scatter_dimension=0, tiled=True),
        lax.psum_scatter(parts[2], ("dp", "fsdp"), scatter_dimension=0, tiled=True),
        lax.psum_scatter(parts[3], ("dp", "fsdp"), scatter_dimension=0, tiled=True),
        lax.psum_scatter(parts[4], ("dp", "fsdp"), scatter_dimension=0, tiled=True),
        lax.psum_scatter(parts[5], ("dp", "fsdp"), scatter_dimension=0, tiled=True),
        lax.psum_scatter(parts[6], ("dp", "fsdp"), scatter_dimension=1, tiled=True),
    )
    return owned


def layout(image_lengths, image_device, small_map, device, rows_dev):
    mine = image_device == device
    lens = jnp.where(mine, image_lengths, 0)
    starts = jnp.cumsum(lens) - lens
    rows = jnp.arange(rows_dev, dtype=jnp.int32)
    inside = (
        mine[None, :]
        & (starts[None, :] <= rows[:, None])
        & (rows[:, None] < (starts + lens)[None, :])
    )
    number = jnp.arange(image_lengths.shape[0], dtype=jnp.int32)
    segment = jnp.sum(jnp.where(inside, number[None, :] + 1, 0), axis=1) - 1
    offset = rows - jnp.sum(jnp.where(inside, starts[None, :], 0), axis=1)
    length = jnp.sum(jnp.where(inside, lens[None, :], 0), axis=1)
    spots = jnp.arange(SHORT, dtype=jnp.int32)
    mapped = jnp.sum(jnp.where(offset[:, None] == spots[None, :], small_map[None, :], 0), axis=1)
    place = jnp.where(length == LONG, offset, jnp.where(length == SHORT, mapped, 0))
    return (segment, place)


def layer_norm_forward_pass(v, norm_gain, shift_bias):
    centred_rows = v - jnp.mean(v, axis=1, keepdims=True)
    inverse_deviation = lax.rsqrt(
        jnp.mean(centred_rows * centred_rows, axis=1, keepdims=True) + EPS
    )
    normalized_rows = centred_rows * inverse_deviation
    return (normalized_rows * norm_gain + shift_bias, normalized_rows, inverse_deviation)


def layer_norm_backward_pass(upstream_gradient, normalized_rows, inverse_deviation, norm_gain):
    normalized_gradient = upstream_gradient * norm_gain
    first_input = jnp.mean(normalized_gradient, axis=1, keepdims=True)
    second_input = jnp.mean(normalized_gradient * normalized_rows, axis=1, keepdims=True)
    return (
        inverse_deviation * (normalized_gradient - first_input - normalized_rows * second_input),
        jnp.sum(upstream_gradient * normalized_rows, axis=0),
        jnp.sum(upstream_gradient, axis=0),
    )


def split_heads(values, groups):
    return values.reshape(values.shape[0], groups, HEADS // groups, HEAD).transpose(1, 0, 2, 3)


def join_heads(values):
    return values.transpose(1, 0, 2, 3).reshape(values.shape[1], D)


def masked_scores(query, keys, same):
    scores = jnp.einsum("thd,shd->hts", query, keys, preferred_element_type=jnp.float32) * HEAD ** (
        -0.5
    )
    return jnp.where(same[None], scores, -1000000000.0)


def attend_forward(qkvb, same):
    groups = HEADS // 4
    query = split_heads(qkvb[:, :D], groups)
    keys = split_heads(qkvb[:, D : 2 * D], groups)
    values = split_heads(qkvb[:, 2 * D :], groups)

    def one_group(item):
        scores = masked_scores(item[0], item[1], same)
        top = jnp.max(scores, axis=2, keepdims=True)
        lse = top + jnp.log(jnp.sum(jnp.exp(scores - top), axis=2, keepdims=True))
        probs = jnp.exp(scores - lse).astype(jnp.bfloat16)
        attended = jnp.einsum("hts,shd->thd", probs, item[2], preferred_element_type=jnp.float32)
        return (attended, lse[:, :, 0])

    attended, lse = lax.map(one_group, (query, keys, values))
    return (join_heads(attended), lse)


def attend_backward(qkvb, dob, lse, same):
    groups = HEADS // 4
    query = split_heads(qkvb[:, :D], groups)
    keys = split_heads(qkvb[:, D : 2 * D], groups)
    values = split_heads(qkvb[:, 2 * D :], groups)
    douts = split_heads(dob, groups)

    def one_group(item):
        scores = masked_scores(item[0], item[1], same)
        probs = jnp.exp(scores - item[4][:, :, None])
        dvalue = jnp.einsum(
            "hts,thd->shd", probs.astype(jnp.bfloat16), item[3], preferred_element_type=jnp.float32
        )
        dprobs = jnp.einsum("thd,shd->hts", item[3], item[2], preferred_element_type=jnp.float32)
        inner = jnp.sum(probs * dprobs, axis=2, keepdims=True)
        dscore = (probs * (dprobs - inner)).astype(jnp.bfloat16)
        dquery = jnp.einsum(
            "hts,shd->thd", dscore, item[1], preferred_element_type=jnp.float32
        ) * HEAD ** (-0.5)
        dkey = jnp.einsum(
            "hts,thd->shd", dscore, item[0], preferred_element_type=jnp.float32
        ) * HEAD ** (-0.5)
        return (dquery, dkey, dvalue)

    dquery, dkey, dvalue = lax.map(one_group, (query, keys, values, douts, lse))
    return jnp.concatenate([join_heads(dquery), join_heads(dkey), join_heads(dvalue)], axis=1)


def gelu_slope(x):
    return (
        0.5 * (1.0 + jax.scipy.special.erf(x * 0.7071067811865476))
        + x * jnp.exp(-0.5 * x * x) * 0.3989422804014327
    )


def on_device(
    tokens,
    grad_out,
    image_lengths,
    image_device,
    small_map,
    ln1_gain,
    ln1_bias,
    qkv_weight,
    q_bias,
    v_bias,
    out_weight,
    out_bias,
    ln2_gain,
    ln2_bias,
    up_weight,
    up_bias,
    down_weight,
    down_bias,
    pos_table,
):
    rows_dev = tokens.shape[0]
    device = lax.axis_index("dp") * lax.axis_size("fsdp") + lax.axis_index("fsdp")
    segment, place = layout(image_lengths, image_device, small_map, device, rows_dev)
    same = segment[:, None] == segment[None, :]
    valid = (segment >= 0).astype(jnp.float32)[:, None]
    table_rows = jnp.arange(LONG, dtype=jnp.int32)
    picker = place[:, None] == table_rows[None, :]
    vectors = jnp.stack(
        [ln1_gain, ln1_bias, q_bias, v_bias, out_bias, ln2_gain, ln2_bias, down_bias]
    )
    shards = (vectors, qkv_weight, out_weight, up_weight, up_bias, down_weight, pos_table)
    whole = fetch(shards)
    vec = whole[0].astype(jnp.float32)
    first_gain, first_centred, bq, bv, bo, second_gain, second_centred, bf2 = (
        vec[0],
        vec[1],
        vec[2],
        vec[3],
        vec[4],
        vec[5],
        vec[6],
        vec[7],
    )
    bf1 = whole[4].astype(jnp.float32)
    activation_rows = tokens.astype(jnp.float32) + jnp.dot(
        picker.astype(jnp.bfloat16), whole[6], preferred_element_type=jnp.float32
    )
    first_normed, first_normalized, first_inverse_deviation = layer_norm_forward_pass(
        activation_rows, first_gain, first_centred
    )
    n1b = first_normed.astype(jnp.bfloat16)
    bias3 = jnp.concatenate([bq, jnp.zeros_like(bq), bv])
    qkvb = (jnp.dot(n1b, whole[1], preferred_element_type=jnp.float32) + bias3).astype(jnp.bfloat16)
    attended, lse = attend_forward(qkvb, same)
    ob = attended.astype(jnp.bfloat16)
    second_activation = (
        activation_rows + jnp.dot(ob, whole[2], preferred_element_type=jnp.float32) + bo
    )
    second_normed, second_normalized, second_inverse_deviation = layer_norm_forward_pass(
        second_activation, second_gain, second_centred
    )
    n2b = second_normed.astype(jnp.bfloat16)
    hpre = jnp.dot(n2b, whole[3], preferred_element_type=jnp.float32) + bf1
    actb = jax.nn.gelu(hpre, approximate=False).astype(jnp.bfloat16)
    output = second_activation + jnp.dot(actb, whole[5], preferred_element_type=jnp.float32) + bf2
    layer_out = output.astype(jnp.bfloat16)
    dy = grad_out.astype(jnp.float32) * valid
    fenced, dy = lax.optimization_barrier((shards, dy))
    back = fetch(fenced)
    dyb = dy.astype(jnp.bfloat16)
    d_down = jnp.einsum("tf,td->fd", actb, dyb, preferred_element_type=jnp.float32)
    d_down_bias = jnp.sum(dy, axis=0)
    dgate = jnp.einsum("td,fd->tf", dyb, back[5], preferred_element_type=jnp.float32)
    dhb = (dgate * gelu_slope(hpre)).astype(jnp.bfloat16)
    d_up = jnp.einsum("td,tf->df", n2b, dhb, preferred_element_type=jnp.float32)
    d_up_bias = jnp.sum(dhb.astype(jnp.float32), axis=0)
    second_norm_gradient = jnp.einsum("tf,df->td", dhb, back[3], preferred_element_type=jnp.float32)
    second_activation_norm_gradient, second_gain_gradient, second_centred_gradient = (
        layer_norm_backward_pass(
            second_norm_gradient, second_normalized, second_inverse_deviation, second_gain
        )
    )
    da2 = dy + second_activation_norm_gradient
    dzb = da2.astype(jnp.bfloat16)
    d_out = jnp.einsum("te,td->ed", ob, dzb, preferred_element_type=jnp.float32)
    d_out_bias = jnp.sum(dzb.astype(jnp.float32), axis=0)
    dob = jnp.einsum("td,ed->te", dzb, back[2], preferred_element_type=jnp.float32).astype(
        jnp.bfloat16
    )
    dqkvb = attend_backward(qkvb, dob, lse, same).astype(jnp.bfloat16)
    d_qkv = jnp.einsum("td,te->de", n1b, dqkvb, preferred_element_type=jnp.float32)
    dqkv_sum = jnp.sum(dqkvb.astype(jnp.float32), axis=0)
    first_norm_gradient = jnp.einsum(
        "te,de->td", dqkvb, back[1], preferred_element_type=jnp.float32
    )
    first_activation_gradient, first_gain_gradient, first_centred_gradient = (
        layer_norm_backward_pass(
            first_norm_gradient, first_normalized, first_inverse_deviation, first_gain
        )
    )
    da = da2 + first_activation_gradient
    tokens_grad = da.astype(jnp.bfloat16)
    d_pos = jnp.dot(picker.astype(jnp.float32).T, da, precision=lax.Precision.HIGHEST)
    d_vectors = jnp.stack(
        [
            first_gain_gradient,
            first_centred_gradient,
            dqkv_sum[:D],
            dqkv_sum[2 * D :],
            d_out_bias,
            second_gain_gradient,
            second_centred_gradient,
            d_down_bias,
        ]
    )
    flat_parts = (
        d_vectors,
        d_qkv.reshape(-1, 128),
        d_out.reshape(-1, 128),
        d_up.reshape(-1, 128),
        d_up_bias,
        d_down,
        d_pos,
    )
    owned = reduce_grads(flat_parts)
    gv = owned[0]
    qkv_owned = owned[1].reshape(-1, 3 * D)
    out_owned = owned[2].reshape(-1, D)
    up_owned = owned[3].reshape(-1, FF)
    return (
        layer_out,
        tokens_grad,
        gv[0],
        gv[1],
        qkv_owned,
        gv[2],
        gv[3],
        out_owned,
        gv[4],
        gv[5],
        gv[6],
        up_owned,
        owned[4],
        owned[5],
        gv[7],
        owned[6],
    )


BF = jnp.bfloat16
F32 = jnp.float32
AXES = ("dp", "fsdp")
CORE, XBIT, YBIT, ZBIT, FAR = 1, 2, 4, 8, 16
PACK = 384
LIVE = -(-2 * LONG // 64) * 64
REST = PACK - LIVE
ROWS = 2 * PACK
BACK = 2 * LIVE
HALF_FF = FF // 2
QKV = 3 * D // 2
HALF_D = D // 2
SMALL = 384
HALF_QKV = QKV // 2
CUT = SMALL + HALF_QKV
VEC0 = LONG
SEGMENTS = ((0, 0, LIVE, 0), (1, 0, LIVE, LIVE), (0, LIVE, REST, BACK), (1, LIVE, REST, BACK + REST))
NT = (((1,), (1,)), ((), ()))
TN = (((0,), (0,)), ((), ()))


def swap(value, mask):
    return lax.ppermute(value, AXES, [(i, i ^ mask) for i in range(32)])


def coords():
    dp = lax.axis_index("dp")
    fs = lax.axis_index("fsdp")
    return dp // 2, dp % 2, fs // 2, fs % 2


def chip_of(rel):
    z, y, x, _ = coords()
    dz, dy, dx = rel
    bits = 0
    for part, off, width in ((z // 2, dz // 2, 8), (z % 2, dz % 2, 4), (y, dy, 2), (x, dx, 1)):
        bits = bits + (1 - part if off else part) * width
    return bits


ZORDER = (0, 2, 1, 3)
ENTRIES_ZXY = (
    [(0, (k,), h, (z, 0, 0), h) for k, z in enumerate(ZORDER) for h in range(2)]
    + [(1, (k,), h, (z, 0, 1), h) for k, z in enumerate(ZORDER) for h in range(2)]
    + [(2, (k,), h, (z, 1, 0), h) for k, z in enumerate(ZORDER) for h in range(2)]
    + [(3, (k,), h, (z, 1, 1), h) for k, z in enumerate(ZORDER[:2]) for h in range(2)]
    + [(4, (k,), h, (z, 1, 1), h) for k, z in enumerate(ZORDER[2:]) for h in range(2)]
)
QUADS = (((0, 0), 0), ((0, 1), 0), ((0, 0), 1), ((1, 0), 1))
SIDE_A = ((1, 0), (1, 1))
SIDE_B = ((0, 1), (1, 1))
ENTRIES_XZY_GATHER = (
    [
        (k // 2, (k % 2, q), 0, (z,) + QUADS[q][0], QUADS[q][1])
        for k, z in enumerate(ZORDER)
        for q in range(4)
    ]
    + [(2, (k, q), 0, (z,) + SIDE_A[q], 0) for k, z in enumerate(ZORDER) for q in range(2)]
    + [(3, (k, q), 0, (z,) + SIDE_B[q], 1) for k, z in enumerate(ZORDER) for q in range(2)]
)
ENTRIES_XZY_SCATTER = (
    [
        (0, (k, q), 0, (z,) + QUADS[q][0], QUADS[q][1])
        for k, z in enumerate(ZORDER)
        for q in range(4)
    ]
    + [(1, (k, q), 0, (z,) + SIDE_A[q], 0) for k, z in enumerate(ZORDER) for q in range(2)]
    + [(2, (k, q), 0, (z,) + SIDE_B[q], 1) for k, z in enumerate(ZORDER) for q in range(2)]
)


def after(value, *done):
    return lax.optimization_barrier((value, done))[0]


def send_all(*pairs, wait=()):
    values = tuple(value for value, _ in pairs)
    if wait:
        values, _ = lax.optimization_barrier((values, tuple(wait)))
    return tuple(swap(value, mask) for value, (_, mask) in zip(values, pairs))


def corners(from_x, from_y, wait=()):
    return send_all((from_x[:2], YBIT), (from_y[2:], XBIT), wait=wait)


def add(*values):
    total = values[0].astype(F32)
    for value in values[1:]:
        total = total + value.astype(F32)
    return total


def corner_pairs(parts):
    return (parts[3], XBIT), (parts[4], YBIT)


def scatter_shapes(kind, rows, width):
    if kind == "zxy":
        return [(4, 2 * rows, width)] * 3 + [(2, 2 * rows, width)] * 2
    return [(4, 4, rows, width), (4, 2, rows, width), (4, 2, rows, width)]


SCATTER_ENTRIES = {"zxy": ENTRIES_ZXY, "xzy": ENTRIES_XZY_SCATTER}


def piece_of(refs, entry, rows, lanes=None):
    array, index, row, _, _ = entry
    width = pl.ds(*lanes) if lanes else slice(None)
    return refs[array].at[index + (pl.ds(rows * row, rows), width)]


def start_all(copies, sems, first=0):
    started = []
    for i, (src, dst) in enumerate(copies):
        copy = pltpu.make_async_copy(src, dst, sems.at[first + i])
        copy.start()
        started.append(copy)
    return started


def wait_all(started):
    for copy in started:
        copy.wait()


def core_rows(entry):
    core = coords()[3]
    side = core if entry[4] == 0 else 1 - core
    return pl.multiple_of(chip_of(entry[3]) * 64 + side * 32, 32)


def z_of(dz):
    z = coords()[0]
    high, low = z // 2, z % 2
    return 2 * (1 - high if dz // 2 else high) + (1 - low if dz % 2 else low)


def half_rows(entry):
    return pl.multiple_of(chip_of(entry[3]) * 128 + 64 * entry[4], 64)


def tile(i, width):
    return pl.ds(pl.multiple_of(i * width, width), width)


ANY = pl.BlockSpec(memory_space=pl.ANY)
VMEM = pl.BlockSpec(memory_space=pltpu.VMEM)


def launch(kernel, ins, outs, scratch=(), flops=0, limit=56):
    size = sum(int(np.prod(o[0])) * jnp.dtype(o[1]).itemsize for o in outs)
    for value, _ in ins:
        size += value.size * value.dtype.itemsize
    return pl.pallas_call(
        kernel,
        out_shape=[jax.ShapeDtypeStruct(o[0], o[1]) for o in outs],
        in_specs=[spec for _, spec in ins],
        out_specs=[o[2] if len(o) > 2 else VMEM for o in outs],
        scratch_shapes=list(scratch),
        cost_estimate=pl.CostEstimate(flops=int(flops), bytes_accessed=int(size), transcendentals=0),
        compiler_params=pltpu.CompilerParams(vmem_limit_bytes=limit << 20),
    )(*[value for value, _ in ins])


def dma(count):
    return pltpu.SemaphoreType.DMA((count,))


def norm_rows(v):
    mean = jnp.mean(v, axis=1, keepdims=True)
    centred = v - mean
    inverse = lax.rsqrt(jnp.mean(centred * centred, axis=1, keepdims=True) + EPS)
    return centred * inverse, mean, inverse


def stats(mean, inverse):
    lane = lax.broadcasted_iota(jnp.int32, (mean.shape[0], 128), 1)
    return jnp.where(lane == 0, mean, inverse)


def normed(v, stat):
    return (v - stat[:, 0:1]) * stat[:, 1:2], stat[:, 1:2]


def gelu_parts(h):
    bell = jnp.exp(h * h * -0.5)
    base = 1.0 + jnp.abs(h) * (0.3275911 * 0.7071067811865476)
    t = pl.reciprocal(base, approx=True)
    t = t * (2.0 - base * t)
    poly = 0.5 * 1.061405429
    for factor in (-1.453152027, 1.421413741, -0.284496736, 0.254829592):
        poly = poly * t + 0.5 * factor
    tail = poly * t * bell
    return jnp.where(h >= 0, 1.0 - tail, tail), bell


PIECES = ((0, 384), (384, 384), (768, 256))


def norm_back(dn, hat, inverse, gain):
    scaled = dn * gain
    first = jnp.mean(scaled, axis=1, keepdims=True)
    second = jnp.mean(scaled * hat, axis=1, keepdims=True)
    return inverse * (scaled - first - hat * second)


def slot_of(block):
    which, j = divmod(block, 4)
    return 768 * (j // 2) + 256 * which + 128 * (j % 2)


def prepare_kernel(pos_ref, bias_ref, qkv_ref, up_ref, out_ref, keep_ref, send_ref, out2_ref):
    core = coords()[3]
    eye = (
        lax.broadcasted_iota(jnp.int32, (32, 32), 0) == lax.broadcasted_iota(jnp.int32, (32, 32), 1)
    ).astype(BF)
    small = lax.dot_general(eye, pos_ref[...], NT, preferred_element_type=F32)
    first_row = lax.broadcasted_iota(jnp.int32, (32, 128), 0) == 0
    bias = jnp.where(first_row, bias_ref[...].astype(F32), 0.0)
    small = jnp.concatenate([small, bias], axis=1).astype(BF)
    keep_ref[:, :SMALL] = small
    send_ref[:, :SMALL] = small
    for src, first, count in ((qkv_ref, SMALL, 12), (up_ref, SMALL + QKV, 16)):
        for j in range(count):
            own = pl.ds(pl.multiple_of(256 * j + 128 * core, 128), 128)
            other = pl.ds(pl.multiple_of(256 * j + 128 * (1 - core), 128), 128)
            to = first + (slot_of(j) if count == 12 else 128 * j)
            keep_ref[:, to : to + 128] = src[:, own]
            send_ref[:, to : to + 128] = src[:, other]
    out2_ref[:32] = out_ref[:, :HALF_D]
    out2_ref[32:] = out_ref[:, HALF_D:]


def prepare(pos, bias, qkv, up, out):
    shapes = [(32, SMALL + QKV + HALF_FF)] * 2 + [(64, HALF_D)]
    return launch(
        prepare_kernel,
        [(v, VMEM) for v in (pos, bias, qkv, up, out)],
        [(s, BF) for s in shapes],
        limit=8,
    )


def fill_bias(bias_ref, vec_ref, half):
    core = coords()[3]
    for j in range(2):
        own = pl.ds(pl.multiple_of(256 * (2 * half + j) + 128 * core, 128), 128)
        bias_ref[0:1, 128 * j : 128 * (j + 1)] = vec_ref[2:3, own]
        bias_ref[0:1, 256 + 128 * j : 256 + 128 * (j + 1)] = jnp.zeros((1, 128), F32)
        bias_ref[0:1, 512 + 128 * j : 512 + 128 * (j + 1)] = vec_ref[3:4, own]


def first_kernel(own_hbm, sib_hbm, place_ref, *refs):
    parts, refs = refs[:5], refs[5:]
    a_hbm, n1_hbm, wq_hbm, qkv_ref, vec_ref, bf1_ref, stat_ref = refs[:7]
    tok_ref, a_ref, n1_ref, wq_ref, small_ref, bias_ref, sems, out_sems = refs[7:]
    core = coords()[3]
    count = len(ENTRIES_ZXY)
    one = start_all(
        [
            (piece_of(parts, e, 32, (0, SMALL)), small_ref.at[pl.ds(core_rows(e), 32), :])
            for e in ENTRIES_ZXY
        ]
        + [
            (
                (own_hbm if which == 0 else sib_hbm).at[pl.ds(start, size), :],
                tok_ref.at[pl.ds(to, size), :],
            )
            for which, start, size, to in SEGMENTS
        ],
        sems,
    )
    two = start_all(
        [
            (piece_of(parts, e, 32, (SMALL, HALF_QKV)), wq_ref.at[pl.ds(core_rows(e), 32), :])
            for e in ENTRIES_ZXY
        ],
        sems,
        count + 4,
    )
    wait_all(one)
    lane = lax.broadcasted_iota(jnp.int32, (16, 256), 1)
    pick = (lane == lax.broadcasted_iota(jnp.int32, (16, 256), 0) + VEC0).astype(BF)
    vec_ref[...] = lax.dot_general(pick, small_ref[:, :256], NT, preferred_element_type=F32)
    for chip in range(16):
        row = pl.multiple_of(64 * chip + 32 * core, 32)
        bf1_ref[:, 128 * chip : 128 * (chip + 1)] = small_ref[pl.ds(row, 16), 256:384][:1].astype(F32)
    fill_bias(bias_ref, vec_ref, 0)
    hot = (place_ref[...] == lax.broadcasted_iota(jnp.int32, (ROWS, 256), 1)).astype(BF)
    for j in range(2):
        at = slice(512 * j, 512 * (j + 1))
        a_ref[:, at] = tok_ref[:, at].astype(F32) + lax.dot_general(
            hot, small_ref[at, :256], NT, preferred_element_type=F32
        )
    gain, shift = vec_ref[0:1, :], vec_ref[1:2, :]

    def rows(i, carry):
        hat, mean, inverse = norm_rows(a_ref[tile(i, 64), :])
        n1_ref[tile(i, 64), :] = (hat * gain + shift).astype(BF)
        stat_ref[tile(i, 64), :] = stats(mean, inverse)
        return carry

    lax.fori_loop(0, ROWS // 64, rows, 0)
    outs = start_all([(a_ref, a_hbm), (n1_ref, n1_hbm)], out_sems)
    wait_all(two)
    outs += start_all([(wq_ref, wq_hbm)], out_sems, 2)

    def columns(j, carry):
        at = tile(j, 256)
        product = jnp.dot(n1_ref[...], wq_ref[:, at], preferred_element_type=F32)
        qkv_ref[:, at] = (product + bias_ref[0:1, at]).astype(BF)
        return carry

    lax.fori_loop(0, 3, columns, 0)
    wait_all(outs)


def first_stage(own, sib, place, gathered):
    return launch(
        first_kernel,
        [(own, ANY), (sib, ANY), (place, VMEM)] + [(g, ANY) for g in gathered],
        [
            ((ROWS, D), F32, ANY),
            ((ROWS, D), BF, ANY),
            ((D, HALF_QKV), BF, ANY),
            ((ROWS, HALF_QKV), BF),
            ((16, D), F32),
            ((1, HALF_FF), F32),
            ((ROWS, 128), F32),
        ],
        [
            pltpu.VMEM((ROWS, D), BF),
            pltpu.VMEM((ROWS, D), F32),
            pltpu.VMEM((ROWS, D), BF),
            pltpu.VMEM((D, HALF_QKV), BF),
            pltpu.VMEM((D, SMALL), BF),
            pltpu.VMEM((8, HALF_QKV), F32),
            dma(2 * len(ENTRIES_ZXY) + 4),
            dma(3),
        ],
        flops=1.2e9,
    )


def second_kernel(n1_hbm, vec_ref, *refs):
    parts, refs = refs[:5], refs[5:]
    wq_hbm, qkv_ref, left_ref, right_ref, n1_ref, wq_ref, bias_ref, sems, out_sem = refs
    count = len(ENTRIES_ZXY)
    one = start_all(
        [(n1_hbm, n1_ref)]
        + [
            (piece_of(parts, e, 32, (0, HALF_QKV)), wq_ref.at[pl.ds(core_rows(e), 32), :])
            for e in ENTRIES_ZXY
        ],
        sems,
    )
    two = start_all(
        [
            (
                piece_of(parts, e, 32, (HALF_QKV, HALF_D)),
                (left_ref, right_ref)[e[4]].at[chip_of(e[3])],
            )
            for e in ENTRIES_ZXY
        ],
        sems,
        count + 1,
    )
    fill_bias(bias_ref, vec_ref, 1)
    wait_all(one)
    outs = start_all([(wq_ref, wq_hbm)], out_sem)

    def columns(j, carry):
        at = tile(j, 256)
        product = jnp.dot(n1_ref[...], wq_ref[:, at], preferred_element_type=F32)
        qkv_ref[:, at] = (product + bias_ref[0:1, at]).astype(BF)
        return carry

    lax.fori_loop(0, 3, columns, 0)
    wait_all(two + outs)


def second_stage(n1, vec, gathered):
    return launch(
        second_kernel,
        [(n1, ANY), (vec, VMEM)] + [(g, ANY) for g in gathered],
        [((D, HALF_QKV), BF, ANY), ((ROWS, HALF_QKV), BF)] + [((16, 32, HALF_D), BF)] * 2,
        [
            pltpu.VMEM((ROWS, D), BF),
            pltpu.VMEM((D, HALF_QKV), BF),
            pltpu.VMEM((8, HALF_QKV), F32),
            dma(2 * len(ENTRIES_ZXY) + 1),
            dma(1),
        ],
        flops=1.2e9,
    )


def pack_rows(ref, pack):
    main = ref[LIVE * pack : LIVE * (pack + 1), :]
    return jnp.concatenate([main, ref[BACK + REST * pack : BACK + REST * (pack + 1), :]])


def attend_kernel(q_ref, k_ref, v_ref, col_ref, row_ref, o_ref, lse_ref):
    first = lax.broadcasted_iota(jnp.int32, (PACK, 128), 1) < HEAD
    for pack in range(2):
        q, k, v = (pack_rows(r, pack) for r in (q_ref, k_ref, v_ref))
        same = pack_rows(col_ref, pack) == row_ref[pack : pack + 1, :]
        outs, logs = [], []
        for h in range(2):
            mine = first if h == 0 else ~first
            scores = lax.dot_general(
                jnp.where(mine, q * HEAD ** (-0.5), 0), k, NT, preferred_element_type=F32
            )
            scores = jnp.where(same, scores, -1000000000.0)
            top = jnp.max(scores, axis=1, keepdims=True)
            powers = jnp.exp(scores - top)
            total = jnp.sum(powers, axis=1, keepdims=True)
            mixed = jnp.dot(powers.astype(BF), v, preferred_element_type=F32)
            outs.append(mixed * (1.0 / total))
            logs.append(top + jnp.log(total))
        o = jnp.where(first, outs[0], outs[1]).astype(BF)
        lse = jnp.where(first, logs[0], logs[1])
        o_ref[LIVE * pack : LIVE * (pack + 1), :] = o[:LIVE]
        o_ref[BACK + REST * pack : BACK + REST * (pack + 1), :] = o[LIVE:]
        lse_ref[LIVE * pack : LIVE * (pack + 1), :] = lse[:LIVE]


def attend(qkv, col, row):
    part = lambda off: pl.BlockSpec((ROWS, 128), lambda j: (0, j + off))
    return pl.pallas_call(
        attend_kernel,
        grid=(2,),
        in_specs=[
            part(0),
            part(2),
            part(4),
            pl.BlockSpec((ROWS, 1), lambda j: (0, 0)),
            pl.BlockSpec((2, PACK), lambda j: (0, 0)),
        ],
        out_specs=[part(0), pl.BlockSpec((BACK, 128), lambda j: (0, j))],
        out_shape=[
            jax.ShapeDtypeStruct((ROWS, 256), BF),
            jax.ShapeDtypeStruct((BACK, 256), F32),
        ],
        cost_estimate=pl.CostEstimate(flops=int(8e8), bytes_accessed=4000000, transcendentals=0),
        compiler_params=pltpu.CompilerParams(vmem_limit_bytes=32 << 20),
    )(qkv, qkv, qkv, col, row)


def attend_back(q_ref, g_ref, o_ref, lse_ref, col_ref, row_ref, out_ref):
    first = lax.broadcasted_iota(jnp.int32, (LIVE, 128), 1) < HEAD
    scale = HEAD ** (-0.5)

    def pair(i, carry):
        pack, j = i // 2, i % 2
        at = pl.ds(pl.multiple_of(LIVE * pack, LIVE), LIVE)
        lanes = lambda which: pl.ds(pl.multiple_of(256 * which + 128 * j, 128), 128)
        q, k, v = (q_ref[at, lanes(which)] for which in range(3))
        g = g_ref[at, lanes(0)]
        weighted = g.astype(F32) * o_ref[at, lanes(0)].astype(F32)
        logs = lse_ref[at, lanes(0)]
        same = col_ref[at, :] == row_ref[pl.ds(pack, 1), :LIVE]
        dq, dk, dv = [], [], []
        for h in range(2):
            mine = first if h == 0 else ~first
            lse = logs[:, HEAD * h : HEAD * h + 1]
            inner = jnp.sum(jnp.where(mine, weighted, 0.0), axis=1, keepdims=True)
            qs = jnp.where(mine, q * scale, 0)
            scores = lax.dot_general(qs, k, NT, preferred_element_type=F32)
            probs = jnp.where(same, jnp.exp(scores - lse), 0.0)
            dprobs = lax.dot_general(jnp.where(mine, g, 0), v, NT, preferred_element_type=F32)
            ds = (probs * (dprobs - inner)).astype(BF)
            dv.append(lax.dot_general(probs.astype(BF), g, TN, preferred_element_type=F32))
            dq.append(jnp.dot(ds, k, preferred_element_type=F32))
            dk.append(lax.dot_general(ds, q, TN, preferred_element_type=F32))
        out_ref[at, lanes(0)] = (jnp.where(first, dq[0], dq[1]) * scale).astype(BF)
        out_ref[at, lanes(1)] = (jnp.where(first, dk[0], dk[1]) * scale).astype(BF)
        out_ref[at, lanes(2)] = jnp.where(first, dv[0], dv[1]).astype(BF)
        return carry

    lax.fori_loop(0, 4, pair, 0)


def head_rows(k, core):
    return (k // 2) * 4 + 2 * core + k % 2


def project_kernel(o0_ref, o1_ref, a_hbm, vec_ref, own0, own1, other0, other1, *refs):
    wo_ref, sum_ref, send0_ref, send1_ref, a_ref, sems = refs
    core = coords()[3]
    copies = []
    for k in range(8):
        head = head_rows(k, core)
        for parts, row in (((own0, own1), 32 * core), ((other0, other1), 32 - 32 * core)):
            at = pl.ds(pl.multiple_of(64 * k + row, 32), 32)
            for half, part in enumerate(parts):
                copies.append((part.at[head], wo_ref.at[at, pl.ds(HALF_D * half, HALF_D)]))
    started = start_all(copies + [(a_hbm, a_ref)], sems)
    wait_all(started)
    for j in range(2):
        at = slice(512 * j, 512 * (j + 1))
        part = jnp.dot(o0_ref[...], wo_ref[:256, at], preferred_element_type=F32) + jnp.dot(
            o1_ref[...], wo_ref[256:, at], preferred_element_type=F32
        )
        (send0_ref, send1_ref)[j][...] = part.astype(BF)
        sum_ref[:, at] = a_ref[:, at] + part + vec_ref[4:5, at]


def project(o, a, vec, own, other):
    return launch(
        project_kernel,
        [(o[0], VMEM), (o[1], VMEM), (a, ANY), (vec, VMEM)] + [(v, ANY) for v in (*own, *other)],
        [((HALF_D, D), BF), ((ROWS, D), F32), ((ROWS, HALF_D), BF), ((ROWS, HALF_D), BF)],
        [pltpu.VMEM((ROWS, D), F32), dma(33)],
        flops=0.8e9,
    )


SWAPPED = ((0, LIVE, LIVE), (LIVE, 0, LIVE), (BACK, BACK + REST, REST), (BACK + REST, BACK, REST))


def widen_kernel(sum_hbm, got0_hbm, got1_hbm, vec_ref, bf1_ref, own_hbm, sib_hbm, col_ref, *refs):
    parts, refs = refs[:5], refs[5:]
    n2_hbm, act_hbm, slope_hbm, stat_ref = refs[:4]
    outs, refs = refs[4:7], refs[7:]
    a2_ref, got_ref, n2_ref, wu_ref, act_ref, slope_ref, dy_ref, whole_ref, h0, h1 = refs[:10]
    sems, out_sems, grad_sems = refs[10:]
    first = start_all(
        [(sum_hbm, a2_ref)]
        + [
            (src.at[pl.ds(start, size), :], got_ref.at[pl.ds(to, size), pl.ds(HALF_D * i, HALF_D)])
            for i, src in enumerate((got0_hbm, got1_hbm))
            for to, start, size in SWAPPED
        ],
        sems,
    )
    grads = start_all(
        [
            (src.at[pl.ds(0, LIVE), :], dy_ref.at[pl.ds(LIVE * i, LIVE), :])
            for i, src in enumerate((own_hbm, sib_hbm))
        ],
        sems,
        9,
    )
    weights = start_all(
        [(piece_of(parts, e, 32), wu_ref.at[pl.ds(core_rows(e), 32), :]) for e in ENTRIES_ZXY],
        sems,
        11,
    )
    gain, shift = vec_ref[5:6, :], vec_ref[6:7, :]
    wait_all(first)

    def rows(i, carry):
        at = tile(i, 64)
        a2 = a2_ref[at, :] + got_ref[at, :].astype(F32)
        hat, mean, inverse = norm_rows(a2)
        n2_ref[at, :] = (hat * gain + shift).astype(BF)
        stat_ref[at, :] = stats(mean, inverse)
        return carry

    lax.fori_loop(0, ROWS // 64, rows, 0)
    wait_all(weights)
    sent = start_all([(n2_ref.at[pl.ds(0, BACK), :], n2_hbm)], out_sems)
    steps = HALF_FF // 512
    hidden = (h0, h1)

    def product(j):
        hidden[j % 2][...] = jnp.dot(
            n2_ref[...], wu_ref[:, 512 * j : 512 * (j + 1)], preferred_element_type=F32
        )

    product(0)
    for j in range(steps):
        if j + 1 < steps:
            product(j + 1)
        at = slice(512 * j, 512 * (j + 1))
        h = hidden[j % 2][...] + bf1_ref[:, at]
        area, bell = gelu_parts(h)
        act_ref[j] = (h * area).astype(BF)
        slope_ref[j] = (
            area[:BACK] + h[:BACK] * bell[:BACK] * 0.3989422804014327
        ).astype(BF)
        sent += start_all(
            [(act_ref.at[j], act_hbm.at[j]), (slope_ref.at[j], slope_hbm.at[j])],
            out_sems,
            1 + 2 * j,
        )
    wait_all(grads)
    dy_ref[...] = jnp.where(col_ref[:BACK, :] >= 0, dy_ref[...], 0)

    for k, dz in enumerate(ZORDER):
        at = tile(z_of(dz), 512)
        part = lax.dot_general(
            act_ref[z_of(dz), :BACK, :], dy_ref[...], TN, preferred_element_type=F32
        )
        whole_ref[at, :] = part.astype(BF)
        mine = [e for e in ENTRIES_XZY_SCATTER if e[3][0] == dz]
        sent += start_all(
            [(whole_ref.at[pl.ds(half_rows(e), 64), :], piece_of(outs, e, 64)) for e in mine],
            grad_sems,
            len(mine) * k,
        )
    wait_all(sent)


def widen(total, got, vec, bf1, own, sib, col, gathered):
    return launch(
        widen_kernel,
        [(total, ANY), (got[0], ANY), (got[1], ANY), (vec, VMEM), (bf1, VMEM), (own, ANY), (sib, ANY), (col, VMEM)]
        + [(g, ANY) for g in gathered],
        [
            ((BACK, D), BF, ANY),
            ((4, ROWS, 512), BF, ANY),
            ((4, BACK, 512), BF, ANY),
            ((ROWS, 128), F32),
        ]
        + [(s, BF, ANY) for s in scatter_shapes("xzy", 64, D)],
        [
            pltpu.VMEM((ROWS, D), F32),
            pltpu.VMEM((ROWS, D), BF),
            pltpu.VMEM((ROWS, D), BF),
            pltpu.VMEM((D, HALF_FF), BF),
            pltpu.VMEM((4, ROWS, 512), BF),
            pltpu.VMEM((4, BACK, 512), BF),
            pltpu.VMEM((BACK, D), BF),
            pltpu.VMEM((HALF_FF, D), BF),
            pltpu.VMEM((ROWS, 512), F32),
            pltpu.VMEM((ROWS, 512), F32),
            dma(11 + len(ENTRIES_ZXY)),
            dma(1 + 2 * (HALF_FF // 512)),
            dma(len(ENTRIES_XZY_SCATTER)),
        ],
        flops=5.8e9,
    )


def hidden_grad_kernel(own_hbm, sib_hbm, col_ref, slope_hbm, n2_hbm, *refs):
    ups, parts, refs = refs[:5], refs[5:9], refs[9:]
    sum_ref, part_hbm, sends, outs, refs = refs[0], refs[1], refs[2:5], refs[5:10], refs[10:]
    dy_ref, slope_ref, n2_ref, n2t_ref, wu_ref, wd_ref, dh_ref, whole_ref = refs[:8]
    part_ref, send_ref, sems, slope_sems, wd_sems, out_sems, last_sems = refs[8:]
    one = start_all(
        [(n2_hbm, n2_ref)]
        + [
            (src.at[pl.ds(0, LIVE), :], dy_ref.at[pl.ds(LIVE * i, LIVE), :])
            for i, src in enumerate((own_hbm, sib_hbm))
        ],
        sems,
    )

    def load(k):
        dz = ZORDER[k]
        mine = [e for e in ENTRIES_XZY_GATHER if e[3][0] == dz]
        return start_all(
            [(piece_of(parts, e, 64), wd_ref.at[pl.ds(half_rows(e), 64), :]) for e in mine],
            wd_sems,
            len(mine) * k,
        ) + start_all([(slope_hbm.at[z_of(dz)], slope_ref.at[z_of(dz)])], slope_sems, k)

    loads = [copy for k in range(4) for copy in load(k)]
    two = start_all(
        [(piece_of(ups, e, 32), wu_ref.at[pl.ds(core_rows(e), 32), :]) for e in ENTRIES_ZXY],
        sems,
        3,
    )
    wait_all(one)
    n2t_ref[...] = n2_ref[...].T
    dy_ref[...] = jnp.where(col_ref[:BACK, :] >= 0, dy_ref[...], 0)
    wait_all(loads)

    def block(j, carry):
        at = tile(j, 512)
        gate = lax.dot_general(dy_ref[...], wd_ref[at, :], NT, preferred_element_type=F32)
        dh = (gate * slope_ref[j].astype(F32)).astype(BF)
        dh_ref[:, at] = dh
        sum_ref[:, at] = jnp.sum(dh.astype(F32), axis=0, keepdims=True)
        whole_ref[:, at] = jnp.dot(
            n2t_ref[...], dh_ref[:, at], preferred_element_type=F32
        ).astype(BF)
        return carry

    lax.fori_loop(0, 4, block, 0)
    sent = start_all(
        [(whole_ref.at[pl.ds(core_rows(e), 32), :], piece_of(outs, e, 32)) for e in ENTRIES_ZXY],
        out_sems,
    )
    wait_all(two)

    def columns(j, carry):
        at = tile(j, 512)
        part = lax.dot_general(dh_ref[...], wu_ref[at, :], NT, preferred_element_type=F32)
        part_ref[:, at] = part
        send_ref[:, at] = part.astype(BF)
        return carry

    lax.fori_loop(0, 2, columns, 0)
    for j, (to, width) in enumerate(PIECES):
        sent += start_all([(send_ref.at[:, pl.ds(to, width)], sends[j])], last_sems, j)
    sent += start_all([(part_ref, part_hbm)], last_sems, 3)
    wait_all(sent)


def hidden_grads(own, sib, col, slope, n2, up_blocks, down_blocks):
    return launch(
        hidden_grad_kernel,
        [(own, ANY), (sib, ANY), (col, VMEM), (slope, ANY), (n2, ANY)]
        + [(g, ANY) for g in up_blocks + down_blocks],
        [
            ((1, HALF_FF), F32),
            ((BACK, D), F32, ANY),
        ]
        + [((BACK, width), BF, ANY) for _, width in PIECES]
        + [(s, BF, ANY) for s in scatter_shapes("zxy", 32, HALF_FF)],
        [
            pltpu.VMEM((BACK, D), BF),
            pltpu.VMEM((4, BACK, 512), BF),
            pltpu.VMEM((BACK, D), BF),
            pltpu.VMEM((D, BACK), BF),
            pltpu.VMEM((D, HALF_FF), BF),
            pltpu.VMEM((HALF_FF, D), BF),
            pltpu.VMEM((BACK, HALF_FF), BF),
            pltpu.VMEM((D, HALF_FF), BF),
            pltpu.VMEM((BACK, D), F32),
            pltpu.VMEM((BACK, D), BF),
            dma(3 + len(ENTRIES_ZXY)),
            dma(4),
            dma(len(ENTRIES_XZY_GATHER)),
            dma(len(ENTRIES_ZXY)),
            dma(4),
        ],
        flops=7.5e9,
    )


def middle_kernel(part_hbm, got0_hbm, got1_hbm, got2_hbm, sum_hbm, z0_hbm, z1_hbm, *refs):
    stat_ref, own_hbm, sib_hbm, col_ref, vec_ref, o0_ref, o1_ref, wo_hbm = refs[:8]
    da2_ref, do0_ref, do1_ref, sums_ref, mine_ref, send_ref = refs[8:14]
    part_ref, got_ref, a2_ref, z_ref, dy_ref, wo_ref, dz_ref, whole_ref, sems = refs[14:]
    core = coords()[3]
    one = start_all(
        [
            (part_hbm, part_ref),
            (sum_hbm.at[pl.ds(0, BACK), :], a2_ref),
            (own_hbm.at[pl.ds(0, LIVE), :], dy_ref.at[pl.ds(0, LIVE), :]),
            (sib_hbm.at[pl.ds(0, LIVE), :], dy_ref.at[pl.ds(LIVE, LIVE), :]),
        ]
        + [
            (src.at[pl.ds(start, LIVE), :], dst.at[pl.ds(LIVE - start, LIVE), pl.ds(off, width)])
            for dst, src, off, width in (
                (got_ref, got0_hbm, *PIECES[0]),
                (got_ref, got1_hbm, *PIECES[1]),
                (got_ref, got2_hbm, *PIECES[2]),
                (z_ref, z0_hbm, 0, HALF_D),
                (z_ref, z1_hbm, HALF_D, HALF_D),
            )
            for start in (0, LIVE)
        ]
        + [(wo_hbm, wo_ref)],
        sems,
    )
    gain = vec_ref[5:6, :]
    wait_all(one)

    def rows(i, sums):
        at = tile(i, 64)
        dn = part_ref[at, :] + got_ref[at, :].astype(F32)
        a2 = a2_ref[at, :] + z_ref[at, :].astype(F32)
        hat, inverse = normed(a2, stat_ref[at, :])
        dy = jnp.where(col_ref[at, :] >= 0, dy_ref[at, :].astype(F32), 0.0)
        da2 = dy + norm_back(dn, hat, inverse, gain)
        dz = da2.astype(BF)
        dz_ref[at, :] = dz
        if sums is None:
            return 0
        da2_ref[at, :] = da2
        return tuple(
            s + jnp.sum(v.reshape(8, 8, D), axis=0)
            for s, v in zip(sums, (dn * hat, dn, dz.astype(F32), dy))
        )

    steps = LIVE // 64
    sums = lax.fori_loop(0, steps, rows, (jnp.zeros((8, D), F32),) * 4)
    lax.fori_loop(steps, 2 * steps, lambda i, c: rows(i, None), 0)
    for i, s in enumerate(sums):
        sums_ref[i : i + 1, :] = jnp.sum(s, axis=0, keepdims=True)
    sums_ref[4:8, :] = jnp.zeros((4, D), F32)
    for half, (do_ref, o_ref) in enumerate(((do0_ref, o0_ref), (do1_ref, o1_ref))):
        at = slice(256 * half, 256 * (half + 1))
        do_ref[...] = lax.dot_general(
            dz_ref[...], wo_ref[at, :], NT, preferred_element_type=F32
        ).astype(BF)
        whole_ref[at, :] = lax.dot_general(
            o_ref[:BACK, :], dz_ref[...], TN, preferred_element_type=F32
        ).astype(BF)
    for k in range(8):
        mine_ref[k] = whole_ref[pl.ds(pl.multiple_of(64 * k + 32 * core, 32), 32), :]
        send_ref[k] = whole_ref[pl.ds(pl.multiple_of(64 * k + 32 - 32 * core, 32), 32), :]


def middle(part, got, total, z, stat, own, sib, col, vec, o, wo):
    ins = [(v, ANY) for v in (part, *got, total, *z)]
    ins += [(stat, VMEM), (own, ANY), (sib, ANY), (col, VMEM), (vec, VMEM)]
    ins += [(o[0], VMEM), (o[1], VMEM), (wo, ANY)]
    return launch(
        middle_kernel,
        ins,
        [
            ((LIVE, D), F32),
            ((BACK, 256), BF),
            ((BACK, 256), BF),
            ((8, D), F32),
            ((8, 32, D), BF),
            ((8, 32, D), BF),
        ],
        [
            pltpu.VMEM((BACK, D), F32),
            pltpu.VMEM((BACK, D), BF),
            pltpu.VMEM((BACK, D), F32),
            pltpu.VMEM((BACK, D), BF),
            pltpu.VMEM((BACK, D), BF),
            pltpu.VMEM((HALF_D, D), BF),
            pltpu.VMEM((BACK, D), BF),
            pltpu.VMEM((HALF_D, D), BF),
            dma(15),
        ],
        flops=1.4e9,
    )


def back_one_kernel(q_ref, g_ref, o_ref, lse_ref, col_ref, row_ref, n1_hbm, *refs):
    mine_ref, theirs_ref, out_ref, n1t_hbm = refs[:4]
    outs, refs = refs[4:9], refs[9:]
    n1_ref, n1t_ref, whole_ref, sems, sent_sem = refs
    count = len(ENTRIES_ZXY)
    load = start_all([(n1_hbm.at[pl.ds(0, BACK), :], n1_ref)], sent_sem)
    two = []
    for i, e in enumerate(ENTRIES_ZXY):
        rel, half = e[3], e[4]
        _, y, _, core = coords()
        chip = chip_of(rel)
        slot = (chip // 4) * 2 + chip % 2
        at = pl.ds(HALF_D * half, HALF_D)
        dst = piece_of(outs, e, 32, (HALF_QKV, HALF_D))
        here = (y if rel[1] == 0 else 1 - y) == core
        sem = sems.at[count + i]
        two.append(pltpu.make_async_copy(mine_ref.at[slot, :, at], dst, sem))

        @pl.when(here)
        def _():
            pltpu.make_async_copy(mine_ref.at[slot, :, at], dst, sem).start()

        @pl.when(jnp.logical_not(here))
        def _():
            pltpu.make_async_copy(theirs_ref.at[slot, :, at], dst, sem).start()

    attend_back(q_ref, g_ref, o_ref, lse_ref, col_ref, row_ref, out_ref)
    wait_all(load)
    n1t_ref[...] = n1_ref[...].T
    load = start_all([(n1t_ref, n1t_hbm)], sent_sem)
    whole_ref[...] = jnp.dot(n1t_ref[...], out_ref[...], preferred_element_type=F32).astype(BF)
    one = start_all(
        [
            (whole_ref.at[pl.ds(core_rows(e), 32), :], piece_of(outs, e, 32, (0, HALF_QKV)))
            for e in ENTRIES_ZXY
        ],
        sems,
    )
    wait_all(one + two + load)


def back_one(qkv, do, o, lse, col, row, n1, mine, theirs):
    return launch(
        back_one_kernel,
        [(v, VMEM) for v in (qkv, do, o, lse, col, row)]
        + [(n1, ANY), (mine, VMEM), (theirs, VMEM)],
        [((BACK, HALF_QKV), BF), ((D, BACK), BF, ANY)]
        + [(s, BF, ANY) for s in scatter_shapes("zxy", 32, HALF_QKV + HALF_D)],
        [
            pltpu.VMEM((BACK, D), BF),
            pltpu.VMEM((D, BACK), BF),
            pltpu.VMEM((D, HALF_QKV), BF),
            dma(2 * len(ENTRIES_ZXY)),
            dma(1),
        ],
        flops=2.5e9,
    )


def back_two_kernel(q_ref, g_ref, o_ref, lse_ref, col_ref, row_ref, one_ref, *refs):
    w0_hbm, w1_hbm, out_ref, own_ref, send_ref, w0_ref, w1_ref, sems = refs
    load = start_all([(w0_hbm, w0_ref), (w1_hbm, w1_ref)], sems)
    attend_back(q_ref, g_ref, o_ref, lse_ref, col_ref, row_ref, out_ref)
    wait_all(load)
    for j in range(2):
        at = slice(512 * j, 512 * (j + 1))
        total = lax.dot_general(
            one_ref[...], w0_ref[at, :], NT, preferred_element_type=F32
        ) + lax.dot_general(out_ref[...], w1_ref[at, :], NT, preferred_element_type=F32)
        own_ref[:, at] = total[:LIVE]
        send_ref[:, at] = total[LIVE:].astype(BF)


def back_two(qkv, do, o, lse, col, row, one, w0, w1):
    return launch(
        back_two_kernel,
        [(v, VMEM) for v in (qkv, do, o, lse, col, row, one)] + [(w0, ANY), (w1, ANY)],
        [((BACK, HALF_QKV), BF), ((LIVE, D), F32), ((LIVE, D), BF)],
        [pltpu.VMEM((D, HALF_QKV), BF), pltpu.VMEM((D, HALF_QKV), BF), dma(2)],
        flops=3.2e9,
    )


def last_kernel(n1t_hbm, one_ref, two_ref, dn_ref, got_ref, a_hbm, stat_ref, *refs):
    da2_ref, vec_ref, place_ref, sums_ref, upsum_ref, tok_ref = refs[:6]
    outs, refs = refs[6:11], refs[11:]
    n1t_ref, a_ref, whole_ref, small_ref, da_ref, rows_ref, sems, in_sems = refs
    core = coords()[3]
    count = len(ENTRIES_ZXY)
    load = start_all([(n1t_hbm, n1t_ref), (a_hbm.at[pl.ds(0, LIVE), :], a_ref)], in_sems)
    wait_all(load)

    def columns(j, carry):
        at = tile(j, 256)
        part = jnp.dot(n1t_ref[...], two_ref[:, at], preferred_element_type=F32)
        whole_ref[:, at] = part.astype(BF)
        return carry

    lax.fori_loop(0, 3, columns, 0)
    one = start_all(
        [
            (whole_ref.at[pl.ds(core_rows(e), 32), :], piece_of(outs, e, 32, (SMALL, HALF_QKV)))
            for e in ENTRIES_ZXY
        ],
        sems,
    )
    gain = vec_ref[0:1, :]

    def rows(i, sums):
        at = tile(i, 64)
        dn = dn_ref[at, :] + got_ref[at, :].astype(F32)
        hat, inverse = normed(a_ref[at, :], stat_ref[at, :])
        da = da2_ref[at, :] + norm_back(dn, hat, inverse, gain)
        da_ref[at, :] = da.astype(BF)
        tok_ref[at, :] = da.astype(BF)
        return tuple(
            s + jnp.sum(v.reshape(8, 8, D), axis=0) for s, v in zip(sums, (dn * hat, dn))
        )

    sums = lax.fori_loop(0, LIVE // 64, rows, (jnp.zeros((8, D), F32),) * 2)
    tok_ref[LIVE:, :] = jnp.zeros((REST, D), BF)
    lane = lax.broadcasted_iota(jnp.int32, (LIVE, 256), 1)
    hot = (place_ref[:LIVE, :] == lane).astype(BF)
    small = lax.dot_general(da_ref[...], hot, TN, preferred_element_type=F32)
    rows_ref[...] = jnp.zeros((16, D), F32)
    rows_ref[0:1, :] = jnp.sum(sums[0], axis=0, keepdims=True)
    rows_ref[1:2, :] = jnp.sum(sums[1], axis=0, keepdims=True)
    for half, src in enumerate((one_ref, two_ref)):
        total = jnp.sum(src[...].astype(F32), axis=0, keepdims=True)
        for j in range(2):
            own = pl.ds(pl.multiple_of(256 * (2 * half + j) + 128 * core, 128), 128)
            rows_ref[2:3, own] = total[:, 128 * j : 128 * (j + 1)]
            rows_ref[3:4, own] = total[:, 512 + 128 * j : 512 + 128 * (j + 1)]
    rows_ref[4:5, :] = sums_ref[2:3, :]
    rows_ref[5:6, :] = sums_ref[0:1, :]
    rows_ref[6:7, :] = sums_ref[1:2, :]
    rows_ref[7:8, :] = sums_ref[3:4, :]
    spot = lax.broadcasted_iota(jnp.int32, (16, 256), 0)
    place = (lax.broadcasted_iota(jnp.int32, (16, 256), 1) == spot + VEC0).astype(BF)
    value = rows_ref[...]
    for _ in range(2):
        piece = value.astype(BF)
        small = small + lax.dot_general(piece, place, TN, preferred_element_type=F32)
        value = value - piece.astype(F32)
    small_ref[:, :256] = small.astype(BF)
    small_ref[:, 256:] = jnp.zeros((D, SMALL - 256), BF)
    top = lax.broadcasted_iota(jnp.int32, (16, 128), 0) == 0
    for chip in range(16):
        row = pl.multiple_of(64 * chip + 32 * core, 32)
        bias = jnp.where(top, upsum_ref[:, 128 * chip : 128 * (chip + 1)], 0.0)
        small_ref[pl.ds(row, 16), 256:384] = bias.astype(BF)
    three = start_all(
        [
            (small_ref.at[pl.ds(core_rows(e), 32), :], piece_of(outs, e, 32, (0, SMALL)))
            for e in ENTRIES_ZXY
        ],
        sems,
        count,
    )
    wait_all(one + three)


def last_stage(n1t, one, two, dn, got, a, stat, da2, vec, place, sums, upsum):
    return launch(
        last_kernel,
        [(n1t, ANY)]
        + [(v, VMEM) for v in (one, two, dn, got)]
        + [(a, ANY)]
        + [(v, VMEM) for v in (stat, da2, vec, place, sums, upsum)],
        [((PACK, D), BF)] + [(s, BF, ANY) for s in scatter_shapes("zxy", 32, CUT)],
        [
            pltpu.VMEM((D, BACK), BF),
            pltpu.VMEM((LIVE, D), F32),
            pltpu.VMEM((D, HALF_QKV), BF),
            pltpu.VMEM((D, SMALL), BF),
            pltpu.VMEM((LIVE, D), BF),
            pltpu.VMEM((16, D), F32),
            dma(2 * len(ENTRIES_ZXY)),
            dma(2),
        ],
        flops=1.2e9,
    )


def output_kernel(act_hbm, sum_hbm, z0_hbm, z1_hbm, vec_ref, *refs):
    parts, (own_ref, send_ref) = refs[:4], refs[4:6]
    act_ref, a2_ref, z_ref, wd_ref, sems = refs[6:]
    copies = [
        (piece_of(parts, e, 64), wd_ref.at[pl.ds(half_rows(e), 64), :]) for e in ENTRIES_XZY_GATHER
    ]
    copies += [(act_hbm, act_ref)]
    for which, start, size, to in SEGMENTS:
        if which == 0:
            at = pl.ds(start, size)
            copies.append((sum_hbm.at[pl.ds(to, size), :], a2_ref.at[at, :]))
            src = pl.ds(to + size, size)
            copies.append((z0_hbm.at[src, :], z_ref.at[at, pl.ds(0, HALF_D)]))
            copies.append((z1_hbm.at[src, :], z_ref.at[at, pl.ds(HALF_D, HALF_D)]))
    wait_all(start_all(copies, sems))
    for j in range(2):
        at = slice(512 * j, 512 * (j + 1))
        part = jnp.dot(act_ref[0], wd_ref[:512, at], preferred_element_type=F32)
        for k in range(1, 4):
            part += jnp.dot(
                act_ref[k], wd_ref[512 * k : 512 * (k + 1), at], preferred_element_type=F32
            )
        a2 = a2_ref[:, at] + z_ref[:, at].astype(F32) + vec_ref[7:8, at]
        for which, start, size, to in SEGMENTS:
            if which == 0:
                own_ref[start : start + size, at] = part[to : to + size] + a2[start : start + size]
            else:
                send_ref[start : start + size, at] = part[to : to + size].astype(BF)


def output_stage(act, total, z, vec, gathered):
    return launch(
        output_kernel,
        [(act, ANY), (total, ANY), (z[0], ANY), (z[1], ANY), (vec, VMEM)]
        + [(g, ANY) for g in gathered],
        [((PACK, D), F32), ((PACK, D), BF)],
        [
            pltpu.VMEM((4, ROWS, 512), BF),
            pltpu.VMEM((PACK, D), F32),
            pltpu.VMEM((PACK, D), BF),
            pltpu.VMEM((HALF_FF, D), BF),
            dma(len(ENTRIES_XZY_GATHER) + 7),
        ],
        flops=3.2e9,
    )


def merge_kernel(x_hbm, y_hbm, a_hbm, b_hbm, x_out, y_out, *scratch):
    x_ref, y_ref, a_ref, b_ref, sems, out_sems = scratch
    upper, lower = pl.ds(2, 2), pl.ds(0, 2)
    wait_all(
        start_all(
            [
                (x_hbm.at[upper], x_ref),
                (b_hbm, b_ref),
                (y_hbm.at[lower], y_ref),
                (a_hbm, a_ref),
            ],
            sems,
        )
    )
    x_ref[...] = (x_ref[...].astype(F32) + b_ref[...].astype(F32)).astype(BF)
    y_ref[...] = (y_ref[...].astype(F32) + a_ref[...].astype(F32)).astype(BF)
    wait_all(start_all([(x_ref, x_out.at[upper]), (y_ref, y_out.at[lower])], out_sems))


def to_neighbours(parts, got_a, got_b):
    whole = parts[1].shape
    half = pltpu.VMEM((2,) + whole[1:], BF)
    return pl.pallas_call(
        merge_kernel,
        out_shape=[jax.ShapeDtypeStruct(whole, BF)] * 2,
        in_specs=[ANY] * 4,
        out_specs=[ANY] * 2,
        scratch_shapes=[half] * 4 + [dma(4), dma(2)],
        input_output_aliases={0: 0, 1: 1},
        cost_estimate=pl.CostEstimate(flops=0, bytes_accessed=3000000, transcendentals=0),
        compiler_params=pltpu.CompilerParams(vmem_limit_bytes=8 << 20),
    )(parts[1], parts[2], got_a, got_b)


def split_kernel(count, *refs):
    values, (keep_ref, send_ref) = refs[:count], refs[count:]
    total = values[0][0].astype(F32)
    if count == 3 and total.ndim == 2:
        total = total + values[1][0].astype(F32) + values[2][0].astype(F32)
    else:
        total = total + jnp.concatenate([v[0].astype(F32) for v in values[1:]])

    @pl.when(pl.program_id(0) < 2)
    def _():
        keep_ref[0] = total

    @pl.when(pl.program_id(0) >= 2)
    def _():
        send_ref[0] = total.astype(BF)


def split_sum(*values):
    block = values[0].shape[1:]
    spec = lambda shape, at: pl.BlockSpec(
        (1,) + shape, lambda k: (at(k),) + (0,) * len(shape)
    )
    return pl.pallas_call(
        functools.partial(split_kernel, len(values)),
        grid=(4,),
        in_specs=[spec(v.shape[1:], lambda k: k) for v in values],
        out_specs=[
            spec(block, lambda k: jnp.minimum(k, 1)),
            spec(block, lambda k: jnp.maximum(k - 2, 0)),
        ],
        out_shape=[
            jax.ShapeDtypeStruct((2,) + block, F32),
            jax.ShapeDtypeStruct((2,) + block, BF),
        ],
        cost_estimate=pl.CostEstimate(flops=0, bytes_accessed=6000000, transcendentals=0),
        compiler_params=pltpu.CompilerParams(vmem_limit_bytes=16 << 20),
    )(*values)


def finish_kernel(a_ref, b_ref, up_ref, a_got, b_got, up_got, small_ref, qkv_ref, grad_ref, out_ref):
    core = coords()[3]
    small_ref[...] = b_ref[:32, :SMALL] + b_got[:, :SMALL]
    for j in range(12):
        at = slot_of(j)
        mine = pl.ds(pl.multiple_of(256 * j + 128 * core, 128), 128)
        other = pl.ds(pl.multiple_of(256 * j + 128 - 128 * core, 128), 128)
        own, got = (a_ref, a_got) if at < HALF_QKV else (b_ref, b_got)
        at = slice(at, at + 128) if at < HALF_QKV else slice(at + SMALL - HALF_QKV, at + SMALL - HALF_QKV + 128)
        qkv_ref[:, mine] = own[:32, at]
        qkv_ref[:, other] = got[:, at]
    for j in range(16):
        at = slice(128 * j, 128 * (j + 1))
        mine = pl.ds(pl.multiple_of(256 * j + 128 * core, 128), 128)
        other = pl.ds(pl.multiple_of(256 * j + 128 - 128 * core, 128), 128)
        grad_ref[:, mine] = up_ref[:32, at]
        grad_ref[:, other] = up_got[:, at]
    out_ref[:, :HALF_D] = a_ref[:32, HALF_QKV:]
    out_ref[:, HALF_D:] = a_ref[32:, HALF_QKV:]


def finish(a_sum, b_sum, up_sum, a_got, b_got, up_got):
    return launch(
        finish_kernel,
        [(v, VMEM) for v in (a_sum, b_sum, up_sum, a_got, b_got, up_got)],
        [((32, SMALL), F32), ((32, 3 * D), F32), ((32, FF), F32), ((32, D), F32)],
        limit=8,
    )


def in_order(own, sib):
    return jnp.concatenate([own[:LIVE], sib[:LIVE], own[LIVE:], sib[LIVE:]])


def fast_on_device(
    tokens,
    grad_out,
    image_lengths,
    image_device,
    small_map,
    ln1_gain,
    ln1_bias,
    qkv_weight,
    q_bias,
    v_bias,
    out_weight,
    out_bias,
    ln2_gain,
    ln2_bias,
    up_weight,
    up_bias,
    down_weight,
    down_bias,
    pos_table,
):
    device = lax.axis_index("dp") * 4 + lax.axis_index("fsdp")
    seg, place = layout(image_lengths, image_device, small_map, device, PACK)
    seg2, place2 = layout(image_lengths, image_device, small_map, device ^ 1, PACK)
    col = in_order(seg, seg2)[:, None]
    row = jnp.stack([seg, seg2])
    place = in_order(place, place2)[:, None]

    vectors = [ln1_gain, ln1_bias, q_bias, v_bias, out_bias, ln2_gain, ln2_bias, down_bias]
    table = jnp.concatenate([pos_table, jnp.stack(vectors), jnp.zeros((103, 32), BF)])
    keep, send, out2 = prepare(table, up_bias[None, :], qkv_weight, up_weight, out_weight)
    got = swap(send, CORE)
    chunk_1 = jnp.concatenate([keep[:, :CUT], got[:, :CUT]])
    rest = slice(CUT, SMALL + QKV)
    chunk_2 = jnp.concatenate([jnp.concatenate([keep[:, rest], got[:, rest]]), out2], axis=1)
    chunk_u = jnp.concatenate([keep[:, SMALL + QKV :], got[:, SMALL + QKV :]])
    down_a, down_b = down_weight[:64], down_weight[64:]
    sib_tokens = swap(tokens, CORE)
    sib_grad = swap(grad_out, CORE)

    (far_1,) = send_all((chunk_1, FAR))
    pair_1 = jnp.stack([chunk_1, far_1])
    (near_1,) = send_all((pair_1, ZBIT))
    down_x, down_y = send_all((down_a, XBIT), (down_b, YBIT), wait=(far_1,))
    line_1 = jnp.concatenate([pair_1, near_1])
    x_1, y_1 = send_all((line_1, XBIT), (line_1, YBIT), wait=(down_x, down_y))
    (far_2,) = send_all((chunk_2, FAR), wait=(near_1, down_x, down_y))
    pair_2 = jnp.stack([chunk_2, far_2])
    (near_2,) = send_all((pair_2, ZBIT))
    line_2 = jnp.concatenate([pair_2, near_2])
    corner_1 = corners(x_1, y_1)
    gathered_1 = [line_1, x_1, y_1, *corner_1]
    x_2, y_2 = send_all((line_2, XBIT), (line_2, YBIT), wait=corner_1)
    (far_u,) = send_all((chunk_u, FAR), wait=(near_2, *corner_1))
    pair_u = jnp.stack([chunk_u, far_u])
    a, n1, wq0, qkv0, vec, bf1, stat1 = first_stage(tokens, sib_tokens, place, gathered_1)
    (near_u,) = send_all((pair_u, ZBIT), wait=(stat1,))
    line_u = jnp.concatenate([pair_u, near_u])
    corner_2 = corners(x_2, y_2, wait=(stat1,))
    gathered_2 = [line_2, x_2, y_2, *corner_2]
    o0, lse0 = attend(after(qkv0, x_2, y_2, sib_grad), col, row)
    x_u, y_u = send_all((line_u, XBIT), (line_u, YBIT), wait=(*corner_2, lse0))
    quad_d = jnp.stack([down_a, down_x, down_b, down_y])
    (far_d,) = send_all((quad_d, FAR), wait=(near_u,))
    wq1, qkv1, *out_own = second_stage(n1, vec, gathered_2)
    out_other = [swap(half, CORE) for half in out_own]
    o1, lse1 = attend(qkv1, col, row)
    o = (o0, o1)
    pair_d = jnp.stack([quad_d, after(far_d, lse1)])
    wo, total, *send = project(o, a, vec, out_own, out_other)
    z = [swap(part, CORE) for part in send]
    corner_u = corners(x_u, y_u, wait=(send[0],))
    gathered_u = [line_u, x_u, y_u, *corner_u]
    (near_d,) = send_all((pair_d, ZBIT), wait=(lse1,))
    pairs_d = (pair_d, near_d)
    side_a = jnp.concatenate([p[:, :2] for p in pairs_d])
    side_b = jnp.concatenate([p[:, 2:] for p in pairs_d])
    gathered_d = [*pairs_d, *send_all((side_a, YBIT), (side_b, XBIT), wait=corner_u)]
    n2, act, slope, stat2, *d_parts = widen(
        total, z, vec, bf1, grad_out, sib_grad, col, gathered_u
    )

    keep, side_a, side_b = d_parts
    side_a, side_b = send_all((side_a, YBIT), (side_b, XBIT), wait=gathered_d[2:])
    up_bias_sum, part, *u_parts = hidden_grads(
        grad_out, sib_grad, col, slope, n2, gathered_u, gathered_d
    )
    got = [swap(piece, CORE) for piece in u_parts[:3]]
    u_parts = u_parts[3:]
    d_keep, d_send = split_sum(keep, side_a, side_b)
    u_got = send_all(*corner_pairs(u_parts), wait=(side_a, side_b))
    (d_near,) = send_all((d_send, ZBIT))
    da2, do0, do1, sums, mine, theirs = middle(
        after(part, d_send), got, total, z, stat2, grad_out, sib_grad, col, vec, o, wo
    )
    theirs = swap(theirs, CORE)

    u_x, u_y = to_neighbours(u_parts, *(after(u, sums) for u in u_got))
    u_line = send_all((u_x, XBIT), (u_y, YBIT))
    d_one, n1t, *a_parts = back_one(
        qkv0, after(do0, u_x, u_y), o0, lse0, col, row, n1, mine, theirs
    )
    d_pair = add(d_keep, after(d_near, d_one))
    d_send = d_pair[1].astype(BF)
    (d_far,) = send_all((d_send, FAR))
    d_two, dn, send = back_two(
        qkv1, after(do1, d_send), o1, lse1, col, row, d_one, wq0, wq1
    )
    u_keep, u_send = split_sum(u_parts[0], *(after(u, send) for u in u_line))
    a_got = send_all(*corner_pairs(a_parts), wait=(*u_line, send))
    (u_near,) = send_all((u_send, ZBIT))
    tokens_grad, *b_parts = last_stage(
        n1t, d_one, d_two, dn, swap(send, CORE), a, stat1, da2, vec, place, sums, up_bias_sum
    )
    a_x, a_y = to_neighbours(a_parts, *(after(v, tokens_grad) for v in a_got))
    a_line = send_all((a_x, XBIT), (a_y, YBIT))
    u_pair = add(u_keep, after(u_near, tokens_grad))
    u_send = u_pair[1].astype(BF)
    (u_far,) = send_all((u_send, FAR))
    own, send = output_stage(
        after(act, a_x, a_y, u_send, tokens_grad), total, z, vec, gathered_d
    )
    layer_out = (own + swap(send, CORE).astype(F32)).astype(BF)

    b_got = send_all(*corner_pairs(b_parts))
    d_quad = add(d_pair[0], after(d_far, own))
    b_x, b_y = to_neighbours(b_parts, *(after(v, own) for v in b_got))
    a_keep, a_send = split_sum(a_parts[0], *a_line)
    b_line = send_all((b_x, XBIT), (b_y, YBIT))
    d_x, d_y = send_all(
        (d_quad[1].astype(BF), XBIT), (d_quad[3].astype(BF), YBIT), wait=b_line
    )
    down_sum = jnp.concatenate([add(d_quad[0], d_x), add(d_quad[2], d_y)])
    (a_near,) = send_all((a_send, ZBIT))
    up_sum = add(u_pair[0], after(u_far, *b_line))
    a_pair = add(a_keep, a_near)
    (a_far,) = send_all((a_pair[1].astype(BF), FAR))
    b_keep, b_send = split_sum(b_parts[0], *b_line)
    (b_near,) = send_all((b_send, ZBIT))
    a_sum = add(a_pair[0], a_far)
    b_pair = add(b_keep, b_near)
    (b_far,) = send_all((b_pair[1].astype(BF), FAR))
    b_sum = add(b_pair[0], b_far)

    up_got = swap(up_sum[32:], CORE)
    a_got = swap(a_sum[32:, :HALF_QKV], CORE)
    b_got = swap(b_sum[32:], CORE)
    small, qkv_grad, up_grad, out_grad = finish(a_sum, b_sum, up_sum, a_got, b_got, up_got)
    gv = small[:, VEC0 : VEC0 + 8].T
    return (
        layer_out,
        tokens_grad,
        gv[0],
        gv[1],
        qkv_grad,
        gv[2],
        gv[3],
        out_grad,
        gv[4],
        gv[5],
        gv[6],
        up_grad,
        small[0, 256:],
        down_sum,
        gv[7],
        small[:, :LONG].T,
    )


def solution(mesh):
    in_specs = (
        P(("dp", "fsdp"), None),
        P(("dp", "fsdp"), None),
        P(),
        P(),
        P(),
        P(("dp", "fsdp")),
        P(("dp", "fsdp")),
        P(("dp", "fsdp"), None),
        P(("dp", "fsdp")),
        P(("dp", "fsdp")),
        P(("dp", "fsdp"), None),
        P(("dp", "fsdp")),
        P(("dp", "fsdp")),
        P(("dp", "fsdp")),
        P(("dp", "fsdp"), None),
        P(("dp", "fsdp")),
        P(("dp", "fsdp"), None),
        P(("dp", "fsdp")),
        P(None, ("dp", "fsdp")),
    )
    out_specs = (
        P(("dp", "fsdp"), None),
        P(("dp", "fsdp"), None),
        P(("dp", "fsdp")),
        P(("dp", "fsdp")),
        P(("dp", "fsdp"), None),
        P(("dp", "fsdp")),
        P(("dp", "fsdp")),
        P(("dp", "fsdp"), None),
        P(("dp", "fsdp")),
        P(("dp", "fsdp")),
        P(("dp", "fsdp")),
        P(("dp", "fsdp"), None),
        P(("dp", "fsdp")),
        P(("dp", "fsdp"), None),
        P(("dp", "fsdp")),
        P(None, ("dp", "fsdp")),
    )
    eight_by_four = mesh.shape["dp"] == 8 and mesh.shape["fsdp"] == 4
    return jax.shard_map(
        fast_on_device if eight_by_four else on_device, mesh=mesh, in_specs=in_specs, out_specs=out_specs, check_vma=False
    )
```
